32 devices in a mesh: dp: 8 (over z, x), ctx: 4 (over y, core).
Axes of the slice: x: 2, y: 2, z: 4, core: 2. Of those that a mesh axis runs over, the one named last changes fastest.
Arguments:
- tokens: bfloat16 [16, 2048, 768], P('dp', 'ctx'), may hold values from -6 to 6
- cotangent: bfloat16 [16, 2048, 768], P('dp', 'ctx'), may hold values from -6 to 6
- lengths: int32 [16], P('dp'), may hold values from 1 to 2048, as said below
- adapter_ids: int32 [16], P('dp'), may hold values from 0 to 7
- norm_gain: float32 [768], replicated, may hold values from 0.5 to 1.5
- w_in: bfloat16 [768, 3352], P('dp'), may hold values from -0.21875 to 0.21875
- conv_weight: float32 [4, 1792], replicated, may hold values from -3 to 3
- conv_bias: float32 [1792], replicated, may hold values from -1.5 to 1.5
- dt_bias: float32 [24], replicated, may hold values from -7 to -2
- a_log: float32 [24], replicated, may hold values from 0 to 1.5
- skip_scale: float32 [24], replicated, may hold values from 0.5 to 1.5
- inner_gain: float32 [1536], replicated, may hold values from 0.5 to 1.5
- w_out: bfloat16 [1536, 768], P('dp'), may hold values from -0.15625 to 0.15625
- in_a: bfloat16 [8, 768, 16], replicated, may hold values from -0.21875 to 0.21875
- in_b: bfloat16 [8, 16, 3072], replicated, may hold values from -1.5 to 1.5
- out_a: bfloat16 [8, 1536, 16], replicated, may hold values from -0.15625 to 0.15625
- out_b: bfloat16 [8, 16, 768], replicated, may hold values from -1.5 to 1.5
Outputs:
- output: bfloat16 [16, 2048, 768], P('dp', 'ctx')
- input_grad: float32 [16, 2048, 768], P('dp', 'ctx')
- grad_in_a: float32 [8, 768, 16], P(None, 'dp')
- grad_in_b: float32 [8, 16, 3072], P(None, None, 'dp')
- grad_out_a: float32 [8, 1536, 16], P(None, 'dp')
- grad_out_b: float32 [8, 16, 768], P(None, None, 'dp')
The draws below stay inside these ranges and needn't reach their ends.
Inputs may be any that keep to these rules, and one draw needn't show every extreme that they name: `lengths`: in each aligned group of 2 sequences (those of one index of dp) one sequence, drawn from the seed, has length 2048; the others at least 512.
All inputs are finite; a program needn't handle non-finite values.
Results may differ from the reference program's by a relative error of at most 0.0081.
Values may be sent and summed in bfloat16 or wider, within the bound.
No kernel may reach another device: no remote copies, remote signals or barrier semaphores. Data moves between devices by JAX's collectives and lax.ppermute only.
A program may use at most 256 MiB of HBM per device.

```python
import jax
import jax.numpy as jnp
from jax import lax

D = 768
HEADS = 24
HDIM = 64
NSTATE = 128
INNER = 1536
CONV = 4
BLOCK = 256
RANK = 16
ADAPT = 8
MICRO = 2
CONV_CH = 1792
ZX = 3072
PROJ = 3352
SLOTS = 2048
SEQS = 16


def draw_lengths(key, part):
    key = jax.random.fold_in(key, 11)
    first_key, second_key = jax.random.split(key)
    ragged = jax.random.randint(first_key, (SEQS,), SLOTS // 4, SLOTS + 1)
    chosen = jax.random.randint(second_key, (SEQS // MICRO,), 0, MICRO)
    position = jnp.arange(SEQS)
    longest = position % MICRO == chosen[position // MICRO]
    return jnp.where(longest, SLOTS, ragged).astype(jnp.int32)


def touch_ends(drawn, stream_key, least, top_value):
    longest = drawn.shape.index(max(drawn.shape))
    spots = []
    for shift in (0, 1):
        where = [jax.random.randint(jax.random.fold_in(stream_key, axis), (), 0, length) for axis, length in enumerate(drawn.shape)]
        where[longest] = (where[longest] + shift) % drawn.shape[longest]
        spots.append(tuple(where))
    return drawn.at[spots[0]].set(least).at[spots[1]].set(top_value)


def level_of(own_key, shape, pieces, smallest, largest):
    loudness = 1.0
    for axis_at, parts in pieces:
        heights = jax.random.uniform(jax.random.fold_in(jax.random.fold_in(own_key, 6), axis_at), (parts,), jnp.float32, smallest / len(pieces), largest / len(pieces))
        loudness = loudness * jnp.repeat(jnp.exp(heights), shape[axis_at] // parts).reshape((-1,) + (1,) * (len(shape) - 1 - axis_at))
    return loudness


def centred(stream_key, extent, width, most, pieces=(), kind=jnp.bfloat16):
    array = jax.random.normal(stream_key, extent, jnp.float32) * width
    if len(pieces) > 0:
        array = level_of(stream_key, extent, pieces, -0.22, 0.18) * array
    return jnp.clip(array, min=-most, max=most).astype(kind)


def setup_inputs(seed: int = 0) -> dict:
    key_list = jax.random.split(jax.random.key(seed), 18)
    return {
        "tokens": centred(key_list[0], (SEQS, SLOTS, D), 1.0, 6.0, ((0, 8), (1, 4))),
        "cotangent": centred(key_list[1], (SEQS, SLOTS, D), 1.0, 6.0, ((0, 8), (1, 4))),
        "lengths": draw_lengths(jax.random.fold_in(key_list[17], 71), 0),
        "adapter_ids": touch_ends(jax.random.randint(key_list[3], (SEQS,), 0, ADAPT), jax.random.fold_in(key_list[3], 1), 0, ADAPT - 1).astype(jnp.int32),
        "norm_gain": jnp.clip(1.0 + 0.1 * jax.random.normal(key_list[4], (D,), jnp.float32), 0.5, 1.5),
        "w_in": centred(key_list[5], (D, PROJ), D ** -0.5, 0.21875, ((0, 8),)),
        "conv_weight": centred(key_list[6], (CONV, CONV_CH), CONV ** -0.5, 3.0, (), jnp.float32),
        "conv_bias": centred(key_list[7], (CONV_CH,), 0.3, 1.5, (), jnp.float32),
        "dt_bias": jnp.clip(jax.random.uniform(key_list[8], (HEADS,), jnp.float32, -7.0, -2.0), -7.0, -2.0),
        "a_log": jnp.clip(jax.random.uniform(key_list[9], (HEADS,), jnp.float32, 0.0, 1.5), 0.0, 1.5),
        "skip_scale": jnp.clip(jax.random.uniform(key_list[10], (HEADS,), jnp.float32, 0.5, 1.5), 0.5, 1.5),
        "inner_gain": jnp.clip(1.0 + 0.1 * jax.random.normal(key_list[11], (INNER,), jnp.float32), 0.5, 1.5),
        "w_out": centred(key_list[12], (INNER, D), INNER ** -0.5, 0.15625, ((0, 8),)),
        "in_a": centred(key_list[13], (ADAPT, D, RANK), D ** -0.5, 0.21875),
        "in_b": centred(key_list[14], (ADAPT, RANK, ZX), RANK ** -0.5, 1.5),
        "out_a": centred(key_list[15], (ADAPT, INNER, RANK), INNER ** -0.5, 0.15625),
        "out_b": centred(key_list[16], (ADAPT, RANK, D), RANK ** -0.5, 1.5),
    }


epsilon = 1e-05
precise = lax.Precision.HIGHEST

@jax.custom_vjp
def low(v):
    return lax.optimization_barrier(v.astype(jnp.bfloat16)).astype(jnp.float32)

@jax.custom_vjp
def low_back(v):
    return v

def low_keep(v):
    return (low(v), None)

def low_pass(kept, grad):
    return (grad,)

def back_keep(v):
    return (v, None)

def back_low(kept, grad):
    return (low(grad),)
low.defvjp(low_keep, low_pass)
low_back.defvjp(back_keep, back_low)

def matmul(left, right):
    return jnp.dot(left, right, precision=precise, preferred_element_type=jnp.float32)

def conv_silu(extended, conv_weight, conv_bias):
    length_out = extended.shape[0] - conv_weight.shape[0] + 1
    summed = conv_bias[None, :] + conv_weight[0][None, :] * extended[:length_out]
    for offset in range(1, conv_weight.shape[0]):
        summed = summed + conv_weight[offset][None, :] * extended[offset:offset + length_out]
    return jax.nn.silu(summed)

def block_logs(step_dt, a_rate):
    blocks = step_dt.shape[0] // BLOCK
    return jnp.cumsum((step_dt * a_rate[None, :]).reshape(blocks, BLOCK, HEADS), axis=1)

def block_terms(ssm_x, coef_b, step_dt, a_rate):
    blocks = ssm_x.shape[0] // BLOCK
    cum_log = block_logs(step_dt, a_rate)
    to_end = jnp.exp(cum_log[:, -1:, :] - cum_log) * step_dt.reshape(blocks, BLOCK, HEADS)
    states = jnp.einsum('cqh,cqn,cqhp->chpn', to_end, coef_b.reshape(blocks, BLOCK, NSTATE), ssm_x.reshape(blocks, BLOCK, HEADS, HDIM), precision=precise)
    return (states, jnp.exp(cum_log[:, -1, :]))

def block_outputs(ssm_x, coef_b, coef_c, step_dt, a_rate, states, totals, h_in):
    blocks = ssm_x.shape[0] // BLOCK

    def advance(carried, block_item):
        return (block_item[1][:, None, None] * carried + block_item[0], carried)
    _, incoming = lax.scan(advance, h_in, (states, totals))
    cum_log = block_logs(step_dt, a_rate)
    b_blocks = coef_b.reshape(blocks, BLOCK, NSTATE)
    c_blocks = coef_c.reshape(blocks, BLOCK, NSTATE)
    x_blocks = (ssm_x * step_dt[:, :, None]).reshape(blocks, BLOCK, HEADS, HDIM)
    scores = jnp.einsum('cqn,csn->cqs', c_blocks, b_blocks, precision=precise)
    log_heads = jnp.transpose(cum_log, (0, 2, 1))
    gaps = log_heads[:, :, :, None] - log_heads[:, :, None, :]
    causal = jnp.arange(BLOCK)[:, None] >= jnp.arange(BLOCK)[None, :]
    weights = jnp.exp(jnp.where(causal, gaps, -1e+30)) * scores[:, None]
    inside = jnp.einsum('chqs,cshp->cqhp', weights, x_blocks, precision=precise)
    from_state = jnp.einsum('cqn,chpn->cqhp', c_blocks, incoming, precision=precise)
    from_state = from_state * jnp.exp(cum_log)[:, :, :, None]
    return (inside + from_state).reshape(ssm_x.shape[0], HEADS * HDIM)

def mixer_tail(y_ssm, ssm_x, gate_in, skip_scale, inner_gain):
    with_skip = y_ssm + (ssm_x * skip_scale[None, :, None]).reshape(y_ssm.shape)
    gated = with_skip * jax.nn.silu(gate_in)
    return gated * lax.rsqrt(lax.optimization_barrier(jnp.mean(gated * gated, -1, keepdims=True)) + epsilon) * inner_gain

def sequence_forward(x_rows, length, adapter, tables, frozen):
    norm_gain, w_in, conv_weight, conv_bias, dt_bias, a_log, skip_scale, inner_gain, w_out = frozen
    table_ia, table_ib, table_oa, table_ob = tables
    normed = low(x_rows * lax.rsqrt(lax.optimization_barrier(jnp.mean(x_rows * x_rows, -1, keepdims=True)) + epsilon) * norm_gain)
    latent = low_back(low(matmul(normed, table_ia[adapter])))
    projected = matmul(normed, w_in)
    projected = jnp.concatenate([projected[:, :ZX] + matmul(latent, table_ib[adapter]), projected[:, ZX:]], axis=1)
    projected = low_back(projected)
    gate_in = projected[:, :INNER]
    xbc_low = low(projected[:, INNER:INNER + CONV_CH])
    dt_raw = projected[:, INNER + CONV_CH:]
    extended = jnp.concatenate([jnp.zeros((CONV - 1, CONV_CH), jnp.float32), xbc_low], axis=0)
    activated = conv_silu(extended, conv_weight, conv_bias)
    ssm_x = activated[:, :INNER].reshape(-1, HEADS, HDIM)
    coef_b = activated[:, INNER:INNER + NSTATE]
    coef_c = activated[:, INNER + NSTATE:]
    step_dt = jax.nn.softplus(dt_raw + dt_bias[None, :])
    a_rate = -jnp.exp(a_log)
    states, totals = block_terms(ssm_x, coef_b, step_dt, a_rate)
    h_zero = jnp.zeros((HEADS, HDIM, NSTATE), jnp.float32)
    y_ssm = block_outputs(ssm_x, coef_b, coef_c, step_dt, a_rate, states, totals, h_zero)
    hidden = low(mixer_tail(y_ssm, ssm_x, gate_in, skip_scale, inner_gain))
    latent_out = low_back(low(matmul(hidden, table_oa[adapter])))
    mixed = matmul(hidden, w_out) + matmul(latent_out, table_ob[adapter])
    valid = (jnp.arange(x_rows.shape[0]) < length).astype(jnp.float32)[:, None]
    return valid * (x_rows + mixed)

def reference(tokens, cotangent, lengths, adapter_ids, norm_gain, w_in, conv_weight, conv_bias, dt_bias, a_log, skip_scale, inner_gain, w_out, in_a, in_b, out_a, out_b):
    frozen = (norm_gain.astype(jnp.float32), w_in.astype(jnp.float32), conv_weight.astype(jnp.float32), conv_bias.astype(jnp.float32), dt_bias.astype(jnp.float32), a_log.astype(jnp.float32), skip_scale.astype(jnp.float32), inner_gain.astype(jnp.float32), w_out.astype(jnp.float32))
    sequence = jax.checkpoint(sequence_forward)

    def forward(x_all, table_ia, table_ib, table_oa, table_ob):
        tables = (table_ia, table_ib, table_oa, table_ob)

        def one_sequence(seq_item):
            return sequence(seq_item[0], seq_item[1], seq_item[2], tables, frozen)
        return lax.map(one_sequence, (x_all, lengths, adapter_ids))
    result, pullback = jax.vjp(forward, tokens.astype(jnp.float32), in_a.astype(jnp.float32), in_b.astype(jnp.float32), out_a.astype(jnp.float32), out_b.astype(jnp.float32))
    gradients = pullback(cotangent.astype(jnp.float32))
    return (result.astype(jnp.bfloat16), gradients[0], gradients[1], gradients[2], gradients[3], gradients[4])
```

```python
import functools

import jax
import jax.numpy as jnp
from jax import lax
from jax.experimental import pallas as pl
from jax.experimental.pallas import tpu as pltpu
from jax.sharding import PartitionSpec as P

HEADS = 24
HDIM = 64
NSTATE = 128
INNER = 1536
CONV_CH = 1792
ZX = 3072
DM = 768
RANK = 16
CHUNK = 128
TILE = 256
RIM = 16
GROUP = 32
LANES = 128
VMEM_LIMIT = 60 * 1024 * 1024

epsilon = 1e-05
bf16 = jnp.bfloat16
f32 = jnp.float32


def dot(left, right):
    return jnp.dot(left, right, preferred_element_type=f32)


def dot_t(left, right):
    return lax.dot_general(
        left, right, (((1,), (1,)), ((), ())), preferred_element_type=f32
    )


def dot_precise(left, right):
    return jnp.dot(
        left, right, preferred_element_type=f32, precision=lax.Precision.HIGHEST
    )


def parts_of(v):
    lane = lax.broadcasted_iota(jnp.int32, v.shape, 1)
    high = v.astype(bf16).astype(f32)
    rest = v - high
    middle = rest.astype(bf16).astype(f32)
    kept = jnp.where(lane < GROUP, high, jnp.where(lane < 2 * GROUP, middle, rest - middle))
    return jnp.where(lane < 3 * GROUP, kept, 0.0).astype(bf16)


def causal(rows):
    t = lax.broadcasted_iota(jnp.int32, (rows, rows), 0)
    s = lax.broadcasted_iota(jnp.int32, (rows, rows), 1)
    return t >= s


def lane_tile(t, width=TILE):
    return pl.ds(t * width, width)


def norm_kernel(ids, x_ref, rim_ref, gain_ref, a_ref, nrm_ref, nrim_ref, lat_ref, lrim_ref):
    def normed(x):
        x = x.astype(f32)
        mean = jnp.mean(x * x, -1, keepdims=True)
        return (x * lax.rsqrt(mean + epsilon) * gain_ref[...]).astype(bf16)

    rows = x_ref.shape[1]
    strip = 64

    def body(i, carry):
        r = pl.ds(pl.multiple_of(i * strip, strip), strip)
        nrm_ref[0, r, :] = normed(x_ref[0, r, :])
        return carry

    lax.fori_loop(0, rows // strip, body, 0)
    nrim_ref[0] = normed(rim_ref[0])
    lat_ref[0] = dot(nrm_ref[0], a_ref[0]).astype(bf16)
    lrim_ref[0] = dot(nrim_ref[0], a_ref[0]).astype(bf16)


def norm_call(ids, tokens, rim, gain, in_a):
    seqs, rows, _ = tokens.shape
    block = lambda *shape: pl.BlockSpec((1,) + shape, lambda s, ids: (s, 0, 0))
    return pl.pallas_call(
        norm_kernel,
        grid_spec=pltpu.PrefetchScalarGridSpec(
            num_scalar_prefetch=1,
            grid=(seqs,),
            in_specs=[
                block(rows, DM),
                block(RIM, DM),
                pl.BlockSpec((1, DM), lambda s, ids: (0, 0)),
                pl.BlockSpec((1, DM, RANK), lambda s, ids: (ids[s], 0, 0)),
            ],
            out_specs=[block(rows, DM), block(RIM, DM), block(rows, RANK), block(RIM, RANK)],
        ),
        out_shape=[
            jax.ShapeDtypeStruct((seqs, rows, DM), bf16),
            jax.ShapeDtypeStruct((seqs, RIM, DM), bf16),
            jax.ShapeDtypeStruct((seqs, rows, RANK), bf16),
            jax.ShapeDtypeStruct((seqs, RIM, RANK), bf16),
        ],
        compiler_params=pltpu.CompilerParams(vmem_limit_bytes=VMEM_LIMIT),
        name="norm",
    )(ids, tokens, rim, gain, in_a)


def front_kernel(
    ids, nrm_ref, nrim_ref, lat_ref, lrim_ref, wx_ref, wdt_ref, bx_ref, cw_ref, cb_ref, dtb_ref,
    rate_ref, expand_ref, act_ref, dact_ref, dt_ref, cum_ref, sig_ref, pay_ref,
    nrm_s, lat_s, xs, bt_s, w_s,
):
    rows = nrm_ref.shape[1]
    nrm_s[0:RIM, :] = nrim_ref[0]
    nrm_s[RIM:, :] = nrm_ref[0]
    lat_s[0:RIM, :] = lrim_ref[0]
    lat_s[RIM:, :] = lat_ref[0]
    raw = dot(nrm_ref[0], wdt_ref[...]) + dtb_ref[...]
    step = jnp.maximum(raw, 0.0) + jnp.log1p(jnp.exp(-jnp.abs(raw)))
    dt_ref[...] = step
    sig_ref[...] = 1.0 / (1.0 + jnp.exp(-raw))
    logs = step * rate_ref[...]
    lower = causal(CHUNK).astype(f32)
    before = jnp.zeros((1, LANES), f32)
    whole = []
    for c in range(rows // CHUNK):
        r = slice(c * CHUNK, (c + 1) * CHUNK)
        cum = dot_precise(lower, logs[r])
        cum_ref[r, :] = cum
        whole.append(cum + before)
        before = before + cum[CHUNK - 1 : CHUNK]
    for c in range(rows // CHUNK):
        r = slice(c * CHUNK, (c + 1) * CHUNK)
        w_s[r, :] = parts_of(jnp.exp(before - whole[c]) * step[r])
    total = parts_of(jnp.broadcast_to(jnp.exp(before), (8, LANES)))

    def tile_in(cols, base, out_cols, state):
        xs[...] = base.astype(bf16).astype(f32)
        weights = [cw_ref[j : j + 1, cols] for j in range(4)]
        bias = cb_ref[:, cols]
        strip = 64
        for i in range(rows // strip):
            at = RIM + i * strip
            pre = bias + weights[0] * xs[at - 3 : at - 3 + strip, :]
            for j in range(1, 4):
                pre = pre + weights[j] * xs[at - 3 + j : at - 3 + j + strip, :]
            gate = 1.0 / (1.0 + jnp.exp(-pre))
            act = pre * gate
            r = slice(i * strip, (i + 1) * strip)
            act_ref[r, out_cols] = act.astype(bf16)
            dact_ref[r, out_cols] = (gate + act * (1.0 - gate)).astype(bf16)

    last = slice(INNER, CONV_CH)
    tile_in(last, dot(nrm_s[...], wx_ref[:, last]), last, None)
    bt_s[...] = jnp.transpose(act_ref[:, INNER : INNER + NSTATE].astype(f32)).astype(bf16)

    def tile_body(t, carry):
        cols = pl.ds(pl.multiple_of(t * TILE, TILE), TILE)
        base = dot(nrm_s[...], wx_ref[:, cols]) + dot(lat_s[...], bx_ref[0, :, cols])
        tile_in(cols, base, cols, None)
        scaled = (act_ref[:, cols].astype(f32) * dot(w_s[...], expand_ref[:, cols])).astype(bf16)
        pay_ref[0:NSTATE, cols] = dot(bt_s[...], scaled).astype(bf16)
        decay = dot(total, expand_ref[:, cols])
        high = decay.astype(bf16)
        row = lax.broadcasted_iota(jnp.int32, (RIM, TILE), 0)
        low = decay - high.astype(f32)
        both = jnp.where(row == 0, high.astype(f32)[0:1], jnp.where(row == 1, low[0:1], 0.0))
        pay_ref[NSTATE:, cols] = both.astype(bf16)
        return carry

    lax.fori_loop(0, INNER // TILE, tile_body, 0)


def front_call(seq, ids, nrm, nrim, lat, lrim, wx, wdt, in_b, conv_w, conv_b, dtb, rate, expand):
    rows = nrm.shape[1]
    block = lambda *shape: pl.BlockSpec((1,) + shape, lambda i, ids: (seq, 0, 0))
    whole = lambda a: pl.BlockSpec(a.shape, lambda i, ids: (0,) * a.ndim)
    outs = [
        ((rows, CONV_CH), bf16),
        ((rows, CONV_CH), bf16),
        ((rows, LANES), f32),
        ((rows, LANES), f32),
        ((rows, LANES), f32),
        ((NSTATE + RIM, INNER), bf16),
    ]
    return pl.pallas_call(
        front_kernel,
        grid_spec=pltpu.PrefetchScalarGridSpec(
            num_scalar_prefetch=1,
            grid=(1,),
            in_specs=[
                block(rows, DM),
                block(RIM, DM),
                block(rows, RANK),
                block(RIM, RANK),
                whole(wx),
                whole(wdt),
                pl.BlockSpec((1, RANK, INNER), lambda i, ids: (ids[seq], 0, 1)),
                whole(conv_w),
                whole(conv_b),
                whole(dtb),
                whole(rate),
                whole(expand),
            ],
            out_specs=[pl.BlockSpec(s, lambda i, ids: (0, 0)) for s, _ in outs],
            scratch_shapes=[
                pltpu.VMEM((rows + RIM, DM), bf16),
                pltpu.VMEM((rows + RIM, RANK), bf16),
                pltpu.VMEM((rows + RIM, TILE), f32),
                pltpu.VMEM((NSTATE, rows), bf16),
                pltpu.VMEM((rows, LANES), bf16),
            ],
        ),
        out_shape=[jax.ShapeDtypeStruct(s, d) for s, d in outs],
        compiler_params=pltpu.CompilerParams(vmem_limit_bytes=VMEM_LIMIT),
        name="front",
    )(ids, nrm, nrim, lat, lrim, wx, wdt, in_b, conv_w, conv_b, dtb, rate, expand)


def decayed(cum, cum_t, heads, masked):
    out = []
    for h in heads:
        gap = jnp.minimum(cum[:, h : h + 1] - cum_t[h : h + 1, :], 0.0)
        out.append(jnp.exp(gap))
    return out


def split_heads(pair):
    lane = lax.broadcasted_iota(jnp.int32, pair.shape, 1)
    zero = jnp.zeros_like(pair)
    first = jnp.where(lane < HDIM, pair, zero)
    second = jnp.where(lane < HDIM, zero, pair)
    return jnp.concatenate([first, second], axis=0)


def middle_kernel(
    ids, lens, x_ref, cot_ref, nrm_ref, lat_ref, act_ref, dt_ref, cum_ref, h_ref, wg_ref, bg_ref, wo_ref,
    oa_ref, ob_ref, skip_ref, gain_ref, expand_ref,
    out_ref, dy_ref, dg_ref, hc_ref, rowt_ref, pay_ref, tb_ref, ta_ref,
    gate_s, y_s, z_s, dh_s, hid_s, r_s, state_s, grad_s, run_s, prod_s, *, seq,
):
    step = pl.program_id(0)
    rows = act_ref.shape[0]
    strip = 16

    @pl.when(step == 0)
    def _():
        state_s[...] = h_ref[...]
        grad_s[...] = jnp.zeros_like(grad_s)
        run_s[...] = jnp.ones_like(run_s)
        tb_ref[...] = jnp.zeros_like(tb_ref)
        ta_ref[...] = jnp.zeros_like(ta_ref)

    gate_s[...] = dot(nrm_ref[0], wg_ref[...]) + dot(lat_ref[0], bg_ref[0])
    position = step * rows + lax.broadcasted_iota(jnp.int32, (rows, 1), 0)
    valid = position < lens[seq]
    g = jnp.where(valid, cot_ref[0], jnp.zeros((), bf16))
    d_lat = dot_t(g, ob_ref[0]).astype(bf16)
    dh_s[...] = dot_t(g, wo_ref[...]) + dot_t(d_lat, oa_ref[0])

    keep = causal(CHUNK)
    for c in range(rows // CHUNK):
        r = slice(c * CHUNK, (c + 1) * CHUNK)
        b = act_ref[r, INNER : INNER + NSTATE]
        cc = act_ref[r, INNER + NSTATE :]
        b_t = jnp.transpose(b.astype(f32)).astype(bf16)
        masked = jnp.where(keep, dot_t(cc, b), 0.0)
        dt = dt_ref[r, :]
        cum = cum_ref[r, :]
        cum_t = jnp.transpose(cum)
        p_ec = parts_of(jnp.exp(cum))
        p_dt = parts_of(dt)
        p_w = parts_of(jnp.exp(cum[CHUNK - 1 : CHUNK] - cum) * dt)
        for t in range(INNER // TILE):
            cols = slice(t * TILE, (t + 1) * TILE)
            ec = dot(p_ec, expand_ref[:, cols])
            x = act_ref[r, cols].astype(f32)
            xd = (x * dot(p_dt, expand_ref[:, cols])).astype(bf16)
            xw = (x * dot(p_w, expand_ref[:, cols])).astype(bf16)
            state = state_s[:, cols]
            low = state.astype(bf16)
            hc_ref[c, :, cols] = low
            far = dot(cc, low) * ec
            state_s[:, cols] = state * ec[CHUNK - 1 : CHUNK] + dot(b_t, xw)
            for k in range(2):
                head = t * 4 + k * 2
                m1, m2 = (
                    (w * masked).astype(bf16) for w in decayed(cum, cum_t, (head, head + 1), masked)
                )
                pair = split_heads(xd[:, k * LANES : (k + 1) * LANES])
                near = dot(jnp.concatenate([m1, m2], axis=1), pair)
                y_s[r, t * TILE + k * LANES : t * TILE + (k + 1) * LANES] = (
                    near + far[:, k * LANES : (k + 1) * LANES]
                )

    def forward_strip(i, carry):
        r = pl.ds(pl.multiple_of(i * strip, strip), strip)
        total = jnp.zeros((strip, LANES), f32)
        for t in range(INNER // TILE):
            cols = slice(t * TILE, (t + 1) * TILE)
            gate = gate_s[r, cols]
            u = y_s[r, cols] + skip_ref[:, cols] * act_ref[r, cols].astype(f32)
            sig = 1.0 / (1.0 + jnp.exp(-gate))
            silu = gate * sig
            z = u * silu
            square = z * z
            total = total + square[:, :LANES] + square[:, LANES:]
            z_s[r, cols] = z
            gate_s[r, cols] = silu
            prod_s[r, cols] = u * (sig + silu * (1.0 - sig))
        root = lax.rsqrt(jnp.sum(total, -1, keepdims=True) / INNER + epsilon)
        r_s[r, :] = jnp.broadcast_to(root, (strip, LANES))
        for t in range(INNER // TILE):
            cols = slice(t * TILE, (t + 1) * TILE)
            hid_s[r, cols] = (z_s[r, cols] * root * gain_ref[:, cols]).astype(bf16)
        return carry

    lax.fori_loop(0, rows // strip, forward_strip, 0)

    hidden = hid_s[...]
    lat_out = dot(hidden, oa_ref[0]).astype(bf16)
    mixed = dot(hidden, wo_ref[...]) + dot(lat_out, ob_ref[0])
    out_ref[...] = jnp.where(valid, x_ref[0].astype(f32) + mixed, 0.0).astype(bf16)
    tb_ref[...] += dot(jnp.transpose(lat_out.astype(f32)).astype(bf16), g)
    ta_ref[...] += dot(jnp.transpose(d_lat.astype(f32)).astype(bf16), hidden)

    def backward_strip(i, carry):
        r = pl.ds(pl.multiple_of(i * strip, strip), strip)
        total = jnp.zeros((strip, LANES), f32)
        for t in range(INNER // TILE):
            cols = slice(t * TILE, (t + 1) * TILE)
            dh = dh_s[r, cols] * gain_ref[:, cols]
            dh_s[r, cols] = dh
            both = dh * z_s[r, cols]
            total = total + both[:, :LANES] + both[:, LANES:]
        root = r_s[r, 0:1]
        back = jnp.sum(total, -1, keepdims=True) * (root * root * root) / INNER
        for t in range(INNER // TILE):
            cols = slice(t * TILE, (t + 1) * TILE)
            dz = dh_s[r, cols] * root - z_s[r, cols] * back
            dy = (dz * gate_s[r, cols]).astype(bf16)
            dy_ref[r, cols] = dy
            dg_ref[r, cols] = (dz * prod_s[r, cols]).astype(bf16)
            hid_s[r, cols] = (dy.astype(f32) * y_s[r, cols]).astype(bf16)
        return carry

    lax.fori_loop(0, rows // strip, backward_strip, 0)
    rowt_ref[...] = dot_t(hid_s[...], expand_ref[...])

    for c in range(rows // CHUNK):
        r = slice(c * CHUNK, (c + 1) * CHUNK)
        c_t = jnp.transpose(act_ref[r, INNER + NSTATE :].astype(f32)).astype(bf16)
        p_ec = parts_of(jnp.exp(cum_ref[r, :]))
        for t in range(INNER // TILE):
            cols = slice(t * TILE, (t + 1) * TILE)
            ec = dot(p_ec, expand_ref[:, cols])
            scaled = (dy_ref[r, cols].astype(f32) * ec).astype(bf16)
            grad_s[:, cols] += run_s[:, cols] * dot(c_t, scaled)
            run_s[:, cols] = run_s[:, cols] * ec[CHUNK - 1 : CHUNK]

    @pl.when(step == pl.num_programs(0) - 1)
    def _():
        pay_ref[0:NSTATE, :] = grad_s[...].astype(bf16)
        decay = run_s[...]
        high = decay.astype(bf16).astype(f32)
        row = lax.broadcasted_iota(jnp.int32, (RIM, INNER), 0)
        both = jnp.where(row == 0, high, jnp.where(row == 1, decay - high, 0.0))
        pay_ref[NSTATE:, :] = both.astype(bf16)


def middle_call(
    seq, ids, lens, tokens, cotangent, nrm, lat, act, dt, cum, h_in, wg, in_b, wo, out_a, out_b, skip,
    gain, expand,
):
    rows = act.shape[0]
    block = 2 * CHUNK
    steps = rows // block
    by_seq = lambda *shape: pl.BlockSpec((1,) + shape, lambda i, *_: (seq, i, 0))
    by_row = lambda *shape: pl.BlockSpec(shape, lambda i, *_: (i, 0))
    whole = lambda a: pl.BlockSpec(a.shape, lambda i, *_: (0,) * a.ndim)
    chosen = lambda a, width: pl.BlockSpec(
        (1, a.shape[1], width), lambda i, ids, lens: (ids[seq], 0, 0)
    )
    outs = [
        ((rows, DM), bf16),
        ((rows, INNER), bf16),
        ((rows, INNER), bf16),
        ((rows // CHUNK, NSTATE, INNER), bf16),
        ((rows, LANES), f32),
        ((NSTATE + RIM, INNER), bf16),
        ((RANK, DM), f32),
        ((RANK, INNER), f32),
    ]
    return pl.pallas_call(
        functools.partial(middle_kernel, seq=seq),
        grid_spec=pltpu.PrefetchScalarGridSpec(
            num_scalar_prefetch=2,
            grid=(steps,),
            in_specs=[
                by_seq(block, DM),
                by_seq(block, DM),
                by_seq(block, DM),
                by_seq(block, RANK),
                by_row(block, CONV_CH),
                by_row(block, LANES),
                by_row(block, LANES),
                whole(h_in),
                whole(wg),
                chosen(in_b, INNER),
                whole(wo),
                chosen(out_a, RANK),
                chosen(out_b, DM),
                whole(skip),
                whole(gain),
                whole(expand),
            ],
            out_specs=[
                by_row(block, DM),
                by_row(block, INNER),
                by_row(block, INNER),
                pl.BlockSpec((block // CHUNK, NSTATE, INNER), lambda i, *_: (i, 0, 0)),
                by_row(block, LANES),
                pl.BlockSpec((NSTATE + RIM, INNER), lambda i, *_: (0, 0)),
                pl.BlockSpec((RANK, DM), lambda i, *_: (0, 0)),
                pl.BlockSpec((RANK, INNER), lambda i, *_: (0, 0)),
            ],
            scratch_shapes=[
                pltpu.VMEM((block, INNER), f32),
                pltpu.VMEM((block, INNER), f32),
                pltpu.VMEM((block, INNER), f32),
                pltpu.VMEM((block, INNER), f32),
                pltpu.VMEM((block, INNER), bf16),
                pltpu.VMEM((block, LANES), f32),
                pltpu.VMEM((NSTATE, INNER), f32),
                pltpu.VMEM((NSTATE, INNER), f32),
                pltpu.VMEM((1, INNER), f32),
                pltpu.VMEM((block, INNER), f32),
            ],
        ),
        out_shape=[jax.ShapeDtypeStruct(s, d) for s, d in outs],
        compiler_params=pltpu.CompilerParams(vmem_limit_bytes=VMEM_LIMIT),
        name="middle",
    )(ids, lens, tokens, cotangent, nrm, lat, act, dt, cum, h_in, wg, in_b, wo, out_a, out_b, skip, gain, expand)


def scan_back_kernel(
    act_ref, dact_ref, dt_ref, cum_ref, sig_ref, rowt_ref, dy_ref, hc_ref, dh_ref, skip_ref, rate_ref,
    cw_ref, expand_ref, dx_ref, draw_ref, tail_ref, head_ref,
    grad_s, end_s, pre_s,
):
    step = pl.program_id(0)
    rows = act_ref.shape[0]
    keep = causal(CHUNK)
    upper = causal(CHUNK).astype(f32).T
    row = lax.broadcasted_iota(jnp.int32, (CHUNK, LANES), 0)
    lane = lax.broadcasted_iota(jnp.int32, (CHUNK, LANES), 1)

    @pl.when(step == 0)
    def _():
        grad_s[...] = dh_ref[...]
        pre_s[rows : rows + 8, :] = jnp.zeros((8, CONV_CH), f32)

    @pl.when(step > 0)
    def _():
        pre_s[rows : rows + 8, :] = pre_s[0:8, :]

    for c in reversed(range(rows // CHUNK)):
        r = slice(c * CHUNK, (c + 1) * CHUNK)
        b = act_ref[r, INNER : INNER + NSTATE]
        cc = act_ref[r, INNER + NSTATE :]
        b_t = jnp.transpose(b.astype(f32)).astype(bf16)
        c_t = jnp.transpose(cc.astype(f32)).astype(bf16)
        masked = jnp.where(keep, dot_t(cc, b), 0.0)
        dt = dt_ref[r, :]
        cum = cum_ref[r, :]
        cum_t = jnp.transpose(cum)
        p_ec = parts_of(jnp.exp(cum))
        p_dt = parts_of(dt)
        p_w = parts_of(jnp.exp(cum[CHUNK - 1 : CHUNK] - cum))
        d_scores = jnp.zeros((CHUNK, CHUNK), f32)
        d_b = jnp.zeros((CHUNK, NSTATE), f32)
        d_c = jnp.zeros((CHUNK, NSTATE), f32)
        col = jnp.zeros((CHUNK, LANES), f32)
        ends = jnp.zeros((8, LANES), f32)
        for t in range(INNER // TILE):
            cols = slice(t * TILE, (t + 1) * TILE)
            spread = expand_ref[:, cols]
            ec = dot(p_ec, spread)
            dts = dot(p_dt, spread)
            w = dot(p_w, spread)
            x = act_ref[r, cols].astype(f32)
            xd = (x * dts).astype(bf16)
            dy = dy_ref[r, cols]
            dye = (dy.astype(f32) * ec).astype(bf16)
            grad = grad_s[:, cols]
            grad_low = grad.astype(bf16)
            state = hc_ref[c, :, cols]
            far = dot(b, grad_low) * w
            xw = (xd.astype(f32) * w).astype(bf16)
            d_b = d_b + dot_t(xw, grad_low)
            d_c = d_c + dot_t(dye, state)
            out_state = state.astype(f32) * ec[CHUNK - 1 : CHUNK] + dot(b_t, xw)
            end = jnp.sum(grad * out_state, axis=0, keepdims=True)
            end_high = end.astype(bf16)
            end_low = (end - end_high.astype(f32)).astype(bf16)
            ends = ends + dot_t(jnp.broadcast_to(end_high, (8, TILE)), spread)
            ends = ends + dot_t(jnp.broadcast_to(end_low, (8, TILE)), spread)
            grad_s[:, cols] = grad * ec[CHUNK - 1 : CHUNK] + dot(c_t, dye)
            near = []
            for k in range(2):
                head = t * 4 + k * 2
                lanes = slice(k * LANES, (k + 1) * LANES)
                w1, w2 = decayed(cum, cum_t, (head, head + 1), masked)
                both = jnp.concatenate([w1 * masked, w2 * masked], axis=1)
                dy_pair = dy[:, lanes]
                d_both = dot_t(dy_pair, split_heads(xd[:, lanes]))
                d_scores = d_scores + w1 * d_both[:, :CHUNK] + w2 * d_both[:, CHUNK:]
                turned = jnp.transpose(both).astype(bf16)
                two = dot(turned, dy_pair)
                near.append(jnp.where(lane < HDIM, two[:CHUNK], two[CHUNK:]))
            d_xd = jnp.concatenate(near, axis=1) + far
            col = col + dot_t((d_xd * x).astype(bf16), spread)
            d_x = d_xd * dts + skip_ref[:, cols] * dy.astype(f32)
            pre_s[r, cols] = d_x * dact_ref[r, cols].astype(f32)
        d_low = jnp.where(keep, d_scores, 0.0)
        d_c = d_c + dot(d_low.astype(bf16), b)
        d_b = d_b + dot(jnp.transpose(d_low).astype(bf16), cc)
        at_b = slice(INNER, INNER + NSTATE)
        at_c = slice(INNER + NSTATE, CONV_CH)
        pre_s[r, at_b] = d_b * dact_ref[r, at_b].astype(f32)
        pre_s[r, at_c] = d_c * dact_ref[r, at_c].astype(f32)
        d_cum = rowt_ref[r, :] - dt * col
        d_cum = d_cum + jnp.where(row == CHUNK - 1, ends[0:1], 0.0)
        d_log = dot_precise(upper, d_cum)
        d_raw = (d_log * rate_ref[...] + col) * sig_ref[r, :]
        draw_ref[r, :] = jnp.where(lane < HEADS, d_raw, 0.0).astype(bf16)

    strip = 64
    for t in range(CONV_CH // TILE):
        cols = slice(t * TILE, (t + 1) * TILE)
        weights = [cw_ref[j : j + 1, cols] for j in range(4)]
        for i in range(rows // strip):
            at = i * strip
            total = weights[3] * pre_s[at : at + strip, cols]
            for j in range(3):
                total = total + weights[j] * pre_s[at + 3 - j : at + 3 - j + strip, cols]
            dx_ref[at : at + strip, cols] = total.astype(bf16)
            if i == rows // strip - 1:
                end = total[strip - RIM :, :]

                @pl.when(step == 0)
                def _(end=end, cols=cols):
                    tail_ref[:, cols] = end

    @pl.when(step == pl.num_programs(0) - 1)
    def _():
        head_ref[...] = pre_s[0:RIM, :].astype(bf16)


def scan_back_call(act, dact, dt, cum, sig, rowt, dy, hc, dh, skip, rate, conv_w, expand):
    rows = act.shape[0]
    block = 2 * CHUNK
    steps = rows // block
    by_row = lambda *shape: pl.BlockSpec(shape, lambda i: (steps - 1 - i, 0))
    whole = lambda a: pl.BlockSpec(a.shape, lambda i: (0,) * a.ndim)
    outs = [
        ((rows, CONV_CH), bf16),
        ((rows, LANES), bf16),
        ((RIM, CONV_CH), f32),
        ((RIM, CONV_CH), bf16),
    ]
    return pl.pallas_call(
        scan_back_kernel,
        grid=(steps,),
        in_specs=[
            by_row(block, CONV_CH),
            by_row(block, CONV_CH),
            by_row(block, LANES),
            by_row(block, LANES),
            by_row(block, LANES),
            by_row(block, LANES),
            by_row(block, INNER),
            pl.BlockSpec((block // CHUNK, NSTATE, INNER), lambda i: (steps - 1 - i, 0, 0)),
            whole(dh),
            whole(skip),
            whole(rate),
            whole(conv_w),
            whole(expand),
        ],
        out_specs=[
            by_row(block, CONV_CH),
            by_row(block, LANES),
            pl.BlockSpec((RIM, CONV_CH), lambda i: (0, 0)),
            pl.BlockSpec((RIM, CONV_CH), lambda i: (0, 0)),
        ],
        scratch_shapes=[
            pltpu.VMEM((NSTATE, INNER), f32),
            pltpu.VMEM((8, INNER), f32),
            pltpu.VMEM((block + 8, CONV_CH), f32),
        ],
        out_shape=[jax.ShapeDtypeStruct(s, d) for s, d in outs],
        compiler_params=pltpu.CompilerParams(vmem_limit_bytes=VMEM_LIMIT),
        name="scan_back",
    )(act, dact, dt, cum, sig, rowt, dy, hc, dh, skip, rate, conv_w, expand)


def input_back_kernel(
    ids, lens, x_ref, cot_ref, nrm_ref, lat_ref, dg_ref, dx_ref, draw_ref, tail_ref, next_ref, cw_ref,
    wg_ref, wx_ref, wdt_ref, ia_ref, ib_ref, gain_ref, out_ref, tb_ref, ta_ref, dx_s, dn_s, *, seq,
):
    rows = dx_ref.shape[0]
    dx_s[...] = dx_ref[...]
    row = lax.broadcasted_iota(jnp.int32, (RIM, CONV_CH), 0)
    later = next_ref[...].astype(f32)
    total = tail_ref[...]
    for back in range(1, 4):
        term = jnp.zeros((1, CONV_CH), f32)
        for j in range(0, 4 - back):
            term = term + cw_ref[j : j + 1, :] * later[3 - back - j : 4 - back - j, :]
        total = total + jnp.where(row == RIM - back, term, 0.0)
    dx_s[rows - RIM :, :] = total.astype(bf16)
    d_gate = dg_ref[...]
    d_xbc = dx_s[...]
    d_x = dx_s[:, :INNER]
    d_lat = (dot_t(d_gate, ib_ref[0, :, :INNER]) + dot_t(d_x, ib_ref[0, :, INNER:])).astype(bf16)
    lat_t = jnp.transpose(lat_ref[0].astype(f32)).astype(bf16)
    tb_ref[:, :INNER] = dot(lat_t, d_gate)
    tb_ref[:, INNER:] = dot(lat_t, d_x)
    ta_ref[...] = dot(jnp.transpose(d_lat.astype(f32)).astype(bf16), nrm_ref[0])
    dn_s[...] = (
        dot_t(d_gate, wg_ref[...])
        + dot_t(d_xbc, wx_ref[...])
        + dot_t(draw_ref[...], wdt_ref[...])
        + dot_t(d_lat, ia_ref[0])
    )
    strip = 32

    def body(i, carry):
        r = pl.ds(pl.multiple_of(i * strip, strip), strip)
        x = x_ref[0, r, :].astype(f32)
        root = lax.rsqrt(jnp.mean(x * x, -1, keepdims=True) + epsilon)
        dn = dn_s[r, :] * gain_ref[...]
        back = jnp.mean(dn * x, -1, keepdims=True) * (root * root * root)
        position = i * strip + lax.broadcasted_iota(jnp.int32, (strip, 1), 0)
        kept = jnp.where(position < lens[seq], cot_ref[0, r, :].astype(f32), 0.0)
        out_ref[r, :] = dn * root - x * back + kept
        return carry

    lax.fori_loop(0, rows // strip, body, 0)


def input_back_call(
    seq, ids, lens, tokens, cotangent, nrm, lat, dg, dx, draw, tail, later, conv_w, wg, wx, wdt, in_a, in_b, gain
):
    rows = dx.shape[0]
    by_seq = lambda *shape: pl.BlockSpec((1,) + shape, lambda i, *_: (seq, 0, 0))
    whole = lambda a: pl.BlockSpec(a.shape, lambda i, *_: (0,) * a.ndim)
    chosen = lambda a: pl.BlockSpec((1,) + a.shape[1:], lambda i, ids, lens: (ids[seq], 0, 0))
    outs = [((rows, DM), f32), ((RANK, ZX), f32), ((RANK, DM), f32)]
    return pl.pallas_call(
        functools.partial(input_back_kernel, seq=seq),
        grid_spec=pltpu.PrefetchScalarGridSpec(
            num_scalar_prefetch=2,
            grid=(1,),
            in_specs=[
                by_seq(rows, DM),
                by_seq(rows, DM),
                by_seq(rows, DM),
                by_seq(rows, RANK),
                whole(dg),
                whole(dx),
                whole(draw),
                whole(tail),
                whole(later),
                whole(conv_w),
                whole(wg),
                whole(wx),
                whole(wdt),
                chosen(in_a),
                chosen(in_b),
                whole(gain),
            ],
            out_specs=[pl.BlockSpec(s, lambda i, *_: (0, 0)) for s, _ in outs],
            scratch_shapes=[pltpu.VMEM((rows, CONV_CH), bf16), pltpu.VMEM((rows, DM), f32)],
        ),
        out_shape=[jax.ShapeDtypeStruct(s, d) for s, d in outs],
        compiler_params=pltpu.CompilerParams(vmem_limit_bytes=VMEM_LIMIT),
        name="input_back",
    )(ids, lens, tokens, cotangent, nrm, lat, dg, dx, draw, tail, later, conv_w, wg, wx, wdt, in_a, in_b, gain)


def shifted(value, axis, steps):
    count = lax.axis_size(axis)
    pairs = [(i, i + steps) for i in range(count) if 0 <= i + steps < count]
    return lax.ppermute(value, axis, pairs)


def swapped(value, axis, bit):
    return lax.ppermute(value, axis, [(i, i ^ bit) for i in range(lax.axis_size(axis))])


def unpacked(payload):
    state = payload[:NSTATE].astype(f32)
    decay = payload[NSTATE : NSTATE + 1].astype(f32) + payload[NSTATE + 1 : NSTATE + 2].astype(f32)
    return state, decay


def packed(state, decay):
    high = decay.astype(bf16)
    low = (decay - high.astype(f32)).astype(bf16)
    rest = jnp.zeros((RIM - 2, INNER), bf16)
    return jnp.concatenate([state.astype(bf16), high, low, rest], axis=0)


def joined(first, second):
    return second[1] * first[0] + second[0], first[1] * second[1]


def entering(payload, reverse):
    count = lax.axis_size("ctx")
    place = lax.axis_index("ctx")
    sign = -1 if reverse else 1
    late = (place % 2 == 0) if reverse else (place % 2 == 1)
    own = unpacked(payload)
    other = unpacked(swapped(payload, "ctx", 1))
    first = jax.tree.map(lambda a, b: jnp.where(late, a, b), other, own)
    second = jax.tree.map(lambda a, b: jnp.where(late, a, b), own, other)
    both = joined(first, second)
    chips = count // 2
    before = unpacked(shifted(packed(*both), "ctx", 2 * sign))
    step, run = 1, None
    while 2 * step < chips + 1 and step * 2 < chips:
        run = joined(before, both) if run is None else run
        far = unpacked(shifted(packed(*run), "ctx", 4 * step * sign))
        before = joined(far, before)
        run = joined(far, run)
        step *= 2
    return jnp.where(late, other[1] * before[0] + other[0], before[0])


def shards(
    tokens, cotangent, lengths, adapter_ids, norm_gain, w_in, conv_weight, conv_bias, dt_bias, a_log,
    skip_scale, inner_gain, w_out, in_a, in_b, out_a, out_b,
):
    seqs, slots, _ = tokens.shape
    owners = lax.axis_size("dp")
    ids = adapter_ids
    lens = jnp.clip(lengths - lax.axis_index("ctx") * slots, 0, slots).astype(jnp.int32)

    def grouped(row):
        padded = jnp.pad(row.reshape(-1, HEADS), ((0, 0), (0, GROUP - HEADS)))
        return jnp.tile(padded, (1, LANES // GROUP))

    rate = grouped(-jnp.exp(a_log))
    dtb = grouped(dt_bias)
    lane = jnp.arange(LANES)[:, None]
    head = jnp.arange(INNER)[None, :] // HDIM
    expand = ((lane % GROUP == head) & (lane < 3 * GROUP)).astype(bf16)
    skip = jnp.repeat(skip_scale, HDIM)[None, :]
    gain = inner_gain[None, :]
    n_gain = norm_gain[None, :]
    conv_b = conv_bias[None, :]

    gate_cols, rest = w_in[:, :INNER], w_in[:, INNER:]
    rest = jnp.pad(rest, ((0, 0), (0, 15 * LANES - rest.shape[1])))
    full_rest = lax.all_gather(rest, "dp", axis=0, tiled=True)
    full_gate = lax.all_gather(gate_cols, "dp", axis=0, tiled=True)
    full_out = lax.all_gather(w_out, "dp", axis=0, tiled=True)
    wx = full_rest[:, :CONV_CH]
    wdt = grouped(full_rest[:, CONV_CH : CONV_CH + HEADS])

    rim = shifted(tokens[:, slots - RIM :], "ctx", 1)
    nrm, nrim, lat, lrim = norm_call(ids, tokens, rim, n_gain, in_a)
    fronts = [
        front_call(s, ids, nrm, nrim, lat, lrim, wx, wdt, in_b, conv_weight, conv_b, dtb, rate, expand)
        for s in range(seqs)
    ]
    states = [entering(front[5], False) for front in fronts]
    middles = [
        middle_call(
            s, ids, lens, tokens, cotangent, nrm, lat, fronts[s][0], fronts[s][2], fronts[s][3], states[s],
            full_gate, in_b, full_out, out_a, out_b, skip, gain, expand,
        )
        for s in range(seqs)
    ]
    grads = [entering(mid[5], True) for mid in middles]
    backs = []
    for s in range(seqs):
        act, dact, dt, cum, sig, _ = fronts[s]
        _, dy, _, hc, rowt, _, _, _ = middles[s]
        backs.append(
            scan_back_call(act, dact, dt, cum, sig, rowt, dy, hc, grads[s], skip, rate, conv_weight, expand)
        )
    nexts = [shifted(back[3], "ctx", -1) for back in backs]
    lasts = [
        input_back_call(
            s, ids, lens, tokens, cotangent, nrm, lat, middles[s][2], backs[s][0], backs[s][1], backs[s][2],
            nexts[s], conv_weight, full_gate, wx, wdt, in_a, in_b, n_gain,
        )
        for s in range(seqs)
    ]

    def by_owner(terms):
        stacked = jnp.stack(terms)
        return stacked.reshape(seqs, RANK, owners, -1).transpose(2, 0, 1, 3)

    kinds = (
        [last[2] for last in lasts],
        [last[1] for last in lasts],
        [mid[7] for mid in middles],
        [mid[6] for mid in middles],
    )
    pieces = [by_owner(terms) for terms in kinds]
    widths = [piece.shape[-1] for piece in pieces]
    sent = jnp.concatenate(pieces, axis=-1).astype(bf16)
    got = lax.all_to_all(sent, "dp", 0, 0)
    every = lax.all_gather(adapter_ids, "dp", axis=0, tiled=True)
    chosen = (every[None, :] == jnp.arange(in_a.shape[0])[:, None]).astype(f32)
    flat = got.reshape(owners * seqs, -1).astype(f32)
    mine = jnp.sum(chosen[:, :, None] * flat[None], axis=1)
    bit = 1
    while bit < lax.axis_size("ctx"):
        mine = mine + swapped(mine, "ctx", bit)
        bit *= 2
    mine = mine.reshape(in_a.shape[0], RANK, -1)
    cuts = [sum(widths[:k]) for k in range(5)]
    g_ia, g_ib, g_oa, g_ob = (mine[:, :, cuts[k] : cuts[k + 1]] for k in range(4))
    return (
        jnp.stack([mid[0] for mid in middles]),
        jnp.stack([last[0] for last in lasts]),
        jnp.swapaxes(g_ia, 1, 2),
        g_ib,
        jnp.swapaxes(g_oa, 1, 2),
        g_ob,
    )


def solution(mesh):
    split = P("dp", "ctx", None)
    return jax.shard_map(
        shards,
        mesh=mesh,
        in_specs=(
            split, split, P("dp"), P("dp"), P(), P("dp", None), P(), P(), P(), P(), P(), P(),
            P("dp", None), P(), P(), P(), P(),
        ),
        out_specs=(
            split, split, P(None, "dp", None), P(None, None, "dp"), P(None, "dp", None), P(None, None, "dp"),
        ),
        check_vma=False,
    )
```

```python
import functools

import jax
import jax.numpy as jnp
from jax import lax
from jax.experimental import pallas as pl
from jax.experimental.pallas import tpu as pltpu
from jax.sharding import PartitionSpec as P

HEADS = 24
HDIM = 64
NSTATE = 128
INNER = 1536
CONV_CH = 1792
ZX = 3072
DM = 768
RANK = 16
ADAPT = 8
CHUNK = 128
TILE = 256
RIM = 16
GROUP = 32
LANES = 128
VMEM_LIMIT = 60 * 1024 * 1024

epsilon = 1e-05
bf16 = jnp.bfloat16
f32 = jnp.float32


def dot(left, right):
    return jnp.dot(left, right, preferred_element_type=f32)


def dot_t(left, right):
    return lax.dot_general(
        left, right, (((1,), (1,)), ((), ())), preferred_element_type=f32
    )


def dot_precise(left, right):
    return jnp.dot(
        left, right, preferred_element_type=f32, precision=lax.Precision.HIGHEST
    )


def parts_of(v):
    lane = lax.broadcasted_iota(jnp.int32, v.shape, 1)
    high = v.astype(bf16).astype(f32)
    rest = v - high
    middle = rest.astype(bf16).astype(f32)
    kept = jnp.where(lane < GROUP, high, jnp.where(lane < 2 * GROUP, middle, rest - middle))
    return jnp.where(lane < 3 * GROUP, kept, 0.0).astype(bf16)


def causal(rows):
    t = lax.broadcasted_iota(jnp.int32, (rows, rows), 0)
    s = lax.broadcasted_iota(jnp.int32, (rows, rows), 1)
    return t >= s


def sigmoid(v):
    return 0.5 * jnp.tanh(0.5 * v) + 0.5


def turned(v):
    return jnp.transpose(v.astype(f32)).astype(bf16)


class Operand:
    def __init__(self, arrays, shape, copies):
        self.arrays, self.shape, self.copies = list(arrays), tuple(shape), copies


def view(array, pick=None, shape=None):
    pick = pick or (lambda scalars, ref: ref)
    return Operand([array], shape or array.shape, lambda scalars, refs, to: [(pick(scalars, refs[0]), to)])


def streamed(kernel, name, scalars, operands, outs, scratch, micros, parts=1, shared=None):
    arrays = [array for operand in operands for array in operand.arrays]
    n_scalar, n_array, n_in, n_out = len(scalars), len(arrays), len(operands), len(outs)
    kinds = [operand.arrays[0].dtype for operand in operands]
    slots, slot, begun = shared or (None, None, None)
    n_begun = 0 if begun is None else 1

    def body(*refs):
        refs = list(refs)
        take = lambda n: [refs.pop(0) for _ in range(n)]
        smem, sources, _, targets, ins, results = (
            take(n) for n in (n_scalar, n_array, n_begun, n_out, n_in, n_out)
        )
        if shared:
            targets[0] = targets[0].at[slot]
        in_sems, out_sems = refs.pop(-2), refs.pop(-1)
        waiting = {}
        for k, operand in enumerate(operands):
            mine = [sources.pop(0) for _ in operand.arrays]
            for source, target in operand.copies(smem, mine, ins[k]):
                pltpu.make_async_copy(source, target, in_sems.at[k]).start()
            waiting[id(ins[k])] = pltpu.make_async_copy(ins[k], ins[k], in_sems.at[k])

        def ready(*wanted):
            for ref in wanted:
                if id(ref) in waiting:
                    waiting.pop(id(ref)).wait()

        pieces = {}

        def outgoing(k, part, whole_array):
            if whole_array:
                return pltpu.make_async_copy(results[k], targets[k], out_sems.at[k, 0])
            rows = results[k].shape[0] // parts
            at = pl.ds(pl.multiple_of(part * rows, rows), rows)
            return pltpu.make_async_copy(results[k].at[at], targets[k].at[at], out_sems.at[k, part])

        def send(ref, part=None):
            k = [id(result) for result in results].index(id(ref))
            pieces[k] = part is None
            outgoing(k, part, part is None).start()

        kernel(*smem, *ins, *results, *refs, ready=ready, send=send)
        ready(*ins)
        for k, whole_array in pieces.items():
            for part in range(1 if whole_array else parts):
                outgoing(k, part, whole_array).wait()

    anywhere = pl.BlockSpec(memory_space=pl.ANY)
    full = [((slots,) + shape if shared and k == 0 else shape, kind) for k, (shape, kind) in enumerate(outs)]
    return pl.pallas_call(
        body,
        in_specs=[pl.BlockSpec(memory_space=pltpu.SMEM)] * n_scalar + [anywhere] * (n_array + n_begun),
        out_specs=[anywhere] * n_out,
        out_shape=[jax.ShapeDtypeStruct(shape, kind) for shape, kind in full],
        scratch_shapes=[pltpu.VMEM(operand.shape, kind) for operand, kind in zip(operands, kinds)]
        + [pltpu.VMEM(shape, kind) for shape, kind in outs]
        + scratch
        + [pltpu.SemaphoreType.DMA((n_in,)), pltpu.SemaphoreType.DMA((n_out, parts))],
        input_output_aliases={n_scalar + n_array: 0} if n_begun else {},
        compiler_params=pltpu.CompilerParams(vmem_limit_bytes=VMEM_LIMIT),
        cost_estimate=pl.CostEstimate(flops=micros * 1000000000, bytes_accessed=1000000, transcendentals=0),
        name=name,
    )(*scalars, *arrays, *([begun] if n_begun else []))


def of_sequence(array, seq):
    return view(array, lambda scalars, ref: ref.at[seq], array.shape[1:])


def of_adapter(array, seq, start=0, width=None):
    width = width or array.shape[2]
    pick = lambda scalars, ref: ref.at[scalars[0][seq], :, pl.ds(start, width)]
    return view(array, pick, (array.shape[1], width))


def split_decay(decay):
    high = decay.astype(bf16).astype(f32)
    row = lax.broadcasted_iota(jnp.int32, (RIM, decay.shape[1]), 0)
    return jnp.where(row == 0, high, jnp.where(row == 1, decay - high, 0.0)).astype(bf16)


def decay_of(payload_ref, cols):
    rows = payload_ref[NSTATE:, cols].astype(f32)
    return rows[0:1] + rows[1:2]


def norm_kernel(
    ids, x0_ref, x1_ref, rim_ref, gain_ref, a0_ref, a1_ref, nrm_ref, nrim_ref, lat_ref, lrim_ref, *, ready, send
):
    def normed(x):
        x = x.astype(f32)
        mean = jnp.mean(x * x, -1, keepdims=True)
        return (x * lax.rsqrt(mean + epsilon) * gain_ref[...]).astype(bf16)

    strip = 64
    ready(gain_ref, rim_ref)
    for s, (x_ref, a_ref) in enumerate(((x0_ref, a0_ref), (x1_ref, a1_ref))):
        ready(x_ref, a_ref)
        for i in range(x_ref.shape[0] // strip):
            r = slice(i * strip, (i + 1) * strip)
            nrm_ref[s, r, :] = normed(x_ref[r, :])
        nrim_ref[s] = normed(rim_ref[s])
        lat_ref[s] = dot_t(nrm_ref[s], a_ref[...]).astype(bf16)
        lrim_ref[s] = dot_t(nrim_ref[s], a_ref[...]).astype(bf16)
    for ref in (nrm_ref, nrim_ref, lat_ref, lrim_ref):
        send(ref)


def norm_call(ids, tokens, rim, gain, in_a):
    seqs, rows, _ = tokens.shape
    outs = [
        ((seqs, rows, DM), bf16),
        ((seqs, RIM, DM), bf16),
        ((seqs, rows, RANK), bf16),
        ((seqs, RIM, RANK), bf16),
    ]
    operands = [
        of_sequence(tokens, 0), of_sequence(tokens, 1), view(rim), view(gain), of_adapter(in_a, 0), of_adapter(in_a, 1),
    ]
    return streamed(norm_kernel, "norm", [ids], operands, outs, [], 3)


def front_kernel(
    ids, place, nrm_ref, nrim_ref, lat_ref, lrim_ref, wdt_ref, dtb_ref, rate_ref, cw_ref, cb_ref, wx_ref, bx_ref,
    expand_ref, act_ref, dact_ref, dt_ref, cum_ref, sig_ref, pay_ref,
    nrm_s, lat_s, xs, bt_s, w_s, *, ready, send,
):
    rows = nrm_ref.shape[0]
    ready(nrm_ref, nrim_ref, lat_ref, lrim_ref)
    nrm_s[0:RIM, :] = nrim_ref[...]
    nrm_s[RIM:, :] = nrm_ref[...]
    lat_s[0:RIM, :] = lrim_ref[...]
    lat_s[RIM:, :] = lat_ref[...]
    ready(wdt_ref, dtb_ref, rate_ref)
    raw = dot(nrm_ref[...], wdt_ref[...]) + dtb_ref[...]
    step = jnp.maximum(raw, 0.0) + jnp.log1p(jnp.exp(-jnp.abs(raw)))
    dt_ref[...] = step
    sig_ref[...] = sigmoid(raw)
    logs = step * rate_ref[...]
    lower = causal(CHUNK).astype(f32)
    before = jnp.zeros((1, LANES), f32)
    whole = []
    for c in range(rows // CHUNK):
        r = slice(c * CHUNK, (c + 1) * CHUNK)
        cum = dot_precise(lower, logs[r])
        cum_ref[r, :] = cum
        whole.append(cum + before)
        before = before + cum[CHUNK - 1 : CHUNK]
    for c in range(rows // CHUNK):
        r = slice(c * CHUNK, (c + 1) * CHUNK)
        w_s[r, :] = parts_of(jnp.exp(before - whole[c]) * step[r])
    total = parts_of(jnp.broadcast_to(jnp.exp(before), (8, LANES)))
    for ref in (dt_ref, cum_ref, sig_ref):
        send(ref)
    ready(cw_ref, cb_ref, wx_ref, bx_ref, expand_ref)

    def activate(cols, base):
        xs[...] = base.astype(bf16).astype(f32)
        weights = [cw_ref[j : j + 1, cols] for j in range(4)]
        bias = cb_ref[:, cols]
        strip = 64
        for i in range(rows // strip):
            at = RIM + i * strip
            pre = bias + weights[0] * xs[at - 3 : at - 3 + strip, :]
            for j in range(1, 4):
                pre = pre + weights[j] * xs[at - 3 + j : at - 3 + j + strip, :]
            gate = sigmoid(pre)
            act = pre * gate
            r = slice(i * strip, (i + 1) * strip)
            act_ref[r, cols] = act.astype(bf16)
            dact_ref[r, cols] = (gate + act * (1.0 - gate)).astype(bf16)

    last = slice(INNER, CONV_CH)
    activate(last, dot(nrm_s[...], wx_ref[:, last]))
    bt_s[...] = turned(act_ref[:, INNER : INNER + NSTATE])

    def tile_body(t, carry):
        cols = pl.ds(pl.multiple_of(t * TILE, TILE), TILE)
        activate(cols, dot(nrm_s[...], wx_ref[:, cols]) + dot(lat_s[...], bx_ref[:, cols]))
        scaled = (act_ref[:, cols].astype(f32) * dot(w_s[...], expand_ref[:, cols])).astype(bf16)
        pay_ref[0:NSTATE, cols] = dot(bt_s[...], scaled).astype(bf16)
        pay_ref[NSTATE:, cols] = split_decay(dot(total, expand_ref[:, cols])[0:1])
        return carry

    lax.fori_loop(0, INNER // TILE, tile_body, 0)
    for ref in (pay_ref, act_ref, dact_ref):
        send(ref)


def front_call(seq, ids, place, nrm, nrim, lat, lrim, wx, wdt, in_b, conv_w, conv_b, dtb, rate, expand):
    rows = nrm.shape[1]
    outs = [
        ((rows, CONV_CH), bf16),
        ((rows, CONV_CH), bf16),
        ((rows, LANES), f32),
        ((rows, LANES), f32),
        ((rows, LANES), f32),
        ((NSTATE + RIM, INNER), bf16),
    ]
    scratch = [
        pltpu.VMEM((rows + RIM, DM), bf16),
        pltpu.VMEM((rows + RIM, RANK), bf16),
        pltpu.VMEM((rows + RIM, TILE), f32),
        pltpu.VMEM((NSTATE, rows), bf16),
        pltpu.VMEM((rows, LANES), bf16),
    ]
    operands = [of_sequence(a, seq) for a in (nrm, nrim, lat, lrim)]
    operands += [wdt] + [view(a) for a in (dtb, rate, conv_w, conv_b)] + [wx]
    operands += [of_adapter(in_b, seq, INNER, INNER), view(expand)]
    return streamed(front_kernel, "front", [ids, place], operands, outs, scratch, 13)


def decayed(cum, cum_t, heads):
    out = []
    for h in heads:
        gap = jnp.minimum(cum[:, h : h + 1] - cum_t[h : h + 1, :], 0.0)
        out.append(jnp.exp(gap))
    return out


def split_heads(pair):
    lane = lax.broadcasted_iota(jnp.int32, pair.shape, 1)
    zero = jnp.zeros_like(pair)
    first = jnp.where(lane < HDIM, pair, zero)
    second = jnp.where(lane < HDIM, zero, pair)
    return jnp.concatenate([first, second], axis=0)


def state_in(late, other_ref, before_ref, cols):
    before = before_ref[0:NSTATE, cols].astype(f32)
    joint = decay_of(other_ref, cols) * before + other_ref[0:NSTATE, cols].astype(f32)
    return jnp.where(late == 1, joint, before)


def scan_kernel(
    late, act_ref, dt_ref, cum_ref, expand_ref, other_ref, before_ref, y_ref, hc_ref, state_s, *, ready, send
):
    keep = causal(CHUNK)
    ready(act_ref, dt_ref, cum_ref, expand_ref, other_ref, before_ref)
    for t in range(INNER // TILE):
        cols = slice(t * TILE, (t + 1) * TILE)
        state_s[:, cols] = state_in(late[0], other_ref, before_ref, cols)

    def one_chunk(c, carry):
        r = pl.ds(pl.multiple_of(c * CHUNK, CHUNK), CHUNK)
        b = act_ref[r, INNER : INNER + NSTATE]
        cc = act_ref[r, INNER + NSTATE :]
        b_t = turned(b)
        masked = jnp.where(keep, dot_t(cc, b), 0.0)
        dt = dt_ref[r, :]
        cum = cum_ref[r, :]
        cum_t = jnp.transpose(cum)
        p_ec = parts_of(jnp.exp(cum))
        p_dt = parts_of(dt)
        p_w = parts_of(jnp.exp(cum[CHUNK - 1 : CHUNK] - cum) * dt)
        for t in range(INNER // TILE):
            cols = slice(t * TILE, (t + 1) * TILE)
            ec = dot(p_ec, expand_ref[:, cols])
            x = act_ref[r, cols].astype(f32)
            xd = (x * dot(p_dt, expand_ref[:, cols])).astype(bf16)
            xw = (x * dot(p_w, expand_ref[:, cols])).astype(bf16)
            state = state_s[:, cols]
            low = state.astype(bf16)
            hc_ref[c, :, cols] = low
            far = dot(cc, low) * ec
            state_s[:, cols] = state * ec[CHUNK - 1 : CHUNK] + dot(b_t, xw)
            for k in range(2):
                lanes = slice(k * LANES, (k + 1) * LANES)
                head = t * 4 + k * 2
                weights = [
                    (w * masked).astype(bf16) for w in decayed(cum, cum_t, (head, head + 1))
                ]
                near = dot(jnp.concatenate(weights, axis=1), split_heads(xd[:, lanes]))
                y_ref[r, t * TILE + k * LANES : t * TILE + (k + 1) * LANES] = near + far[:, lanes]
        send(y_ref, c)
        send(hc_ref, c)
        return carry

    lax.fori_loop(0, act_ref.shape[0] // CHUNK, one_chunk, 0)


def scan_call(late, act, dt, cum, other, before, expand):
    rows = act.shape[0]
    chunks = rows // CHUNK
    outs = [((rows, INNER), f32), ((chunks, NSTATE, INNER), bf16)]
    scratch = [pltpu.VMEM((NSTATE, INNER), f32)]
    operands = [view(a) for a in (act, dt, cum, expand, other, before)]
    return streamed(scan_kernel, "scan", [late], operands, outs, scratch, 9, chunks)


def middle_kernel(
    ids, lens, place, nrm_ref, lat_ref, bg_ref, wg_ref, cot_ref, b_ref, a_ref, wo_ref, y_ref, skip_ref, gain_ref,
    act_ref, x_ref, cum_ref, expand_ref,
    out_ref, dy_ref, dg_ref, rowt_ref, pay_ref, tb_ref, ta_ref,
    gate_s, z_s, dh_s, hid_s, prod_s, grad_s, run_s, *, seq, ready, send,
):
    block = gate_s.shape[0]
    steps = act_ref.shape[0] // block
    strip = 16
    grad_s[...] = jnp.zeros_like(grad_s)
    run_s[...] = jnp.ones_like(run_s)
    tb_ref[...] = jnp.zeros_like(tb_ref)
    ta_ref[...] = jnp.zeros_like(ta_ref)
    ready(nrm_ref, lat_ref, bg_ref, wg_ref)

    def one_step(step, first):
        base = pl.multiple_of(step * block, block)
        mine = pl.ds(base, block)
        gate_s[...] = dot(nrm_ref[mine, :], wg_ref[...]) + dot(lat_ref[mine, :], bg_ref[...])
        if first:
            ready(cot_ref, b_ref, a_ref, wo_ref)
        position = base + lax.broadcasted_iota(jnp.int32, (block, 1), 0)
        valid = position < lens[seq]
        g = jnp.where(valid, cot_ref[mine, :], jnp.zeros((), bf16))
        d_lat = dot_t(g, b_ref[...]).astype(bf16)
        dh_s[...] = dot_t(g, wo_ref[...]) + dot(d_lat, a_ref[...])
        if first:
            ready(y_ref, skip_ref, gain_ref, act_ref)

        roots = []
        for i in range(block // strip):
            here = slice(i * strip, (i + 1) * strip)
            r = pl.ds(base + i * strip, strip)
            total = jnp.zeros((strip, LANES), f32)
            for t in range(INNER // TILE):
                cols = slice(t * TILE, (t + 1) * TILE)
                gate = gate_s[here, cols]
                u = y_ref[r, cols] + skip_ref[:, cols] * act_ref[r, cols].astype(f32)
                sig = sigmoid(gate)
                silu = gate * sig
                z = u * silu
                square = z * z
                total = total + square[:, :LANES] + square[:, LANES:]
                z_s[here, cols] = z
                gate_s[here, cols] = silu
                prod_s[here, cols] = u * (sig + silu * (1.0 - sig))
            root = lax.rsqrt(jnp.sum(total, -1, keepdims=True) / INNER + epsilon)
            roots.append(root)
            for t in range(INNER // TILE):
                cols = slice(t * TILE, (t + 1) * TILE)
                hid_s[here, cols] = (z_s[here, cols] * root * gain_ref[:, cols]).astype(bf16)

        if first:
            ready(x_ref, cum_ref, expand_ref)
        hidden = hid_s[...]
        lat_out = dot_t(hidden, a_ref[...]).astype(bf16)
        mixed = dot(hidden, wo_ref[...]) + dot(lat_out, b_ref[...])
        out_ref[mine, :] = jnp.where(valid, x_ref[mine, :].astype(f32) + mixed, 0.0).astype(bf16)
        send(out_ref, step)
        tb_ref[...] += dot(turned(lat_out), g)
        ta_ref[...] += dot(turned(d_lat), hidden)

        for i in range(block // strip):
            here = slice(i * strip, (i + 1) * strip)
            r = pl.ds(base + i * strip, strip)
            total = jnp.zeros((strip, LANES), f32)
            for t in range(INNER // TILE):
                cols = slice(t * TILE, (t + 1) * TILE)
                dh = dh_s[here, cols] * gain_ref[:, cols]
                dh_s[here, cols] = dh
                both = dh * z_s[here, cols]
                total = total + both[:, :LANES] + both[:, LANES:]
            root = roots[i]
            back = jnp.sum(total, -1, keepdims=True) * (root * root * root) / INNER
            for t in range(INNER // TILE):
                cols = slice(t * TILE, (t + 1) * TILE)
                dz = dh_s[here, cols] * root - z_s[here, cols] * back
                dy = (dz * gate_s[here, cols]).astype(bf16)
                dy_ref[r, cols] = dy
                dg_ref[r, cols] = (dz * prod_s[here, cols]).astype(bf16)
                hid_s[here, cols] = (dy.astype(f32) * y_ref[r, cols]).astype(bf16)
        send(dy_ref, step)
        send(dg_ref, step)

        rowt_ref[mine, :] = dot_t(hid_s[...], expand_ref[...])
        send(rowt_ref, step)

        for c in range(block // CHUNK):
            r = pl.ds(base + c * CHUNK, CHUNK)
            c_t = turned(act_ref[r, INNER + NSTATE :])
            p_ec = parts_of(jnp.exp(cum_ref[r, :]))
            for t in range(INNER // TILE):
                cols = slice(t * TILE, (t + 1) * TILE)
                ec = dot(p_ec, expand_ref[:, cols])
                scaled = (dy_ref[r, cols].astype(f32) * ec).astype(bf16)
                grad_s[:, cols] += run_s[:, cols] * dot(c_t, scaled)
                run_s[:, cols] = run_s[:, cols] * ec[CHUNK - 1 : CHUNK]

    for step in range(steps):
        one_step(step, step == 0)
    pay_ref[0:NSTATE, :] = grad_s[...].astype(bf16)
    pay_ref[NSTATE:, :] = split_decay(run_s[...])
    for ref in (pay_ref, tb_ref, ta_ref):
        send(ref)


def middle_call(
    seq, ids, lens, place, begun, tokens, cotangent, nrm, lat, act, cum, y, wg, in_b, wo, out_a, out_b, skip, gain, expand
):
    rows = act.shape[0]
    block = 2 * CHUNK
    outs = [
        ((rows, DM), bf16),
        ((rows, INNER), bf16),
        ((rows, INNER), bf16),
        ((rows, LANES), f32),
        ((NSTATE + RIM, INNER), bf16),
        ((RANK, DM), f32),
        ((RANK, INNER), f32),
    ]
    scratch = [
        pltpu.VMEM((block, INNER), f32),
        pltpu.VMEM((block, INNER), f32),
        pltpu.VMEM((block, INNER), f32),
        pltpu.VMEM((block, INNER), bf16),
        pltpu.VMEM((block, INNER), f32),
        pltpu.VMEM((NSTATE, INNER), f32),
        pltpu.VMEM((1, INNER), f32),
    ]
    operands = [
        of_sequence(nrm, seq), of_sequence(lat, seq), of_adapter(in_b, seq, 0, INNER), wg,
        of_sequence(cotangent, seq), of_adapter(out_b, seq), of_adapter(out_a, seq), wo, view(y), view(skip),
        view(gain), view(act), of_sequence(tokens, seq), view(cum), view(expand),
    ]
    kernel = functools.partial(middle_kernel, seq=seq)
    shared = (tokens.shape[0], seq, begun)
    return streamed(kernel, "middle", [ids, lens, place], operands, outs, scratch, 15, rows // block, shared)


def scan_back_kernel(
    late, act_ref, dact_ref, dt_ref, cum_ref, sig_ref, rowt_ref, dy_ref, hc_ref, other_ref, before_ref,
    skip_ref, rate_ref, cw_ref, expand_ref, dx_ref, draw_ref, tail_ref, head_ref,
    grad_s, pre_s, *, ready, send,
):
    block = pre_s.shape[0] - 8
    steps = act_ref.shape[0] // block
    keep = causal(CHUNK)
    upper = causal(CHUNK).astype(f32).T
    row = lax.broadcasted_iota(jnp.int32, (CHUNK, LANES), 0)
    lane = lax.broadcasted_iota(jnp.int32, (CHUNK, LANES), 1)
    at_b = slice(INNER, INNER + NSTATE)
    at_c = slice(INNER + NSTATE, CONV_CH)
    ready(act_ref, dact_ref, dt_ref, cum_ref, sig_ref, rowt_ref, dy_ref, hc_ref, other_ref, before_ref)
    ready(skip_ref, rate_ref, cw_ref, expand_ref)
    for t in range(INNER // TILE):
        cols = slice(t * TILE, (t + 1) * TILE)
        grad_s[:, cols] = state_in(late[0], other_ref, before_ref, cols)
    pre_s[0:8, :] = jnp.zeros((8, CONV_CH), f32)

    def one_step(turn, carry):
        step = steps - 1 - turn
        base = pl.multiple_of(step * block, block)
        pre_s[block : block + 8, :] = pre_s[0:8, :]
        for c in reversed(range(block // CHUNK)):
            here = slice(c * CHUNK, (c + 1) * CHUNK)
            r = pl.ds(base + c * CHUNK, CHUNK)
            b = act_ref[r, at_b]
            cc = act_ref[r, at_c]
            b_t = turned(b)
            c_t = turned(cc)
            masked = jnp.where(keep, dot_t(cc, b), 0.0)
            dt = dt_ref[r, :]
            cum = cum_ref[r, :]
            cum_t = jnp.transpose(cum)
            p_ec = parts_of(jnp.exp(cum))
            p_dt = parts_of(dt)
            p_w = parts_of(jnp.exp(cum[CHUNK - 1 : CHUNK] - cum))
            d_scores = jnp.zeros((CHUNK, CHUNK), f32)
            d_b = jnp.zeros((CHUNK, NSTATE), f32)
            d_c = jnp.zeros((CHUNK, NSTATE), f32)
            col = jnp.zeros((CHUNK, LANES), f32)
            ends = jnp.zeros((8, LANES), f32)
            for t in range(INNER // TILE):
                cols = slice(t * TILE, (t + 1) * TILE)
                spread = expand_ref[:, cols]
                ec = dot(p_ec, spread)
                dts = dot(p_dt, spread)
                w = dot(p_w, spread)
                x = act_ref[r, cols].astype(f32)
                xd = (x * dts).astype(bf16)
                dy = dy_ref[r, cols]
                dye = (dy.astype(f32) * ec).astype(bf16)
                grad = grad_s[:, cols]
                grad_low = grad.astype(bf16)
                state = hc_ref[step * (block // CHUNK) + c, :, cols]
                far = dot(b, grad_low) * w
                xw = (xd.astype(f32) * w).astype(bf16)
                d_b = d_b + dot_t(xw, grad_low)
                d_c = d_c + dot_t(dye, state)
                out_state = state.astype(f32) * ec[CHUNK - 1 : CHUNK] + dot(b_t, xw)
                end = jnp.sum(grad * out_state, axis=0, keepdims=True)
                end_high = end.astype(bf16)
                end_low = (end - end_high.astype(f32)).astype(bf16)
                ends = ends + dot_t(jnp.broadcast_to(end_high, (8, TILE)), spread)
                ends = ends + dot_t(jnp.broadcast_to(end_low, (8, TILE)), spread)
                grad_s[:, cols] = grad * ec[CHUNK - 1 : CHUNK] + dot(c_t, dye)
                near = []
                for k in range(2):
                    head = t * 4 + k * 2
                    lanes = slice(k * LANES, (k + 1) * LANES)
                    w1, w2 = decayed(cum, cum_t, (head, head + 1))
                    both = jnp.concatenate([w1 * masked, w2 * masked], axis=1)
                    dy_pair = dy[:, lanes]
                    d_both = dot_t(dy_pair, split_heads(xd[:, lanes]))
                    d_scores = d_scores + w1 * d_both[:, :CHUNK] + w2 * d_both[:, CHUNK:]
                    two = dot(turned(both), dy_pair)
                    near.append(jnp.where(lane < HDIM, two[:CHUNK], two[CHUNK:]))
                d_xd = jnp.concatenate(near, axis=1) + far
                col = col + dot_t((d_xd * x).astype(bf16), spread)
                d_x = d_xd * dts + skip_ref[:, cols] * dy.astype(f32)
                pre_s[here, cols] = d_x * dact_ref[r, cols].astype(f32)
            d_low = jnp.where(keep, d_scores, 0.0)
            d_c = d_c + dot(d_low.astype(bf16), b)
            d_b = d_b + dot(turned(d_low), cc)
            pre_s[here, at_b] = d_b * dact_ref[r, at_b].astype(f32)
            pre_s[here, at_c] = d_c * dact_ref[r, at_c].astype(f32)
            d_cum = rowt_ref[r, :] - dt * col
            d_cum = d_cum + jnp.where(row == CHUNK - 1, ends[0:1], 0.0)
            d_log = dot_precise(upper, d_cum)
            d_raw = (d_log * rate_ref[...] + col) * sig_ref[r, :]
            draw_ref[r, :] = jnp.where(lane < HEADS, d_raw, 0.0).astype(bf16)

        strip = 64
        for t in range(CONV_CH // TILE):
            cols = slice(t * TILE, (t + 1) * TILE)
            weights = [cw_ref[j : j + 1, cols] for j in range(4)]
            for i in range(block // strip):
                at = i * strip
                total = weights[3] * pre_s[at : at + strip, cols]
                for j in range(3):
                    total = total + weights[j] * pre_s[at + 3 - j : at + 3 - j + strip, cols]
                dx_ref[pl.ds(base + at, strip), cols] = total.astype(bf16)
                if i == block // strip - 1:
                    end = total[strip - RIM :, :]

                    @pl.when(turn == 0)
                    def _(end=end, cols=cols):
                        tail_ref[:, cols] = end

        send(dx_ref, step)
        send(draw_ref, step)
        return carry

    lax.fori_loop(0, steps, one_step, 0)
    head_ref[...] = pre_s[0:RIM, :].astype(bf16)
    send(head_ref)
    send(tail_ref)


def scan_back_call(late, act, dact, dt, cum, sig, rowt, dy, hc, other, before, skip, rate, conv_w, expand):
    rows = act.shape[0]
    block = 2 * CHUNK
    outs = [
        ((rows, CONV_CH), bf16),
        ((rows, LANES), bf16),
        ((RIM, CONV_CH), f32),
        ((RIM, CONV_CH), bf16),
    ]
    scratch = [pltpu.VMEM((NSTATE, INNER), f32), pltpu.VMEM((block + 8, CONV_CH), f32)]
    arrays = (act, dact, dt, cum, sig, rowt, dy, hc, other, before, skip, rate, conv_w, expand)
    operands = [view(a) for a in arrays]
    return streamed(scan_back_kernel, "scan_back", [late], operands, outs, scratch, 19, rows // block)


def terms_kernel(
    ids, tail_ref, next_ref, cw_ref, bx_ref, dx_ref, bg_ref, dg_ref, lat_ref, nrm_ref,
    last_ref, d_lat_ref, tb_ref, ta_ref, *, ready, send,
):
    rows = dx_ref.shape[0]
    ready(tail_ref, next_ref, cw_ref)
    row = lax.broadcasted_iota(jnp.int32, (RIM, CONV_CH), 0)
    later = next_ref[...].astype(f32)
    total = tail_ref[...]
    for back in range(1, 4):
        term = jnp.zeros((1, CONV_CH), f32)
        for j in range(0, 4 - back):
            term = term + cw_ref[j : j + 1, :] * later[3 - back - j : 4 - back - j, :]
        total = total + jnp.where(row == RIM - back, term, 0.0)
    last_ref[...] = total.astype(bf16)
    ready(bx_ref, dx_ref)
    dx_ref[rows - RIM :, :] = last_ref[...]
    d_x = dx_ref[:, :INNER]
    d_lat = dot_t(d_x, bx_ref[...])
    ready(bg_ref, dg_ref)
    d_gate = dg_ref[...]
    d_lat = (d_lat + dot_t(d_gate, bg_ref[...])).astype(bf16)
    d_lat_ref[...] = d_lat
    ready(lat_ref, nrm_ref)
    lat_t = turned(lat_ref[...])
    tb_ref[:, :INNER] = dot(lat_t, d_gate)
    tb_ref[:, INNER:] = dot(lat_t, d_x)
    ta_ref[...] = dot(turned(d_lat), nrm_ref[...])
    for ref in (tb_ref, ta_ref, last_ref, d_lat_ref):
        send(ref)


def terms_call(seq, ids, tail, later, conv_w, dx, dg, lat, nrm, in_b):
    rows = dx.shape[0]
    outs = [((RIM, CONV_CH), bf16), ((rows, RANK), bf16), ((RANK, ZX), f32), ((RANK, DM), f32)]
    operands = [
        view(tail), view(later), view(conv_w), of_adapter(in_b, seq, INNER, INNER), view(dx),
        of_adapter(in_b, seq, 0, INNER), view(dg), of_sequence(lat, seq), of_sequence(nrm, seq),
    ]
    return streamed(terms_kernel, "terms", [ids], operands, outs, [], 6)


def input_back_kernel(
    ids, lens, place, dg_ref, wg_ref, last_ref, dx_ref, wx_ref, draw_ref, wdt_ref, d_lat_ref, a_ref, gain_ref, x_ref,
    cot_ref, out_ref, dn_s, *, seq, ready, send,
):
    rows = dx_ref.shape[0]
    ready(dg_ref, wg_ref)
    dn_s[...] = dot_t(dg_ref[...], wg_ref[...])
    ready(last_ref, dx_ref, wx_ref, draw_ref, wdt_ref, d_lat_ref, a_ref)
    dx_ref[rows - RIM :, :] = last_ref[...]
    dn_s[...] += (
        dot_t(dx_ref[...], wx_ref[...]) + dot_t(draw_ref[...], wdt_ref[...]) + dot(d_lat_ref[...], a_ref[...])
    )
    ready(gain_ref, x_ref, cot_ref)
    strip = 32
    for i in range(rows // strip):
        r = slice(i * strip, (i + 1) * strip)
        x = x_ref[r, :].astype(f32)
        root = lax.rsqrt(jnp.mean(x * x, -1, keepdims=True) + epsilon)
        dn = dn_s[r, :] * gain_ref[...]
        back = jnp.mean(dn * x, -1, keepdims=True) * (root * root * root)
        position = i * strip + lax.broadcasted_iota(jnp.int32, (strip, 1), 0)
        kept = jnp.where(position < lens[seq], cot_ref[r, :].astype(f32), 0.0)
        out_ref[r, :] = dn * root - x * back + kept
    send(out_ref)


def input_back_call(seq, ids, lens, place, begun, tokens, cotangent, dg, last, dx, draw, d_lat, wg, wx, wdt, in_a, gain):
    rows = dx.shape[0]
    outs = [((rows, DM), f32)]
    operands = [view(dg), wg, view(last), view(dx), wx, view(draw), wdt, view(d_lat)]
    operands += [of_adapter(in_a, seq), view(gain), of_sequence(tokens, seq), of_sequence(cotangent, seq)]
    kernel = functools.partial(input_back_kernel, seq=seq)
    scratch = [pltpu.VMEM((rows, DM), f32)]
    shared = (tokens.shape[0], seq, begun)
    return streamed(kernel, "input_back", [ids, lens, place], operands, outs, scratch, 9, 1, shared)[0]


def shifted(value, axis, steps):
    count = lax.axis_size(axis)
    pairs = [(i, i + steps) for i in range(count) if 0 <= i + steps < count]
    return lax.ppermute(value, axis, pairs)


def swapped(value, axis, bit):
    return lax.ppermute(value, axis, [(i, i ^ bit) for i in range(lax.axis_size(axis))])


def after(value, other):
    return lax.optimization_barrier((value, other))[0]


def my_half(shard, core, half):
    return lax.dynamic_slice_in_dim(shard, core * half, half, 0)


def gathered_early(meanwhile, shard):
    owners = lax.axis_size("dp")
    rows, width = shard.shape
    half = rows // 2
    shapes = [(rows * owners, CONV_CH), (rows * owners, LANES)]
    if half % 16 or owners % 2:
        full = lax.all_gather(shard, "dp", axis=0, tiled=True)
        marked = full.reshape(owners, rows, width)[:, 0, CONV_CH + HEADS : CONV_CH + GROUP]
        return view(full[:, :CONV_CH]), view(full[:, CONV_CH:]), marked
    core = lax.axis_index("ctx") % 2
    own = {0: my_half(shard, core, half)}
    for k in range(2, owners, 2):
        own[k] = swapped(own[0], "dp", k)
    for k in range(0, owners, 2):
        source = own[k] if k == 0 else after(own[k], (own[k - 1], meanwhile))
        own[k + 1] = swapped(source, "dp", 1)
    pieces = [own[k] for k in range(owners)] + [swapped(own[k], "ctx", 1) for k in range(owners)]

    def copies(scalars, refs, to, columns):
        place = scalars[-1]
        pairs = []
        for n, piece in enumerate(refs):
            side = place[1] if n < owners else 1 - place[1]
            at = pl.multiple_of((place[0] ^ (n % owners)) * rows + side * half, 16)
            pairs.append((piece.at[:, columns], to.at[pl.ds(at, half)]))
        return pairs

    main = functools.partial(copies, columns=pl.ds(0, CONV_CH))
    rest = functools.partial(copies, columns=pl.ds(CONV_CH, LANES))
    marks = jnp.stack([own[k][0, CONV_CH + HEADS : CONV_CH + GROUP] for k in range(owners)])
    turn = jnp.arange(owners)
    found = (turn[:, None] ^ lax.axis_index("dp")) == turn[None, :]
    marked = jnp.sum(jnp.where(found[:, :, None], marks[None], 0.0), axis=1)
    return Operand(pieces, shapes[0], main), Operand(pieces, shapes[1], rest), marked


def gathered_late(gate, out, start, hold):
    owners = lax.axis_size("dp")
    rows = gate.shape[0]
    half = rows // 2
    if half % 16:
        return (
            view(lax.all_gather(gate, "dp", axis=0, tiled=True)),
            view(lax.all_gather(out, "dp", axis=0, tiled=True)),
        )
    core = lax.axis_index("ctx") % 2
    both = jnp.concatenate([gate, out[:rows], out[rows:]], axis=1)
    mine = lax.all_gather(after(my_half(both, core, half), start), "dp", axis=0, tiled=True)
    mine = after(mine, hold())
    pieces = [mine, swapped(mine, "ctx", 1)]

    def gate_copies(scalars, refs, to):
        place = scalars[-1]
        pairs = []
        for n, piece in enumerate(refs):
            side = place[1] if n == 0 else 1 - place[1]
            for d in range(owners):
                at = pl.multiple_of(d * rows + side * half, 16)
                pairs.append((piece.at[pl.ds(d * half, half), pl.ds(0, INNER)], to.at[pl.ds(at, half)]))
        return pairs

    def out_copies(scalars, refs, to):
        place = scalars[-1]
        pairs = []
        for n, piece in enumerate(refs):
            side = place[1] if n == 0 else 1 - place[1]
            for d in range(owners):
                for k in range(2):
                    at = pl.multiple_of((2 * d + k) * rows + side * half, 16)
                    columns = pl.ds(INNER + k * DM, DM)
                    pairs.append((piece.at[pl.ds(d * half, half), columns], to.at[pl.ds(at, half)]))
        return pairs

    return (
        Operand(pieces, (rows * owners, INNER), gate_copies),
        Operand(pieces, (2 * rows * owners, DM), out_copies),
    )


def join_kernel(swap, one_ref, two_ref, out_ref, *, ready, send):
    ready(one_ref, two_ref)
    for t in range(INNER // TILE):
        cols = slice(t * TILE, (t + 1) * TILE)
        d_one, d_two = decay_of(one_ref, cols), decay_of(two_ref, cols)
        one = one_ref[0:NSTATE, cols].astype(f32)
        two = two_ref[0:NSTATE, cols].astype(f32)
        state = jnp.where(swap[0] == 1, d_one * two + one, d_two * one + two)
        out_ref[0:NSTATE, cols] = state.astype(bf16)
        out_ref[NSTATE:, cols] = split_decay(d_one * d_two)
    send(out_ref)


def joined(one, two, swap):
    return streamed(join_kernel, "join", [swap], [view(one), view(two)], [(one.shape, bf16)], [], 1)[0]


def exchanged(payload, late, reverse, earlier=None):
    chips = lax.axis_size("ctx") // 2
    sign = -1 if reverse else 1
    in_order = jnp.zeros((1,), jnp.int32)
    if earlier is not None:
        payload = after(payload, earlier[2])
    other = swapped(payload, "ctx", 1)
    both = joined(payload, other, late)
    before = shifted(both, "ctx", 2 * sign)
    step, run = 1, both
    while 2 * step < chips:
        run = joined(before, both, in_order) if step == 1 else joined(far, run, in_order)
        far = shifted(run, "ctx", 4 * step * sign)
        before = joined(far, before, in_order)
        step *= 2
    return other, both, before


def shards(
    tokens, cotangent, lengths, adapter_ids, norm_gain, w_in, conv_weight, conv_bias, dt_bias, a_log,
    skip_scale, inner_gain, w_out, in_a, in_b, out_a, out_b,
):
    seqs, slots, _ = tokens.shape
    owners = lax.axis_size("dp")
    ids = adapter_ids
    lens = jnp.clip(lengths - lax.axis_index("ctx") * slots, 0, slots).astype(jnp.int32)

    def grouped(row):
        padded = jnp.pad(row.reshape(-1, HEADS), ((0, 0), (0, GROUP - HEADS)))
        return jnp.tile(padded, (1, LANES // GROUP))

    rate = grouped(-jnp.exp(a_log))
    dtb = grouped(dt_bias)
    lane = jnp.arange(LANES)[:, None]
    head = jnp.arange(INNER)[None, :] // HDIM
    expand = ((lane % GROUP == head) & (lane < 3 * GROUP)).astype(bf16)
    skip = jnp.repeat(skip_scale, HDIM)[None, :]
    gain = inner_gain[None, :]
    n_gain = norm_gain[None, :]
    conv_b = conv_bias[None, :]

    marks = jnp.broadcast_to(ids.astype(bf16)[None, :], (w_in.shape[0], seqs))
    marks = jnp.pad(marks, ((0, 0), (0, GROUP - HEADS - seqs)))
    steps = jnp.concatenate([w_in[:, INNER + CONV_CH :], marks], axis=1)
    in_a, out_a = jnp.swapaxes(in_a, 1, 2), jnp.swapaxes(out_a, 1, 2)
    rim = shifted(tokens[:, slots - RIM :], "ctx", 1)
    nrm, nrim, lat, lrim = norm_call(ids, tokens, rim, n_gain, in_a)
    wx, wdt, marked = gathered_early(
        nrm,
        jnp.concatenate([w_in[:, INNER : INNER + CONV_CH]] + [steps] * (LANES // GROUP), axis=1)
    )

    core = lax.axis_index("ctx") % 2
    place = jnp.stack([lax.axis_index("dp"), core]).astype(jnp.int32)
    late = core.reshape(1).astype(jnp.int32)
    early = 1 - late
    front = functools.partial(
        front_call, in_b=in_b, wx=wx, wdt=wdt, conv_w=conv_weight, conv_b=conv_b, dtb=dtb, rate=rate, expand=expand
    )
    fronts, states = [], []
    for s in range(seqs):
        ready = nrm if s == 0 else after(nrm, states[-1][1])
        fronts.append(front(s, ids, place, ready, nrim, lat, lrim))
        states.append(exchanged(fronts[s][5], late, False, states[-1] if s else None))
    full_gate, full_out = gathered_late(w_in[:, :INNER], w_out, marked, lambda: fronts[-1][5])
    scans = []
    for s in range(seqs):
        act, _, dt, cum, _, _ = fronts[s]
        other, _, before = states[s]
        ready = act if s == 0 else after(act, (scans[-1][0], states[s][1]))
        scans.append(scan_call(late, ready, dt, cum, other, before, expand))
    middles, grads = [], []
    for s in range(seqs):
        act, _, _, cum, _, _ = fronts[s]
        ready = after(nrm, scans[-1][0]) if s == 0 else after(nrm, grads[-1][1])
        middles.append(
            middle_call(
                s, ids, lens, place, middles[-1][0] if s else None, tokens, cotangent, ready, lat, act, cum, scans[s][0], full_gate, in_b, full_out,
                out_a, out_b, skip, gain, expand,
            )
        )
        grads.append(exchanged(middles[s][4], early, True, grads[-1] if s else None))
    backs, nexts = [], []
    for s in range(seqs):
        act, dact, dt, cum, sig, _ = fronts[s]
        _, dy, _, rowt, _, _, _ = middles[s]
        other, _, before = grads[s]
        ready = after(act, grads[-1][1])
        backs.append(
            scan_back_call(
                early, ready, dact, dt, cum, sig, rowt, dy, scans[s][1], other, before, skip, rate, conv_weight,
                expand,
            )
        )
        nexts.append(shifted(backs[s][3], "ctx", -1))
    terms = [
        terms_call(
            s, ids, backs[s][2], nexts[s], conv_weight, backs[s][0], middles[s][2], lat, nrm, in_b
        )
        for s in range(seqs)
    ]

    def by_owner(terms):
        stacked = jnp.stack(terms)
        return stacked.reshape(seqs, RANK, owners, -1).transpose(2, 0, 1, 3)

    kinds = (
        [term[3] for term in terms],
        [term[2] for term in terms],
        [mid[6] for mid in middles],
        [mid[5] for mid in middles],
    )
    pieces = [by_owner(terms) for terms in kinds]
    widths = [piece.shape[-1] for piece in pieces]
    sent = jnp.concatenate(pieces, axis=-1).astype(bf16)
    got = lax.all_to_all(sent, "dp", 0, 0)
    held = after(tokens, sent)
    input_grad = None
    for s in range(seqs):
        input_grad = input_back_call(
            s, ids, lens, place, input_grad, held, cotangent, middles[s][2], terms[s][0], backs[s][0], backs[s][1],
            terms[s][1], full_gate, wx, wdt, in_a, n_gain,
        )
    every = marked[:, :seqs].reshape(1, -1)
    chosen = (every.astype(f32) == jnp.arange(ADAPT, dtype=f32)[:, None]).astype(f32)
    flat = got.reshape(owners * seqs, -1).astype(f32)
    mine = jnp.sum(chosen[:, :, None] * flat[None], axis=1)
    bit = 1
    while bit < lax.axis_size("ctx"):
        mine = mine + swapped(mine.astype(bf16), "ctx", bit).astype(f32)
        bit *= 2
    mine = mine.reshape(ADAPT, RANK, -1)
    cuts = [sum(widths[:k]) for k in range(5)]
    g_ia, g_ib, g_oa, g_ob = (mine[:, :, cuts[k] : cuts[k + 1]] for k in range(4))
    return (
        middles[-1][0],
        input_grad,
        jnp.swapaxes(g_ia, 1, 2),
        g_ib,
        jnp.swapaxes(g_oa, 1, 2),
        g_ob,
    )


def solution(mesh):
    split = P("dp", "ctx", None)
    return jax.shard_map(
        shards,
        mesh=mesh,
        in_specs=(
            split, split, P("dp"), P("dp"), P(), P("dp", None), P(), P(), P(), P(), P(), P(),
            P("dp", None), P(), P(), P(), P(),
        ),
        out_specs=(
            split, split, P(None, "dp", None), P(None, None, "dp"), P(None, "dp", None), P(None, None, "dp"),
        ),
        check_vma=False,
    )
```

```python
import functools

import jax
import jax.numpy as jnp
from jax import lax
from jax.experimental import pallas as pl
from jax.experimental.pallas import tpu as pltpu
from jax.sharding import PartitionSpec as P

HEADS = 24
HDIM = 64
NSTATE = 128
INNER = 1536
CONV_CH = 1792
ZX = 3072
DM = 768
RANK = 16
ADAPT = 8
CHUNK = 128
TILE = 256
RIM = 16
GROUP = 32
LANES = 128
VMEM_LIMIT = 60 * 1024 * 1024

epsilon = 1e-05
bf16 = jnp.bfloat16
f32 = jnp.float32


def dot(left, right):
    return jnp.dot(left, right, preferred_element_type=f32)


def dot_t(left, right):
    return lax.dot_general(
        left, right, (((1,), (1,)), ((), ())), preferred_element_type=f32
    )


def dot_precise(left, right):
    return jnp.dot(
        left, right, preferred_element_type=f32, precision=lax.Precision.HIGHEST
    )


def parts_of(v):
    lane = lax.broadcasted_iota(jnp.int32, v.shape, 1)
    high = v.astype(bf16).astype(f32)
    rest = v - high
    middle = rest.astype(bf16).astype(f32)
    kept = jnp.where(lane < GROUP, high, jnp.where(lane < 2 * GROUP, middle, rest - middle))
    return jnp.where(lane < 3 * GROUP, kept, 0.0).astype(bf16)


def causal(rows):
    t = lax.broadcasted_iota(jnp.int32, (rows, rows), 0)
    s = lax.broadcasted_iota(jnp.int32, (rows, rows), 1)
    return t >= s


def sigmoid(v):
    return 0.5 * jnp.tanh(0.5 * v) + 0.5


def turned(v):
    return jnp.transpose(v.astype(f32)).astype(bf16)


class Operand:
    def __init__(self, arrays, shape, copies):
        self.arrays, self.shape, self.copies = list(arrays), tuple(shape), copies


def view(array, pick=None, shape=None):
    pick = pick or (lambda scalars, ref: ref)
    return Operand([array], shape or array.shape, lambda scalars, refs, to: [(pick(scalars, refs[0]), to)])


def streamed(kernel, name, scalars, operands, outs, scratch, micros, shared=None):
    arrays = [array for operand in operands for array in operand.arrays]
    n_scalar, n_array, n_in, n_out = len(scalars), len(arrays), len(operands), len(outs)
    kinds = [operand.arrays[0].dtype for operand in operands]
    slots, slot, begun = shared or (None, None, None)
    n_begun = 0 if begun is None else 1

    def body(*refs):
        refs = list(refs)
        take = lambda n: [refs.pop(0) for _ in range(n)]
        smem, sources, _, targets, ins, results = (
            take(n) for n in (n_scalar, n_array, n_begun, n_out, n_in, n_out)
        )
        if shared:
            targets[0] = targets[0].at[slot]
        in_sems, out_sems = refs.pop(-2), refs.pop(-1)
        waiting = {}
        for k, operand in enumerate(operands):
            mine = [sources.pop(0) for _ in operand.arrays]
            for source, target in operand.copies(smem, mine, ins[k]):
                pltpu.make_async_copy(source, target, in_sems.at[k]).start()
            waiting[id(ins[k])] = pltpu.make_async_copy(ins[k], ins[k], in_sems.at[k])

        def ready(*wanted):
            for ref in wanted:
                if id(ref) in waiting:
                    waiting.pop(id(ref)).wait()

        sent = []

        def send(ref, *at):
            k = [id(result) for result in results].index(id(ref))
            if k not in sent:
                sent.append(k)
            source, target = (results[k].at[at], targets[k].at[at]) if at else (results[k], targets[k])
            pltpu.make_async_copy(source, target, out_sems.at[k]).start()

        kernel(*smem, *ins, *results, *refs, ready=ready, send=send)
        ready(*ins)
        for k in sent:
            pltpu.make_async_copy(results[k], targets[k], out_sems.at[k]).wait()

    anywhere = pl.BlockSpec(memory_space=pl.ANY)
    full = [((slots,) + shape if shared and k == 0 else shape, kind) for k, (shape, kind) in enumerate(outs)]
    return pl.pallas_call(
        body,
        in_specs=[pl.BlockSpec(memory_space=pltpu.SMEM)] * n_scalar + [anywhere] * (n_array + n_begun),
        out_specs=[anywhere] * n_out,
        out_shape=[jax.ShapeDtypeStruct(shape, kind) for shape, kind in full],
        scratch_shapes=[pltpu.VMEM(operand.shape, kind) for operand, kind in zip(operands, kinds)]
        + [pltpu.VMEM(shape, kind) for shape, kind in outs]
        + scratch
        + [pltpu.SemaphoreType.DMA((n_in,)), pltpu.SemaphoreType.DMA((n_out,))],
        input_output_aliases={n_scalar + n_array: 0} if n_begun else {},
        compiler_params=pltpu.CompilerParams(vmem_limit_bytes=VMEM_LIMIT),
        cost_estimate=pl.CostEstimate(flops=micros * 1000000000, bytes_accessed=1000000, transcendentals=0),
        name=name,
    )(*scalars, *arrays, *([begun] if n_begun else []))


def of_sequence(array, seq):
    return view(array, lambda scalars, ref: ref.at[seq], array.shape[1:])


def of_adapter(array, seq, start=0, width=None):
    width = width or array.shape[2]
    pick = lambda scalars, ref: ref.at[scalars[0][seq], :, pl.ds(start, width)]
    return view(array, pick, (array.shape[1], width))


def split_decay(decay):
    high = decay.astype(bf16).astype(f32)
    row = lax.broadcasted_iota(jnp.int32, (RIM, decay.shape[1]), 0)
    return jnp.where(row == 0, high, jnp.where(row == 1, decay - high, 0.0)).astype(bf16)


def decay_of(payload_ref, cols):
    rows = payload_ref[NSTATE:, cols].astype(f32)
    return rows[0:1] + rows[1:2]


def norm_kernel(
    ids, x0_ref, x1_ref, rim_ref, gain_ref, a0_ref, a1_ref, nrm_ref, nrim_ref, lat_ref, lrim_ref, *, ready, send
):
    def normed(x):
        x = x.astype(f32)
        mean = jnp.mean(x * x, -1, keepdims=True)
        return (x * lax.rsqrt(mean + epsilon) * gain_ref[...]).astype(bf16)

    strip = 64
    ready(gain_ref, rim_ref)
    for s, (x_ref, a_ref) in enumerate(((x0_ref, a0_ref), (x1_ref, a1_ref))):
        ready(x_ref, a_ref)
        for i in range(x_ref.shape[0] // strip):
            r = slice(i * strip, (i + 1) * strip)
            nrm_ref[s, r, :] = normed(x_ref[r, :])
        nrim_ref[s] = normed(rim_ref[s])
        lat_ref[s] = dot_t(nrm_ref[s], a_ref[...]).astype(bf16)
        lrim_ref[s] = dot_t(nrim_ref[s], a_ref[...]).astype(bf16)
    for ref in (nrm_ref, nrim_ref, lat_ref, lrim_ref):
        send(ref)


def norm_call(ids, tokens, rim, gain, in_a):
    seqs, rows, _ = tokens.shape
    outs = [
        ((seqs, rows, DM), bf16),
        ((seqs, RIM, DM), bf16),
        ((seqs, rows, RANK), bf16),
        ((seqs, RIM, RANK), bf16),
    ]
    operands = [
        of_sequence(tokens, 0), of_sequence(tokens, 1), view(rim), view(gain), of_adapter(in_a, 0), of_adapter(in_a, 1),
    ]
    return streamed(norm_kernel, "norm", [ids], operands, outs, [], 3)


def front_kernel(
    ids, place, nrm_ref, nrim_ref, lat_ref, lrim_ref, wdt_ref, dtb_ref, rate_ref, cw_ref, cb_ref, wx_ref, bx_ref,
    expand_ref, act_ref, dact_ref, dt_ref, cum_ref, sig_ref, pay_ref, marks_ref,
    nrm_s, lat_s, xs, bt_s, w_s, *, ready, send,
):
    rows = nrm_ref.shape[0]
    ready(nrm_ref, nrim_ref, lat_ref, lrim_ref)
    nrm_s[0:RIM, :] = nrim_ref[...]
    nrm_s[RIM:, :] = nrm_ref[...]
    lat_s[0:RIM, :] = lrim_ref[...]
    lat_s[RIM:, :] = lat_ref[...]
    ready(wdt_ref, dtb_ref, rate_ref)
    owners = marks_ref.shape[0]
    for d in range(owners):
        at = d * (wdt_ref.shape[0] // owners)
        marks_ref[d : d + 1, :] = wdt_ref[at : at + 8, :].astype(f32)[0:1]
    send(marks_ref)
    raw = dot(nrm_ref[...], wdt_ref[...]) + dtb_ref[...]
    step = jnp.maximum(raw, 0.0) + jnp.log1p(jnp.exp(-jnp.abs(raw)))
    dt_ref[...] = step
    sig_ref[...] = sigmoid(raw)
    logs = step * rate_ref[...]
    lower = causal(CHUNK).astype(f32)
    before = jnp.zeros((1, LANES), f32)
    whole = []
    for c in range(rows // CHUNK):
        r = slice(c * CHUNK, (c + 1) * CHUNK)
        cum = dot_precise(lower, logs[r])
        cum_ref[r, :] = cum
        whole.append(cum + before)
        before = before + cum[CHUNK - 1 : CHUNK]
    for c in range(rows // CHUNK):
        r = slice(c * CHUNK, (c + 1) * CHUNK)
        w_s[r, :] = parts_of(jnp.exp(before - whole[c]) * step[r])
    total = parts_of(jnp.broadcast_to(jnp.exp(before), (8, LANES)))
    for ref in (dt_ref, cum_ref, sig_ref):
        send(ref)
    ready(cw_ref, cb_ref, wx_ref, bx_ref, expand_ref)

    def activate(cols, base):
        weights = [cw_ref[j : j + 1, cols] for j in range(4)]
        bias = cb_ref[:, cols]
        low = base.astype(bf16).astype(f32)
        for k in range(2):
            xs[k] = low[:, k * LANES : (k + 1) * LANES]
        strip = 64
        for i in range(rows // strip):
            at = RIM + i * strip
            halves = []
            for k in range(2):
                lanes = slice(k * LANES, (k + 1) * LANES)
                pre = bias[:, lanes] + weights[0][:, lanes] * xs[k, at - 3 : at - 3 + strip, :]
                for j in range(1, 4):
                    pre = pre + weights[j][:, lanes] * xs[k, at - 3 + j : at - 3 + j + strip, :]
                halves.append(pre)
            pre = jnp.concatenate(halves, axis=1)
            gate = sigmoid(pre)
            act = pre * gate
            r = slice(i * strip, (i + 1) * strip)
            act_ref[r, cols] = act.astype(bf16)
            dact_ref[r, cols] = (gate + act * (1.0 - gate)).astype(bf16)
        send(act_ref, slice(None), cols)
        send(dact_ref, slice(None), cols)

    last = pl.ds(INNER, CONV_CH - INNER)
    activate(last, dot(nrm_s[...], wx_ref[:, last]))
    bt_s[...] = turned(act_ref[:, INNER : INNER + NSTATE])
    for t in range(INNER // TILE):
        cols = pl.ds(t * TILE, TILE)
        activate(cols, dot(nrm_s[...], wx_ref[:, cols]) + dot(lat_s[...], bx_ref[:, cols]))
        scaled = (act_ref[:, cols].astype(f32) * dot(w_s[...], expand_ref[:, cols])).astype(bf16)
        pay_ref[0:NSTATE, cols] = dot(bt_s[...], scaled).astype(bf16)
        pay_ref[NSTATE:, cols] = split_decay(dot(total, expand_ref[:, cols])[0:1])
    send(pay_ref)


def front_call(seq, ids, place, nrm, nrim, lat, lrim, wx, wdt, in_b, conv_w, conv_b, dtb, rate, expand):
    rows = nrm.shape[1]
    owners = lax.axis_size("dp")
    outs = [
        ((rows, CONV_CH), bf16),
        ((rows, CONV_CH), bf16),
        ((rows, LANES), f32),
        ((rows, LANES), f32),
        ((rows, LANES), f32),
        ((NSTATE + RIM, INNER), bf16),
        ((owners, LANES), f32),
    ]
    scratch = [
        pltpu.VMEM((rows + RIM, DM), bf16),
        pltpu.VMEM((rows + RIM, RANK), bf16),
        pltpu.VMEM((2, rows + RIM, LANES), f32),
        pltpu.VMEM((NSTATE, rows), bf16),
        pltpu.VMEM((rows, LANES), bf16),
    ]
    operands = [of_sequence(a, seq) for a in (nrm, nrim, lat, lrim)]
    operands += [wdt] + [view(a) for a in (dtb, rate, conv_w, conv_b)] + [wx]
    operands += [of_adapter(in_b, seq, INNER, INNER), view(expand)]
    return streamed(front_kernel, "front", [ids, place], operands, outs, scratch, 13)


def decayed(cum, cum_t, heads):
    out = []
    for h in heads:
        gap = jnp.minimum(cum[:, h : h + 1] - cum_t[h : h + 1, :], 0.0)
        out.append(jnp.exp(gap))
    return out


def split_heads(pair):
    lane = lax.broadcasted_iota(jnp.int32, pair.shape, 1)
    zero = jnp.zeros_like(pair)
    first = jnp.where(lane < HDIM, pair, zero)
    second = jnp.where(lane < HDIM, zero, pair)
    return jnp.concatenate([first, second], axis=0)


def join_payloads(swap, one_ref, two_ref, out_ref):
    for t in range(INNER // TILE):
        cols = slice(t * TILE, (t + 1) * TILE)
        d_one, d_two = decay_of(one_ref, cols), decay_of(two_ref, cols)
        one = one_ref[0:NSTATE, cols].astype(f32)
        two = two_ref[0:NSTATE, cols].astype(f32)
        state = jnp.where(swap == 1, d_one * two + one, d_two * one + two)
        out_ref[0:NSTATE, cols] = state.astype(bf16)
        out_ref[NSTATE:, cols] = split_decay(d_one * d_two)


def state_in(late, other_ref, before_ref, cols):
    before = before_ref[0:NSTATE, cols].astype(f32)
    joint = decay_of(other_ref, cols) * before + other_ref[0:NSTATE, cols].astype(f32)
    return jnp.where(late == 1, joint, before)


def scan_kernel(
    flags, own_ref, other_ref, act_ref, dt_ref, cum_ref, expand_ref, y_ref, hc_ref, both_ref, state_s, *, ready, send
):
    keep = causal(CHUNK)
    ready(own_ref, other_ref)
    join_payloads(flags[0], own_ref, other_ref, both_ref)
    send(both_ref)
    state_s[...] = jnp.zeros_like(state_s)
    ready(act_ref, dt_ref, cum_ref, expand_ref)

    def one_chunk(c, carry):
        r = pl.ds(pl.multiple_of(c * CHUNK, CHUNK), CHUNK)
        b = act_ref[r, INNER : INNER + NSTATE]
        cc = act_ref[r, INNER + NSTATE :]
        b_t = turned(b)
        masked = jnp.where(keep, dot_t(cc, b), 0.0)
        dt = dt_ref[r, :]
        cum = cum_ref[r, :]
        cum_t = jnp.transpose(cum)
        p_ec = parts_of(jnp.exp(cum))
        p_dt = parts_of(dt)
        p_w = parts_of(jnp.exp(cum[CHUNK - 1 : CHUNK] - cum) * dt)
        p_all = jnp.concatenate([p_ec, p_dt, p_w], axis=0)
        for t in range(INNER // TILE):
            cols = slice(t * TILE, (t + 1) * TILE)
            spreads = dot(p_all, expand_ref[:, cols])
            ec = spreads[:CHUNK]
            x = act_ref[r, cols].astype(f32)
            xd = (x * spreads[CHUNK : 2 * CHUNK]).astype(bf16)
            xw = (x * spreads[2 * CHUNK :]).astype(bf16)
            state = state_s[:, cols]
            low = state.astype(bf16)
            hc_ref[c, :, cols] = low
            far = dot(cc, low) * ec
            state_s[:, cols] = state * ec[CHUNK - 1 : CHUNK] + dot(b_t, xw)
            for k in range(2):
                lanes = slice(k * LANES, (k + 1) * LANES)
                head = t * 4 + k * 2
                weights = [
                    (w * masked).astype(bf16) for w in decayed(cum, cum_t, (head, head + 1))
                ]
                near = dot(jnp.concatenate(weights, axis=1), split_heads(xd[:, lanes]))
                y_ref[r, t * TILE + k * LANES : t * TILE + (k + 1) * LANES] = near + far[:, lanes]
        send(y_ref, r)
        send(hc_ref, pl.ds(c, 1))
        return carry

    lax.fori_loop(0, act_ref.shape[0] // CHUNK, one_chunk, 0)


def scan_call(flags, own, other, act, dt, cum, expand):
    rows = act.shape[0]
    chunks = rows // CHUNK
    outs = [((rows, INNER), f32), ((chunks, NSTATE, INNER), bf16), (own.shape, bf16)]
    scratch = [pltpu.VMEM((NSTATE, INNER), f32)]
    operands = [view(a) for a in (own, other, act, dt, cum, expand)]
    return streamed(scan_kernel, "scan", [flags], operands, outs, scratch, 9)


def middle_kernel(
    ids, lens, flags, place, nrm_ref, lat_ref, bg_ref, wg_ref, cot_ref, b_ref, a_ref, wo_ref, other_ref, before_ref,
    y_ref, act_ref, cum_ref, expand_ref, skip_ref, gain_ref, x_ref,
    out_ref, dy_ref, dg_ref, rowt_ref, pay_ref, tb_ref, ta_ref, enter_ref, runs_ref,
    tb_s, ta_s, gate_s, z_s, dh_s, hid_s, prod_s, ec_s, grad_s, run_s, *, seq, ready, send,
):
    block = gate_s.shape[0]
    steps = act_ref.shape[0] // block
    strip = 16
    grad_s[...] = jnp.zeros_like(grad_s)
    run_s[...] = jnp.ones_like(run_s)
    tb_s[...] = jnp.zeros_like(tb_s)
    ta_s[...] = jnp.zeros_like(ta_s)
    ready(nrm_ref, lat_ref, bg_ref, wg_ref)

    def one_step(step, first):
        base = pl.multiple_of(step * block, block)
        mine = pl.ds(base, block)
        gate_s[...] = dot(nrm_ref[mine, :], wg_ref[...]) + dot(lat_ref[mine, :], bg_ref[...])
        if first:
            ready(cot_ref, b_ref, a_ref, wo_ref)
        position = base + lax.broadcasted_iota(jnp.int32, (block, 1), 0)
        valid = position < lens[seq]
        g = jnp.where(valid, cot_ref[mine, :], jnp.zeros((), bf16))
        d_lat = dot_t(g, b_ref[...]).astype(bf16)
        dh_s[...] = dot_t(g, wo_ref[...]) + dot(d_lat, a_ref[...])
        if first:
            ready(other_ref, before_ref)
            for t in range(INNER // TILE):
                cols = slice(t * TILE, (t + 1) * TILE)
                enter_ref[:, cols] = state_in(flags[0], other_ref, before_ref, cols).astype(bf16)
            send(enter_ref)
            ready(y_ref, act_ref, cum_ref, expand_ref, skip_ref, gain_ref)

        for c in range(block // CHUNK):
            here = slice(c * CHUNK, (c + 1) * CHUNK)
            r = pl.ds(base + c * CHUNK, CHUNK)
            cc = act_ref[r, INNER + NSTATE :]
            p_ec = parts_of(jnp.exp(cum_ref[r, :]))
            at = step * (block // CHUNK) + c
            runs_ref[at : at + 1, :] = run_s[...]
            for t in range(INNER // TILE):
                cols = slice(t * TILE, (t + 1) * TILE)
                ec = dot(p_ec, expand_ref[:, cols])
                ec_s[here, cols] = ec
                run = run_s[:, cols]
                y_ref[r, cols] += dot(cc, enter_ref[:, cols]) * (ec * run)
                run_s[:, cols] = run * ec[CHUNK - 1 : CHUNK]

        roots = []
        for i in range(block // strip):
            here = slice(i * strip, (i + 1) * strip)
            r = pl.ds(base + i * strip, strip)
            total = jnp.zeros((strip, LANES), f32)
            for t in range(INNER // TILE):
                cols = slice(t * TILE, (t + 1) * TILE)
                gate = gate_s[here, cols]
                u = y_ref[r, cols] + skip_ref[:, cols] * act_ref[r, cols].astype(f32)
                sig = sigmoid(gate)
                silu = gate * sig
                z = u * silu
                square = z * z
                total = total + square[:, :LANES] + square[:, LANES:]
                z_s[here, cols] = z
                gate_s[here, cols] = silu
                prod_s[here, cols] = u * (sig + silu * (1.0 - sig))
            root = lax.rsqrt(jnp.sum(total, -1, keepdims=True) / INNER + epsilon)
            roots.append(root)
            for t in range(INNER // TILE):
                cols = slice(t * TILE, (t + 1) * TILE)
                hid_s[here, cols] = (z_s[here, cols] * root * gain_ref[:, cols]).astype(bf16)

        if first:
            ready(x_ref)
        hidden = hid_s[...]
        lat_out = dot_t(hidden, a_ref[...]).astype(bf16)
        mixed = dot(hidden, wo_ref[...]) + dot(lat_out, b_ref[...])
        out_ref[mine, :] = jnp.where(valid, x_ref[mine, :].astype(f32) + mixed, 0.0).astype(bf16)
        send(out_ref, mine)
        tb_s[...] += dot(turned(lat_out), g)
        ta_s[...] += dot(turned(d_lat), hidden)

        for i in range(block // strip):
            here = slice(i * strip, (i + 1) * strip)
            r = pl.ds(base + i * strip, strip)
            total = jnp.zeros((strip, LANES), f32)
            for t in range(INNER // TILE):
                cols = slice(t * TILE, (t + 1) * TILE)
                dh = dh_s[here, cols] * gain_ref[:, cols]
                dh_s[here, cols] = dh
                both = dh * z_s[here, cols]
                total = total + both[:, :LANES] + both[:, LANES:]
            root = roots[i]
            back = jnp.sum(total, -1, keepdims=True) * (root * root * root) / INNER
            for t in range(INNER // TILE):
                cols = slice(t * TILE, (t + 1) * TILE)
                dz = dh_s[here, cols] * root - z_s[here, cols] * back
                dy = (dz * gate_s[here, cols]).astype(bf16)
                dy_ref[r, cols] = dy
                dg_ref[r, cols] = (dz * prod_s[here, cols]).astype(bf16)
                hid_s[here, cols] = (dy.astype(f32) * y_ref[r, cols]).astype(bf16)
        send(dy_ref, mine)
        send(dg_ref, mine)

        rowt_ref[mine, :] = dot_t(hid_s[...], expand_ref[...])
        send(rowt_ref, mine)

        for c in range(block // CHUNK):
            r = pl.ds(base + c * CHUNK, CHUNK)
            here = slice(c * CHUNK, (c + 1) * CHUNK)
            c_t = turned(act_ref[r, INNER + NSTATE :])
            at = step * (block // CHUNK) + c
            for t in range(INNER // TILE):
                cols = slice(t * TILE, (t + 1) * TILE)
                scaled = (dy_ref[r, cols].astype(f32) * ec_s[here, cols]).astype(bf16)
                grad_s[:, cols] += runs_ref[at : at + 1, cols] * dot(c_t, scaled)

    for step in range(steps):
        one_step(step, step == 0)
    pay_ref[0:NSTATE, :] = grad_s[...].astype(bf16)
    pay_ref[NSTATE:, :] = split_decay(run_s[...])
    tb_ref[...] = tb_s[...].astype(bf16)
    ta_ref[...] = ta_s[...].astype(bf16)
    for ref in (pay_ref, tb_ref, ta_ref, runs_ref):
        send(ref)


def middle_call(
    seq, ids, lens, place, flags, begun, tokens, cotangent, nrm, lat, act, cum, other, before, y, wg, in_b, wo, out_a, out_b, skip, gain, expand
):
    rows = act.shape[0]
    block = 2 * CHUNK
    outs = [
        ((rows, DM), bf16),
        ((rows, INNER), bf16),
        ((rows, INNER), bf16),
        ((rows, LANES), f32),
        ((NSTATE + RIM, INNER), bf16),
        ((RANK, DM), bf16),
        ((RANK, INNER), bf16),
        ((NSTATE, INNER), bf16),
        ((max(8, rows // CHUNK), INNER), f32),
    ]
    scratch = [
        pltpu.VMEM((RANK, DM), f32),
        pltpu.VMEM((RANK, INNER), f32),
        pltpu.VMEM((block, INNER), f32),
        pltpu.VMEM((block, INNER), f32),
        pltpu.VMEM((block, INNER), f32),
        pltpu.VMEM((block, INNER), bf16),
        pltpu.VMEM((block, INNER), f32),
        pltpu.VMEM((block, INNER), f32),
        pltpu.VMEM((NSTATE, INNER), f32),
        pltpu.VMEM((1, INNER), f32),
    ]
    operands = [
        of_sequence(nrm, seq), of_sequence(lat, seq), of_adapter(in_b, seq, 0, INNER), wg,
        of_sequence(cotangent, seq), of_adapter(out_b, seq), of_adapter(out_a, seq), wo, view(other), view(before),
        view(y), view(act), view(cum), view(expand), view(skip), view(gain), of_sequence(tokens, seq),
    ]
    kernel = functools.partial(middle_kernel, seq=seq)
    shared = (tokens.shape[0], seq, begun)
    return streamed(kernel, "middle", [ids, lens, flags, place], operands, outs, scratch, 15, shared)


def scan_back_kernel(
    flags, other_ref, before_ref, act_ref, dact_ref, dt_ref, cum_ref, sig_ref, rowt_ref, dy_ref, hc_ref,
    enter_ref, runs_ref, skip_ref, rate_ref, cw_ref, expand_ref, dx_ref, draw_ref, tail_ref, head_ref,
    grad_s, pre_s, end_s, *, ready, send,
):
    block = pre_s.shape[0] - 8
    steps = act_ref.shape[0] // block
    keep = causal(CHUNK)
    upper = causal(CHUNK).astype(f32).T
    row = lax.broadcasted_iota(jnp.int32, (CHUNK, LANES), 0)
    lane = lax.broadcasted_iota(jnp.int32, (CHUNK, LANES), 1)
    at_b = slice(INNER, INNER + NSTATE)
    at_c = slice(INNER + NSTATE, CONV_CH)
    ready(other_ref, before_ref)
    for t in range(INNER // TILE):
        cols = slice(t * TILE, (t + 1) * TILE)
        grad_s[:, cols] = state_in(flags[0], other_ref, before_ref, cols)
    ready(act_ref, dact_ref, dt_ref, cum_ref, sig_ref, rowt_ref, dy_ref, hc_ref, enter_ref, runs_ref)
    ready(skip_ref, rate_ref, cw_ref, expand_ref)
    pre_s[0:8, :] = jnp.zeros((8, CONV_CH), f32)

    def one_step(turn, carry):
        step = steps - 1 - turn
        base = pl.multiple_of(step * block, block)
        pre_s[block : block + 8, :] = pre_s[0:8, :]
        for c in reversed(range(block // CHUNK)):
            here = slice(c * CHUNK, (c + 1) * CHUNK)
            r = pl.ds(base + c * CHUNK, CHUNK)
            b = act_ref[r, at_b]
            cc = act_ref[r, at_c]
            b_t = turned(b)
            c_t = turned(cc)
            masked = jnp.where(keep, dot_t(cc, b), 0.0)
            dt = dt_ref[r, :]
            cum = cum_ref[r, :]
            cum_t = jnp.transpose(cum)
            p_ec = parts_of(jnp.exp(cum))
            p_dt = parts_of(dt)
            p_w = parts_of(jnp.exp(cum[CHUNK - 1 : CHUNK] - cum))
            p_all = jnp.concatenate([p_ec, p_dt, p_w], axis=0)
            d_scores = jnp.zeros((CHUNK, CHUNK), f32)
            d_b = jnp.zeros((CHUNK, NSTATE), f32)
            d_c = jnp.zeros((CHUNK, NSTATE), f32)
            col = jnp.zeros((CHUNK, LANES), f32)
            for t in range(INNER // TILE):
                cols = slice(t * TILE, (t + 1) * TILE)
                spread = expand_ref[:, cols]
                spreads = dot(p_all, spread)
                ec, dts, w = (spreads[k * CHUNK : (k + 1) * CHUNK] for k in range(3))
                x = act_ref[r, cols].astype(f32)
                xd = (x * dts).astype(bf16)
                dy = dy_ref[r, cols]
                dye = (dy.astype(f32) * ec).astype(bf16)
                grad = grad_s[:, cols]
                grad_low = grad.astype(bf16)
                at = step * (block // CHUNK) + c
                state = hc_ref[at, :, cols].astype(f32)
                state = state + runs_ref[pl.ds(at, 1), cols] * enter_ref[:, cols].astype(f32)
                far = dot(b, grad_low) * w
                xw = (xd.astype(f32) * w).astype(bf16)
                d_b = d_b + dot_t(xw, grad_low)
                d_c = d_c + dot_t(dye, state.astype(bf16))
                out_state = state * ec[CHUNK - 1 : CHUNK] + dot(b_t, xw)
                end = jnp.sum(grad * out_state, axis=0, keepdims=True)
                end_s[:, cols] = split_decay(end)
                grad_s[:, cols] = grad * ec[CHUNK - 1 : CHUNK] + dot(c_t, dye)
                near = []
                for k in range(2):
                    head = t * 4 + k * 2
                    lanes = slice(k * LANES, (k + 1) * LANES)
                    w1, w2 = decayed(cum, cum_t, (head, head + 1))
                    back = jnp.concatenate([turned(w1 * masked), turned(w2 * masked)], axis=1)
                    dy_pair = dy[:, lanes]
                    d_both = dot_t(dy_pair, split_heads(xd[:, lanes]))
                    d_scores = d_scores + w1 * d_both[:, :CHUNK] + w2 * d_both[:, CHUNK:]
                    near.append(dot(back, split_heads(dy_pair)))
                d_xd = jnp.concatenate(near, axis=1) + far
                col = col + dot_t((d_xd * x).astype(bf16), spread)
                d_x = d_xd * dts + skip_ref[:, cols] * dy.astype(f32)
                pre_s[here, cols] = d_x * dact_ref[r, cols].astype(f32)
            ends = jnp.sum(dot_t(end_s[...], expand_ref[...]), axis=0, keepdims=True)
            d_low = jnp.where(keep, d_scores, 0.0)
            d_c = d_c + dot(d_low.astype(bf16), b)
            d_b = d_b + dot(turned(d_low), cc)
            pre_s[here, at_b] = d_b * dact_ref[r, at_b].astype(f32)
            pre_s[here, at_c] = d_c * dact_ref[r, at_c].astype(f32)
            d_cum = rowt_ref[r, :] - dt * col
            d_cum = d_cum + jnp.where(row == CHUNK - 1, ends, 0.0)
            d_log = dot_precise(upper, d_cum)
            d_raw = (d_log * rate_ref[...] + col) * sig_ref[r, :]
            draw_ref[r, :] = jnp.where(lane < HEADS, d_raw, 0.0).astype(bf16)

        strip = 64
        for t in range(CONV_CH // TILE):
            cols = slice(t * TILE, (t + 1) * TILE)
            weights = [cw_ref[j : j + 1, cols] for j in range(4)]
            for i in range(block // strip):
                at = i * strip
                total = weights[3] * pre_s[at : at + strip, cols]
                for j in range(3):
                    total = total + weights[j] * pre_s[at + 3 - j : at + 3 - j + strip, cols]
                dx_ref[pl.ds(base + at, strip), cols] = total.astype(bf16)
                if i == block // strip - 1:
                    end = total[strip - RIM :, :]

                    @pl.when(turn == 0)
                    def _(end=end, cols=cols):
                        tail_ref[:, cols] = end

        send(dx_ref, pl.ds(base, block))
        send(draw_ref, pl.ds(base, block))
        return carry

    lax.fori_loop(0, steps, one_step, 0)
    head_ref[...] = pre_s[0:RIM, :].astype(bf16)
    send(head_ref)
    send(tail_ref)


def scan_back_call(
    flags, other, before, act, dact, dt, cum, sig, rowt, dy, hc, enter, runs, skip, rate, conv_w, expand
):
    rows = act.shape[0]
    block = 2 * CHUNK
    outs = [
        ((rows, CONV_CH), bf16),
        ((rows, LANES), bf16),
        ((RIM, CONV_CH), f32),
        ((RIM, CONV_CH), bf16),
    ]
    scratch = [
        pltpu.VMEM((NSTATE, INNER), f32),
        pltpu.VMEM((block + 8, CONV_CH), f32),
        pltpu.VMEM((RIM, INNER), bf16),
    ]
    arrays = (
        other, before, act, dact, dt, cum, sig, rowt, dy, hc, enter, runs, skip, rate, conv_w, expand,
    )
    operands = [view(a) for a in arrays]
    return streamed(scan_back_kernel, "scan_back", [flags], operands, outs, scratch, 19)


def terms_kernel(
    ids, tail_ref, next_ref, cw_ref, bx_ref, dx_ref, bg_ref, dg_ref, lat_ref, nrm_ref,
    last_ref, d_lat_ref, tb_ref, ta_ref, *, ready, send,
):
    rows = dx_ref.shape[0]
    ready(tail_ref, next_ref, cw_ref)
    row = lax.broadcasted_iota(jnp.int32, (RIM, CONV_CH), 0)
    later = next_ref[...].astype(f32)
    total = tail_ref[...]
    for back in range(1, 4):
        term = jnp.zeros((1, CONV_CH), f32)
        for j in range(0, 4 - back):
            term = term + cw_ref[j : j + 1, :] * later[3 - back - j : 4 - back - j, :]
        total = total + jnp.where(row == RIM - back, term, 0.0)
    last_ref[...] = total.astype(bf16)
    ready(bx_ref, dx_ref)
    dx_ref[rows - RIM :, :] = last_ref[...]
    d_x = dx_ref[:, :INNER]
    d_lat = dot_t(d_x, bx_ref[...])
    ready(bg_ref, dg_ref)
    d_gate = dg_ref[...]
    d_lat = (d_lat + dot_t(d_gate, bg_ref[...])).astype(bf16)
    d_lat_ref[...] = d_lat
    ready(lat_ref, nrm_ref)
    lat_t = turned(lat_ref[...])
    tb_ref[:, :INNER] = dot(lat_t, d_gate).astype(bf16)
    tb_ref[:, INNER:] = dot(lat_t, d_x).astype(bf16)
    ta_ref[...] = dot(turned(d_lat), nrm_ref[...]).astype(bf16)
    for ref in (tb_ref, ta_ref, last_ref, d_lat_ref):
        send(ref)


def terms_call(seq, ids, tail, later, conv_w, dx, dg, lat, nrm, in_b):
    rows = dx.shape[0]
    outs = [((RIM, CONV_CH), bf16), ((rows, RANK), bf16), ((RANK, ZX), bf16), ((RANK, DM), bf16)]
    operands = [
        view(tail), view(later), view(conv_w), of_adapter(in_b, seq, INNER, INNER), view(dx),
        of_adapter(in_b, seq, 0, INNER), view(dg), of_sequence(lat, seq), of_sequence(nrm, seq),
    ]
    return streamed(terms_kernel, "terms", [ids], operands, outs, [], 6)


def input_back_kernel(
    ids, lens, place, dg_ref, wg_ref, last_ref, dx_ref, wx_ref, draw_ref, wdt_ref, d_lat_ref, a_ref, gain_ref, x_ref,
    cot_ref, out_ref, dn_s, *, seq, ready, send,
):
    rows = dx_ref.shape[0]
    ready(dg_ref, wg_ref)
    dn_s[...] = dot_t(dg_ref[...], wg_ref[...])
    ready(last_ref, dx_ref, wx_ref, draw_ref, wdt_ref, d_lat_ref, a_ref)
    dx_ref[rows - RIM :, :] = last_ref[...]
    dn_s[...] += (
        dot_t(dx_ref[...], wx_ref[...]) + dot_t(draw_ref[...], wdt_ref[...]) + dot(d_lat_ref[...], a_ref[...])
    )
    ready(gain_ref, x_ref, cot_ref)
    strip = 32
    for i in range(rows // strip):
        r = slice(i * strip, (i + 1) * strip)
        x = x_ref[r, :].astype(f32)
        root = lax.rsqrt(jnp.mean(x * x, -1, keepdims=True) + epsilon)
        dn = dn_s[r, :] * gain_ref[...]
        back = jnp.mean(dn * x, -1, keepdims=True) * (root * root * root)
        position = i * strip + lax.broadcasted_iota(jnp.int32, (strip, 1), 0)
        kept = jnp.where(position < lens[seq], cot_ref[r, :].astype(f32), 0.0)
        out_ref[r, :] = dn * root - x * back + kept
    send(out_ref)


def input_back_call(seq, ids, lens, place, begun, tokens, cotangent, dg, last, dx, draw, d_lat, wg, wx, wdt, in_a, gain):
    rows = dx.shape[0]
    outs = [((rows, DM), f32)]
    operands = [view(dg), wg, view(last), view(dx), wx, view(draw), wdt, view(d_lat)]
    operands += [of_adapter(in_a, seq), view(gain), of_sequence(tokens, seq), of_sequence(cotangent, seq)]
    kernel = functools.partial(input_back_kernel, seq=seq)
    scratch = [pltpu.VMEM((rows, DM), f32)]
    shared = (tokens.shape[0], seq, begun)
    return streamed(kernel, "input_back", [ids, lens, place], operands, outs, scratch, 9, shared)[0]


def shifted(value, axis, steps):
    count = lax.axis_size(axis)
    pairs = [(i, i + steps) for i in range(count) if 0 <= i + steps < count]
    return lax.ppermute(value, axis, pairs)


def swapped(value, axis, bit):
    return lax.ppermute(value, axis, [(i, i ^ bit) for i in range(lax.axis_size(axis))])


def after(value, other):
    return lax.optimization_barrier((value, other))[0]


def my_half(shard, core, half):
    return lax.dynamic_slice_in_dim(shard, core * half, half, 0)


def gathered_early(meanwhile, shard):
    owners = lax.axis_size("dp")
    rows, width = shard.shape
    half = rows // 2
    shapes = [(rows * owners, CONV_CH), (rows * owners, LANES)]
    if half % 16 or owners % 2:
        full = lax.all_gather(shard, "dp", axis=0, tiled=True)
        return view(full[:, :CONV_CH]), view(full[:, CONV_CH:]), full[0:1]
    core = lax.axis_index("ctx") % 2
    own = {0: my_half(shard, core, half)}
    for k in range(2, owners, 2):
        own[k] = swapped(own[0], "dp", k)
    for k in range(0, owners, 2):
        source = own[k] if k == 0 else after(own[k], (own[k - 1], meanwhile))
        own[k + 1] = swapped(source, "dp", 1)
    pieces = [own[k] for k in range(owners)] + [swapped(own[k], "ctx", 1) for k in range(owners)]

    def copies(scalars, refs, to, columns):
        place = scalars[-1]
        pairs = []
        for n, piece in enumerate(refs):
            side = place[1] if n < owners else 1 - place[1]
            at = pl.multiple_of((place[0] ^ (n % owners)) * rows + side * half, 16)
            pairs.append((piece.at[:, columns], to.at[pl.ds(at, half)]))
        return pairs

    main = functools.partial(copies, columns=pl.ds(0, CONV_CH))
    rest = functools.partial(copies, columns=pl.ds(CONV_CH, LANES))
    return Operand(pieces, shapes[0], main), Operand(pieces, shapes[1], rest), own[owners - 2]


def gathered_late(gate, out, start, hold):
    owners = lax.axis_size("dp")
    rows = gate.shape[0]
    half = rows // 2
    if half % 16:
        return (
            view(lax.all_gather(gate, "dp", axis=0, tiled=True)),
            view(lax.all_gather(out, "dp", axis=0, tiled=True)),
        )
    core = lax.axis_index("ctx") % 2
    both = jnp.concatenate([gate, out[:rows], out[rows:]], axis=1)
    mine = lax.all_gather(after(my_half(both, core, half), start), "dp", axis=0, tiled=True)
    mine = after(mine, hold)
    pieces = [mine, swapped(mine, "ctx", 1)]

    def gate_copies(scalars, refs, to):
        place = scalars[-1]
        pairs = []
        for n, piece in enumerate(refs):
            side = place[1] if n == 0 else 1 - place[1]
            for d in range(owners):
                at = pl.multiple_of(d * rows + side * half, 16)
                pairs.append((piece.at[pl.ds(d * half, half), pl.ds(0, INNER)], to.at[pl.ds(at, half)]))
        return pairs

    def out_copies(scalars, refs, to):
        place = scalars[-1]
        pairs = []
        for n, piece in enumerate(refs):
            side = place[1] if n == 0 else 1 - place[1]
            for d in range(owners):
                for k in range(2):
                    at = pl.multiple_of((2 * d + k) * rows + side * half, 16)
                    columns = pl.ds(INNER + k * DM, DM)
                    pairs.append((piece.at[pl.ds(d * half, half), columns], to.at[pl.ds(at, half)]))
        return pairs

    return (
        Operand(pieces, (rows * owners, INNER), gate_copies),
        Operand(pieces, (2 * rows * owners, DM), out_copies),
    )


def join_kernel(swap, one_ref, two_ref, out_ref, *, ready, send):
    ready(one_ref, two_ref)
    join_payloads(swap[0], one_ref, two_ref, out_ref)
    send(out_ref)


def joined(one, two, swap):
    return streamed(join_kernel, "join", [swap], [view(one), view(two)], [(one.shape, bf16)], [], 1)[0]


def from_before(both, reverse):
    chips = lax.axis_size("ctx") // 2
    sign = -1 if reverse else 1
    in_order = jnp.zeros((1,), jnp.int32)
    before = shifted(both, "ctx", 2 * sign)
    step, run = 1, both
    while 2 * step < chips:
        run = joined(before, both, in_order) if step == 1 else joined(far, run, in_order)
        far = shifted(run, "ctx", 4 * step * sign)
        before = joined(far, before, in_order)
        step *= 2
    return before


def shards(
    tokens, cotangent, lengths, adapter_ids, norm_gain, w_in, conv_weight, conv_bias, dt_bias, a_log,
    skip_scale, inner_gain, w_out, in_a, in_b, out_a, out_b,
):
    seqs, slots, _ = tokens.shape
    owners = lax.axis_size("dp")
    ids = adapter_ids
    lens = jnp.clip(lengths - lax.axis_index("ctx") * slots, 0, slots).astype(jnp.int32)

    def grouped(row):
        padded = jnp.pad(row.reshape(-1, HEADS), ((0, 0), (0, GROUP - HEADS)))
        return jnp.tile(padded, (1, LANES // GROUP))

    rate = grouped(-jnp.exp(a_log))
    dtb = grouped(dt_bias)
    lane = jnp.arange(LANES)[:, None]
    head = jnp.arange(INNER)[None, :] // HDIM
    expand = ((lane % GROUP == head) & (lane < 3 * GROUP)).astype(bf16)
    skip = jnp.repeat(skip_scale, HDIM)[None, :]
    gain = inner_gain[None, :]
    n_gain = norm_gain[None, :]
    conv_b = conv_bias[None, :]

    marks = jnp.broadcast_to(ids.astype(bf16)[None, :], (w_in.shape[0], seqs))
    marks = jnp.pad(marks, ((0, 0), (0, GROUP - HEADS - seqs)))
    steps = jnp.concatenate([w_in[:, INNER + CONV_CH :], marks], axis=1)
    in_a, out_a = jnp.swapaxes(in_a, 1, 2), jnp.swapaxes(out_a, 1, 2)
    rim = shifted(tokens[:, slots - RIM :], "ctx", 1)
    nrm, nrim, lat, lrim = norm_call(ids, tokens, rim, n_gain, in_a)
    wx, wdt, arrived = gathered_early(
        nrm,
        jnp.concatenate([w_in[:, INNER : INNER + CONV_CH]] + [steps] * (LANES // GROUP), axis=1)
    )

    core = lax.axis_index("ctx") % 2
    place = jnp.stack([lax.axis_index("dp"), core]).astype(jnp.int32)
    late = core.reshape(1).astype(jnp.int32)
    early = 1 - late
    front = functools.partial(
        front_call, in_b=in_b, wx=wx, wdt=wdt, conv_w=conv_weight, conv_b=conv_b, dtb=dtb, rate=rate, expand=expand
    )
    fronts, others = [], []
    for s in range(seqs):
        ready = nrm if s == 0 else after(nrm, fronts[-1][5])
        fronts.append(front(s, ids, place, ready, nrim, lat, lrim))
        others.append(swapped(fronts[s][5], "ctx", 1))
    scans, befores = [], []
    for s in range(seqs):
        act, _, dt, cum, _, own, _ = fronts[s]
        ready = after(act, fronts[-1][5]) if s == 0 else after(act, scans[-1][0])
        scans.append(scan_call(late, own, others[s], ready, dt, cum, expand))
        befores.append(from_before(scans[s][2], False))
    full_gate, full_out = gathered_late(w_in[:, :INNER], w_out, arrived, scans[0][0])
    middles, other_grads, later_grads = [], [], []
    for s in range(seqs):
        act, _, _, cum, _, _, _ = fronts[s]
        ready = after(nrm, scans[-1][0]) if s == 0 else after(nrm, both)
        middles.append(
            middle_call(
                s, ids, lens, place, late, middles[-1][0] if s else None, tokens, cotangent, ready, lat, act, cum,
                others[s], befores[s], scans[s][0], full_gate, in_b, full_out, out_a, out_b, skip, gain, expand,
            )
        )
        payload = after(middles[s][4], later_grads[-1]) if s else middles[s][4]
        other_grads.append(swapped(payload, "ctx", 1))
        both = joined(payload, other_grads[s], early)
        later_grads.append(from_before(both, True))
    backs, nexts = [], []
    for s in range(seqs):
        act, dact, dt, cum, sig, _, _ = fronts[s]
        _, dy, _, rowt, _, _, _, enter, runs = middles[s]
        ready = after(act, both) if s == 0 else after(act, backs[-1][3])
        backs.append(
            scan_back_call(
                early, other_grads[s], later_grads[s], ready, dact, dt, cum, sig, rowt, dy, scans[s][1], enter, runs,
                skip, rate, conv_weight, expand,
            )
        )
        nexts.append(shifted(backs[s][3], "ctx", -1))
    terms = [
        terms_call(
            s, ids, backs[s][2], nexts[s], conv_weight, backs[s][0], middles[s][2], lat, nrm, in_b
        )
        for s in range(seqs)
    ]

    def by_owner(terms):
        stacked = jnp.stack(terms)
        return stacked.reshape(seqs, RANK, owners, -1).transpose(2, 0, 1, 3)

    kinds = (
        [term[3] for term in terms],
        [term[2] for term in terms],
        [mid[6] for mid in middles],
        [mid[5] for mid in middles],
    )
    pieces = [by_owner(terms) for terms in kinds]
    widths = [piece.shape[-1] for piece in pieces]
    sent = jnp.concatenate(pieces, axis=-1)
    got = lax.all_to_all(sent, "dp", 0, 0)
    held = after(tokens, sent)
    input_grad = None
    for s in range(seqs):
        if s == 1:
            got = after(got, input_grad)
        input_grad = input_back_call(
            s, ids, lens, place, input_grad, held, cotangent, middles[s][2], terms[s][0], backs[s][0], backs[s][1],
            terms[s][1], full_gate, wx, wdt, in_a, n_gain,
        )
    every = fronts[0][6][:, HEADS : HEADS + seqs].reshape(1, -1)
    chosen = (every == jnp.arange(ADAPT, dtype=f32)[:, None]).astype(f32)
    flat = got.reshape(owners * seqs, -1).astype(f32)
    mine = jnp.sum(chosen[:, :, None] * flat[None], axis=1)
    bit = 1
    while bit < lax.axis_size("ctx"):
        mine = mine + swapped(mine.astype(bf16), "ctx", bit).astype(f32)
        bit *= 2
    mine = mine.reshape(ADAPT, RANK, -1)
    cuts = [sum(widths[:k]) for k in range(5)]
    g_ia, g_ib, g_oa, g_ob = (mine[:, :, cuts[k] : cuts[k + 1]] for k in range(4))
    return (
        middles[-1][0],
        input_grad,
        jnp.swapaxes(g_ia, 1, 2),
        g_ib,
        jnp.swapaxes(g_oa, 1, 2),
        g_ob,
    )


def solution(mesh):
    split = P("dp", "ctx", None)
    return jax.shard_map(
        shards,
        mesh=mesh,
        in_specs=(
            split, split, P("dp"), P("dp"), P(), P("dp", None), P(), P(), P(), P(), P(), P(),
            P("dp", None), P(), P(), P(), P(),
        ),
        out_specs=(
            split, split, P(None, "dp", None), P(None, None, "dp"), P(None, "dp", None), P(None, None, "dp"),
        ),
        check_vma=False,
    )
```

```python
import functools

import jax
import jax.numpy as jnp
from jax import lax
from jax.experimental import pallas as pl
from jax.experimental.pallas import tpu as pltpu
from jax.sharding import PartitionSpec as P

HEADS = 24
HDIM = 64
NSTATE = 128
INNER = 1536
CONV_CH = 1792
ZX = 3072
DM = 768
RANK = 16
ADAPT = 8
CHUNK = 128
TILE = 256
RIM = 16
GROUP = 32
LANES = 128
VMEM_LIMIT = 60 * 1024 * 1024

epsilon = 1e-05
bf16 = jnp.bfloat16
f32 = jnp.float32


def dot(left, right):
    return jnp.dot(left, right, preferred_element_type=f32)


def dot_t(left, right):
    return lax.dot_general(
        left, right, (((1,), (1,)), ((), ())), preferred_element_type=f32
    )


def dot_precise(left, right):
    return jnp.dot(
        left, right, preferred_element_type=f32, precision=lax.Precision.HIGHEST
    )


def parts_of(v):
    lane = lax.broadcasted_iota(jnp.int32, v.shape, 1)
    high = v.astype(bf16).astype(f32)
    rest = v - high
    middle = rest.astype(bf16).astype(f32)
    kept = jnp.where(lane < GROUP, high, jnp.where(lane < 2 * GROUP, middle, rest - middle))
    return jnp.where(lane < 3 * GROUP, kept, 0.0).astype(bf16)


def causal(rows):
    t = lax.broadcasted_iota(jnp.int32, (rows, rows), 0)
    s = lax.broadcasted_iota(jnp.int32, (rows, rows), 1)
    return t >= s


def sigmoid(v):
    return 0.5 * jnp.tanh(0.5 * v) + 0.5


def turned(v):
    return jnp.transpose(v.astype(f32)).astype(bf16)


class Operand:
    def __init__(self, arrays, shape, copies, parts=1, late=False):
        self.arrays, self.shape, self.copies, self.parts = list(arrays), tuple(shape), copies, parts
        self.late = late


def view(array, pick=None, shape=None):
    pick = pick or (lambda scalars, ref: ref)
    return Operand([array], shape or array.shape, lambda scalars, refs, to: [(pick(scalars, refs[0]), to)])


def later(operand):
    return Operand(operand.arrays, operand.shape, operand.copies, operand.parts, True)


def in_parts(array, parts):
    def copies(scalars, refs, to):
        size = array.shape[0] // parts
        return [(refs[0].at[pl.ds(p * size, size)], to.at[pl.ds(p * size, size)]) for p in range(parts)]

    return Operand([array], array.shape, copies, parts)


def streamed(kernel, name, scalars, operands, outs, scratch, micros, shared=None):
    arrays = [array for operand in operands for array in operand.arrays]
    n_scalar, n_array, n_in, n_out = len(scalars), len(arrays), len(operands), len(outs)
    kinds = [operand.arrays[0].dtype for operand in operands]
    slots, slot, begun = shared or (None, None, None)
    parted_in = any(operand.parts > 1 for operand in operands)
    n_begun = 0 if begun is None else 1

    def body(*refs):
        refs = list(refs)
        take = lambda n: [refs.pop(0) for _ in range(n)]
        smem, sources, _, targets, ins, results = (
            take(n) for n in (n_scalar, n_array, n_begun, n_out, n_in, n_out)
        )
        if shared:
            targets[0] = targets[0].at[slot]
        in_sems, out_sems = refs.pop(-2), refs.pop(-1)
        waiting, parted, late, first_sem = {}, [], [], 0
        for k, operand in enumerate(operands):
            mine = [sources.pop(0) for _ in operand.arrays]
            copies = operand.copies(smem, mine, ins[k])
            if operand.parts == 1:
                sem = in_sems.at[first_sem]
                for source, target in copies:
                    copy = pltpu.make_async_copy(source, target, sem)
                    if operand.late:
                        late.append(copy)
                    else:
                        copy.start()
                waiting[id(ins[k])] = [pltpu.make_async_copy(ins[k], ins[k], sem)]
            else:
                made = [
                    pltpu.make_async_copy(source, target, in_sems.at[first_sem + p])
                    for p, (source, target) in enumerate(copies)
                ]
                waiting[id(ins[k])] = made
                parted.append(list(made))
            first_sem += operand.parts
        while any(parted):
            for made in parted:
                if made:
                    made.pop().start()
        for copy in late:
            copy.start()

        def ready(*wanted):
            for ref in wanted:
                for copy in waiting.pop(id(ref), ()):
                    copy.wait()

        def ready_last(*wanted):
            for ref in wanted:
                waiting[id(ref)].pop().wait()

        sent = []

        def send(ref, *at):
            k = [id(result) for result in results].index(id(ref))
            if k not in sent:
                sent.append(k)
            source, target = (results[k].at[at], targets[k].at[at]) if at else (results[k], targets[k])
            pltpu.make_async_copy(source, target, out_sems.at[k]).start()

        more = {"ready_last": ready_last} if parted_in else {}
        kernel(*smem, *ins, *results, *refs, ready=ready, send=send, **more)
        ready(*ins)
        for k in sent:
            pltpu.make_async_copy(results[k], targets[k], out_sems.at[k]).wait()

    anywhere = pl.BlockSpec(memory_space=pl.ANY)
    full = [((slots,) + shape if shared and k == 0 else shape, kind) for k, (shape, kind) in enumerate(outs)]
    return pl.pallas_call(
        body,
        in_specs=[pl.BlockSpec(memory_space=pltpu.SMEM)] * n_scalar + [anywhere] * (n_array + n_begun),
        out_specs=[anywhere] * n_out,
        out_shape=[jax.ShapeDtypeStruct(shape, kind) for shape, kind in full],
        scratch_shapes=[pltpu.VMEM(operand.shape, kind) for operand, kind in zip(operands, kinds)]
        + [pltpu.VMEM(shape, kind) for shape, kind in outs]
        + scratch
        + [pltpu.SemaphoreType.DMA((sum(operand.parts for operand in operands),)), pltpu.SemaphoreType.DMA((n_out,))],
        input_output_aliases={n_scalar + n_array: 0} if n_begun else {},
        compiler_params=pltpu.CompilerParams(vmem_limit_bytes=VMEM_LIMIT),
        cost_estimate=pl.CostEstimate(flops=micros * 1000000000, bytes_accessed=1000000, transcendentals=0),
        name=name,
    )(*scalars, *arrays, *([begun] if n_begun else []))


def of_sequence(array, seq):
    return view(array, lambda scalars, ref: ref.at[seq], array.shape[1:])


def of_adapter(array, seq, start=0, width=None):
    width = width or array.shape[2]
    pick = lambda scalars, ref: ref.at[scalars[0][seq], :, pl.ds(start, width)]
    return view(array, pick, (array.shape[1], width))


def split_decay(decay):
    high = decay.astype(bf16).astype(f32)
    row = lax.broadcasted_iota(jnp.int32, (RIM, decay.shape[1]), 0)
    return jnp.where(row == 0, high, jnp.where(row == 1, decay - high, 0.0)).astype(bf16)


def decay_of(payload_ref, cols):
    rows = payload_ref[NSTATE:, cols].astype(f32)
    return rows[0:1] + rows[1:2]


def norm_kernel(
    ids, x0_ref, x1_ref, rim_ref, gain_ref, a0_ref, a1_ref, nrm_ref, nrim_ref, lat_ref, lrim_ref, *, ready, send
):
    def normed(x):
        x = x.astype(f32)
        mean = jnp.mean(x * x, -1, keepdims=True)
        return (x * lax.rsqrt(mean + epsilon) * gain_ref[...]).astype(bf16)

    strip = 64
    ready(gain_ref, rim_ref)
    for s, (x_ref, a_ref) in enumerate(((x0_ref, a0_ref), (x1_ref, a1_ref))):
        ready(x_ref, a_ref)
        for i in range(x_ref.shape[0] // strip):
            r = slice(i * strip, (i + 1) * strip)
            nrm_ref[s, r, :] = normed(x_ref[r, :])
        nrim_ref[s] = normed(rim_ref[s])
        lat_ref[s] = dot_t(nrm_ref[s], a_ref[...]).astype(bf16)
        lrim_ref[s] = dot_t(nrim_ref[s], a_ref[...]).astype(bf16)
    for ref in (nrm_ref, nrim_ref, lat_ref, lrim_ref):
        send(ref)


def norm_call(ids, tokens, rim, gain, in_a):
    seqs, rows, _ = tokens.shape
    outs = [
        ((seqs, rows, DM), bf16),
        ((seqs, RIM, DM), bf16),
        ((seqs, rows, RANK), bf16),
        ((seqs, RIM, RANK), bf16),
    ]
    operands = [
        of_sequence(tokens, 0), of_sequence(tokens, 1), view(rim), view(gain), of_adapter(in_a, 0), of_adapter(in_a, 1),
    ]
    return streamed(norm_kernel, "norm", [ids], operands, outs, [], 3)


def front_kernel(
    ids, place, nrm_ref, nrim_ref, lat_ref, lrim_ref, wdt_ref, dtb_ref, rate_ref, cw_ref, cb_ref, wx_ref, bx_ref,
    expand_ref, act_ref, dact_ref, dt_ref, cum_ref, sig_ref, pay_ref, marks_ref,
    nrm_s, lat_s, xs, bt_s, w_s, *, ready, send,
):
    rows = nrm_ref.shape[0]
    ready(nrm_ref, nrim_ref, lat_ref, lrim_ref)
    nrm_s[0:RIM, :] = nrim_ref[...]
    nrm_s[RIM:, :] = nrm_ref[...]
    lat_s[0:RIM, :] = lrim_ref[...]
    lat_s[RIM:, :] = lat_ref[...]
    ready(wdt_ref, dtb_ref, rate_ref)
    owners = marks_ref.shape[0]
    for d in range(owners):
        at = d * (wdt_ref.shape[0] // owners)
        marks_ref[d : d + 1, :] = wdt_ref[at : at + 8, :].astype(f32)[0:1]
    send(marks_ref)
    raw = dot(nrm_ref[...], wdt_ref[...]) + dtb_ref[...]
    step = jnp.maximum(raw, 0.0) + jnp.log1p(jnp.exp(-jnp.abs(raw)))
    dt_ref[...] = step
    sig_ref[...] = sigmoid(raw)
    logs = step * rate_ref[...]
    lower = causal(CHUNK).astype(f32)
    before = jnp.zeros((1, LANES), f32)
    whole = []
    for c in range(rows // CHUNK):
        r = slice(c * CHUNK, (c + 1) * CHUNK)
        cum = dot_precise(lower, logs[r])
        cum_ref[r, :] = cum
        whole.append(cum + before)
        before = before + cum[CHUNK - 1 : CHUNK]
    for c in range(rows // CHUNK):
        r = slice(c * CHUNK, (c + 1) * CHUNK)
        w_s[r, :] = parts_of(jnp.exp(before - whole[c]) * step[r])
    total = parts_of(jnp.broadcast_to(jnp.exp(before), (8, LANES)))
    for ref in (dt_ref, cum_ref, sig_ref):
        send(ref)
    ready(cw_ref, cb_ref, wx_ref, bx_ref, expand_ref)

    def activate(cols, base):
        weights = [cw_ref[j : j + 1, cols] for j in range(4)]
        bias = cb_ref[:, cols]
        low = base.astype(bf16).astype(f32)
        for k in range(2):
            xs[k] = low[:, k * LANES : (k + 1) * LANES]
        strip = 64
        for i in range(rows // strip):
            at = RIM + i * strip
            halves = []
            for k in range(2):
                lanes = slice(k * LANES, (k + 1) * LANES)
                pre = bias[:, lanes] + weights[0][:, lanes] * xs[k, at - 3 : at - 3 + strip, :]
                for j in range(1, 4):
                    pre = pre + weights[j][:, lanes] * xs[k, at - 3 + j : at - 3 + j + strip, :]
                halves.append(pre)
            pre = jnp.concatenate(halves, axis=1)
            gate = sigmoid(pre)
            act = pre * gate
            r = slice(i * strip, (i + 1) * strip)
            act_ref[r, cols] = act.astype(bf16)
            dact_ref[r, cols] = (gate + act * (1.0 - gate)).astype(bf16)
        send(act_ref, slice(None), cols)
        send(dact_ref, slice(None), cols)

    last = pl.ds(INNER, CONV_CH - INNER)
    activate(last, dot(nrm_s[...], wx_ref[:, last]))
    bt_s[...] = turned(act_ref[:, INNER : INNER + NSTATE])
    def tile_body(t, carry):
        cols = pl.ds(pl.multiple_of(t * TILE, TILE), TILE)
        activate(cols, dot(nrm_s[...], wx_ref[:, cols]) + dot(lat_s[...], bx_ref[:, cols]))
        scaled = (act_ref[:, cols].astype(f32) * dot(w_s[...], expand_ref[:, cols])).astype(bf16)
        pay_ref[0:NSTATE, cols] = dot(bt_s[...], scaled).astype(bf16)
        pay_ref[NSTATE:, cols] = split_decay(dot(total, expand_ref[:, cols])[0:1])
        return carry

    lax.fori_loop(0, INNER // TILE, tile_body, 0)
    send(pay_ref)


def front_call(seq, ids, place, nrm, nrim, lat, lrim, wx, wdt, in_b, conv_w, conv_b, dtb, rate, expand):
    rows = nrm.shape[1]
    owners = lax.axis_size("dp")
    outs = [
        ((rows, CONV_CH), bf16),
        ((rows, CONV_CH), bf16),
        ((rows, LANES), f32),
        ((rows, LANES), f32),
        ((rows, LANES), f32),
        ((NSTATE + RIM, INNER), bf16),
        ((owners, LANES), f32),
    ]
    scratch = [
        pltpu.VMEM((rows + RIM, DM), bf16),
        pltpu.VMEM((rows + RIM, RANK), bf16),
        pltpu.VMEM((2, rows + RIM, LANES), f32),
        pltpu.VMEM((NSTATE, rows), bf16),
        pltpu.VMEM((rows, LANES), bf16),
    ]
    operands = [of_sequence(a, seq) for a in (nrm, nrim, lat, lrim)]
    operands += [wdt] + [view(a) for a in (dtb, rate, conv_w, conv_b)] + [wx]
    operands += [of_adapter(in_b, seq, INNER, INNER), view(expand)]
    return streamed(front_kernel, "front", [ids, place], operands, outs, scratch, 13)


def column(values, head):
    return jnp.broadcast_to(values[:, head : head + 1], values.shape)


def beside(one, two):
    lane = lax.broadcasted_iota(jnp.int32, one.shape, 1)
    return jnp.where(lane < HDIM, one, two)


def decays(cum, cum_t, head):
    gap = column(cum, head) - cum_t[head : head + 1, :]
    return jnp.exp(jnp.minimum(gap, -gap))


def split_heads(pair):
    lane = lax.broadcasted_iota(jnp.int32, pair.shape, 1)
    zero = jnp.zeros_like(pair)
    first = jnp.where(lane < HDIM, pair, zero)
    second = jnp.where(lane < HDIM, zero, pair)
    return jnp.concatenate([first, second], axis=0)


def join_payloads(swap, one_ref, two_ref, out_ref):
    for t in range(INNER // TILE):
        cols = slice(t * TILE, (t + 1) * TILE)
        d_one, d_two = decay_of(one_ref, cols), decay_of(two_ref, cols)
        one = one_ref[0:NSTATE, cols].astype(f32)
        two = two_ref[0:NSTATE, cols].astype(f32)
        state = jnp.where(swap == 1, d_one * two + one, d_two * one + two)
        out_ref[0:NSTATE, cols] = state.astype(bf16)
        out_ref[NSTATE:, cols] = split_decay(d_one * d_two)


def state_in(late, other_ref, before_ref, cols):
    before = before_ref[0:NSTATE, cols].astype(f32)
    joint = decay_of(other_ref, cols) * before + other_ref[0:NSTATE, cols].astype(f32)
    return jnp.where(late == 1, joint, before)


def scan_kernel(
    flags, own_ref, other_ref, act_ref, dt_ref, cum_ref, y_ref, hc_ref, both_ref, state_s, *, ready, send
):
    keep = causal(CHUNK)
    ready(own_ref, other_ref)
    join_payloads(flags[0], own_ref, other_ref, both_ref)
    send(both_ref)
    state_s[...] = jnp.zeros_like(state_s)
    ready(act_ref, dt_ref, cum_ref)

    def one_chunk(c, carry):
        r = pl.ds(pl.multiple_of(c * CHUNK, CHUNK), CHUNK)
        b = act_ref[r, INNER : INNER + NSTATE]
        cc = act_ref[r, INNER + NSTATE :]
        b_t = turned(b)
        masked = jnp.where(keep, dot_t(cc, b), 0.0)
        dt = dt_ref[r, :]
        cum = cum_ref[r, :]
        cum_t = jnp.transpose(cum)
        for t in range(INNER // LANES):
            cols = slice(t * LANES, (t + 1) * LANES)
            heads = (2 * t, 2 * t + 1)
            cums = beside(*(column(cum, head) for head in heads))
            steps = beside(*(column(dt, head) for head in heads))
            ec = jnp.exp(cums)
            xd = act_ref[r, cols].astype(f32) * steps
            xw = (xd * jnp.exp(cums[CHUNK - 1 : CHUNK] - cums)).astype(bf16)
            state = state_s[:, cols]
            low = state.astype(bf16)
            hc_ref[c, :, cols] = low
            far = dot(cc, low) * ec
            state_s[:, cols] = state * ec[CHUNK - 1 : CHUNK] + dot(b_t, xw)
            weights = [(decays(cum, cum_t, head) * masked).astype(bf16) for head in heads]
            near = dot(jnp.concatenate(weights, axis=1), split_heads(xd.astype(bf16)))
            y_ref[r, cols] = near + far
        send(y_ref, r)
        send(hc_ref, pl.ds(c, 1))
        return carry

    chunks = act_ref.shape[0] // CHUNK
    lax.fori_loop(0, chunks, one_chunk, 0)
    hc_ref[chunks] = state_s[...].astype(bf16)
    send(hc_ref, pl.ds(chunks, 1))


def scan_call(flags, own, other, act, dt, cum):
    rows = act.shape[0]
    chunks = rows // CHUNK
    outs = [((rows, INNER), f32), ((chunks + 1, NSTATE, INNER), bf16), (own.shape, bf16)]
    scratch = [pltpu.VMEM((NSTATE, INNER), f32)]
    operands = [view(a) for a in (own, other, act, dt, cum)]
    return streamed(scan_kernel, "scan", [flags], operands, outs, scratch, 9)


def woven(one, two):
    order = [((n + 0.5) / len(steps), k, step) for k, steps in enumerate((one, two)) for n, step in enumerate(steps)]
    for _, _, step in sorted(order, key=lambda item: item[:2]):
        step()


def middle_kernel(
    ids, lens, flags, place, nrm_ref, lat_ref, bg_ref, wg_ref, cot_ref, b_ref, a_ref, wo_ref, other_ref, before_ref,
    cum_ref, expand_ref, y_ref, act_ref, skip_ref, gain_ref, x_ref,
    out_ref, dy_ref, dg_ref, rowt_ref, pay_ref, tb_ref, ta_ref, enter_ref, runs_ref, d_lat_ref, tg_ref,
    gate_s, z_s, dh_s, hid_s, prod_s, ec_s, grad_s, tb_s, ta_s, tg_s, *, seq, ready, send,
):
    rows = act_ref.shape[0]
    block = 2 * CHUNK
    strip = 16
    tiles = [slice(t * TILE, (t + 1) * TILE) for t in range(INNER // TILE)]
    blocks = [slice(k * block, (k + 1) * block) for k in range(rows // block)]
    kept = [{} for _ in blocks]

    def project(k):
        r = blocks[k]

        def gate_tile(cols):
            gate_s[r, cols] = dot(nrm_ref[r, :], wg_ref[:, cols]) + dot(lat_ref[r, :], bg_ref[:, cols])

        def cut():
            if k == 0:
                ready(cot_ref, b_ref, a_ref, wo_ref)
            position = k * block + lax.broadcasted_iota(jnp.int32, (block, 1), 0)
            kept[k]["valid"] = position < lens[seq]
            kept[k]["g"] = jnp.where(kept[k]["valid"], cot_ref[r, :], jnp.zeros((), bf16))
            kept[k]["d_lat"] = dot_t(kept[k]["g"], b_ref[...]).astype(bf16)

        def hidden_tile(cols):
            d_hidden = dot_t(kept[k]["g"], wo_ref[cols, :]) + dot(kept[k]["d_lat"], a_ref[:, cols])
            dh_s[r, cols] = d_hidden * gain_ref[:, cols]

        def far_tile(cols):
            if k == 0 and cols.start == 0:
                ready(other_ref, before_ref, cum_ref, expand_ref, y_ref, act_ref, skip_ref)
                before = jnp.zeros((1, LANES), f32)
                logs = []
                for c in range(rows // CHUNK):
                    logs.append(cum_ref[c * CHUNK : (c + 1) * CHUNK, :] + before)
                    before = logs[-1][CHUNK - 1 : CHUNK]
                kept[0]["logs"] = logs
                runs_ref[0] = jnp.ones((1, INNER), f32)
            if k == 0:
                enter_ref[:, cols] = state_in(flags[0], other_ref, before_ref, cols).astype(bf16)
            if cols.start == 0:
                own = kept[0]["logs"][2 * k : 2 * k + 2]
                kept[k]["parts"] = parts_of(jnp.exp(jnp.concatenate(own, axis=0)))
            ec = dot(kept[k]["parts"], expand_ref[:, cols])
            ec_s[r, cols] = ec
            for c in range(2):
                runs_ref[2 * k + c + 1, :, cols] = ec[(c + 1) * CHUNK - 1 : (c + 1) * CHUNK]
            y_ref[r, cols] += dot(act_ref[r, INNER + NSTATE :], enter_ref[:, cols]) * ec

        steps = [functools.partial(gate_tile, cols) for cols in tiles] + [cut]
        if k == 0:
            steps.append(lambda: ready(gain_ref))
        steps += [functools.partial(hidden_tile, cols) for cols in tiles]
        return steps + [functools.partial(far_tile, cols) for cols in tiles]

    def forward(k):
        def one(i):
            r = slice(k * block + i * strip, k * block + (i + 1) * strip)
            total = jnp.zeros((strip, LANES), f32)
            for cols in tiles:
                gate = gate_s[r, cols]
                u = y_ref[r, cols] + skip_ref[:, cols] * act_ref[r, cols].astype(f32)
                sig = sigmoid(gate)
                silu = gate * sig
                z = u * silu
                square = z * z
                total = total + square[:, :LANES] + square[:, LANES:]
                z_s[r, cols] = z
                gate_s[r, cols] = silu
                prod_s[r, cols] = u * (sig + silu * (1.0 - sig))
            root = lax.rsqrt(jnp.sum(total, -1, keepdims=True) / INNER + epsilon)
            kept[k][i] = root
            for cols in tiles:
                hid_s[r, cols] = (z_s[r, cols] * root * gain_ref[:, cols]).astype(bf16)

        return [functools.partial(one, i) for i in range(block // strip)]

    def mix(k):
        r = blocks[k]

        def latent():
            if k == 0:
                ready(x_ref)
            lat_out = dot_t(hid_s[r, :], a_ref[...]).astype(bf16)
            kept[k]["lat_out"] = lat_out
            more = dot(turned(lat_out), kept[k]["g"])
            tb_s[...] = more if k == 0 else tb_s[...] + more

        def out_tile(n):
            cols = slice(n * TILE, (n + 1) * TILE)
            mixed = dot(hid_s[r, :], wo_ref[:, cols]) + dot(kept[k]["lat_out"], b_ref[:, cols])
            x = x_ref[r, cols].astype(f32)
            out_ref[r, cols] = jnp.where(kept[k]["valid"], x + mixed, 0.0).astype(bf16)

        def term_tile(cols):
            more = dot(turned(kept[k]["d_lat"]), hid_s[r, cols])
            ta_s[:, cols] = more if k == 0 else ta_s[:, cols] + more

        steps = [latent] + [functools.partial(out_tile, n) for n in range(DM // TILE)]
        steps.append(lambda: send(out_ref, pl.ds(k * block, block)))
        return steps + [functools.partial(term_tile, cols) for cols in tiles]

    def backward(k):
        def one(i):
            r = slice(k * block + i * strip, k * block + (i + 1) * strip)
            total = jnp.zeros((strip, LANES), f32)
            for cols in tiles:
                both = dh_s[r, cols] * z_s[r, cols]
                total = total + both[:, :LANES] + both[:, LANES:]
            root = kept[k][i]
            back = jnp.sum(total, -1, keepdims=True) * (root * root * root) / INNER
            for cols in tiles:
                dz = dh_s[r, cols] * root - z_s[r, cols] * back
                dy = (dz * gate_s[r, cols]).astype(bf16)
                dy_ref[r, cols] = dy
                dg_ref[r, cols] = (dz * prod_s[r, cols]).astype(bf16)
                hid_s[r, cols] = (dy.astype(f32) * y_ref[r, cols]).astype(bf16)

        return [functools.partial(one, i) for i in range(block // strip)]

    def finish(k):
        r = blocks[k]
        at = pl.ds(k * block, block)

        def out():
            send(dy_ref, at)
            send(dg_ref, at)
            rowt_ref[r, :] = dot_t(hid_s[r, :], expand_ref[...])
            send(rowt_ref, at)

        def state_tile(cols):
            if cols.start == 0:
                kept[k]["c_t"] = turned(act_ref[r, INNER + NSTATE :])
            scaled = (dy_ref[r, cols].astype(f32) * ec_s[r, cols]).astype(bf16)
            more = dot(kept[k]["c_t"], scaled)
            grad_s[:, cols] = more if k == 0 else grad_s[:, cols] + more

        def latent():
            d_lat_ref[r, :] = dot_t(dg_ref[r, :], bg_ref[...])

        def term_tile(cols):
            more = dot(turned(lat_ref[r, :]), dg_ref[r, cols])
            tg_s[:, cols] = more if k == 0 else tg_s[:, cols] + more

        steps = [out] + [functools.partial(state_tile, cols) for cols in tiles] + [latent]
        return steps + [functools.partial(term_tile, cols) for cols in tiles]

    ready(nrm_ref, lat_ref, bg_ref, wg_ref)
    last = len(blocks) - 1
    stages = [project, forward, mix, backward, finish]
    for turn in range(len(stages) + last):
        now = [stages[turn - k](k) for k in range(last + 1) if 0 <= turn - k < len(stages)]
        steps = now.pop(0)
        for other in now:
            order = []
            woven([functools.partial(order.append, step) for step in steps], [functools.partial(order.append, step) for step in other])
            steps = order
        for step in steps:
            step()
    send(enter_ref)
    pay_ref[0:NSTATE, :] = grad_s[...].astype(bf16)
    pay_ref[NSTATE:, :] = split_decay(runs_ref[rows // CHUNK])
    tb_ref[...] = tb_s[...].astype(bf16)
    ta_ref[...] = ta_s[...].astype(bf16)
    tg_ref[...] = tg_s[...].astype(bf16)
    for ref in (pay_ref, tb_ref, ta_ref, tg_ref, d_lat_ref, runs_ref):
        send(ref)


def middle_call(
    seq, ids, lens, place, flags, begun, tokens, cotangent, nrm, lat, act, cum, other, before, y, wg, in_b, wo, out_a,
    out_b, skip, gain, expand,
):
    rows = act.shape[0]
    outs = [
        ((rows, DM), bf16),
        ((rows, INNER), bf16),
        ((rows, INNER), bf16),
        ((rows, LANES), f32),
        ((NSTATE + RIM, INNER), bf16),
        ((RANK, DM), bf16),
        ((RANK, INNER), bf16),
        ((NSTATE, INNER), bf16),
        ((rows // CHUNK + 1, 1, INNER), f32),
        ((rows, RANK), f32),
        ((RANK, INNER), bf16),
    ]
    wide = pltpu.VMEM((rows, INNER), f32)
    scratch = [
        wide, wide, wide, pltpu.VMEM((rows, INNER), bf16), wide, wide, pltpu.VMEM((NSTATE, INNER), f32),
        pltpu.VMEM((RANK, DM), f32), pltpu.VMEM((RANK, INNER), f32), pltpu.VMEM((RANK, INNER), f32),
    ]
    operands = [
        of_sequence(nrm, seq), of_sequence(lat, seq), of_adapter(in_b, seq, 0, INNER), wg,
        of_sequence(cotangent, seq), of_adapter(out_b, seq), of_adapter(out_a, seq), wo, view(other), view(before),
        view(cum), view(expand), view(y), view(act), view(skip), view(gain), of_sequence(tokens, seq),
    ]
    kernel = functools.partial(middle_kernel, seq=seq)
    shared = (tokens.shape[0], seq, begun)
    return streamed(kernel, "middle", [ids, lens, flags, place], operands, outs, scratch, 15, shared)


def scan_back_kernel(
    flags, other_ref, before_ref, enter_ref, runs_ref, dt_ref, cum_ref, skip_ref, expand_ref, hc_ref, act_ref, dy_ref,
    dact_ref, rowt_ref, sig_ref, rate_ref, cw_ref, lat_ref, nrm_ref, bx_ref, d_lat_gate_ref,
    dx_ref, draw_ref, tail_ref, head_ref, d_lat_ref, tb_ref, ta_ref,
    grad_s, pre_s, next_s, *, ready, ready_last, send,
):
    rows = act_ref.shape[0]
    chunks = rows // CHUNK
    keep = causal(CHUNK)
    upper = causal(CHUNK).astype(f32).T
    row = lax.broadcasted_iota(jnp.int32, (CHUNK, LANES), 0)
    lane = lax.broadcasted_iota(jnp.int32, (CHUNK, LANES), 1)
    at_b = slice(INNER, INNER + NSTATE)
    at_c = slice(INNER + NSTATE, CONV_CH)
    ready(other_ref, before_ref)
    for t in range(INNER // TILE):
        cols = slice(t * TILE, (t + 1) * TILE)
        grad_s[:, cols] = state_in(flags[0], other_ref, before_ref, cols)
    ready(enter_ref, runs_ref)
    ready_last(hc_ref)
    next_s[...] = hc_ref[chunks].astype(f32) + runs_ref[chunks] * enter_ref[...].astype(f32)
    pre_s[:, rows : rows + 8, :] = jnp.zeros((CONV_CH // LANES, 8, LANES), f32)
    ready(dt_ref, cum_ref, skip_ref, expand_ref)
    for c in reversed(range(chunks)):
        r = slice(c * CHUNK, (c + 1) * CHUNK)
        ready_last(hc_ref, act_ref, dy_ref, dact_ref)
        b = act_ref[r, at_b]
        cc = act_ref[r, at_c]
        c_t = turned(cc)
        masked = jnp.where(keep, dot_t(cc, b), 0.0)
        dt = dt_ref[r, :]
        cum = cum_ref[r, :]
        cum_t = jnp.transpose(cum)
        masked_t = jnp.transpose(masked)
        d_scores = jnp.zeros((CHUNK, CHUNK), f32)
        d_b = jnp.zeros((CHUNK, NSTATE), f32)
        d_c = jnp.zeros((CHUNK, NSTATE), f32)
        col = jnp.zeros((CHUNK + RIM, LANES), f32)
        for t in range(INNER // LANES):
            cols = slice(t * LANES, (t + 1) * LANES)
            heads = (2 * t, 2 * t + 1)
            cums = beside(*(column(cum, head) for head in heads))
            dts = beside(*(column(dt, head) for head in heads))
            ec = jnp.exp(cums)
            w = jnp.exp(cums[CHUNK - 1 : CHUNK] - cums)
            x = act_ref[r, cols].astype(f32)
            xd = (x * dts).astype(bf16)
            dy = dy_ref[r, cols]
            dye = (dy.astype(f32) * ec).astype(bf16)
            grad = grad_s[:, cols]
            grad_low = grad.astype(bf16)
            state = hc_ref[c, :, cols].astype(f32) + runs_ref[c, :, cols] * enter_ref[:, cols].astype(f32)
            far = dot(b, grad_low) * w
            xw = (xd.astype(f32) * w).astype(bf16)
            d_b = d_b + dot_t(xw, grad_low)
            d_c = d_c + dot_t(dye, state.astype(bf16))
            end = split_decay(jnp.sum(grad * next_s[:, cols], axis=0, keepdims=True))
            next_s[:, cols] = state
            grad_s[:, cols] = grad * ec[CHUNK - 1 : CHUNK] + dot(c_t, dye)
            w1, w2 = (decays(cum, cum_t, head) for head in heads)
            back = jnp.concatenate([w1 * masked_t, w2 * masked_t], axis=1).astype(bf16)
            d_both = dot_t(dy, split_heads(xd))
            d_scores = d_scores + w1 * d_both[:, :CHUNK] + w2 * d_both[:, CHUNK:]
            d_xd = dot(back, split_heads(dy)) + far
            sums = jnp.concatenate([(d_xd * x).astype(bf16), end], axis=0)
            col = col + dot_t(sums, expand_ref[:, cols])
            d_x = d_xd * dts + skip_ref[:, cols] * dy.astype(f32)
            pre_s[t, r, :] = d_x * dact_ref[r, cols].astype(f32)
        ends = col[CHUNK : CHUNK + 1] + col[CHUNK + 1 : CHUNK + 2]
        col = col[:CHUNK]
        d_low = jnp.where(keep, d_scores, 0.0)
        d_c = d_c + dot(d_low.astype(bf16), b)
        d_b = d_b + dot(turned(d_low), cc)
        pre_s[INNER // LANES, r, :] = d_b * dact_ref[r, at_b].astype(f32)
        pre_s[INNER // LANES + 1, r, :] = d_c * dact_ref[r, at_c].astype(f32)
        if c == chunks - 1:
            ready(rowt_ref, sig_ref, rate_ref, cw_ref)
        d_cum = rowt_ref[r, :] - dt * col
        d_cum = d_cum + jnp.where(row == CHUNK - 1, ends, 0.0)
        d_log = dot_precise(upper, d_cum)
        d_raw = (d_log * rate_ref[...] + col) * sig_ref[r, :]
        draw_ref[r, :] = jnp.where(lane < HEADS, d_raw, 0.0).astype(bf16)

        strip = 64
        for t in range(CONV_CH // LANES):
            cols = slice(t * LANES, (t + 1) * LANES)
            weights = [cw_ref[j : j + 1, cols] for j in range(4)]
            for at in range(c * CHUNK, (c + 1) * CHUNK, strip):
                total = weights[3] * pre_s[t, at : at + strip, :]
                for j in range(3):
                    total = total + weights[j] * pre_s[t, at + 3 - j : at + 3 - j + strip, :]
                dx_ref[at : at + strip, cols] = total.astype(bf16)
                if at + strip == rows:
                    tail_ref[:, cols] = total[strip - RIM :, :]
        send(dx_ref, pl.ds(c * CHUNK, CHUNK))
        if c == chunks - 1:
            send(tail_ref)
    for t in range(CONV_CH // LANES):
        head_ref[:, t * LANES : (t + 1) * LANES] = pre_s[t, 0:RIM, :].astype(bf16)
    send(head_ref)
    send(draw_ref)

    ready(lat_ref, nrm_ref, bx_ref, d_lat_gate_ref)
    d_x = dx_ref[:, :INNER]
    d_lat = (d_lat_gate_ref[...] + dot_t(d_x, bx_ref[...])).astype(bf16)
    d_lat_ref[...] = d_lat
    send(d_lat_ref)
    sure = lax.broadcasted_iota(jnp.int32, (rows, RANK), 0) < rows - RIM
    tb_ref[...] = dot(turned(jnp.where(sure, lat_ref[...].astype(f32), 0.0)), d_x)
    ta_ref[...] = dot(turned(jnp.where(sure, d_lat.astype(f32), 0.0)), nrm_ref[...])
    send(tb_ref)
    send(ta_ref)


def scan_back_call(
    seq, ids, flags, other, before, act, dact, dt, cum, sig, rowt, dy, hc, enter, runs, lat, nrm, in_b, d_lat_gate, skip,
    rate, conv_w, expand,
):
    rows = act.shape[0]
    chunks = rows // CHUNK
    outs = [
        ((rows, CONV_CH), bf16),
        ((rows, LANES), bf16),
        ((RIM, CONV_CH), f32),
        ((RIM, CONV_CH), bf16),
        ((rows, RANK), bf16),
        ((RANK, INNER), f32),
        ((RANK, DM), f32),
    ]
    scratch = [
        pltpu.VMEM((NSTATE, INNER), f32),
        pltpu.VMEM((CONV_CH // LANES, rows + 8, LANES), f32),
        pltpu.VMEM((NSTATE, INNER), f32),
    ]
    operands = [view(a) for a in (other, before, enter, runs, dt, cum, skip, expand)]
    operands += [in_parts(hc, chunks + 1), in_parts(act, chunks), in_parts(dy, chunks), in_parts(dact, chunks)]
    operands += [later(view(a)) for a in (rowt, sig, rate, conv_w)]
    operands += [later(of_sequence(lat, seq)), later(of_sequence(nrm, seq))]
    operands += [later(of_adapter(in_b, seq, INNER, INNER)), later(view(d_lat_gate))]

    def kernel(ids, flags, *refs, **calls):
        scan_back_kernel(flags, *refs, **calls)

    return streamed(kernel, "scan_back", [ids, flags], operands, outs, scratch, 19)


def terms_kernel(*refs, seqs, owners, ready, send):
    refs = list(refs)[1:]
    per = 11
    ins, outs = refs[: 1 + per * seqs], refs[1 + per * seqs :]
    cw_ref, sent_ref = ins[0], outs[-1]
    ready(cw_ref)
    row = lax.broadcasted_iota(jnp.int32, (RIM, CONV_CH), 0)
    for s in range(seqs):
        tail_ref, next_ref, bx_ref, gate_ref, lat_ref, nrm_ref, tb_ref, ta_ref, tg_ref, ob_ref, oa_ref = ins[
            1 + per * s : 1 + per * (s + 1)
        ]
        last_ref, d_lat_ref = outs[2 * s : 2 * s + 2]
        ready(*ins[1 + per * s : 1 + per * (s + 1)])
        later_rows = next_ref[...].astype(f32)
        total = tail_ref[...]
        for back in range(1, 4):
            term = jnp.zeros((1, CONV_CH), f32)
            for j in range(0, 4 - back):
                term = term + cw_ref[j : j + 1, :] * later_rows[3 - back - j : 4 - back - j, :]
            total = total + jnp.where(row == RIM - back, term, 0.0)
        last = total.astype(bf16)
        last_ref[...] = last
        d_x = last[:, :INNER]
        d_lat = (gate_ref[...] + dot_t(d_x, bx_ref[...])).astype(bf16)
        d_lat_ref[...] = d_lat
        send(last_ref)
        send(d_lat_ref)
        in_b = (tb_ref[...] + dot(turned(lat_ref[...]), d_x)).astype(bf16)
        in_a = (ta_ref[...] + dot(turned(d_lat), nrm_ref[...])).astype(bf16)
        both = jnp.concatenate([tg_ref[...], in_b], axis=1)
        kinds = [in_a, both, oa_ref[...], ob_ref[...]]
        for d in range(owners):
            pieces = []
            for kind in kinds:
                width = kind.shape[1] // owners
                pieces.append(kind[:, d * width : (d + 1) * width])
            sent_ref[d, s] = jnp.concatenate(pieces, axis=1)
    send(sent_ref)


def terms_call(ids, conv_w, items, lat, nrm, in_b, owners):
    seqs, rows, _ = nrm.shape
    last_rows = lambda scalars, ref: ref.at[pl.ds(rows - RIM, RIM)]
    operands = [view(conv_w)]
    outs = []
    for s, (tail, following, d_lat_gate, tb, ta, tg, ob, oa) in enumerate(items):
        of_last = lambda scalars, ref, s=s: ref.at[s, pl.ds(rows - RIM, RIM)]
        operands += [
            view(tail), view(following), of_adapter(in_b, s, INNER, INNER), view(d_lat_gate, last_rows, (RIM, RANK)),
            view(lat, of_last, (RIM, RANK)), view(nrm, of_last, (RIM, DM)), view(tb), view(ta), view(tg), view(ob),
            view(oa),
        ]
        outs += [((RIM, CONV_CH), bf16), ((RIM, RANK), bf16)]
    width = (2 * DM + ZX + INNER) // owners
    outs.append(((owners, seqs, RANK, width), bf16))
    kernel = functools.partial(terms_kernel, seqs=seqs, owners=owners)
    return streamed(kernel, "terms", [ids], operands, outs, [], 4)


def input_back_kernel(
    ids, lens, place, dg_ref, wg_ref, last_ref, dx_ref, wx_ref, draw_ref, wdt_ref, d_lat_ref, d_lat_last_ref, a_ref,
    gain_ref, x_ref, cot_ref, out_ref, dn_s, *, seq, ready, send,
):
    rows = dx_ref.shape[0]
    ready(dg_ref, wg_ref)
    dn_s[...] = dot_t(dg_ref[...], wg_ref[...])
    ready(last_ref, dx_ref, wx_ref, draw_ref, wdt_ref, d_lat_ref, d_lat_last_ref, a_ref)
    dx_ref[rows - RIM :, :] = last_ref[...]
    d_lat_ref[rows - RIM :, :] = d_lat_last_ref[...]
    dn_s[...] += (
        dot_t(dx_ref[...], wx_ref[...]) + dot_t(draw_ref[...], wdt_ref[...]) + dot(d_lat_ref[...], a_ref[...])
    )
    ready(gain_ref, x_ref, cot_ref)
    strip = 32
    for i in range(rows // strip):
        r = slice(i * strip, (i + 1) * strip)
        x = x_ref[r, :].astype(f32)
        root = lax.rsqrt(jnp.mean(x * x, -1, keepdims=True) + epsilon)
        dn = dn_s[r, :] * gain_ref[...]
        back = jnp.mean(dn * x, -1, keepdims=True) * (root * root * root)
        position = i * strip + lax.broadcasted_iota(jnp.int32, (strip, 1), 0)
        kept = jnp.where(position < lens[seq], cot_ref[r, :].astype(f32), 0.0)
        out_ref[r, :] = dn * root - x * back + kept
    send(out_ref)


def input_back_call(seq, ids, lens, place, begun, tokens, cotangent, dg, last, dx, draw, d_lat, d_lat_last, wg, wx, wdt, in_a, gain):
    rows = dx.shape[0]
    outs = [((rows, DM), f32)]
    operands = [view(dg), wg, view(last), view(dx), wx, view(draw), wdt, view(d_lat), view(d_lat_last)]
    operands += [of_adapter(in_a, seq), view(gain), of_sequence(tokens, seq), of_sequence(cotangent, seq)]
    kernel = functools.partial(input_back_kernel, seq=seq)
    scratch = [pltpu.VMEM((rows, DM), f32)]
    shared = (tokens.shape[0], seq, begun)
    return streamed(kernel, "input_back", [ids, lens, place], operands, outs, scratch, 9, shared)[0]


def shifted(value, axis, steps):
    count = lax.axis_size(axis)
    pairs = [(i, i + steps) for i in range(count) if 0 <= i + steps < count]
    return lax.ppermute(value, axis, pairs)


def swapped(value, axis, bit):
    return lax.ppermute(value, axis, [(i, i ^ bit) for i in range(lax.axis_size(axis))])


def after(value, other):
    return lax.optimization_barrier((value, other))[0]


def my_half(shard, core, half):
    return lax.dynamic_slice_in_dim(shard, core * half, half, 0)


def gathered_early(meanwhile, shard):
    owners = lax.axis_size("dp")
    rows, width = shard.shape
    half = rows // 2
    shapes = [(rows * owners, CONV_CH), (rows * owners, LANES)]
    if half % 16 or owners % 2:
        full = lax.all_gather(shard, "dp", axis=0, tiled=True)
        return view(full[:, :CONV_CH]), view(full[:, CONV_CH:]), None
    core = lax.axis_index("ctx") % 2
    own = {0: my_half(shard, core, half)}
    for k in range(2, owners, 2):
        own[k] = swapped(own[0], "dp", k)
    own[1] = swapped(own[0], "dp", 1)
    for k in range(2, owners, 2):
        waits = (own[3], meanwhile) if k == owners - 2 else own[1]
        own[k + 1] = swapped(after(own[k], waits), "dp", 1)
    pieces = [own[k] for k in range(owners)] + [swapped(own[k], "ctx", 1) for k in range(owners)]

    def copies(scalars, refs, to, columns):
        place = scalars[-1]
        pairs = []
        for n, piece in enumerate(refs):
            side = place[1] if n < owners else 1 - place[1]
            at = pl.multiple_of((place[0] ^ (n % owners)) * rows + side * half, 16)
            pairs.append((piece.at[:, columns], to.at[pl.ds(at, half)]))
        return pairs

    main = functools.partial(copies, columns=pl.ds(0, CONV_CH))
    rest = functools.partial(copies, columns=pl.ds(CONV_CH, LANES))
    arrived = (tuple(own[k] for k in range(2, owners, 2)), own[owners - 1])
    return Operand(pieces, shapes[0], main), Operand(pieces, shapes[1], rest), arrived


def gathered_late(gate, out, arrived, fronts, scans):
    owners = lax.axis_size("dp")
    rows = gate.shape[0]
    half = rows // 2
    if arrived is None:
        return (
            view(lax.all_gather(gate, "dp", axis=0, tiled=True)),
            view(lax.all_gather(out, "dp", axis=0, tiled=True)),
        )
    core = lax.axis_index("ctx") % 2
    mine = my_half(jnp.concatenate([gate, out[:rows], out[rows:]], axis=1), core, half)
    own = {0: mine}
    for k in range(2, owners, 2):
        own[k] = swapped(after(mine, arrived[0][0] if k == 2 else arrived[0]), "dp", k)
    for k in range(0, owners, 2):
        waits = arrived[1] if k <= 2 else fronts[-1][5]
        own[k + 1] = swapped(after(own[k], waits), "dp", 1)
    pieces = [own[k] for k in range(owners)]
    pieces += [swapped(after(own[k], scans[0 if k < 4 else -1][0]), "ctx", 1) for k in range(owners)]

    def placed(scalars, refs):
        place = scalars[-1]
        for n, piece in enumerate(refs):
            side = place[1] if n < owners else 1 - place[1]
            yield piece, place[0] ^ (n % owners), side * half

    def gate_copies(scalars, refs, to):
        pairs = []
        for piece, owner, start in placed(scalars, refs):
            at = pl.multiple_of(owner * rows + start, 16)
            pairs.append((piece.at[:, pl.ds(0, INNER)], to.at[pl.ds(at, half)]))
        return pairs

    def out_copies(scalars, refs, to):
        pairs = []
        for piece, owner, start in placed(scalars, refs):
            for k in range(2):
                at = pl.multiple_of((2 * owner + k) * rows + start, 16)
                pairs.append((piece.at[:, pl.ds(INNER + k * DM, DM)], to.at[pl.ds(at, half)]))
        return pairs

    return (
        Operand(pieces, (rows * owners, INNER), gate_copies),
        Operand(pieces, (2 * rows * owners, DM), out_copies),
    )


def join_kernel(swap, one_ref, two_ref, out_ref, *, ready, send):
    ready(one_ref, two_ref)
    join_payloads(swap[0], one_ref, two_ref, out_ref)
    send(out_ref)


def joined(one, two, swap):
    return streamed(join_kernel, "join", [swap], [view(one), view(two)], [(one.shape, bf16)], [], 1)[0]


def from_before(both, reverse):
    chips = lax.axis_size("ctx") // 2
    sign = -1 if reverse else 1
    in_order = jnp.zeros((1,), jnp.int32)
    before = shifted(both, "ctx", 2 * sign)
    step, run = 1, both
    while 2 * step < chips:
        run = joined(before, both, in_order) if step == 1 else joined(far, run, in_order)
        far = shifted(run, "ctx", 4 * step * sign)
        before = joined(far, before, in_order)
        step *= 2
    return before


def shards(
    tokens, cotangent, lengths, adapter_ids, norm_gain, w_in, conv_weight, conv_bias, dt_bias, a_log,
    skip_scale, inner_gain, w_out, in_a, in_b, out_a, out_b,
):
    seqs, slots, _ = tokens.shape
    owners = lax.axis_size("dp")
    ids = adapter_ids
    lens = jnp.clip(lengths - lax.axis_index("ctx") * slots, 0, slots).astype(jnp.int32)

    def grouped(row):
        padded = jnp.pad(row.reshape(-1, HEADS), ((0, 0), (0, GROUP - HEADS)))
        return jnp.tile(padded, (1, LANES // GROUP))

    rate = grouped(-jnp.exp(a_log))
    dtb = grouped(dt_bias)
    lane = jnp.arange(LANES)[:, None]
    head = jnp.arange(INNER)[None, :] // HDIM
    expand = ((lane % GROUP == head) & (lane < 3 * GROUP)).astype(bf16)
    skip = jnp.repeat(skip_scale, HDIM)[None, :]
    gain = inner_gain[None, :]
    n_gain = norm_gain[None, :]
    conv_b = conv_bias[None, :]

    marks = jnp.broadcast_to(ids.astype(bf16)[None, :], (w_in.shape[0], seqs))
    marks = jnp.pad(marks, ((0, 0), (0, GROUP - HEADS - seqs)))
    steps = jnp.concatenate([w_in[:, INNER + CONV_CH :], marks], axis=1)
    in_a, out_a = jnp.swapaxes(in_a, 1, 2), jnp.swapaxes(out_a, 1, 2)
    rim = shifted(tokens[:, slots - RIM :], "ctx", 1)
    nrm, nrim, lat, lrim = norm_call(ids, tokens, rim, n_gain, in_a)
    wx, wdt, arrived = gathered_early(
        nrm,
        jnp.concatenate([w_in[:, INNER : INNER + CONV_CH]] + [steps] * (LANES // GROUP), axis=1)
    )

    core = lax.axis_index("ctx") % 2
    place = jnp.stack([lax.axis_index("dp"), core]).astype(jnp.int32)
    late = core.reshape(1).astype(jnp.int32)
    early = 1 - late
    front = functools.partial(
        front_call, in_b=in_b, wx=wx, wdt=wdt, conv_w=conv_weight, conv_b=conv_b, dtb=dtb, rate=rate, expand=expand
    )
    fronts, others = [], []
    for s in range(seqs):
        ready = nrm if s == 0 else after(nrm, fronts[-1][5])
        fronts.append(front(s, ids, place, ready, nrim, lat, lrim))
        others.append(swapped(fronts[s][5], "ctx", 1))
    scans, befores = [], []
    for s in range(seqs):
        act, _, dt, cum, _, own, _ = fronts[s]
        ready = after(act, fronts[-1][5]) if s == 0 else after(act, scans[-1][0])
        scans.append(scan_call(late, own, others[s], ready, dt, cum))
        befores.append(from_before(scans[s][2], False))
    full_gate, full_out = gathered_late(w_in[:, :INNER], w_out, arrived, fronts, scans)
    middles, other_grads, later_grads = [], [], []
    for s in range(seqs):
        act, _, _, cum, _, _, _ = fronts[s]
        ready = after(nrm, scans[-1][0]) if s == 0 else after(nrm, both)
        middles.append(
            middle_call(
                s, ids, lens, place, late, middles[-1][0] if s else None, tokens, cotangent, ready, lat, act, cum,
                others[s], befores[s], scans[s][0], full_gate, in_b, full_out, out_a, out_b, skip, gain, expand,
            )
        )
        payload = after(middles[s][4], later_grads[-1] if s else befores[-1])
        other_grads.append(swapped(payload, "ctx", 1))
        both = joined(payload, other_grads[s], early)
        later_grads.append(from_before(both, True))
    backs, nexts = [], []
    for s in range(seqs):
        act, dact, dt, cum, sig, _, _ = fronts[s]
        _, dy, _, rowt, _, _, _, enter, runs, d_lat_gate, _ = middles[s]
        ready = after(act, both) if s == 0 else after(act, backs[-1][3])
        backs.append(
            scan_back_call(
                s, ids, early, other_grads[s], later_grads[s], ready, dact, dt, cum, sig, rowt, dy, scans[s][1], enter,
                runs, lat, nrm, in_b, d_lat_gate, skip, rate, conv_weight, expand,
            )
        )
        nexts.append(shifted(backs[s][3], "ctx", -1))
    items = [
        (back[2], following, mid[9], back[5], back[6], mid[10], mid[5], mid[6])
        for back, following, mid in zip(backs, nexts, middles)
    ]
    *lasts, sent = terms_call(ids, conv_weight, items, lat, nrm, in_b, owners)

    widths = [width // owners for width in (DM, ZX, INNER, DM)]
    got = lax.all_to_all(sent, "dp", 0, 0)
    held = after(tokens, sent)
    input_grad = None
    for s in range(seqs):
        if s == 1:
            got = after(got, input_grad)
        input_grad = input_back_call(
            s, ids, lens, place, input_grad, held, cotangent, middles[s][2], lasts[2 * s], backs[s][0], backs[s][1],
            backs[s][4], lasts[2 * s + 1], full_gate, wx, wdt, in_a, n_gain,
        )
    every = fronts[0][6][:, HEADS : HEADS + seqs].reshape(1, -1)
    chosen = (every == jnp.arange(ADAPT, dtype=f32)[:, None]).astype(f32)
    flat = got.reshape(owners * seqs, -1).astype(f32)
    mine = jnp.sum(chosen[:, :, None] * flat[None], axis=1)
    bit = 1
    while bit < lax.axis_size("ctx"):
        mine = mine + swapped(mine.astype(bf16), "ctx", bit).astype(f32)
        bit *= 2
    mine = mine.reshape(ADAPT, RANK, -1)
    cuts = [sum(widths[:k]) for k in range(5)]
    g_ia, g_ib, g_oa, g_ob = (mine[:, :, cuts[k] : cuts[k + 1]] for k in range(4))
    return (
        middles[-1][0],
        input_grad,
        jnp.swapaxes(g_ia, 1, 2),
        g_ib,
        jnp.swapaxes(g_oa, 1, 2),
        g_ob,
    )


def solution(mesh):
    split = P("dp", "ctx", None)
    return jax.shard_map(
        shards,
        mesh=mesh,
        in_specs=(
            split, split, P("dp"), P("dp"), P(), P("dp", None), P(), P(), P(), P(), P(), P(),
            P("dp", None), P(), P(), P(), P(),
        ),
        out_specs=(
            split, split, P(None, "dp", None), P(None, None, "dp"), P(None, "dp", None), P(None, None, "dp"),
        ),
        check_vma=False,
    )
```

```python
import functools

import jax
import jax.numpy as jnp
from jax import lax
from jax.experimental import pallas as pl
from jax.experimental.pallas import tpu as pltpu
from jax.sharding import PartitionSpec as P

HEADS = 24
HDIM = 64
NSTATE = 128
INNER = 1536
CONV_CH = 1792
ZX = 3072
DM = 768
RANK = 16
ADAPT = 8
CHUNK = 128
TILE = 256
RIM = 16
GROUP = 32
LANES = 128
VMEM_LIMIT = 60 * 1024 * 1024

epsilon = 1e-05
bf16 = jnp.bfloat16
f32 = jnp.float32


def dot(left, right):
    return jnp.dot(left, right, preferred_element_type=f32)


def dot_t(left, right):
    return lax.dot_general(
        left, right, (((1,), (1,)), ((), ())), preferred_element_type=f32
    )


def dot_precise(left, right):
    return jnp.dot(
        left, right, preferred_element_type=f32, precision=lax.Precision.HIGHEST
    )


def parts_of(v):
    lane = lax.broadcasted_iota(jnp.int32, v.shape, 1)
    high = v.astype(bf16).astype(f32)
    rest = v - high
    middle = rest.astype(bf16).astype(f32)
    kept = jnp.where(lane < GROUP, high, jnp.where(lane < 2 * GROUP, middle, rest - middle))
    return jnp.where(lane < 3 * GROUP, kept, 0.0).astype(bf16)


def causal(rows):
    t = lax.broadcasted_iota(jnp.int32, (rows, rows), 0)
    s = lax.broadcasted_iota(jnp.int32, (rows, rows), 1)
    return t >= s


def sigmoid(v):
    return 0.5 * jnp.tanh(0.5 * v) + 0.5


def turned(v):
    return jnp.transpose(v.astype(f32)).astype(bf16)


class Operand:
    def __init__(self, arrays, shape, copies, parts=1, late=False):
        self.arrays, self.shape, self.copies, self.parts = list(arrays), tuple(shape), copies, parts
        self.late = late


def view(array, pick=None, shape=None):
    pick = pick or (lambda scalars, ref: ref)
    return Operand([array], shape or array.shape, lambda scalars, refs, to: [(pick(scalars, refs[0]), to)])


def later(operand):
    return Operand(operand.arrays, operand.shape, operand.copies, operand.parts, True)


def in_parts(array, parts):
    def copies(scalars, refs, to):
        size = array.shape[0] // parts
        return [(refs[0].at[pl.ds(p * size, size)], to.at[pl.ds(p * size, size)]) for p in range(parts)]

    return Operand([array], array.shape, copies, parts)


def streamed(kernel, name, scalars, operands, outs, scratch, micros, shared=None):
    arrays = [array for operand in operands for array in operand.arrays]
    n_scalar, n_array, n_in, n_out = len(scalars), len(arrays), len(operands), len(outs)
    kinds = [operand.arrays[0].dtype for operand in operands]
    slots, slot, begun = shared or (None, None, None)
    parted_in = any(operand.parts > 1 for operand in operands)
    n_begun = 0 if begun is None else 1

    def body(*refs):
        refs = list(refs)
        take = lambda n: [refs.pop(0) for _ in range(n)]
        smem, sources, _, targets, ins, results = (
            take(n) for n in (n_scalar, n_array, n_begun, n_out, n_in, n_out)
        )
        if shared:
            targets[0] = targets[0].at[slot]
        in_sems, out_sems = refs.pop(-2), refs.pop(-1)
        waiting, parted, late, first_sem = {}, [], [], 0
        for k, operand in enumerate(operands):
            mine = [sources.pop(0) for _ in operand.arrays]
            copies = operand.copies(smem, mine, ins[k])
            if operand.parts == 1:
                sem = in_sems.at[first_sem]
                for source, target in copies:
                    copy = pltpu.make_async_copy(source, target, sem)
                    if operand.late:
                        late.append(copy)
                    else:
                        copy.start()
                waiting[id(ins[k])] = [pltpu.make_async_copy(ins[k], ins[k], sem)]
            else:
                made = [
                    pltpu.make_async_copy(source, target, in_sems.at[first_sem + p])
                    for p, (source, target) in enumerate(copies)
                ]
                waiting[id(ins[k])] = made
                parted.append(list(made))
            first_sem += operand.parts
        while any(parted):
            for made in parted:
                if made:
                    made.pop().start()
        for copy in late:
            copy.start()

        def ready(*wanted):
            for ref in wanted:
                for copy in waiting.pop(id(ref), ()):
                    copy.wait()

        def ready_last(*wanted):
            for ref in wanted:
                waiting[id(ref)].pop().wait()

        sent = []

        def send(ref, *at):
            k = [id(result) for result in results].index(id(ref))
            if k not in sent:
                sent.append(k)
            source, target = (results[k].at[at], targets[k].at[at]) if at else (results[k], targets[k])
            pltpu.make_async_copy(source, target, out_sems.at[k]).start()

        more = {"ready_last": ready_last} if parted_in else {}
        kernel(*smem, *ins, *results, *refs, ready=ready, send=send, **more)
        ready(*ins)
        for k in sent:
            pltpu.make_async_copy(results[k], targets[k], out_sems.at[k]).wait()

    anywhere = pl.BlockSpec(memory_space=pl.ANY)
    full = [((slots,) + shape if shared and k == 0 else shape, kind) for k, (shape, kind) in enumerate(outs)]
    return pl.pallas_call(
        body,
        in_specs=[pl.BlockSpec(memory_space=pltpu.SMEM)] * n_scalar + [anywhere] * (n_array + n_begun),
        out_specs=[anywhere] * n_out,
        out_shape=[jax.ShapeDtypeStruct(shape, kind) for shape, kind in full],
        scratch_shapes=[pltpu.VMEM(operand.shape, kind) for operand, kind in zip(operands, kinds)]
        + [pltpu.VMEM(shape, kind) for shape, kind in outs]
        + scratch
        + [pltpu.SemaphoreType.DMA((sum(operand.parts for operand in operands),)), pltpu.SemaphoreType.DMA((n_out,))],
        input_output_aliases={n_scalar + n_array: 0} if n_begun else {},
        compiler_params=pltpu.CompilerParams(vmem_limit_bytes=VMEM_LIMIT),
        cost_estimate=pl.CostEstimate(flops=micros * 1000000000, bytes_accessed=1000000, transcendentals=0),
        name=name,
    )(*scalars, *arrays, *([begun] if n_begun else []))


def of_sequence(array, seq):
    return view(array, lambda scalars, ref: ref.at[seq], array.shape[1:])


def of_adapter(array, seq, start=0, width=None):
    width = width or array.shape[2]
    pick = lambda scalars, ref: ref.at[scalars[0][seq], :, pl.ds(start, width)]
    return view(array, pick, (array.shape[1], width))


def split_decay(decay):
    high = decay.astype(bf16).astype(f32)
    row = lax.broadcasted_iota(jnp.int32, (RIM, decay.shape[1]), 0)
    return jnp.where(row == 0, high, jnp.where(row == 1, decay - high, 0.0)).astype(bf16)


def decay_of(payload_ref, cols):
    rows = payload_ref[NSTATE:, cols].astype(f32)
    return rows[0:1] + rows[1:2]


def norm_kernel(
    ids, x0_ref, x1_ref, rim_ref, gain_ref, a0_ref, a1_ref, nrm_ref, nrim_ref, lat_ref, lrim_ref, *, ready, send
):
    def normed(x):
        x = x.astype(f32)
        mean = jnp.mean(x * x, -1, keepdims=True)
        return (x * lax.rsqrt(mean + epsilon) * gain_ref[...]).astype(bf16)

    strip = 64
    ready(gain_ref, rim_ref)
    for s, (x_ref, a_ref) in enumerate(((x0_ref, a0_ref), (x1_ref, a1_ref))):
        ready(x_ref, a_ref)
        for i in range(x_ref.shape[0] // strip):
            r = slice(i * strip, (i + 1) * strip)
            nrm_ref[s, r, :] = normed(x_ref[r, :])
        nrim_ref[s] = normed(rim_ref[s])
        lat_ref[s] = dot_t(nrm_ref[s], a_ref[...]).astype(bf16)
        lrim_ref[s] = dot_t(nrim_ref[s], a_ref[...]).astype(bf16)
    for ref in (nrm_ref, nrim_ref, lat_ref, lrim_ref):
        send(ref)


def norm_call(ids, tokens, rim, gain, in_a):
    seqs, rows, _ = tokens.shape
    outs = [
        ((seqs, rows, DM), bf16),
        ((seqs, RIM, DM), bf16),
        ((seqs, rows, RANK), bf16),
        ((seqs, RIM, RANK), bf16),
    ]
    operands = [
        of_sequence(tokens, 0), of_sequence(tokens, 1), view(rim), view(gain), of_adapter(in_a, 0), of_adapter(in_a, 1),
    ]
    return streamed(norm_kernel, "norm", [ids], operands, outs, [], 3)


def front_kernel(
    ids, place, nrm_ref, nrim_ref, lat_ref, lrim_ref, wdt_ref, dtb_ref, rate_ref, cw_ref, cb_ref, wx_ref, bx_ref,
    expand_ref, act_ref, dact_ref, dt_ref, cum_ref, sig_ref, pay_ref, marks_ref,
    nrm_s, lat_s, xs, bt_s, w_s, *, ready, send,
):
    rows = nrm_ref.shape[0]
    ready(nrm_ref, nrim_ref, lat_ref, lrim_ref)
    nrm_s[0:RIM, :] = nrim_ref[...]
    nrm_s[RIM:, :] = nrm_ref[...]
    lat_s[0:RIM, :] = lrim_ref[...]
    lat_s[RIM:, :] = lat_ref[...]
    ready(wdt_ref, dtb_ref, rate_ref)
    owners = marks_ref.shape[0]
    for d in range(owners):
        at = d * (wdt_ref.shape[0] // owners)
        marks_ref[d : d + 1, :] = wdt_ref[at : at + 8, :].astype(f32)[0:1]
    send(marks_ref)
    raw = dot(nrm_ref[...], wdt_ref[...]) + dtb_ref[...]
    step = jnp.maximum(raw, 0.0) + jnp.log1p(jnp.exp(-jnp.abs(raw)))
    dt_ref[...] = step
    sig_ref[...] = sigmoid(raw)
    logs = step * rate_ref[...]
    lower = causal(CHUNK).astype(f32)
    before = jnp.zeros((1, LANES), f32)
    whole = []
    for c in range(rows // CHUNK):
        r = slice(c * CHUNK, (c + 1) * CHUNK)
        cum = dot_precise(lower, logs[r])
        cum_ref[r, :] = cum
        whole.append(cum + before)
        before = before + cum[CHUNK - 1 : CHUNK]
    for c in range(rows // CHUNK):
        r = slice(c * CHUNK, (c + 1) * CHUNK)
        w_s[r, :] = parts_of(jnp.exp(before - whole[c]) * step[r])
    total = parts_of(jnp.broadcast_to(jnp.exp(before), (8, LANES)))
    for ref in (dt_ref, cum_ref, sig_ref):
        send(ref)
    ready(cw_ref, cb_ref, wx_ref, bx_ref, expand_ref)

    def activate(cols, base):
        weights = [cw_ref[j : j + 1, cols] for j in range(4)]
        bias = cb_ref[:, cols]
        low = base.astype(bf16).astype(f32)
        for k in range(2):
            xs[k] = low[:, k * LANES : (k + 1) * LANES]
        strip = 64
        for i in range(rows // strip):
            at = RIM + i * strip
            halves = []
            for k in range(2):
                lanes = slice(k * LANES, (k + 1) * LANES)
                pre = bias[:, lanes] + weights[0][:, lanes] * xs[k, at - 3 : at - 3 + strip, :]
                for j in range(1, 4):
                    pre = pre + weights[j][:, lanes] * xs[k, at - 3 + j : at - 3 + j + strip, :]
                halves.append(pre)
            pre = jnp.concatenate(halves, axis=1)
            gate = sigmoid(pre)
            act = pre * gate
            r = slice(i * strip, (i + 1) * strip)
            act_ref[r, cols] = act.astype(bf16)
            dact_ref[r, cols] = (gate + act * (1.0 - gate)).astype(bf16)
        send(act_ref, slice(None), cols)
        send(dact_ref, slice(None), cols)

    last = pl.ds(INNER, CONV_CH - INNER)
    activate(last, dot(nrm_s[...], wx_ref[:, last]))
    bt_s[...] = turned(act_ref[:, INNER : INNER + NSTATE])
    def tile_body(t, carry):
        cols = pl.ds(pl.multiple_of(t * TILE, TILE), TILE)
        activate(cols, dot(nrm_s[...], wx_ref[:, cols]) + dot(lat_s[...], bx_ref[:, cols]))
        scaled = (act_ref[:, cols].astype(f32) * dot(w_s[...], expand_ref[:, cols])).astype(bf16)
        pay_ref[0:NSTATE, cols] = dot(bt_s[...], scaled).astype(bf16)
        pay_ref[NSTATE:, cols] = split_decay(dot(total, expand_ref[:, cols])[0:1])
        return carry

    lax.fori_loop(0, INNER // TILE, tile_body, 0)
    send(pay_ref)


def front_call(seq, ids, place, nrm, nrim, lat, lrim, wx, wdt, in_b, conv_w, conv_b, dtb, rate, expand):
    rows = nrm.shape[1]
    owners = lax.axis_size("dp")
    outs = [
        ((rows, CONV_CH), bf16),
        ((rows, CONV_CH), bf16),
        ((rows, LANES), f32),
        ((rows, LANES), f32),
        ((rows, LANES), f32),
        ((NSTATE + RIM, INNER), bf16),
        ((owners, LANES), f32),
    ]
    scratch = [
        pltpu.VMEM((rows + RIM, DM), bf16),
        pltpu.VMEM((rows + RIM, RANK), bf16),
        pltpu.VMEM((2, rows + RIM, LANES), f32),
        pltpu.VMEM((NSTATE, rows), bf16),
        pltpu.VMEM((rows, LANES), bf16),
    ]
    operands = [of_sequence(a, seq) for a in (nrm, nrim, lat, lrim)]
    operands += [wdt] + [view(a) for a in (dtb, rate, conv_w, conv_b)] + [wx]
    operands += [of_adapter(in_b, seq, INNER, INNER), view(expand)]
    return streamed(front_kernel, "front", [ids, place], operands, outs, scratch, 13)


def column(values, head):
    return jnp.broadcast_to(values[:, head : head + 1], values.shape)


def beside(one, two):
    lane = lax.broadcasted_iota(jnp.int32, one.shape, 1)
    return jnp.where(lane < HDIM, one, two)


def decays(cum, cum_t, head):
    gap = column(cum, head) - cum_t[head : head + 1, :]
    return jnp.exp(jnp.minimum(gap, -gap))


def split_heads(pair):
    lane = lax.broadcasted_iota(jnp.int32, pair.shape, 1)
    zero = jnp.zeros_like(pair)
    first = jnp.where(lane < HDIM, pair, zero)
    second = jnp.where(lane < HDIM, zero, pair)
    return jnp.concatenate([first, second], axis=0)


def join_payloads(swap, one_ref, two_ref, out_ref):
    for t in range(INNER // TILE):
        cols = slice(t * TILE, (t + 1) * TILE)
        d_one, d_two = decay_of(one_ref, cols), decay_of(two_ref, cols)
        one = one_ref[0:NSTATE, cols].astype(f32)
        two = two_ref[0:NSTATE, cols].astype(f32)
        state = jnp.where(swap == 1, d_one * two + one, d_two * one + two)
        out_ref[0:NSTATE, cols] = state.astype(bf16)
        out_ref[NSTATE:, cols] = split_decay(d_one * d_two)


def state_in(late, other_ref, before_ref, cols):
    before = before_ref[0:NSTATE, cols].astype(f32)
    joint = decay_of(other_ref, cols) * before + other_ref[0:NSTATE, cols].astype(f32)
    return jnp.where(late == 1, joint, before)


def scan_kernel(
    flags, own_ref, other_ref, act_ref, dt_ref, cum_ref, y_ref, hc_ref, both_ref, state_s, *, ready, send
):
    keep = causal(CHUNK)
    ready(own_ref, other_ref)
    join_payloads(flags[0], own_ref, other_ref, both_ref)
    send(both_ref)
    state_s[...] = jnp.zeros_like(state_s)
    ready(act_ref, dt_ref, cum_ref)

    def one_chunk(c, carry):
        r = pl.ds(pl.multiple_of(c * CHUNK, CHUNK), CHUNK)
        b = act_ref[r, INNER : INNER + NSTATE]
        cc = act_ref[r, INNER + NSTATE :]
        b_t = turned(b)
        masked = jnp.where(keep, dot_t(cc, b), 0.0)
        dt = dt_ref[r, :]
        cum = cum_ref[r, :]
        cum_t = jnp.transpose(cum)
        for t in range(INNER // LANES):
            cols = slice(t * LANES, (t + 1) * LANES)
            heads = (2 * t, 2 * t + 1)
            cums = beside(*(column(cum, head) for head in heads))
            steps = beside(*(column(dt, head) for head in heads))
            ec = jnp.exp(cums)
            xd = act_ref[r, cols].astype(f32) * steps
            xw = (xd * jnp.exp(cums[CHUNK - 1 : CHUNK] - cums)).astype(bf16)
            state = state_s[:, cols]
            low = state.astype(bf16)
            hc_ref[c, :, cols] = low
            far = dot(cc, low) * ec
            state_s[:, cols] = state * ec[CHUNK - 1 : CHUNK] + dot(b_t, xw)
            weights = [(decays(cum, cum_t, head) * masked).astype(bf16) for head in heads]
            near = dot(jnp.concatenate(weights, axis=1), split_heads(xd.astype(bf16)))
            y_ref[r, cols] = near + far
        send(y_ref, r)
        send(hc_ref, pl.ds(c, 1))
        return carry

    chunks = act_ref.shape[0] // CHUNK
    lax.fori_loop(0, chunks, one_chunk, 0)
    hc_ref[chunks] = state_s[...].astype(bf16)
    send(hc_ref, pl.ds(chunks, 1))


def scan_call(flags, own, other, act, dt, cum):
    rows = act.shape[0]
    chunks = rows // CHUNK
    outs = [((rows, INNER), f32), ((chunks + 1, NSTATE, INNER), bf16), (own.shape, bf16)]
    scratch = [pltpu.VMEM((NSTATE, INNER), f32)]
    operands = [view(a) for a in (own, other, act, dt, cum)]
    return streamed(scan_kernel, "scan", [flags], operands, outs, scratch, 9)


def woven(one, two):
    order = [((n + 0.5) / len(steps), k, step) for k, steps in enumerate((one, two)) for n, step in enumerate(steps)]
    for _, _, step in sorted(order, key=lambda item: item[:2]):
        step()


def middle_kernel(
    ids, lens, flags, place, nrm_ref, lat_ref, bg_ref, wg_ref, cot_ref, b_ref, a_ref, wo_ref, other_ref, before_ref,
    cum_ref, expand_ref, y_ref, act_ref, skip_ref, gain_ref, x_ref,
    out_ref, dy_ref, dg_ref, rowt_ref, pay_ref, tb_ref, ta_ref, enter_ref, runs_ref, d_lat_ref, tg_ref,
    gate_s, z_s, dh_s, hid_s, prod_s, ec_s, grad_s, tb_s, ta_s, tg_s, *, seq, ready, send,
):
    rows = act_ref.shape[0]
    block = 2 * CHUNK
    strip = 16
    tiles = [slice(t * TILE, (t + 1) * TILE) for t in range(INNER // TILE)]
    blocks = [slice(k * block, (k + 1) * block) for k in range(rows // block)]
    kept = [{} for _ in blocks]

    def project(k):
        r = blocks[k]

        def gate_tile(cols):
            gate_s[r, cols] = dot(nrm_ref[r, :], wg_ref[:, cols]) + dot(lat_ref[r, :], bg_ref[:, cols])

        def cut():
            if k == 0:
                ready(cot_ref, b_ref, a_ref, wo_ref)
            position = k * block + lax.broadcasted_iota(jnp.int32, (block, 1), 0)
            kept[k]["valid"] = position < lens[seq]
            kept[k]["g"] = jnp.where(kept[k]["valid"], cot_ref[r, :], jnp.zeros((), bf16))
            kept[k]["d_lat"] = dot_t(kept[k]["g"], b_ref[...]).astype(bf16)

        def hidden_tile(cols):
            d_hidden = dot_t(kept[k]["g"], wo_ref[cols, :]) + dot(kept[k]["d_lat"], a_ref[:, cols])
            dh_s[r, cols] = d_hidden * gain_ref[:, cols]

        def far_tile(cols):
            if k == 0 and cols.start == 0:
                ready(other_ref, before_ref, cum_ref, expand_ref, y_ref, act_ref, skip_ref)
                before = jnp.zeros((1, LANES), f32)
                logs = []
                for c in range(rows // CHUNK):
                    logs.append(cum_ref[c * CHUNK : (c + 1) * CHUNK, :] + before)
                    before = logs[-1][CHUNK - 1 : CHUNK]
                kept[0]["logs"] = logs
                runs_ref[0] = jnp.ones((1, INNER), f32)
            if k == 0:
                enter_ref[:, cols] = state_in(flags[0], other_ref, before_ref, cols).astype(bf16)
            if cols.start == 0:
                own = kept[0]["logs"][2 * k : 2 * k + 2]
                kept[k]["parts"] = parts_of(jnp.exp(jnp.concatenate(own, axis=0)))
            ec = dot(kept[k]["parts"], expand_ref[:, cols])
            ec_s[r, cols] = ec
            for c in range(2):
                runs_ref[2 * k + c + 1, :, cols] = ec[(c + 1) * CHUNK - 1 : (c + 1) * CHUNK]
            y_ref[r, cols] += dot(act_ref[r, INNER + NSTATE :], enter_ref[:, cols]) * ec

        steps = [functools.partial(gate_tile, cols) for cols in tiles] + [cut]
        if k == 0:
            steps.append(lambda: ready(gain_ref))
        steps += [functools.partial(hidden_tile, cols) for cols in tiles]
        return steps + [functools.partial(far_tile, cols) for cols in tiles]

    def forward(k):
        def one(i):
            r = slice(k * block + i * strip, k * block + (i + 1) * strip)
            total = jnp.zeros((strip, LANES), f32)
            for cols in tiles:
                gate = gate_s[r, cols]
                u = y_ref[r, cols] + skip_ref[:, cols] * act_ref[r, cols].astype(f32)
                sig = sigmoid(gate)
                silu = gate * sig
                z = u * silu
                square = z * z
                total = total + square[:, :LANES] + square[:, LANES:]
                z_s[r, cols] = z
                gate_s[r, cols] = silu
                prod_s[r, cols] = u * (sig + silu * (1.0 - sig))
            root = lax.rsqrt(jnp.sum(total, -1, keepdims=True) / INNER + epsilon)
            kept[k][i] = root
            for cols in tiles:
                hid_s[r, cols] = (z_s[r, cols] * root * gain_ref[:, cols]).astype(bf16)

        return [functools.partial(one, i) for i in range(block // strip)]

    def mix(k):
        r = blocks[k]

        def latent():
            if k == 0:
                ready(x_ref)
            lat_out = dot_t(hid_s[r, :], a_ref[...]).astype(bf16)
            kept[k]["lat_out"] = lat_out
            more = dot(turned(lat_out), kept[k]["g"])
            tb_s[...] = more if k == 0 else tb_s[...] + more

        def out_tile(n):
            cols = slice(n * TILE, (n + 1) * TILE)
            mixed = dot(hid_s[r, :], wo_ref[:, cols]) + dot(kept[k]["lat_out"], b_ref[:, cols])
            x = x_ref[r, cols].astype(f32)
            out_ref[r, cols] = jnp.where(kept[k]["valid"], x + mixed, 0.0).astype(bf16)

        def term_tile(cols):
            more = dot(turned(kept[k]["d_lat"]), hid_s[r, cols])
            ta_s[:, cols] = more if k == 0 else ta_s[:, cols] + more

        steps = [latent] + [functools.partial(out_tile, n) for n in range(DM // TILE)]
        steps.append(lambda: send(out_ref, pl.ds(k * block, block)))
        return steps + [functools.partial(term_tile, cols) for cols in tiles]

    def backward(k):
        def one(i):
            r = slice(k * block + i * strip, k * block + (i + 1) * strip)
            total = jnp.zeros((strip, LANES), f32)
            for cols in tiles:
                both = dh_s[r, cols] * z_s[r, cols]
                total = total + both[:, :LANES] + both[:, LANES:]
            root = kept[k][i]
            back = jnp.sum(total, -1, keepdims=True) * (root * root * root) / INNER
            for cols in tiles:
                dz = dh_s[r, cols] * root - z_s[r, cols] * back
                dy = (dz * gate_s[r, cols]).astype(bf16)
                dy_ref[r, cols] = dy
                dg_ref[r, cols] = (dz * prod_s[r, cols]).astype(bf16)
                hid_s[r, cols] = (dy.astype(f32) * y_ref[r, cols]).astype(bf16)

        return [functools.partial(one, i) for i in range(block // strip)]

    def finish(k):
        r = blocks[k]
        at = pl.ds(k * block, block)

        def out():
            send(dy_ref, at)
            send(dg_ref, at)
            rowt_ref[r, :] = dot_t(hid_s[r, :], expand_ref[...])
            send(rowt_ref, at)

        def state_tile(cols):
            if cols.start == 0:
                kept[k]["c_t"] = turned(act_ref[r, INNER + NSTATE :])
            scaled = (dy_ref[r, cols].astype(f32) * ec_s[r, cols]).astype(bf16)
            more = dot(kept[k]["c_t"], scaled)
            grad_s[:, cols] = more if k == 0 else grad_s[:, cols] + more

        def latent():
            d_lat_ref[r, :] = dot_t(dg_ref[r, :], bg_ref[...])

        def term_tile(cols):
            more = dot(turned(lat_ref[r, :]), dg_ref[r, cols])
            tg_s[:, cols] = more if k == 0 else tg_s[:, cols] + more

        steps = [out] + [functools.partial(state_tile, cols) for cols in tiles] + [latent]
        return steps + [functools.partial(term_tile, cols) for cols in tiles]

    ready(nrm_ref, lat_ref, bg_ref, wg_ref)
    last = len(blocks) - 1
    stages = [project, forward, mix, backward, finish]
    for turn in range(len(stages) + last):
        now = [stages[turn - k](k) for k in range(last + 1) if 0 <= turn - k < len(stages)]
        steps = now.pop(0)
        for other in now:
            order = []
            woven([functools.partial(order.append, step) for step in steps], [functools.partial(order.append, step) for step in other])
            steps = order
        for step in steps:
            step()
    send(enter_ref)
    pay_ref[0:NSTATE, :] = grad_s[...].astype(bf16)
    pay_ref[NSTATE:, :] = split_decay(runs_ref[rows // CHUNK])
    tb_ref[...] = tb_s[...].astype(bf16)
    ta_ref[...] = ta_s[...].astype(bf16)
    tg_ref[...] = tg_s[...].astype(bf16)
    for ref in (pay_ref, tb_ref, ta_ref, tg_ref, d_lat_ref, runs_ref):
        send(ref)


def middle_call(
    seq, ids, lens, place, flags, begun, tokens, cotangent, nrm, lat, act, cum, other, before, y, wg, in_b, wo, out_a,
    out_b, skip, gain, expand,
):
    rows = act.shape[0]
    outs = [
        ((rows, DM), bf16),
        ((rows, INNER), bf16),
        ((rows, INNER), bf16),
        ((rows, LANES), f32),
        ((NSTATE + RIM, INNER), bf16),
        ((RANK, DM), bf16),
        ((RANK, INNER), bf16),
        ((NSTATE, INNER), bf16),
        ((rows // CHUNK + 1, 1, INNER), f32),
        ((rows, RANK), f32),
        ((RANK, INNER), bf16),
    ]
    wide = pltpu.VMEM((rows, INNER), f32)
    scratch = [
        wide, wide, wide, pltpu.VMEM((rows, INNER), bf16), wide, wide, pltpu.VMEM((NSTATE, INNER), f32),
        pltpu.VMEM((RANK, DM), f32), pltpu.VMEM((RANK, INNER), f32), pltpu.VMEM((RANK, INNER), f32),
    ]
    operands = [
        of_sequence(nrm, seq), of_sequence(lat, seq), of_adapter(in_b, seq, 0, INNER), wg,
        of_sequence(cotangent, seq), of_adapter(out_b, seq), of_adapter(out_a, seq), wo, view(other), view(before),
        view(cum), view(expand), view(y), view(act), view(skip), view(gain), of_sequence(tokens, seq),
    ]
    kernel = functools.partial(middle_kernel, seq=seq)
    shared = (tokens.shape[0], seq, begun)
    return streamed(kernel, "middle", [ids, lens, flags, place], operands, outs, scratch, 15, shared)


def scan_back_kernel(
    flags, other_ref, before_ref, before_other_ref, enter_ref, runs_ref, dt_ref, cum_ref, skip_ref, expand_ref, hc_ref, act_ref, dy_ref,
    dact_ref, rowt_ref, sig_ref, rate_ref, cw_ref, lat_ref, nrm_ref, bx_ref, d_lat_gate_ref,
    dx_ref, draw_ref, tail_ref, head_ref, d_lat_ref, tb_ref, ta_ref,
    grad_s, pre_s, next_s, *, ready, ready_last, send,
):
    rows = act_ref.shape[0]
    chunks = rows // CHUNK
    keep = causal(CHUNK)
    upper = causal(CHUNK).astype(f32).T
    row = lax.broadcasted_iota(jnp.int32, (CHUNK, LANES), 0)
    lane = lax.broadcasted_iota(jnp.int32, (CHUNK, LANES), 1)
    at_b = slice(INNER, INNER + NSTATE)
    at_c = slice(INNER + NSTATE, CONV_CH)
    ready(other_ref, before_ref, before_other_ref)
    for t in range(INNER // TILE):
        cols = slice(t * TILE, (t + 1) * TILE)
        grad_s[:, cols] = state_in_two(flags, other_ref, before_ref, before_other_ref, cols)
    ready(enter_ref, runs_ref)
    ready_last(hc_ref)
    next_s[...] = hc_ref[chunks].astype(f32) + runs_ref[chunks] * enter_ref[...].astype(f32)
    pre_s[:, rows : rows + 8, :] = jnp.zeros((CONV_CH // LANES, 8, LANES), f32)
    ready(dt_ref, cum_ref, skip_ref, expand_ref)
    for c in reversed(range(chunks)):
        r = slice(c * CHUNK, (c + 1) * CHUNK)
        ready_last(hc_ref, act_ref, dy_ref, dact_ref)
        b = act_ref[r, at_b]
        cc = act_ref[r, at_c]
        c_t = turned(cc)
        masked = jnp.where(keep, dot_t(cc, b), 0.0)
        dt = dt_ref[r, :]
        cum = cum_ref[r, :]
        cum_t = jnp.transpose(cum)
        masked_t = jnp.transpose(masked)
        d_scores = jnp.zeros((CHUNK, CHUNK), f32)
        d_b = jnp.zeros((CHUNK, NSTATE), f32)
        d_c = jnp.zeros((CHUNK, NSTATE), f32)
        col = jnp.zeros((CHUNK + RIM, LANES), f32)
        for t in range(INNER // LANES):
            cols = slice(t * LANES, (t + 1) * LANES)
            heads = (2 * t, 2 * t + 1)
            cums = beside(*(column(cum, head) for head in heads))
            dts = beside(*(column(dt, head) for head in heads))
            ec = jnp.exp(cums)
            w = jnp.exp(cums[CHUNK - 1 : CHUNK] - cums)
            x = act_ref[r, cols].astype(f32)
            xd = (x * dts).astype(bf16)
            dy = dy_ref[r, cols]
            dye = (dy.astype(f32) * ec).astype(bf16)
            grad = grad_s[:, cols]
            grad_low = grad.astype(bf16)
            state = hc_ref[c, :, cols].astype(f32) + runs_ref[c, :, cols] * enter_ref[:, cols].astype(f32)
            far = dot(b, grad_low) * w
            xw = (xd.astype(f32) * w).astype(bf16)
            d_b = d_b + dot_t(xw, grad_low)
            d_c = d_c + dot_t(dye, state.astype(bf16))
            end = split_decay(jnp.sum(grad * next_s[:, cols], axis=0, keepdims=True))
            next_s[:, cols] = state
            grad_s[:, cols] = grad * ec[CHUNK - 1 : CHUNK] + dot(c_t, dye)
            w1, w2 = (decays(cum, cum_t, head) for head in heads)
            back = jnp.concatenate([w1 * masked_t, w2 * masked_t], axis=1).astype(bf16)
            d_both = dot_t(dy, split_heads(xd))
            d_scores = d_scores + w1 * d_both[:, :CHUNK] + w2 * d_both[:, CHUNK:]
            d_xd = dot(back, split_heads(dy)) + far
            sums = jnp.concatenate([(d_xd * x).astype(bf16), end], axis=0)
            col = col + dot_t(sums, expand_ref[:, cols])
            d_x = d_xd * dts + skip_ref[:, cols] * dy.astype(f32)
            pre_s[t, r, :] = d_x * dact_ref[r, cols].astype(f32)
        ends = col[CHUNK : CHUNK + 1] + col[CHUNK + 1 : CHUNK + 2]
        col = col[:CHUNK]
        d_low = jnp.where(keep, d_scores, 0.0)
        d_c = d_c + dot(d_low.astype(bf16), b)
        d_b = d_b + dot(turned(d_low), cc)
        pre_s[INNER // LANES, r, :] = d_b * dact_ref[r, at_b].astype(f32)
        pre_s[INNER // LANES + 1, r, :] = d_c * dact_ref[r, at_c].astype(f32)
        if c == chunks - 1:
            ready(rowt_ref, sig_ref, rate_ref, cw_ref)
        d_cum = rowt_ref[r, :] - dt * col
        d_cum = d_cum + jnp.where(row == CHUNK - 1, ends, 0.0)
        d_log = dot_precise(upper, d_cum)
        d_raw = (d_log * rate_ref[...] + col) * sig_ref[r, :]
        draw_ref[r, :] = jnp.where(lane < HEADS, d_raw, 0.0).astype(bf16)

        strip = 64
        for t in range(CONV_CH // LANES):
            cols = slice(t * LANES, (t + 1) * LANES)
            weights = [cw_ref[j : j + 1, cols] for j in range(4)]
            for at in range(c * CHUNK, (c + 1) * CHUNK, strip):
                total = weights[3] * pre_s[t, at : at + strip, :]
                for j in range(3):
                    total = total + weights[j] * pre_s[t, at + 3 - j : at + 3 - j + strip, :]
                dx_ref[at : at + strip, cols] = total.astype(bf16)
                if at + strip == rows:
                    tail_ref[:, cols] = total[strip - RIM :, :]
        send(dx_ref, pl.ds(c * CHUNK, CHUNK))
        if c == chunks - 1:
            send(tail_ref)
    for t in range(CONV_CH // LANES):
        head_ref[:, t * LANES : (t + 1) * LANES] = pre_s[t, 0:RIM, :].astype(bf16)
    send(head_ref)
    send(draw_ref)

    ready(lat_ref, nrm_ref, bx_ref, d_lat_gate_ref)
    d_x = dx_ref[:, :INNER]
    d_lat = (d_lat_gate_ref[...] + dot_t(d_x, bx_ref[...])).astype(bf16)
    d_lat_ref[...] = d_lat
    send(d_lat_ref)
    sure = lax.broadcasted_iota(jnp.int32, (rows, RANK), 0) < rows - RIM
    tb_ref[...] = dot(turned(jnp.where(sure, lat_ref[...].astype(f32), 0.0)), d_x)
    ta_ref[...] = dot(turned(jnp.where(sure, d_lat.astype(f32), 0.0)), nrm_ref[...])
    send(tb_ref)
    send(ta_ref)


def scan_back_call(
    seq, ids, flags, other, before, before_other, act, dact, dt, cum, sig, rowt, dy, hc, enter, runs, lat, nrm, in_b, d_lat_gate, skip,
    rate, conv_w, expand,
):
    rows = act.shape[0]
    chunks = rows // CHUNK
    outs = [
        ((rows, CONV_CH), bf16),
        ((rows, LANES), bf16),
        ((RIM, CONV_CH), f32),
        ((RIM, CONV_CH), bf16),
        ((rows, RANK), bf16),
        ((RANK, INNER), f32),
        ((RANK, DM), f32),
    ]
    scratch = [
        pltpu.VMEM((NSTATE, INNER), f32),
        pltpu.VMEM((CONV_CH // LANES, rows + 8, LANES), f32),
        pltpu.VMEM((NSTATE, INNER), f32),
    ]
    operands = [view(a) for a in (other, before, before_other, enter, runs, dt, cum, skip, expand)]
    operands += [in_parts(hc, chunks + 1), in_parts(act, chunks), in_parts(dy, chunks), in_parts(dact, chunks)]
    operands += [later(view(a)) for a in (rowt, sig, rate, conv_w)]
    operands += [later(of_sequence(lat, seq)), later(of_sequence(nrm, seq))]
    operands += [later(of_adapter(in_b, seq, INNER, INNER)), later(view(d_lat_gate))]

    def kernel(ids, flags, *refs, **calls):
        scan_back_kernel(flags, *refs, **calls)

    return streamed(kernel, "scan_back", [ids, flags], operands, outs, scratch, 19)


def terms_kernel(*refs, seqs, owners, ready, send):
    refs = list(refs)[1:]
    per = 11
    ins, outs = refs[: 1 + per * seqs], refs[1 + per * seqs :]
    cw_ref, sent_ref = ins[0], outs[-1]
    ready(cw_ref)
    row = lax.broadcasted_iota(jnp.int32, (RIM, CONV_CH), 0)
    for s in range(seqs):
        tail_ref, next_ref, bx_ref, gate_ref, lat_ref, nrm_ref, tb_ref, ta_ref, tg_ref, ob_ref, oa_ref = ins[
            1 + per * s : 1 + per * (s + 1)
        ]
        last_ref, d_lat_ref = outs[2 * s : 2 * s + 2]
        ready(*ins[1 + per * s : 1 + per * (s + 1)])
        later_rows = next_ref[...].astype(f32)
        total = tail_ref[...]
        for back in range(1, 4):
            term = jnp.zeros((1, CONV_CH), f32)
            for j in range(0, 4 - back):
                term = term + cw_ref[j : j + 1, :] * later_rows[3 - back - j : 4 - back - j, :]
            total = total + jnp.where(row == RIM - back, term, 0.0)
        last = total.astype(bf16)
        last_ref[...] = last
        d_x = last[:, :INNER]
        d_lat = (gate_ref[...] + dot_t(d_x, bx_ref[...])).astype(bf16)
        d_lat_ref[...] = d_lat
        send(last_ref)
        send(d_lat_ref)
        in_b = (tb_ref[...] + dot(turned(lat_ref[...]), d_x)).astype(bf16)
        in_a = (ta_ref[...] + dot(turned(d_lat), nrm_ref[...])).astype(bf16)
        both = jnp.concatenate([tg_ref[...], in_b], axis=1)
        kinds = [in_a, both, oa_ref[...], ob_ref[...]]
        for d in range(owners):
            pieces = []
            for kind in kinds:
                width = kind.shape[1] // owners
                pieces.append(kind[:, d * width : (d + 1) * width])
            sent_ref[d, s] = jnp.concatenate(pieces, axis=1)
    send(sent_ref)


def terms_call(ids, conv_w, items, lat, nrm, in_b, owners):
    seqs, rows, _ = nrm.shape
    last_rows = lambda scalars, ref: ref.at[pl.ds(rows - RIM, RIM)]
    operands = [view(conv_w)]
    outs = []
    for s, (tail, following, d_lat_gate, tb, ta, tg, ob, oa) in enumerate(items):
        of_last = lambda scalars, ref, s=s: ref.at[s, pl.ds(rows - RIM, RIM)]
        operands += [
            view(tail), view(following), of_adapter(in_b, s, INNER, INNER), view(d_lat_gate, last_rows, (RIM, RANK)),
            view(lat, of_last, (RIM, RANK)), view(nrm, of_last, (RIM, DM)), view(tb), view(ta), view(tg), view(ob),
            view(oa),
        ]
        outs += [((RIM, CONV_CH), bf16), ((RIM, RANK), bf16)]
    width = (2 * DM + ZX + INNER) // owners
    outs.append(((owners, seqs, RANK, width), bf16))
    kernel = functools.partial(terms_kernel, seqs=seqs, owners=owners)
    return streamed(kernel, "terms", [ids], operands, outs, [], 4)


def input_back_kernel(
    ids, lens, place, dg_ref, wg_ref, last_ref, dx_ref, wx_ref, draw_ref, wdt_ref, d_lat_ref, d_lat_last_ref, a_ref,
    gain_ref, x_ref, cot_ref, out_ref, dn_s, *, seq, ready, send,
):
    rows = dx_ref.shape[0]
    ready(dg_ref, wg_ref)
    dn_s[...] = dot_t(dg_ref[...], wg_ref[...])
    ready(last_ref, dx_ref, wx_ref, draw_ref, wdt_ref, d_lat_ref, d_lat_last_ref, a_ref)
    dx_ref[rows - RIM :, :] = last_ref[...]
    d_lat_ref[rows - RIM :, :] = d_lat_last_ref[...]
    dn_s[...] += (
        dot_t(dx_ref[...], wx_ref[...]) + dot_t(draw_ref[...], wdt_ref[...]) + dot(d_lat_ref[...], a_ref[...])
    )
    ready(gain_ref, x_ref, cot_ref)
    strip = 32
    for i in range(rows // strip):
        r = slice(i * strip, (i + 1) * strip)
        x = x_ref[r, :].astype(f32)
        root = lax.rsqrt(jnp.mean(x * x, -1, keepdims=True) + epsilon)
        dn = dn_s[r, :] * gain_ref[...]
        back = jnp.mean(dn * x, -1, keepdims=True) * (root * root * root)
        position = i * strip + lax.broadcasted_iota(jnp.int32, (strip, 1), 0)
        kept = jnp.where(position < lens[seq], cot_ref[r, :].astype(f32), 0.0)
        out_ref[r, :] = dn * root - x * back + kept
    send(out_ref)


def input_back_call(seq, ids, lens, place, begun, tokens, cotangent, dg, last, dx, draw, d_lat, d_lat_last, wg, wx, wdt, in_a, gain):
    rows = dx.shape[0]
    outs = [((rows, DM), f32)]
    operands = [view(dg), wg, view(last), view(dx), wx, view(draw), wdt, view(d_lat), view(d_lat_last)]
    operands += [of_adapter(in_a, seq), view(gain), of_sequence(tokens, seq), of_sequence(cotangent, seq)]
    kernel = functools.partial(input_back_kernel, seq=seq)
    scratch = [pltpu.VMEM((rows, DM), f32)]
    shared = (tokens.shape[0], seq, begun)
    return streamed(kernel, "input_back", [ids, lens, place], operands, outs, scratch, 9, shared)[0]


def shifted(value, axis, steps):
    count = lax.axis_size(axis)
    pairs = [(i, i + steps) for i in range(count) if 0 <= i + steps < count]
    return lax.ppermute(value, axis, pairs)


def swapped(value, axis, bit):
    return lax.ppermute(value, axis, [(i, i ^ bit) for i in range(lax.axis_size(axis))])


def after(value, other):
    return lax.optimization_barrier((value, other))[0]


def my_half(shard, core, half):
    return lax.dynamic_slice_in_dim(shard, core * half, half, 0)


def gathered_early(meanwhile, shard):
    owners = lax.axis_size("dp")
    rows, width = shard.shape
    half = rows // 2
    shapes = [(rows * owners, CONV_CH), (rows * owners, LANES)]
    if half % 16 or owners % 2:
        full = lax.all_gather(shard, "dp", axis=0, tiled=True)
        return view(full[:, :CONV_CH]), view(full[:, CONV_CH:]), None
    core = lax.axis_index("ctx") % 2
    own = {0: my_half(shard, core, half)}
    for k in range(2, owners, 2):
        own[k] = swapped(own[0], "dp", k)
    own[1] = swapped(own[0], "dp", 1)
    for k in range(2, owners, 2):
        waits = (own[3], meanwhile) if k == owners - 2 else own[1]
        own[k + 1] = swapped(after(own[k], waits), "dp", 1)
    pieces = [own[k] for k in range(owners)] + [swapped(own[k], "ctx", 1) for k in range(owners)]

    def copies(scalars, refs, to, columns):
        place = scalars[-1]
        pairs = []
        for n, piece in enumerate(refs):
            side = place[1] if n < owners else 1 - place[1]
            at = pl.multiple_of((place[0] ^ (n % owners)) * rows + side * half, 16)
            pairs.append((piece.at[:, columns], to.at[pl.ds(at, half)]))
        return pairs

    main = functools.partial(copies, columns=pl.ds(0, CONV_CH))
    rest = functools.partial(copies, columns=pl.ds(CONV_CH, LANES))
    arrived = (tuple(own[k] for k in range(2, owners, 2)), own[owners - 1])
    return Operand(pieces, shapes[0], main), Operand(pieces, shapes[1], rest), arrived


def gathered_late(gate, out, arrived, fronts, scans, befores):
    owners = lax.axis_size("dp")
    rows = gate.shape[0]
    half = rows // 2
    if arrived is None:
        return (
            view(lax.all_gather(gate, "dp", axis=0, tiled=True)),
            view(lax.all_gather(out, "dp", axis=0, tiled=True)),
        )
    core = lax.axis_index("ctx") % 2
    mine = my_half(jnp.concatenate([gate, out[:rows], out[rows:]], axis=1), core, half)
    own = {0: mine}
    for k in range(2, owners, 2):
        own[k] = swapped(after(mine, arrived[0][0] if k == 2 else arrived[0]), "dp", k)
    for k in range(0, owners, 2):
        waits = arrived[1] if k <= 2 else fronts[-1][5]
        own[k + 1] = swapped(after(own[k], waits), "dp", 1)
    pieces = [own[k] for k in range(owners)]
    hold = (scans[-1][0], befores[0])
    pieces += [swapped(after(own[k], scans[0][0] if k < 4 else hold), "ctx", 1) for k in range(owners)]

    def placed(scalars, refs):
        place = scalars[-1]
        for n, piece in enumerate(refs):
            side = place[1] if n < owners else 1 - place[1]
            yield piece, place[0] ^ (n % owners), side * half

    def gate_copies(scalars, refs, to):
        pairs = []
        for piece, owner, start in placed(scalars, refs):
            at = pl.multiple_of(owner * rows + start, 16)
            pairs.append((piece.at[:, pl.ds(0, INNER)], to.at[pl.ds(at, half)]))
        return pairs

    def out_copies(scalars, refs, to):
        pairs = []
        for piece, owner, start in placed(scalars, refs):
            for k in range(2):
                at = pl.multiple_of((2 * owner + k) * rows + start, 16)
                pairs.append((piece.at[:, pl.ds(INNER + k * DM, DM)], to.at[pl.ds(at, half)]))
        return pairs

    return (
        Operand(pieces, (rows * owners, INNER), gate_copies),
        Operand(pieces, (2 * rows * owners, DM), out_copies),
    )


def join_kernel(swap, one_ref, two_ref, out_ref, *, ready, send):
    ready(one_ref, two_ref)
    join_payloads(swap[0], one_ref, two_ref, out_ref)
    send(out_ref)


def joined(one, two, swap):
    return streamed(join_kernel, "join", [swap], [view(one), view(two)], [(one.shape, bf16)], [], 1)[0]


def state_in_two(flags, other_ref, far_ref, far_other_ref, cols):
    far, far_other, other = (ref[0:NSTATE, cols].astype(f32) for ref in (far_ref, far_other_ref, other_ref))
    behind = decay_of(far_ref, cols) * far_other + far
    ahead = decay_of(far_other_ref, cols) * far + far_other
    before = jnp.where(flags[1] == 1, behind, ahead)
    return jnp.where(flags[0] == 1, decay_of(other_ref, cols) * before + other, before)


def from_before(both, reverse):
    chips = lax.axis_size("ctx") // 2
    sign = -1 if reverse else 1
    in_order = jnp.zeros((1,), jnp.int32)
    before = shifted(both, "ctx", 2 * sign)
    step, run = 1, both
    while 2 * step < chips:
        run = joined(before, both, in_order) if step == 1 else joined(far, run, in_order)
        far = shifted(run, "ctx", 4 * step * sign)
        before = joined(far, before, in_order)
        step *= 2
    return before


def shards(
    tokens, cotangent, lengths, adapter_ids, norm_gain, w_in, conv_weight, conv_bias, dt_bias, a_log,
    skip_scale, inner_gain, w_out, in_a, in_b, out_a, out_b,
):
    seqs, slots, _ = tokens.shape
    owners = lax.axis_size("dp")
    ids = adapter_ids
    lens = jnp.clip(lengths - lax.axis_index("ctx") * slots, 0, slots).astype(jnp.int32)

    def grouped(row):
        padded = jnp.pad(row.reshape(-1, HEADS), ((0, 0), (0, GROUP - HEADS)))
        return jnp.tile(padded, (1, LANES // GROUP))

    rate = grouped(-jnp.exp(a_log))
    dtb = grouped(dt_bias)
    lane = jnp.arange(LANES)[:, None]
    head = jnp.arange(INNER)[None, :] // HDIM
    expand = ((lane % GROUP == head) & (lane < 3 * GROUP)).astype(bf16)
    skip = jnp.repeat(skip_scale, HDIM)[None, :]
    gain = inner_gain[None, :]
    n_gain = norm_gain[None, :]
    conv_b = conv_bias[None, :]

    marks = jnp.broadcast_to(ids.astype(bf16)[None, :], (w_in.shape[0], seqs))
    marks = jnp.pad(marks, ((0, 0), (0, GROUP - HEADS - seqs)))
    steps = jnp.concatenate([w_in[:, INNER + CONV_CH :], marks], axis=1)
    in_a, out_a = jnp.swapaxes(in_a, 1, 2), jnp.swapaxes(out_a, 1, 2)
    rim = shifted(tokens[:, slots - RIM :], "ctx", 1)
    nrm, nrim, lat, lrim = norm_call(ids, tokens, rim, n_gain, in_a)
    wx, wdt, arrived = gathered_early(
        nrm,
        jnp.concatenate([w_in[:, INNER : INNER + CONV_CH]] + [steps] * (LANES // GROUP), axis=1)
    )

    core = lax.axis_index("ctx") % 2
    place = jnp.stack([lax.axis_index("dp"), core]).astype(jnp.int32)
    late = core.reshape(1).astype(jnp.int32)
    early = 1 - late
    front = functools.partial(
        front_call, in_b=in_b, wx=wx, wdt=wdt, conv_w=conv_weight, conv_b=conv_b, dtb=dtb, rate=rate, expand=expand
    )
    nrm, (skip, gain, lens, late, early) = lax.optimization_barrier((nrm, (skip, gain, lens, late, early)))
    chips = lax.axis_size("ctx") // 2
    flags_back = jnp.concatenate([early, early if chips == 2 else jnp.ones_like(early)])
    fronts, others = [], []
    for s in range(seqs):
        ready = nrm if s == 0 else after(nrm, fronts[-1][5])
        fronts.append(front(s, ids, place, ready, nrim, lat, lrim))
        others.append(swapped(fronts[s][5], "ctx", 1))
    scans, befores = [], []
    for s in range(seqs):
        act, _, dt, cum, _, own, _ = fronts[s]
        ready = after(act, fronts[-1][5]) if s == 0 else after(act, scans[-1][0])
        scans.append(scan_call(late, own, others[s], ready, dt, cum))
        befores.append(from_before(scans[s][2], False))
    full_gate, full_out = gathered_late(w_in[:, :INNER], w_out, arrived, fronts, scans, befores)
    middles, other_grads, later_grads = [], [], []
    for s in range(seqs):
        act, _, _, cum, _, _, _ = fronts[s]
        ready = after(nrm, scans[-1][0] if s == 0 else middles[-1][4])
        middles.append(
            middle_call(
                s, ids, lens, place, late, middles[-1][0] if s else None, tokens, cotangent, ready, lat, act, cum,
                others[s], befores[s], scans[s][0], full_gate, in_b, full_out, out_a, out_b, skip, gain, expand,
            )
        )
        payload = after(middles[s][4], later_grads[-1] if s and chips > 2 else befores[-1])
        other_grads.append(swapped(payload, "ctx", 1))
        if chips == 2:
            later_grads.append(shifted(payload, "ctx", -2))
        else:
            later_grads.append(from_before(joined(payload, other_grads[s], early), True))
    backs, nexts = [], []
    for s in range(seqs):
        act, dact, dt, cum, sig, _, _ = fronts[s]
        _, dy, _, rowt, _, _, _, enter, runs, d_lat_gate, _ = middles[s]
        hold = middles[-1][4] if s == 0 else backs[-1][3]
        ready = after(act, hold)
        later_other = swapped(after(later_grads[s], hold), "ctx", 1) if chips == 2 else jnp.zeros_like(later_grads[s])
        backs.append(
            scan_back_call(
                s, ids, flags_back, other_grads[s], later_grads[s], later_other, ready, dact, dt, cum, sig, rowt, dy, scans[s][1], enter,
                runs, lat, nrm, in_b, d_lat_gate, skip, rate, conv_weight, expand,
            )
        )
        nexts.append(shifted(backs[s][3], "ctx", -1))
    items = [
        (back[2], following, mid[9], back[5], back[6], mid[10], mid[5], mid[6])
        for back, following, mid in zip(backs, nexts, middles)
    ]
    *lasts, sent = terms_call(ids, conv_weight, items, lat, nrm, in_b, owners)

    widths = [width // owners for width in (DM, ZX, INNER, DM)]
    got = lax.all_to_all(sent, "dp", 0, 0)
    held = after(tokens, sent)
    input_grad = None
    for s in range(seqs):
        if s == 1:
            got = after(got, input_grad)
        input_grad = input_back_call(
            s, ids, lens, place, input_grad, held, cotangent, middles[s][2], lasts[2 * s], backs[s][0], backs[s][1],
            backs[s][4], lasts[2 * s + 1], full_gate, wx, wdt, in_a, n_gain,
        )
    every = fronts[0][6][:, HEADS : HEADS + seqs].reshape(1, -1)
    chosen = (every == jnp.arange(ADAPT, dtype=f32)[:, None]).astype(f32)
    flat = got.reshape(owners * seqs, -1).astype(f32)
    mine = jnp.sum(chosen[:, :, None] * flat[None], axis=1)
    bit = 1
    while bit < lax.axis_size("ctx"):
        mine = mine + swapped(mine.astype(bf16), "ctx", bit).astype(f32)
        bit *= 2
    mine = mine.reshape(ADAPT, RANK, -1)
    cuts = [sum(widths[:k]) for k in range(5)]
    g_ia, g_ib, g_oa, g_ob = (mine[:, :, cuts[k] : cuts[k + 1]] for k in range(4))
    return (
        middles[-1][0],
        input_grad,
        jnp.swapaxes(g_ia, 1, 2),
        g_ib,
        jnp.swapaxes(g_oa, 1, 2),
        g_ob,
    )


def solution(mesh):
    split = P("dp", "ctx", None)
    return jax.shard_map(
        shards,
        mesh=mesh,
        in_specs=(
            split, split, P("dp"), P("dp"), P(), P("dp", None), P(), P(), P(), P(), P(), P(),
            P("dp", None), P(), P(), P(), P(),
        ),
        out_specs=(
            split, split, P(None, "dp", None), P(None, None, "dp"), P(None, "dp", None), P(None, None, "dp"),
        ),
        check_vma=False,
    )
```

```python
import functools

import jax
import jax.numpy as jnp
from jax import lax
from jax.experimental import pallas as pl
from jax.experimental.pallas import tpu as pltpu
from jax.sharding import PartitionSpec as P

HEADS = 24
HDIM = 64
NSTATE = 128
INNER = 1536
CONV_CH = 1792
ZX = 3072
DM = 768
RANK = 16
ADAPT = 8
CHUNK = 128
TILE = 256
RIM = 16
GROUP = 32
LANES = 128
VMEM_LIMIT = 60 * 1024 * 1024

epsilon = 1e-05
bf16 = jnp.bfloat16
f32 = jnp.float32


def dot(left, right):
    return jnp.dot(left, right, preferred_element_type=f32)


def dot_t(left, right):
    return lax.dot_general(
        left, right, (((1,), (1,)), ((), ())), preferred_element_type=f32
    )


def dot_precise(left, right):
    return jnp.dot(
        left, right, preferred_element_type=f32, precision=lax.Precision.HIGHEST
    )


def parts_of(v):
    lane = lax.broadcasted_iota(jnp.int32, v.shape, 1)
    high = v.astype(bf16).astype(f32)
    rest = v - high
    middle = rest.astype(bf16).astype(f32)
    kept = jnp.where(lane < GROUP, high, jnp.where(lane < 2 * GROUP, middle, rest - middle))
    return jnp.where(lane < 3 * GROUP, kept, 0.0).astype(bf16)


def causal(rows):
    t = lax.broadcasted_iota(jnp.int32, (rows, rows), 0)
    s = lax.broadcasted_iota(jnp.int32, (rows, rows), 1)
    return t >= s


def sigmoid(v):
    return 0.5 * jnp.tanh(0.5 * v) + 0.5


def turned(v):
    return jnp.transpose(v.astype(f32)).astype(bf16)


class Operand:
    def __init__(self, arrays, shape, copies, parts=1, late=False):
        self.arrays, self.shape, self.copies, self.parts = list(arrays), tuple(shape), copies, parts
        self.late = late


def view(array, pick=None, shape=None):
    pick = pick or (lambda scalars, ref: ref)
    return Operand([array], shape or array.shape, lambda scalars, refs, to: [(pick(scalars, refs[0]), to)])


def later(operand):
    return Operand(operand.arrays, operand.shape, operand.copies, operand.parts, True)


def in_parts(array, parts):
    def copies(scalars, refs, to):
        size = array.shape[0] // parts
        return [(refs[0].at[pl.ds(p * size, size)], to.at[pl.ds(p * size, size)]) for p in range(parts)]

    return Operand([array], array.shape, copies, parts)


def streamed(kernel, name, scalars, operands, outs, scratch, micros, shared=None):
    arrays = [array for operand in operands for array in operand.arrays]
    n_scalar, n_array, n_in, n_out = len(scalars), len(arrays), len(operands), len(outs)
    kinds = [operand.arrays[0].dtype for operand in operands]
    slots, slot, begun = shared or (None, None, None)
    parted_in = any(operand.parts > 1 for operand in operands)
    n_begun = 0 if begun is None else 1

    def body(*refs):
        refs = list(refs)
        take = lambda n: [refs.pop(0) for _ in range(n)]
        smem, sources, _, targets, ins, results = (
            take(n) for n in (n_scalar, n_array, n_begun, n_out, n_in, n_out)
        )
        if shared:
            targets[0] = targets[0].at[slot]
        in_sems, out_sems = refs.pop(-2), refs.pop(-1)
        waiting, parted, late, first_sem = {}, [], [], 0
        for k, operand in enumerate(operands):
            mine = [sources.pop(0) for _ in operand.arrays]
            copies = operand.copies(smem, mine, ins[k])
            if operand.parts == 1:
                sem = in_sems.at[first_sem]
                for source, target in copies:
                    copy = pltpu.make_async_copy(source, target, sem)
                    if operand.late:
                        late.append(copy)
                    else:
                        copy.start()
                waiting[id(ins[k])] = [pltpu.make_async_copy(ins[k], ins[k], sem)]
            else:
                made = [
                    pltpu.make_async_copy(source, target, in_sems.at[first_sem + p])
                    for p, (source, target) in enumerate(copies)
                ]
                waiting[id(ins[k])] = made
                parted.append(list(made))
            first_sem += operand.parts
        while any(parted):
            for made in parted:
                if made:
                    made.pop().start()
        for copy in late:
            copy.start()

        def ready(*wanted):
            for ref in wanted:
                for copy in waiting.pop(id(ref), ()):
                    copy.wait()

        def ready_last(*wanted):
            for ref in wanted:
                waiting[id(ref)].pop().wait()

        sent = []

        def send(ref, *at):
            k = [id(result) for result in results].index(id(ref))
            if k not in sent:
                sent.append(k)
            source, target = (results[k].at[at], targets[k].at[at]) if at else (results[k], targets[k])
            pltpu.make_async_copy(source, target, out_sems.at[k]).start()

        more = {"ready_last": ready_last} if parted_in else {}
        kernel(*smem, *ins, *results, *refs, ready=ready, send=send, **more)
        ready(*ins)
        for k in sent:
            pltpu.make_async_copy(results[k], targets[k], out_sems.at[k]).wait()

    anywhere = pl.BlockSpec(memory_space=pl.ANY)
    full = [((slots,) + shape if shared and k == 0 else shape, kind) for k, (shape, kind) in enumerate(outs)]
    return pl.pallas_call(
        body,
        in_specs=[pl.BlockSpec(memory_space=pltpu.SMEM)] * n_scalar + [anywhere] * (n_array + n_begun),
        out_specs=[anywhere] * n_out,
        out_shape=[jax.ShapeDtypeStruct(shape, kind) for shape, kind in full],
        scratch_shapes=[pltpu.VMEM(operand.shape, kind) for operand, kind in zip(operands, kinds)]
        + [pltpu.VMEM(shape, kind) for shape, kind in outs]
        + scratch
        + [pltpu.SemaphoreType.DMA((sum(operand.parts for operand in operands),)), pltpu.SemaphoreType.DMA((n_out,))],
        input_output_aliases={n_scalar + n_array: 0} if n_begun else {},
        compiler_params=pltpu.CompilerParams(vmem_limit_bytes=VMEM_LIMIT),
        cost_estimate=pl.CostEstimate(flops=micros * 1000000000, bytes_accessed=1000000, transcendentals=0),
        name=name,
    )(*scalars, *arrays, *([begun] if n_begun else []))


def of_sequence(array, seq):
    return view(array, lambda scalars, ref: ref.at[seq], array.shape[1:])


def of_adapter(array, seq, start=0, width=None):
    width = width or array.shape[2]
    pick = lambda scalars, ref: ref.at[scalars[0][seq], :, pl.ds(start, width)]
    return view(array, pick, (array.shape[1], width))


def split_decay(decay):
    high = decay.astype(bf16).astype(f32)
    row = lax.broadcasted_iota(jnp.int32, (RIM, decay.shape[1]), 0)
    return jnp.where(row == 0, high, jnp.where(row == 1, decay - high, 0.0)).astype(bf16)


def decay_of(payload_ref, cols):
    rows = payload_ref[NSTATE:, cols].astype(f32)
    return rows[0:1] + rows[1:2]


def norm_kernel(
    ids, x0_ref, x1_ref, rim_ref, gain_ref, a0_ref, a1_ref, nrm_ref, nrim_ref, lat_ref, lrim_ref, *, ready, send
):
    def normed(x):
        x = x.astype(f32)
        mean = jnp.mean(x * x, -1, keepdims=True)
        return (x * lax.rsqrt(mean + epsilon) * gain_ref[...]).astype(bf16)

    strip = 64
    ready(gain_ref, rim_ref)
    for s, (x_ref, a_ref) in enumerate(((x0_ref, a0_ref), (x1_ref, a1_ref))):
        ready(x_ref, a_ref)
        for i in range(x_ref.shape[0] // strip):
            r = slice(i * strip, (i + 1) * strip)
            nrm_ref[s, r, :] = normed(x_ref[r, :])
        nrim_ref[s] = normed(rim_ref[s])
        lat_ref[s] = dot_t(nrm_ref[s], a_ref[...]).astype(bf16)
        lrim_ref[s] = dot_t(nrim_ref[s], a_ref[...]).astype(bf16)
    for ref in (nrm_ref, nrim_ref, lat_ref, lrim_ref):
        send(ref)


def norm_call(ids, tokens, rim, gain, in_a):
    seqs, rows, _ = tokens.shape
    outs = [
        ((seqs, rows, DM), bf16),
        ((seqs, RIM, DM), bf16),
        ((seqs, rows, RANK), bf16),
        ((seqs, RIM, RANK), bf16),
    ]
    operands = [
        of_sequence(tokens, 0), of_sequence(tokens, 1), view(rim), view(gain), of_adapter(in_a, 0), of_adapter(in_a, 1),
    ]
    return streamed(norm_kernel, "norm", [ids], operands, outs, [], 3)


def front_kernel(
    ids, place, nrm_s, lat_s, wdt_ref, dtb_ref, rate_ref, cw_ref, cb_ref, wx_ref, bx_ref,
    expand_ref, act_ref, dact_ref, dt_ref, cum_ref, sig_ref, pay_ref, marks_ref,
    xs, bt_s, w_s, *, ready, send,
):
    rows = nrm_s.shape[0] - RIM
    ready(nrm_s, lat_s)
    ready(wdt_ref, dtb_ref, rate_ref)
    owners = marks_ref.shape[0]
    for d in range(owners):
        at = d * (wdt_ref.shape[0] // owners)
        marks_ref[d : d + 1, :] = wdt_ref[at : at + 8, :].astype(f32)[0:1]
    send(marks_ref)
    raw = dot(nrm_s[RIM:, :], wdt_ref[...]) + dtb_ref[...]
    step = jnp.maximum(raw, 0.0) + jnp.log1p(jnp.exp(-jnp.abs(raw)))
    dt_ref[...] = step
    sig_ref[...] = jnp.exp(raw - step)
    logs = step * rate_ref[...]
    lower = causal(CHUNK).astype(f32)
    before = jnp.zeros((1, LANES), f32)
    whole = []
    for c in range(rows // CHUNK):
        r = slice(c * CHUNK, (c + 1) * CHUNK)
        cum = dot_precise(lower, logs[r])
        cum_ref[r, :] = cum
        whole.append(cum + before)
        before = before + cum[CHUNK - 1 : CHUNK]
    for c in range(rows // CHUNK):
        r = slice(c * CHUNK, (c + 1) * CHUNK)
        w_s[r, :] = parts_of(jnp.exp(before - whole[c]) * step[r])
    total = parts_of(jnp.broadcast_to(jnp.exp(before), (8, LANES)))
    for ref in (dt_ref, cum_ref, sig_ref):
        send(ref)
    ready(cw_ref, cb_ref, wx_ref, bx_ref, expand_ref)

    def activate(cols, base):
        weights = [cw_ref[j : j + 1, cols] for j in range(4)]
        bias = cb_ref[:, cols]
        low = base.astype(bf16).astype(f32)
        for k in range(2):
            xs[k] = low[:, k * LANES : (k + 1) * LANES]
        strip = 64
        for i in range(rows // strip):
            at = RIM + i * strip
            halves = []
            for k in range(2):
                lanes = slice(k * LANES, (k + 1) * LANES)
                pre = bias[:, lanes] + weights[0][:, lanes] * xs[k, at - 3 : at - 3 + strip, :]
                for j in range(1, 4):
                    pre = pre + weights[j][:, lanes] * xs[k, at - 3 + j : at - 3 + j + strip, :]
                halves.append(pre)
            pre = jnp.concatenate(halves, axis=1)
            gate = sigmoid(pre)
            act = pre * gate
            r = slice(i * strip, (i + 1) * strip)
            act_ref[r, cols] = act.astype(bf16)
            dact_ref[r, cols] = (gate + act * (1.0 - gate)).astype(bf16)
        send(act_ref, slice(None), cols)
        send(dact_ref, slice(None), cols)

    last = pl.ds(INNER, CONV_CH - INNER)
    activate(last, dot(nrm_s[...], wx_ref[:, last]))
    bt_s[...] = turned(act_ref[:, INNER : INNER + NSTATE])
    def tile_body(t, carry):
        cols = pl.ds(pl.multiple_of(t * TILE, TILE), TILE)
        activate(cols, dot(nrm_s[...], wx_ref[:, cols]) + dot(lat_s[...], bx_ref[:, cols]))
        scaled = (act_ref[:, cols].astype(f32) * dot(w_s[...], expand_ref[:, cols])).astype(bf16)
        pay_ref[0:NSTATE, cols] = dot(bt_s[...], scaled).astype(bf16)
        pay_ref[NSTATE:, cols] = split_decay(dot(total, expand_ref[:, cols])[0:1])
        return carry

    lax.fori_loop(0, INNER // TILE, tile_body, 0)
    send(pay_ref)


def front_call(seq, ids, place, nrm, nrim, lat, lrim, wx, wdt, in_b, conv_w, conv_b, dtb, rate, expand):
    rows = nrm.shape[1]
    owners = lax.axis_size("dp")
    outs = [
        ((rows, CONV_CH), bf16),
        ((rows, CONV_CH), bf16),
        ((rows, LANES), f32),
        ((rows, LANES), f32),
        ((rows, LANES), f32),
        ((NSTATE + RIM, INNER), bf16),
        ((owners, LANES), f32),
    ]
    scratch = [
        pltpu.VMEM((2, rows + RIM, LANES), f32),
        pltpu.VMEM((NSTATE, rows), bf16),
        pltpu.VMEM((rows, LANES), bf16),
    ]
    def rim_first(rim, rest):
        def copies(scalars, refs, to):
            return [(refs[0].at[seq], to.at[pl.ds(0, RIM)]), (refs[1].at[seq], to.at[pl.ds(RIM, rows)])]

        return Operand([rim, rest], (RIM + rows, rest.shape[2]), copies)

    operands = [rim_first(nrim, nrm), rim_first(lrim, lat)]
    operands += [wdt] + [view(a) for a in (dtb, rate, conv_w, conv_b)] + [wx]
    operands += [of_adapter(in_b, seq, INNER, INNER), view(expand)]
    return streamed(front_kernel, "front", [ids, place], operands, outs, scratch, 13)


def column(values, head):
    return jnp.broadcast_to(values[:, head : head + 1], values.shape)


def beside(one, two):
    lane = lax.broadcasted_iota(jnp.int32, one.shape, 1)
    return jnp.where(lane < HDIM, one, two)


def decays(cum, cum_t, head):
    gap = column(cum, head) - cum_t[head : head + 1, :]
    return jnp.exp(jnp.minimum(gap, -gap))


def split_heads(pair):
    lane = lax.broadcasted_iota(jnp.int32, pair.shape, 1)
    zero = jnp.zeros_like(pair)
    first = jnp.where(lane < HDIM, pair, zero)
    second = jnp.where(lane < HDIM, zero, pair)
    return jnp.concatenate([first, second], axis=0)


def join_payloads(swap, one_ref, two_ref, out_ref):
    for t in range(INNER // TILE):
        cols = slice(t * TILE, (t + 1) * TILE)
        d_one, d_two = decay_of(one_ref, cols), decay_of(two_ref, cols)
        one = one_ref[0:NSTATE, cols].astype(f32)
        two = two_ref[0:NSTATE, cols].astype(f32)
        state = jnp.where(swap == 1, d_one * two + one, d_two * one + two)
        out_ref[0:NSTATE, cols] = state.astype(bf16)
        out_ref[NSTATE:, cols] = split_decay(d_one * d_two)


def state_in(late, other_ref, before_ref, cols):
    before = before_ref[0:NSTATE, cols].astype(f32)
    joint = decay_of(other_ref, cols) * before + other_ref[0:NSTATE, cols].astype(f32)
    return jnp.where(late == 1, joint, before)


def scan_kernel(
    flags, own_ref, other_ref, act_ref, dt_ref, cum_ref, y_ref, hc_ref, both_ref, state_s, *, ready, send
):
    keep = causal(CHUNK)
    ready(own_ref, other_ref)
    join_payloads(flags[0], own_ref, other_ref, both_ref)
    send(both_ref)
    state_s[...] = jnp.zeros_like(state_s)
    ready(act_ref, dt_ref, cum_ref)

    def one_chunk(c, carry):
        r = pl.ds(pl.multiple_of(c * CHUNK, CHUNK), CHUNK)
        b = act_ref[r, INNER : INNER + NSTATE]
        cc = act_ref[r, INNER + NSTATE :]
        b_t = turned(b)
        masked = jnp.where(keep, dot_t(cc, b), 0.0)
        dt = dt_ref[r, :]
        cum = cum_ref[r, :]
        cum_t = jnp.transpose(cum)
        for t in range(INNER // LANES):
            cols = slice(t * LANES, (t + 1) * LANES)
            heads = (2 * t, 2 * t + 1)
            cums = beside(*(column(cum, head) for head in heads))
            steps = beside(*(column(dt, head) for head in heads))
            ec = jnp.exp(cums)
            xd = act_ref[r, cols].astype(f32) * steps
            xw = (xd * jnp.exp(cums[CHUNK - 1 : CHUNK] - cums)).astype(bf16)
            state = state_s[:, cols]
            low = state.astype(bf16)
            hc_ref[c, :, cols] = low
            far = dot(cc, low) * ec
            state_s[:, cols] = state * ec[CHUNK - 1 : CHUNK] + dot(b_t, xw)
            weights = [(decays(cum, cum_t, head) * masked).astype(bf16) for head in heads]
            near = dot(jnp.concatenate(weights, axis=1), split_heads(xd.astype(bf16)))
            y_ref[r, cols] = (near + far).astype(bf16)
        send(y_ref, r)
        send(hc_ref, pl.ds(c, 1))
        return carry

    chunks = act_ref.shape[0] // CHUNK
    lax.fori_loop(0, chunks, one_chunk, 0)
    hc_ref[chunks] = state_s[...].astype(bf16)
    send(hc_ref, pl.ds(chunks, 1))


def scan_call(flags, own, other, act, dt, cum):
    rows = act.shape[0]
    chunks = rows // CHUNK
    outs = [((rows, INNER), bf16), ((chunks + 1, NSTATE, INNER), bf16), (own.shape, bf16)]
    scratch = [pltpu.VMEM((NSTATE, INNER), f32)]
    operands = [view(a) for a in (own, other, act, dt, cum)]
    return streamed(scan_kernel, "scan", [flags], operands, outs, scratch, 9)


def woven(one, two):
    order = [((n + 0.5) / len(steps), k, step) for k, steps in enumerate((one, two)) for n, step in enumerate(steps)]
    for _, _, step in sorted(order, key=lambda item: item[:2]):
        step()


def middle_kernel(
    ids, lens, flags, place, nrm_ref, lat_ref, bg_ref, wg_ref, cot_ref, b_ref, a_ref, wo_ref, other_ref, before_ref,
    cum_ref, expand_ref, act_ref, y_ref, skip_ref, gain_ref, x_ref,
    out_ref, dy_ref, dg_ref, rowt_ref, pay_ref, tb_ref, ta_ref, enter_ref, runs_ref, d_lat_ref, tg_ref,
    gate_s, z_s, dh_s, hid_s, prod_s, ec_s, y_s, grad_s, tb_s, ta_s, tg_s, *, seq, ready, send,
):
    rows = act_ref.shape[0]
    block = 2 * CHUNK
    strip = 16
    tiles = [slice(t * TILE, (t + 1) * TILE) for t in range(INNER // TILE)]
    blocks = [slice(k * block, (k + 1) * block) for k in range(rows // block)]
    kept = [{} for _ in blocks]

    position = lax.broadcasted_iota(jnp.int32, (rows, 1), 0)
    valid = position < lens[seq]
    ready(nrm_ref, lat_ref, bg_ref, wg_ref)
    for cols in tiles:
        gate_s[:, cols] = dot(nrm_ref[...], wg_ref[:, cols]) + dot(lat_ref[...], bg_ref[:, cols])
    ready(cot_ref, b_ref, a_ref, gain_ref, wo_ref)
    cot_ref[...] = jnp.where(valid, cot_ref[...], jnp.zeros((), bf16))
    d_lat_t = dot_t(b_ref[...], cot_ref[...]).astype(bf16)
    d_lat = turned(d_lat_t)
    for cols in tiles:
        d_hidden = dot_t(cot_ref[...], wo_ref[cols, :]) + dot(d_lat, a_ref[:, cols])
        dh_s[:, cols] = d_hidden * gain_ref[:, cols]
    ready(other_ref, before_ref, cum_ref, expand_ref)
    before = jnp.zeros((1, LANES), f32)
    logs = []
    for c in range(rows // CHUNK):
        logs.append(cum_ref[c * CHUNK : (c + 1) * CHUNK, :] + before)
        before = logs[-1][CHUNK - 1 : CHUNK]
    runs_ref[0] = jnp.ones((1, INNER), f32)
    spread = parts_of(jnp.exp(jnp.concatenate(logs, axis=0)))
    for cols in tiles:
        enter_ref[:, cols] = state_in(flags[0], other_ref, before_ref, cols).astype(bf16)
        ec = dot(spread, expand_ref[:, cols])
        ec_s[:, cols] = ec
        for c in range(rows // CHUNK):
            runs_ref[c + 1, :, cols] = ec[(c + 1) * CHUNK - 1 : (c + 1) * CHUNK]
    send(enter_ref)
    ready(act_ref, y_ref, skip_ref)

    def project(k):
        r = blocks[k]

        def far_tile(cols):
            far = dot(act_ref[r, INNER + NSTATE :], enter_ref[:, cols]) * ec_s[r, cols]
            y_s[r, cols] = y_ref[r, cols].astype(f32) + far

        return [functools.partial(far_tile, cols) for cols in tiles]

    def forward(k):
        def one(i):
            r = slice(k * block + i * strip, k * block + (i + 1) * strip)
            total = jnp.zeros((strip, LANES), f32)
            for cols in tiles:
                gate = gate_s[r, cols]
                u = y_s[r, cols] + skip_ref[:, cols] * act_ref[r, cols].astype(f32)
                sig = sigmoid(gate)
                silu = gate * sig
                z = u * silu
                square = z * z
                total = total + square[:, :LANES] + square[:, LANES:]
                z_s[r, cols] = z
                gate_s[r, cols] = silu
                prod_s[r, cols] = u * (sig + silu * (1.0 - sig))
            root = lax.rsqrt(jnp.sum(total, -1, keepdims=True) / INNER + epsilon)
            kept[k][i] = root
            for cols in tiles:
                hid_s[r, cols] = (z_s[r, cols] * root * gain_ref[:, cols]).astype(bf16)

        return [functools.partial(one, i) for i in range(block // strip)]

    def mix(k):
        r = blocks[k]

        def latent():
            if k == 0:
                ready(x_ref)
            lat_out_t = dot_t(a_ref[...], hid_s[r, :]).astype(bf16)
            kept[k]["lat_out"] = turned(lat_out_t)
            more = dot(lat_out_t, cot_ref[r, :])
            tb_s[...] = more if k == 0 else tb_s[...] + more

        def out_tile(n):
            cols = slice(n * TILE, (n + 1) * TILE)
            mixed = dot(hid_s[r, :], wo_ref[:, cols]) + dot(kept[k]["lat_out"], b_ref[:, cols])
            x = x_ref[r, cols].astype(f32)
            out_ref[r, cols] = jnp.where(valid[r], x + mixed, 0.0).astype(bf16)

        def term_tile(cols):
            more = dot(d_lat_t[:, r], hid_s[r, cols])
            ta_s[:, cols] = more if k == 0 else ta_s[:, cols] + more

        steps = [latent] + [functools.partial(out_tile, n) for n in range(DM // TILE)]
        steps.append(lambda: send(out_ref, pl.ds(k * block, block)))
        return steps + [functools.partial(term_tile, cols) for cols in tiles]

    def backward(k):
        def one(i):
            r = slice(k * block + i * strip, k * block + (i + 1) * strip)
            total = jnp.zeros((strip, LANES), f32)
            for cols in tiles:
                both = dh_s[r, cols] * z_s[r, cols]
                total = total + both[:, :LANES] + both[:, LANES:]
            root = kept[k][i]
            back = jnp.sum(total, -1, keepdims=True) * (root * root * root) / INNER
            for cols in tiles:
                dz = dh_s[r, cols] * root - z_s[r, cols] * back
                dy = (dz * gate_s[r, cols]).astype(bf16)
                dy_ref[r, cols] = dy
                dg_ref[r, cols] = (dz * prod_s[r, cols]).astype(bf16)
                hid_s[r, cols] = (dy.astype(f32) * y_s[r, cols]).astype(bf16)

        return [functools.partial(one, i) for i in range(block // strip)]

    def finish(k):
        r = blocks[k]
        at = pl.ds(k * block, block)

        def out():
            send(dy_ref, at)
            send(dg_ref, at)
            rowt_ref[r, :] = dot_t(hid_s[r, :], expand_ref[...])
            send(rowt_ref, at)

        def state_tile(cols):
            if cols.start == 0:
                kept[k]["c_t"] = turned(act_ref[r, INNER + NSTATE :])
            scaled = (dy_ref[r, cols].astype(f32) * ec_s[r, cols]).astype(bf16)
            more = dot(kept[k]["c_t"], scaled)
            grad_s[:, cols] = more if k == 0 else grad_s[:, cols] + more

        def latent():
            d_lat_ref[:, r] = dot_t(bg_ref[...], dg_ref[r, :])
            kept[k]["lat_t"] = turned(lat_ref[r, :])

        def term_tile(cols):
            more = dot(kept[k]["lat_t"], dg_ref[r, cols])
            tg_s[:, cols] = more if k == 0 else tg_s[:, cols] + more

        steps = [out] + [functools.partial(state_tile, cols) for cols in tiles] + [latent]
        return steps + [functools.partial(term_tile, cols) for cols in tiles]

    last = len(blocks) - 1
    stages = [project, forward, mix, backward, finish]
    for turn in range(len(stages) + last):
        now = [stages[turn - k](k) for k in range(last + 1) if 0 <= turn - k < len(stages)]
        steps = now.pop(0)
        for other in now:
            order = []
            woven([functools.partial(order.append, step) for step in steps], [functools.partial(order.append, step) for step in other])
            steps = order
        for step in steps:
            step()
    pay_ref[0:NSTATE, :] = grad_s[...].astype(bf16)
    pay_ref[NSTATE:, :] = split_decay(runs_ref[rows // CHUNK])
    tb_ref[...] = tb_s[...].astype(bf16)
    ta_ref[...] = ta_s[...].astype(bf16)
    tg_ref[...] = tg_s[...].astype(bf16)
    for ref in (pay_ref, tb_ref, ta_ref, tg_ref, d_lat_ref, runs_ref):
        send(ref)


def middle_call(
    seq, ids, lens, place, flags, begun, tokens, cotangent, nrm, lat, act, cum, other, before, y, wg, in_b, wo, out_a,
    out_b, skip, gain, expand,
):
    rows = act.shape[0]
    outs = [
        ((rows, DM), bf16),
        ((rows, INNER), bf16),
        ((rows, INNER), bf16),
        ((rows, LANES), f32),
        ((NSTATE + RIM, INNER), bf16),
        ((RANK, DM), bf16),
        ((RANK, INNER), bf16),
        ((NSTATE, INNER), bf16),
        ((rows // CHUNK + 1, 1, INNER), f32),
        ((RANK, rows), f32),
        ((RANK, INNER), bf16),
    ]
    wide = pltpu.VMEM((rows, INNER), f32)
    scratch = [
        wide, wide, wide, pltpu.VMEM((rows, INNER), bf16), wide, wide, wide, pltpu.VMEM((NSTATE, INNER), f32),
        pltpu.VMEM((RANK, DM), f32), pltpu.VMEM((RANK, INNER), f32), pltpu.VMEM((RANK, INNER), f32),
    ]
    operands = [
        of_sequence(nrm, seq), of_sequence(lat, seq), of_adapter(in_b, seq, 0, INNER), wg,
        of_sequence(cotangent, seq), of_adapter(out_b, seq), of_adapter(out_a, seq), wo, view(other), view(before),
        view(cum), view(expand), view(act), view(y), view(skip), view(gain), of_sequence(tokens, seq),
    ]
    kernel = functools.partial(middle_kernel, seq=seq)
    shared = (tokens.shape[0], seq, begun)
    return streamed(kernel, "middle", [ids, lens, flags, place], operands, outs, scratch, 15, shared)


def scan_back_kernel(
    flags, other_ref, before_ref, before_other_ref, enter_ref, runs_ref, dt_ref, cum_ref, skip_ref, expand_ref, hc_ref, act_ref, dy_ref,
    dact_ref, rowt_ref, sig_ref, rate_ref, cw_ref, lat_ref, nrm_ref, bx_ref, d_lat_gate_ref,
    dx_ref, draw_ref, tail_ref, head_ref, d_lat_ref, tb_ref, ta_ref,
    grad_s, pre_s, next_s, *, ready, ready_last, send,
):
    rows = act_ref.shape[0]
    chunks = rows // CHUNK
    keep = causal(CHUNK)
    upper = causal(CHUNK).astype(f32).T
    row = lax.broadcasted_iota(jnp.int32, (CHUNK, LANES), 0)
    lane = lax.broadcasted_iota(jnp.int32, (CHUNK, LANES), 1)
    at_b = slice(INNER, INNER + NSTATE)
    at_c = slice(INNER + NSTATE, CONV_CH)
    ready(other_ref, before_ref, before_other_ref)
    for t in range(INNER // TILE):
        cols = slice(t * TILE, (t + 1) * TILE)
        grad_s[:, cols] = state_in_two(flags, other_ref, before_ref, before_other_ref, cols)
    ready(enter_ref, runs_ref)
    ready_last(hc_ref)
    next_s[...] = hc_ref[chunks].astype(f32) + runs_ref[chunks] * enter_ref[...].astype(f32)
    pre_s[:, rows : rows + 8, :] = jnp.zeros((CONV_CH // LANES, 8, LANES), f32)
    ready(dt_ref, cum_ref, skip_ref, expand_ref)
    for c in reversed(range(chunks)):
        r = slice(c * CHUNK, (c + 1) * CHUNK)
        ready_last(hc_ref, act_ref, dy_ref, dact_ref)
        b = act_ref[r, at_b]
        cc = act_ref[r, at_c]
        c_t = turned(cc)
        masked = jnp.where(keep, dot_t(cc, b), 0.0)
        dt = dt_ref[r, :]
        cum = cum_ref[r, :]
        cum_t = jnp.transpose(cum)
        masked_t = jnp.transpose(masked)
        d_scores = jnp.zeros((CHUNK, CHUNK), f32)
        d_b = jnp.zeros((CHUNK, NSTATE), f32)
        d_c = jnp.zeros((CHUNK, NSTATE), f32)
        col = jnp.zeros((CHUNK + RIM, LANES), f32)
        for t in range(INNER // LANES):
            cols = slice(t * LANES, (t + 1) * LANES)
            heads = (2 * t, 2 * t + 1)
            cums = beside(*(column(cum, head) for head in heads))
            dts = beside(*(column(dt, head) for head in heads))
            ec = jnp.exp(cums)
            w = jnp.exp(cums[CHUNK - 1 : CHUNK] - cums)
            x = act_ref[r, cols].astype(f32)
            xd = (x * dts).astype(bf16)
            dy = dy_ref[r, cols]
            dye = (dy.astype(f32) * ec).astype(bf16)
            grad = grad_s[:, cols]
            grad_low = grad.astype(bf16)
            state = hc_ref[c, :, cols].astype(f32) + runs_ref[c, :, cols] * enter_ref[:, cols].astype(f32)
            far = dot(b, grad_low) * w
            xw = (xd.astype(f32) * w).astype(bf16)
            d_b = d_b + dot_t(xw, grad_low)
            d_c = d_c + dot_t(dye, state.astype(bf16))
            end = split_decay(jnp.sum(grad * next_s[:, cols], axis=0, keepdims=True))
            next_s[:, cols] = state
            grad_s[:, cols] = grad * ec[CHUNK - 1 : CHUNK] + dot(c_t, dye)
            w1, w2 = (decays(cum, cum_t, head) for head in heads)
            back = jnp.concatenate([w1 * masked_t, w2 * masked_t], axis=1).astype(bf16)
            d_both = dot_t(dy, split_heads(xd))
            d_scores = d_scores + w1 * d_both[:, :CHUNK] + w2 * d_both[:, CHUNK:]
            d_xd = dot(back, split_heads(dy)) + far
            sums = jnp.concatenate([(d_xd * x).astype(bf16), end], axis=0)
            col = col + dot_t(sums, expand_ref[:, cols])
            d_x = d_xd * dts + skip_ref[:, cols] * dy.astype(f32)
            pre_s[t, r, :] = d_x * dact_ref[r, cols].astype(f32)
        ends = col[CHUNK : CHUNK + 1] + col[CHUNK + 1 : CHUNK + 2]
        col = col[:CHUNK]
        d_low = jnp.where(keep, d_scores, 0.0)
        d_c = d_c + dot(d_low.astype(bf16), b)
        d_b = d_b + dot(turned(d_low), cc)
        pre_s[INNER // LANES, r, :] = d_b * dact_ref[r, at_b].astype(f32)
        pre_s[INNER // LANES + 1, r, :] = d_c * dact_ref[r, at_c].astype(f32)
        if c == chunks - 1:
            ready(rowt_ref, sig_ref, rate_ref, cw_ref)
        d_cum = rowt_ref[r, :] - dt * col
        d_cum = d_cum + jnp.where(row == CHUNK - 1, ends, 0.0)
        d_log = dot_precise(upper, d_cum)
        d_raw = (d_log * rate_ref[...] + col) * sig_ref[r, :]
        draw_ref[r, :] = jnp.where(lane < HEADS, d_raw, 0.0).astype(bf16)

        strip = 64
        for t in range(CONV_CH // LANES):
            cols = slice(t * LANES, (t + 1) * LANES)
            weights = [cw_ref[j : j + 1, cols] for j in range(4)]
            for at in range(c * CHUNK, (c + 1) * CHUNK, strip):
                total = weights[3] * pre_s[t, at : at + strip, :]
                for j in range(3):
                    total = total + weights[j] * pre_s[t, at + 3 - j : at + 3 - j + strip, :]
                dx_ref[at : at + strip, cols] = total.astype(bf16)
                if at + strip == rows:
                    tail_ref[:, cols] = total[strip - RIM :, :]
        send(dx_ref, pl.ds(c * CHUNK, CHUNK))
        if c == chunks - 1:
            send(tail_ref)
    for t in range(CONV_CH // LANES):
        head_ref[:, t * LANES : (t + 1) * LANES] = pre_s[t, 0:RIM, :].astype(bf16)
    send(head_ref)
    send(draw_ref)

    ready(lat_ref, nrm_ref, bx_ref, d_lat_gate_ref)
    d_x = dx_ref[:, :INNER]
    d_lat_t = (d_lat_gate_ref[...] + dot_t(bx_ref[...], d_x)).astype(bf16)
    d_lat_ref[...] = turned(d_lat_t)
    send(d_lat_ref)
    sure = lax.broadcasted_iota(jnp.int32, (RANK, rows), 1) < rows - RIM
    lat_t = jnp.transpose(lat_ref[...].astype(f32))
    tb_ref[...] = dot(jnp.where(sure, lat_t, 0.0).astype(bf16), d_x)
    ta_ref[...] = dot(jnp.where(sure, d_lat_t.astype(f32), 0.0).astype(bf16), nrm_ref[...])
    send(tb_ref)
    send(ta_ref)


def scan_back_call(
    seq, ids, flags, other, before, before_other, act, dact, dt, cum, sig, rowt, dy, hc, enter, runs, lat, nrm, in_b, d_lat_gate, skip,
    rate, conv_w, expand,
):
    rows = act.shape[0]
    chunks = rows // CHUNK
    outs = [
        ((rows, CONV_CH), bf16),
        ((rows, LANES), bf16),
        ((RIM, CONV_CH), f32),
        ((RIM, CONV_CH), bf16),
        ((rows, RANK), bf16),
        ((RANK, INNER), f32),
        ((RANK, DM), f32),
    ]
    scratch = [
        pltpu.VMEM((NSTATE, INNER), f32),
        pltpu.VMEM((CONV_CH // LANES, rows + 8, LANES), f32),
        pltpu.VMEM((NSTATE, INNER), f32),
    ]
    operands = [view(a) for a in (other, before, before_other, enter, runs, dt, cum, skip, expand)]
    operands += [in_parts(hc, chunks + 1), in_parts(act, chunks), in_parts(dy, chunks), in_parts(dact, chunks)]
    operands += [later(view(a)) for a in (rowt, sig, rate, conv_w)]
    operands += [later(of_sequence(lat, seq)), later(of_sequence(nrm, seq))]
    operands += [later(of_adapter(in_b, seq, INNER, INNER)), later(view(d_lat_gate))]

    def kernel(ids, flags, *refs, **calls):
        scan_back_kernel(flags, *refs, **calls)

    return streamed(kernel, "scan_back", [ids, flags], operands, outs, scratch, 19)


def terms_kernel(*refs, seqs, owners, ready, send):
    refs = list(refs)[1:]
    per = 11
    ins, outs = refs[: 1 + per * seqs], refs[1 + per * seqs :]
    cw_ref, sent_ref = ins[0], outs[-1]
    ready(cw_ref)
    row = lax.broadcasted_iota(jnp.int32, (RIM, CONV_CH), 0)
    for s in range(seqs):
        tail_ref, next_ref, bx_ref, gate_ref, lat_ref, nrm_ref, tb_ref, ta_ref, tg_ref, ob_ref, oa_ref = ins[
            1 + per * s : 1 + per * (s + 1)
        ]
        last_ref, d_lat_ref = outs[2 * s : 2 * s + 2]
        ready(*ins[1 + per * s : 1 + per * (s + 1)])
        later_rows = next_ref[...].astype(f32)
        total = tail_ref[...]
        for back in range(1, 4):
            term = jnp.zeros((1, CONV_CH), f32)
            for j in range(0, 4 - back):
                term = term + cw_ref[j : j + 1, :] * later_rows[3 - back - j : 4 - back - j, :]
            total = total + jnp.where(row == RIM - back, term, 0.0)
        last = total.astype(bf16)
        last_ref[...] = last
        d_x = last[:, :INNER]
        gate_rows = jnp.transpose(gate_ref[...])[LANES - RIM :, :]
        d_lat = (gate_rows + dot_t(d_x, bx_ref[...])).astype(bf16)
        d_lat_ref[...] = d_lat
        send(last_ref)
        send(d_lat_ref)
        in_b = (tb_ref[...] + dot(turned(lat_ref[...]), d_x)).astype(bf16)
        in_a = (ta_ref[...] + dot(turned(d_lat), nrm_ref[...])).astype(bf16)
        both = jnp.concatenate([tg_ref[...], in_b], axis=1)
        kinds = [in_a, both, oa_ref[...], ob_ref[...]]
        for d in range(owners):
            pieces = []
            for kind in kinds:
                width = kind.shape[1] // owners
                pieces.append(kind[:, d * width : (d + 1) * width])
            sent_ref[d, s] = jnp.concatenate(pieces, axis=1)
    send(sent_ref)


def terms_call(ids, conv_w, items, lat, nrm, in_b, owners):
    seqs, rows, _ = nrm.shape
    last_columns = lambda scalars, ref: ref.at[:, pl.ds(rows - LANES, LANES)]
    operands = [view(conv_w)]
    outs = []
    for s, (tail, following, d_lat_gate, tb, ta, tg, ob, oa) in enumerate(items):
        of_last = lambda scalars, ref, s=s: ref.at[s, pl.ds(rows - RIM, RIM)]
        operands += [
            view(tail), view(following), of_adapter(in_b, s, INNER, INNER), view(d_lat_gate, last_columns, (RANK, LANES)),
            view(lat, of_last, (RIM, RANK)), view(nrm, of_last, (RIM, DM)), view(tb), view(ta), view(tg), view(ob),
            view(oa),
        ]
        outs += [((RIM, CONV_CH), bf16), ((RIM, RANK), bf16)]
    width = (2 * DM + ZX + INNER) // owners
    outs.append(((owners, seqs, RANK, width), bf16))
    kernel = functools.partial(terms_kernel, seqs=seqs, owners=owners)
    return streamed(kernel, "terms", [ids], operands, outs, [], 4)


def input_back_kernel(
    ids, lens, place, dg_ref, wg_ref, last_ref, dx_ref, wx_ref, draw_ref, wdt_ref, d_lat_ref, d_lat_last_ref, a_ref,
    gain_ref, x_ref, cot_ref, out_ref, dn_s, *, seq, ready, send,
):
    rows = dx_ref.shape[0]
    ready(dg_ref, wg_ref)
    dn_s[...] = dot_t(dg_ref[...], wg_ref[...])
    ready(last_ref, dx_ref, wx_ref, draw_ref, wdt_ref, d_lat_ref, d_lat_last_ref, a_ref)
    dx_ref[rows - RIM :, :] = last_ref[...]
    d_lat_ref[rows - RIM :, :] = d_lat_last_ref[...]
    dn_s[...] += (
        dot_t(dx_ref[...], wx_ref[...]) + dot_t(draw_ref[...], wdt_ref[...]) + dot(d_lat_ref[...], a_ref[...])
    )
    ready(gain_ref, x_ref, cot_ref)
    strip = 32
    for i in range(rows // strip):
        r = slice(i * strip, (i + 1) * strip)
        x = x_ref[r, :].astype(f32)
        root = lax.rsqrt(jnp.mean(x * x, -1, keepdims=True) + epsilon)
        dn = dn_s[r, :] * gain_ref[...]
        back = jnp.mean(dn * x, -1, keepdims=True) * (root * root * root)
        position = i * strip + lax.broadcasted_iota(jnp.int32, (strip, 1), 0)
        kept = jnp.where(position < lens[seq], cot_ref[r, :].astype(f32), 0.0)
        out_ref[r, :] = dn * root - x * back + kept
    send(out_ref)


def input_back_call(seq, ids, lens, place, begun, tokens, cotangent, dg, last, dx, draw, d_lat, d_lat_last, wg, wx, wdt, in_a, gain):
    rows = dx.shape[0]
    outs = [((rows, DM), f32)]
    operands = [view(dg), wg, view(last), view(dx), wx, view(draw), wdt, view(d_lat), view(d_lat_last)]
    operands += [of_adapter(in_a, seq), view(gain), of_sequence(tokens, seq), of_sequence(cotangent, seq)]
    kernel = functools.partial(input_back_kernel, seq=seq)
    scratch = [pltpu.VMEM((rows, DM), f32)]
    shared = (tokens.shape[0], seq, begun)
    return streamed(kernel, "input_back", [ids, lens, place], operands, outs, scratch, 9, shared)[0]


def shifted(value, axis, steps):
    count = lax.axis_size(axis)
    pairs = [(i, i + steps) for i in range(count) if 0 <= i + steps < count]
    return lax.ppermute(value, axis, pairs)


def swapped(value, axis, bit):
    return lax.ppermute(value, axis, [(i, i ^ bit) for i in range(lax.axis_size(axis))])


def after(value, other):
    return lax.optimization_barrier((value, other))[0]


def my_half(shard, core, half):
    return lax.dynamic_slice_in_dim(shard, core * half, half, 0)


def gathered_early(meanwhile, shard):
    owners = lax.axis_size("dp")
    rows, width = shard.shape
    half = rows // 2
    shapes = [(rows * owners, CONV_CH), (rows * owners, LANES)]
    if half % 16 or owners % 2:
        full = lax.all_gather(shard, "dp", axis=0, tiled=True)
        return view(full[:, :CONV_CH]), view(full[:, CONV_CH:]), None
    core = lax.axis_index("ctx") % 2
    own = {0: my_half(shard, core, half)}
    for k in range(2, owners, 2):
        own[k] = swapped(own[0], "dp", k)
    own[1] = swapped(own[0], "dp", 1)
    for k in range(2, owners, 2):
        waits = (own[min(3, k - 1)], meanwhile) if k == owners - 2 else own[1]
        own[k + 1] = swapped(after(own[k], waits), "dp", 1)
    pieces = [own[k] for k in range(owners)] + [swapped(own[k], "ctx", 1) for k in range(owners)]

    def copies(scalars, refs, to, columns):
        place = scalars[-1]
        pairs = []
        for n, piece in enumerate(refs):
            side = place[1] if n < owners else 1 - place[1]
            at = pl.multiple_of((place[0] ^ (n % owners)) * rows + side * half, 16)
            pairs.append((piece.at[:, columns], to.at[pl.ds(at, half)]))
        return pairs

    main = functools.partial(copies, columns=pl.ds(0, CONV_CH))
    rest = functools.partial(copies, columns=pl.ds(CONV_CH, LANES))
    arrived = (tuple(own[k] for k in range(2, owners, 2)), own[owners - 1])
    return Operand(pieces, shapes[0], main), Operand(pieces, shapes[1], rest), arrived


def gathered_late(gate, out, arrived, fronts, scans, befores):
    owners = lax.axis_size("dp")
    rows = gate.shape[0]
    half = rows // 2
    if arrived is None:
        return (
            view(lax.all_gather(gate, "dp", axis=0, tiled=True)),
            view(lax.all_gather(out, "dp", axis=0, tiled=True)),
        )
    core = lax.axis_index("ctx") % 2
    mine = my_half(jnp.concatenate([gate, out[:rows], out[rows:]], axis=1), core, half)
    own = {0: mine}
    for k in range(2, owners, 2):
        own[k] = swapped(after(mine, arrived[0][0] if k == 2 else arrived[0]), "dp", k)
    for k in range(0, owners, 2):
        waits = arrived[1] if k <= 2 else fronts[-1][5]
        own[k + 1] = swapped(after(own[k], waits), "dp", 1)
    pieces = [own[k] for k in range(owners)]
    hold = (scans[-1][0], befores[0])
    pieces += [swapped(after(own[k], scans[0][0] if k < 4 else hold), "ctx", 1) for k in range(owners)]

    def placed(scalars, refs):
        place = scalars[-1]
        for n, piece in enumerate(refs):
            side = place[1] if n < owners else 1 - place[1]
            yield piece, place[0] ^ (n % owners), side * half

    def gate_copies(scalars, refs, to):
        pairs = []
        for piece, owner, start in placed(scalars, refs):
            at = pl.multiple_of(owner * rows + start, 16)
            pairs.append((piece.at[:, pl.ds(0, INNER)], to.at[pl.ds(at, half)]))
        return pairs

    def out_copies(scalars, refs, to):
        pairs = []
        for piece, owner, start in placed(scalars, refs):
            for k in range(2):
                at = pl.multiple_of((2 * owner + k) * rows + start, 16)
                pairs.append((piece.at[:, pl.ds(INNER + k * DM, DM)], to.at[pl.ds(at, half)]))
        return pairs

    return (
        Operand(pieces, (rows * owners, INNER), gate_copies),
        Operand(pieces, (2 * rows * owners, DM), out_copies),
    )


def join_kernel(swap, one_ref, two_ref, out_ref, *, ready, send):
    ready(one_ref, two_ref)
    join_payloads(swap[0], one_ref, two_ref, out_ref)
    send(out_ref)


def joined(one, two, swap):
    return streamed(join_kernel, "join", [swap], [view(one), view(two)], [(one.shape, bf16)], [], 1)[0]


def state_in_two(flags, other_ref, far_ref, far_other_ref, cols):
    far, far_other, other = (ref[0:NSTATE, cols].astype(f32) for ref in (far_ref, far_other_ref, other_ref))
    behind = decay_of(far_ref, cols) * far_other + far
    ahead = decay_of(far_other_ref, cols) * far + far_other
    before = jnp.where(flags[1] == 1, behind, ahead)
    return jnp.where(flags[0] == 1, decay_of(other_ref, cols) * before + other, before)


def from_before(both, reverse):
    chips = lax.axis_size("ctx") // 2
    sign = -1 if reverse else 1
    in_order = jnp.zeros((1,), jnp.int32)
    before = shifted(both, "ctx", 2 * sign)
    step, run = 1, both
    while 2 * step < chips:
        run = joined(before, both, in_order) if step == 1 else joined(far, run, in_order)
        far = shifted(run, "ctx", 4 * step * sign)
        before = joined(far, before, in_order)
        step *= 2
    return before


def shards(
    tokens, cotangent, lengths, adapter_ids, norm_gain, w_in, conv_weight, conv_bias, dt_bias, a_log,
    skip_scale, inner_gain, w_out, in_a, in_b, out_a, out_b,
):
    seqs, slots, _ = tokens.shape
    owners = lax.axis_size("dp")
    ids = adapter_ids
    lens = jnp.clip(lengths - lax.axis_index("ctx") * slots, 0, slots).astype(jnp.int32)

    def grouped(row):
        padded = jnp.pad(row.reshape(-1, HEADS), ((0, 0), (0, GROUP - HEADS)))
        return jnp.tile(padded, (1, LANES // GROUP))

    rate = grouped(-jnp.exp(a_log))
    dtb = grouped(dt_bias)
    lane = jnp.arange(LANES)[:, None]
    head = jnp.arange(INNER)[None, :] // HDIM
    expand = ((lane % GROUP == head) & (lane < 3 * GROUP)).astype(bf16)
    skip = jnp.repeat(skip_scale, HDIM)[None, :]
    gain = inner_gain[None, :]
    n_gain = norm_gain[None, :]
    conv_b = conv_bias[None, :]

    marks = jnp.broadcast_to(ids.astype(bf16)[None, :], (w_in.shape[0], seqs))
    marks = jnp.pad(marks, ((0, 0), (0, GROUP - HEADS - seqs)))
    steps = jnp.concatenate([w_in[:, INNER + CONV_CH :], marks], axis=1)
    in_a, out_a = jnp.swapaxes(in_a, 1, 2), jnp.swapaxes(out_a, 1, 2)
    rim = shifted(tokens[:, slots - RIM :], "ctx", 1)
    nrm, nrim, lat, lrim = norm_call(ids, tokens, rim, n_gain, in_a)
    wx, wdt, arrived = gathered_early(
        nrm,
        jnp.concatenate([w_in[:, INNER : INNER + CONV_CH]] + [steps] * (LANES // GROUP), axis=1)
    )

    core = lax.axis_index("ctx") % 2
    place = jnp.stack([lax.axis_index("dp"), core]).astype(jnp.int32)
    late = core.reshape(1).astype(jnp.int32)
    early = 1 - late
    front = functools.partial(
        front_call, in_b=in_b, wx=wx, wdt=wdt, conv_w=conv_weight, conv_b=conv_b, dtb=dtb, rate=rate, expand=expand
    )
    nrm, (skip, gain, lens, late, early) = lax.optimization_barrier((nrm, (skip, gain, lens, late, early)))
    chips = lax.axis_size("ctx") // 2
    flags_back = jnp.concatenate([early, early if chips == 2 else jnp.ones_like(early)])
    fronts, others = [], []
    for s in range(seqs):
        ready = nrm if s == 0 else after(nrm, fronts[-1][5])
        fronts.append(front(s, ids, place, ready, nrim, lat, lrim))
        others.append(swapped(fronts[s][5], "ctx", 1))
    scans, befores = [], []
    for s in range(seqs):
        act, _, dt, cum, _, own, _ = fronts[s]
        ready = after(act, fronts[-1][5]) if s == 0 else after(act, scans[-1][0])
        scans.append(scan_call(late, own, others[s], ready, dt, cum))
        befores.append(from_before(scans[s][2], False))
    full_gate, full_out = gathered_late(w_in[:, :INNER], w_out, arrived, fronts, scans, befores)
    middles, other_grads, later_grads = [], [], []
    for s in range(seqs):
        act, _, _, cum, _, _, _ = fronts[s]
        ready = after(nrm, scans[-1][0] if s == 0 else middles[-1][4])
        middles.append(
            middle_call(
                s, ids, lens, place, late, middles[-1][0] if s else None, tokens, cotangent, ready, lat, act, cum,
                others[s], befores[s], scans[s][0], full_gate, in_b, full_out, out_a, out_b, skip, gain, expand,
            )
        )
        payload = after(middles[s][4], later_grads[-1] if s and chips > 2 else befores[-1])
        other_grads.append(swapped(payload, "ctx", 1))
        if chips == 2:
            later_grads.append(shifted(payload, "ctx", -2))
        else:
            later_grads.append(from_before(joined(payload, other_grads[s], early), True))
    backs, nexts = [], []
    for s in range(seqs):
        act, dact, dt, cum, sig, _, _ = fronts[s]
        _, dy, _, rowt, _, _, _, enter, runs, d_lat_gate, _ = middles[s]
        hold = middles[-1][4] if s == 0 else backs[-1][3]
        ready = after(act, hold)
        later_other = swapped(after(later_grads[s], hold), "ctx", 1) if chips == 2 else jnp.zeros_like(later_grads[s])
        backs.append(
            scan_back_call(
                s, ids, flags_back, other_grads[s], later_grads[s], later_other, ready, dact, dt, cum, sig, rowt, dy, scans[s][1], enter,
                runs, lat, nrm, in_b, d_lat_gate, skip, rate, conv_weight, expand,
            )
        )
        nexts.append(shifted(backs[s][3], "ctx", -1))
    items = [
        (back[2], following, mid[9], back[5], back[6], mid[10], mid[5], mid[6])
        for back, following, mid in zip(backs, nexts, middles)
    ]
    *lasts, sent = terms_call(ids, conv_weight, items, lat, nrm, in_b, owners)

    widths = [width // owners for width in (DM, ZX, INNER, DM)]
    got = lax.all_to_all(sent, "dp", 0, 0)
    held = after(tokens, sent)
    input_grad = None
    for s in range(seqs):
        if s == 1:
            got = after(got, input_grad)
        input_grad = input_back_call(
            s, ids, lens, place, input_grad, held, cotangent, middles[s][2], lasts[2 * s], backs[s][0], backs[s][1],
            backs[s][4], lasts[2 * s + 1], full_gate, wx, wdt, in_a, n_gain,
        )
    every = fronts[0][6][:, HEADS : HEADS + seqs].reshape(1, -1)
    chosen = (every == jnp.arange(ADAPT, dtype=f32)[:, None]).astype(f32)
    flat = got.reshape(owners * seqs, -1).astype(f32)
    mine = jnp.sum(chosen[:, :, None] * flat[None], axis=1)
    if lax.axis_size("ctx") == 4:
        low = mine.astype(bf16)
        mine = mine + sum(swapped(low, "ctx", bits).astype(f32) for bits in (1, 2, 3))
    else:
        bit = 1
        while bit < lax.axis_size("ctx"):
            mine = mine + swapped(mine.astype(bf16), "ctx", bit).astype(f32)
            bit *= 2
    mine = mine.reshape(ADAPT, RANK, -1)
    cuts = [sum(widths[:k]) for k in range(5)]
    g_ia, g_ib, g_oa, g_ob = (mine[:, :, cuts[k] : cuts[k + 1]] for k in range(4))
    return (
        middles[-1][0],
        input_grad,
        jnp.swapaxes(g_ia, 1, 2),
        g_ib,
        jnp.swapaxes(g_oa, 1, 2),
        g_ob,
    )


def solution(mesh):
    split = P("dp", "ctx", None)
    return jax.shard_map(
        shards,
        mesh=mesh,
        in_specs=(
            split, split, P("dp"), P("dp"), P(), P("dp", None), P(), P(), P(), P(), P(), P(),
            P("dp", None), P(), P(), P(), P(),
        ),
        out_specs=(
            split, split, P(None, "dp", None), P(None, None, "dp"), P(None, "dp", None), P(None, None, "dp"),
        ),
        check_vma=False,
    )
```

```python
import functools

import jax
import jax.numpy as jnp
from jax import lax
from jax.experimental import pallas as pl
from jax.experimental.pallas import tpu as pltpu
from jax.sharding import PartitionSpec as P

HEADS = 24
HDIM = 64
NSTATE = 128
INNER = 1536
CONV_CH = 1792
ZX = 3072
DM = 768
RANK = 16
ADAPT = 8
CHUNK = 128
TILE = 256
RIM = 16
GROUP = 32
LANES = 128
VMEM_LIMIT = 60 * 1024 * 1024

epsilon = 1e-05
bf16 = jnp.bfloat16
f32 = jnp.float32


def dot(left, right):
    return jnp.dot(left, right, preferred_element_type=f32)


def dot_t(left, right):
    return lax.dot_general(
        left, right, (((1,), (1,)), ((), ())), preferred_element_type=f32
    )


def dot_precise(left, right):
    return jnp.dot(
        left, right, preferred_element_type=f32, precision=lax.Precision.HIGHEST
    )


def parts_of(v):
    lane = lax.broadcasted_iota(jnp.int32, v.shape, 1)
    high = v.astype(bf16).astype(f32)
    rest = v - high
    middle = rest.astype(bf16).astype(f32)
    kept = jnp.where(lane < GROUP, high, jnp.where(lane < 2 * GROUP, middle, rest - middle))
    return jnp.where(lane < 3 * GROUP, kept, 0.0).astype(bf16)


def causal(rows):
    t = lax.broadcasted_iota(jnp.int32, (rows, rows), 0)
    s = lax.broadcasted_iota(jnp.int32, (rows, rows), 1)
    return t >= s


def sigmoid(v):
    return 0.5 * jnp.tanh(0.5 * v) + 0.5


def turned(v):
    return jnp.transpose(v.astype(f32)).astype(bf16)


class Operand:
    def __init__(self, arrays, shape, copies, parts=1, late=False):
        self.arrays, self.shape, self.copies, self.parts = list(arrays), tuple(shape), copies, parts
        self.late = late


def view(array, pick=None, shape=None):
    pick = pick or (lambda scalars, ref: ref)
    return Operand([array], shape or array.shape, lambda scalars, refs, to: [(pick(scalars, refs[0]), to)])


def later(operand):
    return Operand(operand.arrays, operand.shape, operand.copies, operand.parts, True)


def in_parts(array, parts):
    def copies(scalars, refs, to):
        size = array.shape[0] // parts
        return [(refs[0].at[pl.ds(p * size, size)], to.at[pl.ds(p * size, size)]) for p in range(parts)]

    return Operand([array], array.shape, copies, parts)


def streamed(kernel, name, scalars, operands, outs, scratch, micros, shared=None):
    arrays = [array for operand in operands for array in operand.arrays]
    n_scalar, n_array, n_in, n_out = len(scalars), len(arrays), len(operands), len(outs)
    kinds = [operand.arrays[0].dtype for operand in operands]
    slots, slot, begun = shared or (None, None, None)
    parted_in = any(operand.parts > 1 for operand in operands)
    n_begun = 0 if begun is None else 1

    def body(*refs):
        refs = list(refs)
        take = lambda n: [refs.pop(0) for _ in range(n)]
        smem, sources, _, targets, ins, results = (
            take(n) for n in (n_scalar, n_array, n_begun, n_out, n_in, n_out)
        )
        if shared:
            targets[0] = targets[0].at[slot]
        in_sems, out_sems = refs.pop(-2), refs.pop(-1)
        waiting, parted, late, first_sem = {}, [], [], 0
        for k, operand in enumerate(operands):
            mine = [sources.pop(0) for _ in operand.arrays]
            copies = operand.copies(smem, mine, ins[k])
            if operand.parts == 1:
                sem = in_sems.at[first_sem]
                for source, target in copies:
                    copy = pltpu.make_async_copy(source, target, sem)
                    if operand.late:
                        late.append(copy)
                    else:
                        copy.start()
                waiting[id(ins[k])] = [pltpu.make_async_copy(ins[k], ins[k], sem)]
            else:
                made = [
                    pltpu.make_async_copy(source, target, in_sems.at[first_sem + p])
                    for p, (source, target) in enumerate(copies)
                ]
                waiting[id(ins[k])] = made
                parted.append(list(made))
            first_sem += operand.parts
        while any(parted):
            for made in parted:
                if made:
                    made.pop().start()
        for copy in late:
            copy.start()

        def ready(*wanted):
            for ref in wanted:
                for copy in waiting.pop(id(ref), ()):
                    copy.wait()

        def ready_last(*wanted):
            for ref in wanted:
                waiting[id(ref)].pop().wait()

        sent = []

        def send(ref, *at):
            k = [id(result) for result in results].index(id(ref))
            if k not in sent:
                sent.append(k)
            source, target = (results[k].at[at], targets[k].at[at]) if at else (results[k], targets[k])
            pltpu.make_async_copy(source, target, out_sems.at[k]).start()

        more = {"ready_last": ready_last} if parted_in else {}
        kernel(*smem, *ins, *results, *refs, ready=ready, send=send, **more)
        ready(*ins)
        for k in sent:
            pltpu.make_async_copy(results[k], targets[k], out_sems.at[k]).wait()

    anywhere = pl.BlockSpec(memory_space=pl.ANY)
    full = [((slots,) + shape if shared and k == 0 else shape, kind) for k, (shape, kind) in enumerate(outs)]
    return pl.pallas_call(
        body,
        in_specs=[pl.BlockSpec(memory_space=pltpu.SMEM)] * n_scalar + [anywhere] * (n_array + n_begun),
        out_specs=[anywhere] * n_out,
        out_shape=[jax.ShapeDtypeStruct(shape, kind) for shape, kind in full],
        scratch_shapes=[pltpu.VMEM(operand.shape, kind) for operand, kind in zip(operands, kinds)]
        + [pltpu.VMEM(shape, kind) for shape, kind in outs]
        + scratch
        + [pltpu.SemaphoreType.DMA((sum(operand.parts for operand in operands),)), pltpu.SemaphoreType.DMA((n_out,))],
        input_output_aliases={n_scalar + n_array: 0} if n_begun else {},
        compiler_params=pltpu.CompilerParams(vmem_limit_bytes=VMEM_LIMIT),
        cost_estimate=pl.CostEstimate(flops=micros * 400000000, bytes_accessed=1000000, transcendentals=0),
        name=name,
    )(*scalars, *arrays, *([begun] if n_begun else []))


def of_sequence(array, seq):
    return view(array, lambda scalars, ref: ref.at[seq], array.shape[1:])


def of_adapter(array, seq, start=0, width=None):
    width = width or array.shape[2]
    pick = lambda scalars, ref: ref.at[scalars[0][seq], :, pl.ds(start, width)]
    return view(array, pick, (array.shape[1], width))


def split_decay(decay):
    high = decay.astype(bf16).astype(f32)
    row = lax.broadcasted_iota(jnp.int32, (RIM, decay.shape[1]), 0)
    return jnp.where(row == 0, high, jnp.where(row == 1, decay - high, 0.0)).astype(bf16)


def decay_of(payload_ref, cols):
    rows = payload_ref[NSTATE:, cols].astype(f32)
    return rows[0:1] + rows[1:2]


def norm_kernel(
    ids, x0_ref, x1_ref, rim_ref, gain_ref, a0_ref, a1_ref, nrm_ref, nrim_ref, lat_ref, lrim_ref, *, ready, send
):
    def normed(x):
        x = x.astype(f32)
        mean = jnp.mean(x * x, -1, keepdims=True)
        return (x * lax.rsqrt(mean + epsilon) * gain_ref[...]).astype(bf16)

    strip = 64
    ready(gain_ref, rim_ref)
    for s, (x_ref, a_ref) in enumerate(((x0_ref, a0_ref), (x1_ref, a1_ref))):
        ready(x_ref, a_ref)
        for i in range(x_ref.shape[0] // strip):
            r = slice(i * strip, (i + 1) * strip)
            nrm_ref[s, r, :] = normed(x_ref[r, :])
        nrim_ref[s] = normed(rim_ref[s])
        lat_ref[s] = dot_t(nrm_ref[s], a_ref[...]).astype(bf16)
        lrim_ref[s] = dot_t(nrim_ref[s], a_ref[...]).astype(bf16)
    for ref in (nrm_ref, nrim_ref, lat_ref, lrim_ref):
        send(ref)


def norm_call(ids, tokens, rim, gain, in_a):
    seqs, rows, _ = tokens.shape
    outs = [
        ((seqs, rows, DM), bf16),
        ((seqs, RIM, DM), bf16),
        ((seqs, rows, RANK), bf16),
        ((seqs, RIM, RANK), bf16),
    ]
    operands = [
        of_sequence(tokens, 0), of_sequence(tokens, 1), view(rim), view(gain), of_adapter(in_a, 0), of_adapter(in_a, 1),
    ]
    return streamed(norm_kernel, "norm", [ids], operands, outs, [], 3)


def front_kernel(
    ids, place, nrm_s, lat_s, wdt_ref, dtb_ref, rate_ref, cw_ref, cb_ref, wx_ref, bx_ref,
    expand_ref, act_ref, dact_ref, dt_ref, cum_ref, sig_ref, pay_ref, marks_ref,
    xs, bt_s, w_s, *, ready, send,
):
    rows = nrm_s.shape[0] - RIM
    ready(nrm_s, lat_s)
    ready(wdt_ref, dtb_ref, rate_ref)
    owners = marks_ref.shape[0]
    for d in range(owners):
        at = d * (wdt_ref.shape[0] // owners)
        marks_ref[d : d + 1, :] = wdt_ref[at : at + 8, :].astype(f32)[0:1]
    send(marks_ref)
    raw = dot(nrm_s[RIM:, :], wdt_ref[...]) + dtb_ref[...]
    step = jnp.maximum(raw, 0.0) + jnp.log1p(jnp.exp(-jnp.abs(raw)))
    dt_ref[...] = step
    sig_ref[...] = jnp.exp(raw - step)
    logs = step * rate_ref[...]
    lower = causal(CHUNK).astype(f32)
    before = jnp.zeros((1, LANES), f32)
    whole = []
    for c in range(rows // CHUNK):
        r = slice(c * CHUNK, (c + 1) * CHUNK)
        cum = dot_precise(lower, logs[r])
        cum_ref[r, :] = cum
        whole.append(cum + before)
        before = before + cum[CHUNK - 1 : CHUNK]
    for c in range(rows // CHUNK):
        r = slice(c * CHUNK, (c + 1) * CHUNK)
        w_s[r, :] = parts_of(jnp.exp(before - whole[c]) * step[r])
    total = parts_of(jnp.broadcast_to(jnp.exp(before), (8, LANES)))
    for ref in (dt_ref, cum_ref, sig_ref):
        send(ref)
    ready(cw_ref, cb_ref, wx_ref, bx_ref, expand_ref)

    def activate(cols, base):
        weights = [cw_ref[j : j + 1, cols] for j in range(4)]
        bias = cb_ref[:, cols]
        low = base.astype(bf16).astype(f32)
        for k in range(2):
            xs[k] = low[:, k * LANES : (k + 1) * LANES]
        strip = 64
        for i in range(rows // strip):
            at = RIM + i * strip
            halves = []
            for k in range(2):
                lanes = slice(k * LANES, (k + 1) * LANES)
                pre = bias[:, lanes] + weights[0][:, lanes] * xs[k, at - 3 : at - 3 + strip, :]
                for j in range(1, 4):
                    pre = pre + weights[j][:, lanes] * xs[k, at - 3 + j : at - 3 + j + strip, :]
                halves.append(pre)
            pre = jnp.concatenate(halves, axis=1)
            gate = sigmoid(pre)
            act = pre * gate
            r = slice(i * strip, (i + 1) * strip)
            act_ref[r, cols] = act.astype(bf16)
            dact_ref[r, cols] = (gate + act * (1.0 - gate)).astype(bf16)
        send(act_ref, slice(None), cols)
        send(dact_ref, slice(None), cols)

    last = pl.ds(INNER, CONV_CH - INNER)
    activate(last, dot(nrm_s[...], wx_ref[:, last]))
    bt_s[...] = turned(act_ref[:, INNER : INNER + NSTATE])
    def tile_body(t, carry):
        cols = pl.ds(pl.multiple_of(t * TILE, TILE), TILE)
        activate(cols, dot(nrm_s[...], wx_ref[:, cols]) + dot(lat_s[...], bx_ref[:, cols]))
        scaled = (act_ref[:, cols].astype(f32) * dot(w_s[...], expand_ref[:, cols])).astype(bf16)
        pay_ref[0:NSTATE, cols] = dot(bt_s[...], scaled).astype(bf16)
        pay_ref[NSTATE:, cols] = split_decay(dot(total, expand_ref[:, cols])[0:1])
        return carry

    lax.fori_loop(0, INNER // TILE, tile_body, 0)
    send(pay_ref)


def front_call(seq, ids, place, nrm, nrim, lat, lrim, wx, wdt, in_b, conv_w, conv_b, dtb, rate, expand):
    rows = nrm.shape[1]
    owners = lax.axis_size("dp")
    outs = [
        ((rows, CONV_CH), bf16),
        ((rows, CONV_CH), bf16),
        ((rows, LANES), f32),
        ((rows, LANES), f32),
        ((rows, LANES), f32),
        ((NSTATE + RIM, INNER), bf16),
        ((owners, LANES), f32),
    ]
    scratch = [
        pltpu.VMEM((2, rows + RIM, LANES), f32),
        pltpu.VMEM((NSTATE, rows), bf16),
        pltpu.VMEM((rows, LANES), bf16),
    ]
    def rim_first(rim, rest):
        def copies(scalars, refs, to):
            return [(refs[0].at[seq], to.at[pl.ds(0, RIM)]), (refs[1].at[seq], to.at[pl.ds(RIM, rows)])]

        return Operand([rim, rest], (RIM + rows, rest.shape[2]), copies)

    operands = [rim_first(nrim, nrm), rim_first(lrim, lat)]
    operands += [wdt] + [view(a) for a in (dtb, rate, conv_w, conv_b)] + [wx]
    operands += [of_adapter(in_b, seq, INNER, INNER), view(expand)]
    return streamed(front_kernel, "front", [ids, place], operands, outs, scratch, 13)


def column(values, head):
    return jnp.broadcast_to(values[:, head : head + 1], values.shape)


def beside(one, two):
    lane = lax.broadcasted_iota(jnp.int32, one.shape, 1)
    return jnp.where(lane < HDIM, one, two)


def decays(cum, cum_t, head):
    gap = column(cum, head) - cum_t[head : head + 1, :]
    return jnp.exp(jnp.minimum(gap, -gap))


def split_heads(pair):
    lane = lax.broadcasted_iota(jnp.int32, pair.shape, 1)
    zero = jnp.zeros_like(pair)
    first = jnp.where(lane < HDIM, pair, zero)
    second = jnp.where(lane < HDIM, zero, pair)
    return jnp.concatenate([first, second], axis=0)


def join_payloads(swap, one_ref, two_ref, out_ref):
    for t in range(INNER // TILE):
        cols = slice(t * TILE, (t + 1) * TILE)
        d_one, d_two = decay_of(one_ref, cols), decay_of(two_ref, cols)
        one = one_ref[0:NSTATE, cols].astype(f32)
        two = two_ref[0:NSTATE, cols].astype(f32)
        state = jnp.where(swap == 1, d_one * two + one, d_two * one + two)
        out_ref[0:NSTATE, cols] = state.astype(bf16)
        out_ref[NSTATE:, cols] = split_decay(d_one * d_two)


def state_in(late, other_ref, before_ref, cols):
    before = before_ref[0:NSTATE, cols].astype(f32)
    joint = decay_of(other_ref, cols) * before + other_ref[0:NSTATE, cols].astype(f32)
    return jnp.where(late == 1, joint, before)


def scan_kernel(
    flags, own_ref, other_ref, act_ref, dt_ref, cum_ref, y_ref, hc_ref, both_ref, state_s, *, ready, send
):
    keep = causal(CHUNK)
    ready(own_ref, other_ref)
    join_payloads(flags[0], own_ref, other_ref, both_ref)
    send(both_ref)
    state_s[...] = jnp.zeros_like(state_s)
    ready(act_ref, dt_ref, cum_ref)

    def one_chunk(c, carry):
        r = pl.ds(pl.multiple_of(c * CHUNK, CHUNK), CHUNK)
        b = act_ref[r, INNER : INNER + NSTATE]
        cc = act_ref[r, INNER + NSTATE :]
        b_t = turned(b)
        masked = jnp.where(keep, dot_t(cc, b), 0.0)
        dt = dt_ref[r, :]
        cum = cum_ref[r, :]
        cum_t = jnp.transpose(cum)
        for t in range(INNER // LANES):
            cols = slice(t * LANES, (t + 1) * LANES)
            heads = (2 * t, 2 * t + 1)
            cums = beside(*(column(cum, head) for head in heads))
            steps = beside(*(column(dt, head) for head in heads))
            ec = jnp.exp(cums)
            xd = act_ref[r, cols].astype(f32) * steps
            xw = (xd * jnp.exp(cums[CHUNK - 1 : CHUNK] - cums)).astype(bf16)
            state = state_s[:, cols]
            low = state.astype(bf16)
            hc_ref[c, :, cols] = low
            far = dot(cc, low) * ec
            state_s[:, cols] = state * ec[CHUNK - 1 : CHUNK] + dot(b_t, xw)
            weights = [(decays(cum, cum_t, head) * masked).astype(bf16) for head in heads]
            near = dot(jnp.concatenate(weights, axis=1), split_heads(xd.astype(bf16)))
            y_ref[r, cols] = (near + far).astype(bf16)
        send(y_ref, r)
        send(hc_ref, pl.ds(c, 1))
        return carry

    chunks = act_ref.shape[0] // CHUNK
    lax.fori_loop(0, chunks, one_chunk, 0)
    hc_ref[chunks] = state_s[...].astype(bf16)
    send(hc_ref, pl.ds(chunks, 1))


def scan_call(flags, own, other, act, dt, cum):
    rows = act.shape[0]
    chunks = rows // CHUNK
    outs = [((rows, INNER), bf16), ((chunks + 1, NSTATE, INNER), bf16), (own.shape, bf16)]
    scratch = [pltpu.VMEM((NSTATE, INNER), f32)]
    operands = [view(a) for a in (own, other, act, dt, cum)]
    return streamed(scan_kernel, "scan", [flags], operands, outs, scratch, 9)


def woven(one, two):
    order = [((n + 0.5) / len(steps), k, step) for k, steps in enumerate((one, two)) for n, step in enumerate(steps)]
    for _, _, step in sorted(order, key=lambda item: item[:2]):
        step()


def middle_kernel(
    ids, lens, flags, place, nrm_ref, lat_ref, bg_ref, wg_ref, cot_ref, b_ref, a_ref, wo_ref, other_ref, before_ref,
    cum_ref, expand_ref, act_ref, y_ref, skip_ref, gain_ref, x_ref,
    out_ref, dy_ref, dg_ref, rowt_ref, pay_ref, tb_ref, ta_ref, enter_ref, runs_ref, d_lat_ref, tg_ref,
    gate_s, z_s, dh_s, hid_s, prod_s, ec_s, y_s, grad_s, tb_s, ta_s, tg_s, *, seq, ready, send,
):
    rows = act_ref.shape[0]
    block = 2 * CHUNK
    strip = 16
    tiles = [slice(t * TILE, (t + 1) * TILE) for t in range(INNER // TILE)]
    blocks = [slice(k * block, (k + 1) * block) for k in range(rows // block)]
    kept = [{} for _ in blocks]

    position = lax.broadcasted_iota(jnp.int32, (rows, 1), 0)
    valid = position < lens[seq]
    ready(nrm_ref, lat_ref, bg_ref, wg_ref)
    for cols in tiles:
        gate_s[:, cols] = dot(nrm_ref[...], wg_ref[:, cols]) + dot(lat_ref[...], bg_ref[:, cols])
    ready(cot_ref, b_ref, a_ref, gain_ref, wo_ref)
    cot_ref[...] = jnp.where(valid, cot_ref[...], jnp.zeros((), bf16))
    d_lat_t = dot_t(b_ref[...], cot_ref[...]).astype(bf16)
    d_lat = turned(d_lat_t)
    for cols in tiles:
        d_hidden = dot_t(cot_ref[...], wo_ref[cols, :]) + dot(d_lat, a_ref[:, cols])
        dh_s[:, cols] = d_hidden * gain_ref[:, cols]
    ready(other_ref, before_ref, cum_ref, expand_ref)
    before = jnp.zeros((1, LANES), f32)
    logs = []
    for c in range(rows // CHUNK):
        logs.append(cum_ref[c * CHUNK : (c + 1) * CHUNK, :] + before)
        before = logs[-1][CHUNK - 1 : CHUNK]
    runs_ref[0] = jnp.ones((1, INNER), f32)
    spread = parts_of(jnp.exp(jnp.concatenate(logs, axis=0)))
    for cols in tiles:
        enter_ref[:, cols] = state_in(flags[0], other_ref, before_ref, cols).astype(bf16)
        ec = dot(spread, expand_ref[:, cols])
        ec_s[:, cols] = ec
        for c in range(rows // CHUNK):
            runs_ref[c + 1, :, cols] = ec[(c + 1) * CHUNK - 1 : (c + 1) * CHUNK]
    send(enter_ref)
    ready(act_ref, y_ref, skip_ref)

    def project(k):
        r = blocks[k]

        def far_tile(cols):
            far = dot(act_ref[r, INNER + NSTATE :], enter_ref[:, cols]) * ec_s[r, cols]
            y_s[r, cols] = y_ref[r, cols].astype(f32) + far

        return [functools.partial(far_tile, cols) for cols in tiles]

    def forward(k):
        def one(i):
            r = slice(k * block + i * strip, k * block + (i + 1) * strip)
            total = jnp.zeros((strip, LANES), f32)
            for cols in tiles:
                gate = gate_s[r, cols]
                u = y_s[r, cols] + skip_ref[:, cols] * act_ref[r, cols].astype(f32)
                sig = sigmoid(gate)
                silu = gate * sig
                z = u * silu
                square = z * z
                total = total + square[:, :LANES] + square[:, LANES:]
                z_s[r, cols] = z
                gate_s[r, cols] = silu
                prod_s[r, cols] = u * (sig + silu * (1.0 - sig))
            root = lax.rsqrt(jnp.sum(total, -1, keepdims=True) / INNER + epsilon)
            kept[k][i] = root
            for cols in tiles:
                hid_s[r, cols] = (z_s[r, cols] * root * gain_ref[:, cols]).astype(bf16)

        return [functools.partial(one, i) for i in range(block // strip)]

    def mix(k):
        r = blocks[k]

        def latent():
            if k == 0:
                ready(x_ref)
            lat_out_t = dot_t(a_ref[...], hid_s[r, :]).astype(bf16)
            kept[k]["lat_out"] = turned(lat_out_t)
            more = dot(lat_out_t, cot_ref[r, :])
            tb_s[...] = more if k == 0 else tb_s[...] + more

        def out_tile(n):
            cols = slice(n * TILE, (n + 1) * TILE)
            mixed = dot(hid_s[r, :], wo_ref[:, cols]) + dot(kept[k]["lat_out"], b_ref[:, cols])
            x = x_ref[r, cols].astype(f32)
            out_ref[r, cols] = jnp.where(valid[r], x + mixed, 0.0).astype(bf16)

        def term_tile(cols):
            more = dot(d_lat_t[:, r], hid_s[r, cols])
            ta_s[:, cols] = more if k == 0 else ta_s[:, cols] + more

        steps = [latent] + [functools.partial(out_tile, n) for n in range(DM // TILE)]
        steps.append(lambda: send(out_ref, pl.ds(k * block, block)))
        return steps + [functools.partial(term_tile, cols) for cols in tiles]

    def backward(k):
        def one(i):
            r = slice(k * block + i * strip, k * block + (i + 1) * strip)
            total = jnp.zeros((strip, LANES), f32)
            for cols in tiles:
                both = dh_s[r, cols] * z_s[r, cols]
                total = total + both[:, :LANES] + both[:, LANES:]
            root = kept[k][i]
            back = jnp.sum(total, -1, keepdims=True) * (root * root * root) / INNER
            for cols in tiles:
                dz = dh_s[r, cols] * root - z_s[r, cols] * back
                dy = (dz * gate_s[r, cols]).astype(bf16)
                dy_ref[r, cols] = dy
                dg_ref[r, cols] = (dz * prod_s[r, cols]).astype(bf16)
                hid_s[r, cols] = (dy.astype(f32) * y_s[r, cols]).astype(bf16)

        return [functools.partial(one, i) for i in range(block // strip)]

    def finish(k):
        r = blocks[k]
        at = pl.ds(k * block, block)

        def out():
            send(dy_ref, at)
            send(dg_ref, at)
            rowt_ref[r, :] = dot_t(hid_s[r, :], expand_ref[...])
            send(rowt_ref, at)

        def state_tile(cols):
            if cols.start == 0:
                kept[k]["c_t"] = turned(act_ref[r, INNER + NSTATE :])
            scaled = (dy_ref[r, cols].astype(f32) * ec_s[r, cols]).astype(bf16)
            more = dot(kept[k]["c_t"], scaled)
            grad_s[:, cols] = more if k == 0 else grad_s[:, cols] + more

        def latent():
            d_lat_ref[:, r] = dot_t(bg_ref[...], dg_ref[r, :])
            kept[k]["lat_t"] = turned(lat_ref[r, :])

        def term_tile(cols):
            more = dot(kept[k]["lat_t"], dg_ref[r, cols])
            tg_s[:, cols] = more if k == 0 else tg_s[:, cols] + more

        steps = [out] + [functools.partial(state_tile, cols) for cols in tiles] + [latent]
        return steps + [functools.partial(term_tile, cols) for cols in tiles]

    last = len(blocks) - 1
    stages = [project, forward, mix, backward, finish]
    for turn in range(len(stages) + last):
        now = [stages[turn - k](k) for k in range(last + 1) if 0 <= turn - k < len(stages)]
        steps = now.pop(0)
        for other in now:
            order = []
            woven([functools.partial(order.append, step) for step in steps], [functools.partial(order.append, step) for step in other])
            steps = order
        for step in steps:
            step()
    pay_ref[0:NSTATE, :] = grad_s[...].astype(bf16)
    pay_ref[NSTATE:, :] = split_decay(runs_ref[rows // CHUNK])
    tb_ref[...] = tb_s[...].astype(bf16)
    ta_ref[...] = ta_s[...].astype(bf16)
    tg_ref[...] = tg_s[...].astype(bf16)
    for ref in (pay_ref, tb_ref, ta_ref, tg_ref, d_lat_ref, runs_ref):
        send(ref)


def middle_call(
    seq, ids, lens, place, flags, begun, tokens, cotangent, nrm, lat, act, cum, other, before, y, wg, in_b, wo, out_a,
    out_b, skip, gain, expand,
):
    rows = act.shape[0]
    outs = [
        ((rows, DM), bf16),
        ((rows, INNER), bf16),
        ((rows, INNER), bf16),
        ((rows, LANES), f32),
        ((NSTATE + RIM, INNER), bf16),
        ((RANK, DM), bf16),
        ((RANK, INNER), bf16),
        ((NSTATE, INNER), bf16),
        ((rows // CHUNK + 1, 1, INNER), f32),
        ((RANK, rows), f32),
        ((RANK, INNER), bf16),
    ]
    wide = pltpu.VMEM((rows, INNER), f32)
    scratch = [
        wide, wide, wide, pltpu.VMEM((rows, INNER), bf16), wide, wide, wide, pltpu.VMEM((NSTATE, INNER), f32),
        pltpu.VMEM((RANK, DM), f32), pltpu.VMEM((RANK, INNER), f32), pltpu.VMEM((RANK, INNER), f32),
    ]
    operands = [
        of_sequence(nrm, seq), of_sequence(lat, seq), of_adapter(in_b, seq, 0, INNER), wg,
        of_sequence(cotangent, seq), of_adapter(out_b, seq), of_adapter(out_a, seq), wo, view(other), view(before),
        view(cum), view(expand), view(act), view(y), view(skip), view(gain), of_sequence(tokens, seq),
    ]
    kernel = functools.partial(middle_kernel, seq=seq)
    shared = (tokens.shape[0], seq, begun)
    return streamed(kernel, "middle", [ids, lens, flags, place], operands, outs, scratch, 15, shared)


def scan_back_kernel(
    flags, other_ref, before_ref, before_other_ref, enter_ref, runs_ref, dt_ref, cum_ref, skip_ref, expand_ref, hc_ref, act_ref, dy_ref,
    dact_ref, rowt_ref, sig_ref, rate_ref, cw_ref, lat_ref, nrm_ref, bx_ref, d_lat_gate_ref,
    dx_ref, draw_ref, tail_ref, head_ref, d_lat_ref, tb_ref, ta_ref,
    grad_s, pre_s, next_s, *, ready, ready_last, send,
):
    rows = act_ref.shape[0]
    chunks = rows // CHUNK
    keep = causal(CHUNK)
    upper = causal(CHUNK).astype(f32).T
    row = lax.broadcasted_iota(jnp.int32, (CHUNK, LANES), 0)
    lane = lax.broadcasted_iota(jnp.int32, (CHUNK, LANES), 1)
    at_b = slice(INNER, INNER + NSTATE)
    at_c = slice(INNER + NSTATE, CONV_CH)
    ready(other_ref, before_ref, before_other_ref)
    for t in range(INNER // TILE):
        cols = slice(t * TILE, (t + 1) * TILE)
        grad_s[:, cols] = state_in_two(flags, other_ref, before_ref, before_other_ref, cols)
    ready(enter_ref, runs_ref)
    ready_last(hc_ref)
    next_s[...] = hc_ref[chunks].astype(f32) + runs_ref[chunks] * enter_ref[...].astype(f32)
    pre_s[:, rows : rows + 8, :] = jnp.zeros((CONV_CH // LANES, 8, LANES), f32)
    ready(dt_ref, cum_ref, skip_ref, expand_ref)
    for c in reversed(range(chunks)):
        r = slice(c * CHUNK, (c + 1) * CHUNK)
        ready_last(hc_ref, act_ref, dy_ref, dact_ref)
        b = act_ref[r, at_b]
        cc = act_ref[r, at_c]
        c_t = turned(cc)
        masked = jnp.where(keep, dot_t(cc, b), 0.0)
        dt = dt_ref[r, :]
        cum = cum_ref[r, :]
        cum_t = jnp.transpose(cum)
        masked_t = jnp.transpose(masked)
        d_scores = jnp.zeros((CHUNK, CHUNK), f32)
        d_b = jnp.zeros((CHUNK, NSTATE), f32)
        d_c = jnp.zeros((CHUNK, NSTATE), f32)
        col = jnp.zeros((CHUNK + RIM, LANES), f32)
        for t in range(INNER // LANES):
            cols = slice(t * LANES, (t + 1) * LANES)
            heads = (2 * t, 2 * t + 1)
            cums = beside(*(column(cum, head) for head in heads))
            dts = beside(*(column(dt, head) for head in heads))
            ec = jnp.exp(cums)
            w = jnp.exp(cums[CHUNK - 1 : CHUNK] - cums)
            x = act_ref[r, cols].astype(f32)
            xd = (x * dts).astype(bf16)
            dy = dy_ref[r, cols]
            dye = (dy.astype(f32) * ec).astype(bf16)
            grad = grad_s[:, cols]
            grad_low = grad.astype(bf16)
            state = hc_ref[c, :, cols].astype(f32) + runs_ref[c, :, cols] * enter_ref[:, cols].astype(f32)
            far = dot(b, grad_low) * w
            xw = (xd.astype(f32) * w).astype(bf16)
            d_b = d_b + dot_t(xw, grad_low)
            d_c = d_c + dot_t(dye, state.astype(bf16))
            end = split_decay(jnp.sum(grad * next_s[:, cols], axis=0, keepdims=True))
            next_s[:, cols] = state
            grad_s[:, cols] = grad * ec[CHUNK - 1 : CHUNK] + dot(c_t, dye)
            w1, w2 = (decays(cum, cum_t, head) for head in heads)
            back = jnp.concatenate([w1 * masked_t, w2 * masked_t], axis=1).astype(bf16)
            d_both = dot_t(dy, split_heads(xd))
            d_scores = d_scores + w1 * d_both[:, :CHUNK] + w2 * d_both[:, CHUNK:]
            d_xd = dot(back, split_heads(dy)) + far
            sums = jnp.concatenate([(d_xd * x).astype(bf16), end], axis=0)
            col = col + dot_t(sums, expand_ref[:, cols])
            d_x = d_xd * dts + skip_ref[:, cols] * dy.astype(f32)
            pre_s[t, r, :] = d_x * dact_ref[r, cols].astype(f32)
        ends = col[CHUNK : CHUNK + 1] + col[CHUNK + 1 : CHUNK + 2]
        col = col[:CHUNK]
        d_low = jnp.where(keep, d_scores, 0.0)
        d_c = d_c + dot(d_low.astype(bf16), b)
        d_b = d_b + dot(turned(d_low), cc)
        pre_s[INNER // LANES, r, :] = d_b * dact_ref[r, at_b].astype(f32)
        pre_s[INNER // LANES + 1, r, :] = d_c * dact_ref[r, at_c].astype(f32)
        if c == chunks - 1:
            ready(rowt_ref, sig_ref, rate_ref, cw_ref)
        d_cum = rowt_ref[r, :] - dt * col
        d_cum = d_cum + jnp.where(row == CHUNK - 1, ends, 0.0)
        d_log = dot_precise(upper, d_cum)
        d_raw = (d_log * rate_ref[...] + col) * sig_ref[r, :]
        draw_ref[r, :] = jnp.where(lane < HEADS, d_raw, 0.0).astype(bf16)

        strip = 64
        for t in range(CONV_CH // LANES):
            cols = slice(t * LANES, (t + 1) * LANES)
            weights = [cw_ref[j : j + 1, cols] for j in range(4)]
            for at in range(c * CHUNK, (c + 1) * CHUNK, strip):
                total = weights[3] * pre_s[t, at : at + strip, :]
                for j in range(3):
                    total = total + weights[j] * pre_s[t, at + 3 - j : at + 3 - j + strip, :]
                dx_ref[at : at + strip, cols] = total.astype(bf16)
                if at + strip == rows:
                    tail_ref[:, cols] = total[strip - RIM :, :]
        send(dx_ref, pl.ds(c * CHUNK, CHUNK))
        if c == chunks - 1:
            send(tail_ref)
    for t in range(CONV_CH // LANES):
        head_ref[:, t * LANES : (t + 1) * LANES] = pre_s[t, 0:RIM, :].astype(bf16)
    send(head_ref)
    send(draw_ref)

    ready(lat_ref, nrm_ref, bx_ref, d_lat_gate_ref)
    d_x = dx_ref[:, :INNER]
    d_lat_t = (d_lat_gate_ref[...] + dot_t(bx_ref[...], d_x)).astype(bf16)
    d_lat_ref[...] = turned(d_lat_t)
    send(d_lat_ref)
    sure = lax.broadcasted_iota(jnp.int32, (RANK, rows), 1) < rows - RIM
    lat_t = jnp.transpose(lat_ref[...].astype(f32))
    tb_ref[...] = dot(jnp.where(sure, lat_t, 0.0).astype(bf16), d_x)
    ta_ref[...] = dot(jnp.where(sure, d_lat_t.astype(f32), 0.0).astype(bf16), nrm_ref[...])
    send(tb_ref)
    send(ta_ref)


def scan_back_call(
    seq, ids, flags, other, before, before_other, act, dact, dt, cum, sig, rowt, dy, hc, enter, runs, lat, nrm, in_b, d_lat_gate, skip,
    rate, conv_w, expand,
):
    rows = act.shape[0]
    chunks = rows // CHUNK
    outs = [
        ((rows, CONV_CH), bf16),
        ((rows, LANES), bf16),
        ((RIM, CONV_CH), f32),
        ((RIM, CONV_CH), bf16),
        ((rows, RANK), bf16),
        ((RANK, INNER), f32),
        ((RANK, DM), f32),
    ]
    scratch = [
        pltpu.VMEM((NSTATE, INNER), f32),
        pltpu.VMEM((CONV_CH // LANES, rows + 8, LANES), f32),
        pltpu.VMEM((NSTATE, INNER), f32),
    ]
    operands = [view(a) for a in (other, before, before_other, enter, runs, dt, cum, skip, expand)]
    operands += [in_parts(hc, chunks + 1), in_parts(act, chunks), in_parts(dy, chunks), in_parts(dact, chunks)]
    operands += [later(view(a)) for a in (rowt, sig, rate, conv_w)]
    operands += [later(of_sequence(lat, seq)), later(of_sequence(nrm, seq))]
    operands += [later(of_adapter(in_b, seq, INNER, INNER)), later(view(d_lat_gate))]

    def kernel(ids, flags, *refs, **calls):
        scan_back_kernel(flags, *refs, **calls)

    return streamed(kernel, "scan_back", [ids, flags], operands, outs, scratch, 19)


def terms_kernel(*refs, seqs, owners, ready, send):
    refs = list(refs)[1:]
    per = 11
    ins, outs = refs[: 1 + per * seqs], refs[1 + per * seqs :]
    cw_ref, sent_ref = ins[0], outs[-1]
    ready(cw_ref)
    row = lax.broadcasted_iota(jnp.int32, (RIM, CONV_CH), 0)
    for s in range(seqs):
        tail_ref, next_ref, bx_ref, gate_ref, lat_ref, nrm_ref, tb_ref, ta_ref, tg_ref, ob_ref, oa_ref = ins[
            1 + per * s : 1 + per * (s + 1)
        ]
        last_ref, d_lat_ref = outs[2 * s : 2 * s + 2]
        ready(*ins[1 + per * s : 1 + per * (s + 1)])
        later_rows = next_ref[...].astype(f32)
        total = tail_ref[...]
        for back in range(1, 4):
            term = jnp.zeros((1, CONV_CH), f32)
            for j in range(0, 4 - back):
                term = term + cw_ref[j : j + 1, :] * later_rows[3 - back - j : 4 - back - j, :]
            total = total + jnp.where(row == RIM - back, term, 0.0)
        last = total.astype(bf16)
        last_ref[...] = last
        d_x = last[:, :INNER]
        gate_rows = jnp.transpose(gate_ref[...])[LANES - RIM :, :]
        d_lat = (gate_rows + dot_t(d_x, bx_ref[...])).astype(bf16)
        d_lat_ref[...] = d_lat
        send(last_ref)
        send(d_lat_ref)
        in_b = (tb_ref[...] + dot(turned(lat_ref[...]), d_x)).astype(bf16)
        in_a = (ta_ref[...] + dot(turned(d_lat), nrm_ref[...])).astype(bf16)
        both = jnp.concatenate([tg_ref[...], in_b], axis=1)
        kinds = [in_a, both, oa_ref[...], ob_ref[...]]
        for d in range(owners):
            pieces = []
            for kind in kinds:
                width = kind.shape[1] // owners
                pieces.append(kind[:, d * width : (d + 1) * width])
            sent_ref[d, s] = jnp.concatenate(pieces, axis=1)
    send(sent_ref)


def terms_call(ids, conv_w, items, lat, nrm, in_b, owners):
    seqs, rows, _ = nrm.shape
    last_columns = lambda scalars, ref: ref.at[:, pl.ds(rows - LANES, LANES)]
    operands = [view(conv_w)]
    outs = []
    for s, (tail, following, d_lat_gate, tb, ta, tg, ob, oa) in enumerate(items):
        of_last = lambda scalars, ref, s=s: ref.at[s, pl.ds(rows - RIM, RIM)]
        operands += [
            view(tail), view(following), of_adapter(in_b, s, INNER, INNER), view(d_lat_gate, last_columns, (RANK, LANES)),
            view(lat, of_last, (RIM, RANK)), view(nrm, of_last, (RIM, DM)), view(tb), view(ta), view(tg), view(ob),
            view(oa),
        ]
        outs += [((RIM, CONV_CH), bf16), ((RIM, RANK), bf16)]
    width = (2 * DM + ZX + INNER) // owners
    outs.append(((owners, seqs, RANK, width), bf16))
    kernel = functools.partial(terms_kernel, seqs=seqs, owners=owners)
    return streamed(kernel, "terms", [ids], operands, outs, [], 4)


def input_back_kernel(
    ids, lens, place, dg_ref, wg_ref, last_ref, dx_ref, early_ref, draw_ref, d_lat_ref, d_lat_last_ref, a_ref,
    gain_ref, x_ref, cot_ref, out_ref, dn_s, *, seq, ready, send,
):
    rows = dx_ref.shape[0]
    block = rows // 2
    ready(dg_ref, wg_ref)
    dn_s[...] = dot_t(dg_ref[...], wg_ref[...])
    ready(last_ref, dx_ref, early_ref, draw_ref, d_lat_ref, d_lat_last_ref, a_ref)
    dx_ref[rows - RIM :, :] = last_ref[...]
    d_lat_ref[rows - RIM :, :] = d_lat_last_ref[...]
    ready(gain_ref, x_ref, cot_ref)
    strip = 32
    for k in range(0, rows, block):
        b = slice(k, k + block)
        more = dot_t(dx_ref[b, :], early_ref[:, :CONV_CH]) + dot_t(draw_ref[b, :], early_ref[:, CONV_CH:])
        dn_s[b, :] += more + dot(d_lat_ref[b, :], a_ref[...])
        for i in range(k, k + block, strip):
            r = slice(i, i + strip)
            x = x_ref[r, :].astype(f32)
            root = lax.rsqrt(jnp.mean(x * x, -1, keepdims=True) + epsilon)
            dn = dn_s[r, :] * gain_ref[...]
            back = jnp.mean(dn * x, -1, keepdims=True) * (root * root * root)
            position = i + lax.broadcasted_iota(jnp.int32, (strip, 1), 0)
            kept = jnp.where(position < lens[seq], cot_ref[r, :].astype(f32), 0.0)
            out_ref[r, :] = dn * root - x * back + kept
        send(out_ref, pl.ds(k, block))


def input_back_call(seq, ids, lens, place, begun, tokens, cotangent, dg, last, dx, draw, d_lat, d_lat_last, wg, early, in_a, gain):
    rows = dx.shape[0]
    outs = [((rows, DM), f32)]
    operands = [view(dg), wg, view(last), view(dx), early, view(draw), view(d_lat), view(d_lat_last)]
    operands += [of_adapter(in_a, seq), view(gain), of_sequence(tokens, seq), of_sequence(cotangent, seq)]
    kernel = functools.partial(input_back_kernel, seq=seq)
    scratch = [pltpu.VMEM((rows, DM), f32)]
    shared = (tokens.shape[0], seq, begun)
    return streamed(kernel, "input_back", [ids, lens, place], operands, outs, scratch, 9, shared)[0]


def shifted(value, axis, steps):
    count = lax.axis_size(axis)
    pairs = [(i, i + steps) for i in range(count) if 0 <= i + steps < count]
    return lax.ppermute(value, axis, pairs)


def swapped(value, axis, bit):
    return lax.ppermute(value, axis, [(i, i ^ bit) for i in range(lax.axis_size(axis))])


def after(value, other):
    return lax.optimization_barrier((value, other))[0]


def my_half(shard, core, half):
    return lax.dynamic_slice_in_dim(shard, core * half, half, 0)


def gathered_early(meanwhile, shard):
    owners = lax.axis_size("dp")
    rows, width = shard.shape
    half = rows // 2
    shapes = [(rows * owners, CONV_CH), (rows * owners, LANES)]
    if half % 16 or owners % 2:
        full = lax.all_gather(shard, "dp", axis=0, tiled=True)
        return view(full[:, :CONV_CH]), view(full[:, CONV_CH:]), view(full), None
    core = lax.axis_index("ctx") % 2
    own = {0: my_half(shard, core, half)}
    for k in range(2, owners, 2):
        own[k] = swapped(own[0], "dp", k)
    own[1] = swapped(own[0], "dp", 1)
    for k in range(2, owners, 2):
        waits = (own[min(3, k - 1)], meanwhile) if k == owners - 2 else own[1]
        own[k + 1] = swapped(after(own[k], waits), "dp", 1)
    pieces = [own[k] for k in range(owners)] + [swapped(own[k], "ctx", 1) for k in range(owners)]

    def copies(scalars, refs, to, columns):
        place = scalars[-1]
        pairs = []
        for n, piece in enumerate(refs):
            side = place[1] if n < owners else 1 - place[1]
            at = pl.multiple_of((place[0] ^ (n % owners)) * rows + side * half, 16)
            pairs.append((piece.at[:, columns], to.at[pl.ds(at, half)]))
        return pairs

    main = functools.partial(copies, columns=pl.ds(0, CONV_CH))
    rest = functools.partial(copies, columns=pl.ds(CONV_CH, LANES))
    all_columns = functools.partial(copies, columns=pl.ds(0, width))
    arrived = (tuple(own[k] for k in range(2, owners, 2)), own[owners - 1])
    both = Operand(pieces, (rows * owners, width), all_columns)
    return Operand(pieces, shapes[0], main), Operand(pieces, shapes[1], rest), both, arrived


def gathered_late(gate, out, arrived, fronts, scans, befores):
    owners = lax.axis_size("dp")
    rows = gate.shape[0]
    half = rows // 2
    if arrived is None:
        return (
            view(lax.all_gather(gate, "dp", axis=0, tiled=True)),
            view(lax.all_gather(out, "dp", axis=0, tiled=True)),
        )
    core = lax.axis_index("ctx") % 2
    mine = my_half(jnp.concatenate([gate, out[:rows], out[rows:]], axis=1), core, half)
    own = {0: mine}
    for k in range(2, owners, 2):
        own[k] = swapped(after(mine, arrived[0][0] if k == 2 else arrived[0]), "dp", k)
    for k in range(0, owners, 2):
        waits = arrived[1] if k <= 2 else fronts[-1][5]
        own[k + 1] = swapped(after(own[k], waits), "dp", 1)
    pieces = [own[k] for k in range(owners)]
    hold = (scans[-1][0], befores[0])
    pieces += [swapped(after(own[k], scans[0][0] if k < 4 else hold), "ctx", 1) for k in range(owners)]

    def placed(scalars, refs):
        place = scalars[-1]
        for n, piece in enumerate(refs):
            side = place[1] if n < owners else 1 - place[1]
            yield piece, place[0] ^ (n % owners), side * half

    def gate_copies(scalars, refs, to):
        pairs = []
        for piece, owner, start in placed(scalars, refs):
            at = pl.multiple_of(owner * rows + start, 16)
            pairs.append((piece.at[:, pl.ds(0, INNER)], to.at[pl.ds(at, half)]))
        return pairs

    def out_copies(scalars, refs, to):
        pairs = []
        for piece, owner, start in placed(scalars, refs):
            for k in range(2):
                at = pl.multiple_of((2 * owner + k) * rows + start, 16)
                pairs.append((piece.at[:, pl.ds(INNER + k * DM, DM)], to.at[pl.ds(at, half)]))
        return pairs

    return (
        Operand(pieces, (rows * owners, INNER), gate_copies),
        Operand(pieces, (2 * rows * owners, DM), out_copies),
    )


def join_kernel(swap, one_ref, two_ref, out_ref, *, ready, send):
    ready(one_ref, two_ref)
    join_payloads(swap[0], one_ref, two_ref, out_ref)
    send(out_ref)


def joined(one, two, swap):
    return streamed(join_kernel, "join", [swap], [view(one), view(two)], [(one.shape, bf16)], [], 1)[0]


def state_in_two(flags, other_ref, far_ref, far_other_ref, cols):
    far, far_other, other = (ref[0:NSTATE, cols].astype(f32) for ref in (far_ref, far_other_ref, other_ref))
    behind = decay_of(far_ref, cols) * far_other + far
    ahead = decay_of(far_other_ref, cols) * far + far_other
    before = jnp.where(flags[1] == 1, behind, ahead)
    return jnp.where(flags[0] == 1, decay_of(other_ref, cols) * before + other, before)


def from_before(both, reverse):
    chips = lax.axis_size("ctx") // 2
    sign = -1 if reverse else 1
    in_order = jnp.zeros((1,), jnp.int32)
    before = shifted(both, "ctx", 2 * sign)
    step, run = 1, both
    while 2 * step < chips:
        run = joined(before, both, in_order) if step == 1 else joined(far, run, in_order)
        far = shifted(run, "ctx", 4 * step * sign)
        before = joined(far, before, in_order)
        step *= 2
    return before


def shards(
    tokens, cotangent, lengths, adapter_ids, norm_gain, w_in, conv_weight, conv_bias, dt_bias, a_log,
    skip_scale, inner_gain, w_out, in_a, in_b, out_a, out_b,
):
    seqs, slots, _ = tokens.shape
    owners = lax.axis_size("dp")
    ids = adapter_ids
    lens = jnp.clip(lengths - lax.axis_index("ctx") * slots, 0, slots).astype(jnp.int32)

    def grouped(row):
        padded = jnp.pad(row.reshape(-1, HEADS), ((0, 0), (0, GROUP - HEADS)))
        return jnp.tile(padded, (1, LANES // GROUP))

    rate = grouped(-jnp.exp(a_log))
    dtb = grouped(dt_bias)
    lane = jnp.arange(LANES)[:, None]
    head = jnp.arange(INNER)[None, :] // HDIM
    expand = ((lane % GROUP == head) & (lane < 3 * GROUP)).astype(bf16)
    skip = jnp.repeat(skip_scale, HDIM)[None, :]
    gain = inner_gain[None, :]
    n_gain = norm_gain[None, :]
    conv_b = conv_bias[None, :]

    marks = jnp.broadcast_to(ids.astype(bf16)[None, :], (w_in.shape[0], seqs))
    marks = jnp.pad(marks, ((0, 0), (0, GROUP - HEADS - seqs)))
    steps = jnp.concatenate([w_in[:, INNER + CONV_CH :], marks], axis=1)
    in_a, out_a = jnp.swapaxes(in_a, 1, 2), jnp.swapaxes(out_a, 1, 2)
    rim = shifted(tokens[:, slots - RIM :], "ctx", 1)
    nrm, nrim, lat, lrim = norm_call(ids, tokens, rim, n_gain, in_a)
    wx, wdt, early_all, arrived = gathered_early(
        nrm,
        jnp.concatenate([w_in[:, INNER : INNER + CONV_CH]] + [steps] * (LANES // GROUP), axis=1)
    )

    core = lax.axis_index("ctx") % 2
    place = jnp.stack([lax.axis_index("dp"), core]).astype(jnp.int32)
    late = core.reshape(1).astype(jnp.int32)
    early = 1 - late
    front = functools.partial(
        front_call, in_b=in_b, wx=wx, wdt=wdt, conv_w=conv_weight, conv_b=conv_b, dtb=dtb, rate=rate, expand=expand
    )
    nrm, (skip, gain, lens, late, early) = lax.optimization_barrier((nrm, (skip, gain, lens, late, early)))
    chips = lax.axis_size("ctx") // 2
    flags_back = jnp.concatenate([early, early if chips == 2 else jnp.ones_like(early)])
    fronts, others = [], []
    for s in range(seqs):
        ready = nrm if s == 0 else after(nrm, fronts[-1][5])
        fronts.append(front(s, ids, place, ready, nrim, lat, lrim))
        others.append(swapped(fronts[s][5], "ctx", 1))
    scans, befores = [], []
    for s in range(seqs):
        act, _, dt, cum, _, own, _ = fronts[s]
        ready = after(act, fronts[-1][5]) if s == 0 else after(act, scans[-1][0])
        scans.append(scan_call(late, own, others[s], ready, dt, cum))
        befores.append(from_before(scans[s][2], False))
    full_gate, full_out = gathered_late(w_in[:, :INNER], w_out, arrived, fronts, scans, befores)
    middles, other_grads, later_grads = [], [], []
    for s in range(seqs):
        act, _, _, cum, _, _, _ = fronts[s]
        ready = after(nrm, scans[-1][0] if s == 0 else middles[-1][4])
        middles.append(
            middle_call(
                s, ids, lens, place, late, middles[-1][0] if s else None, tokens, cotangent, ready, lat, act, cum,
                others[s], befores[s], scans[s][0], full_gate, in_b, full_out, out_a, out_b, skip, gain, expand,
            )
        )
        payload = after(middles[s][4], later_grads[-1] if s and chips > 2 else befores[-1])
        other_grads.append(swapped(payload, "ctx", 1))
        if chips == 2:
            later_grads.append(shifted(payload, "ctx", -2))
        else:
            later_grads.append(from_before(joined(payload, other_grads[s], early), True))
    backs, nexts = [], []
    for s in range(seqs):
        act, dact, dt, cum, sig, _, _ = fronts[s]
        _, dy, _, rowt, _, _, _, enter, runs, d_lat_gate, _ = middles[s]
        hold = middles[-1][4] if s == 0 else backs[-1][3]
        ready = after(act, hold)
        later_other = swapped(after(later_grads[s], hold), "ctx", 1) if chips == 2 else jnp.zeros_like(later_grads[s])
        backs.append(
            scan_back_call(
                s, ids, flags_back, other_grads[s], later_grads[s], later_other, ready, dact, dt, cum, sig, rowt, dy, scans[s][1], enter,
                runs, lat, nrm, in_b, d_lat_gate, skip, rate, conv_weight, expand,
            )
        )
        nexts.append(shifted(backs[s][3], "ctx", -1))
    items = [
        (back[2], following, mid[9], back[5], back[6], mid[10], mid[5], mid[6])
        for back, following, mid in zip(backs, nexts, middles)
    ]
    *lasts, sent = terms_call(ids, conv_weight, items, lat, nrm, in_b, owners)

    widths = [width // owners for width in (DM, ZX, INNER, DM)]
    got = lax.all_to_all(sent, "dp", 0, 0)
    held = after(tokens, sent)
    input_grad = None
    for s in range(seqs):
        if s == 1:
            got = after(got, input_grad)
        input_grad = input_back_call(
            s, ids, lens, place, input_grad, held, cotangent, middles[s][2], lasts[2 * s], backs[s][0], backs[s][1],
            backs[s][4], lasts[2 * s + 1], full_gate, early_all, in_a, n_gain,
        )
    every = fronts[0][6][:, HEADS : HEADS + seqs].reshape(1, -1)
    chosen = (every == jnp.arange(ADAPT, dtype=f32)[:, None]).astype(f32)
    flat = got.reshape(owners * seqs, -1).astype(f32)
    mine = jnp.sum(chosen[:, :, None] * flat[None], axis=1)
    if lax.axis_size("ctx") == 4:
        low = mine.astype(bf16)
        mine = mine + sum(swapped(low, "ctx", bits).astype(f32) for bits in (1, 2, 3))
    else:
        bit = 1
        while bit < lax.axis_size("ctx"):
            mine = mine + swapped(mine.astype(bf16), "ctx", bit).astype(f32)
            bit *= 2
    mine = mine.reshape(ADAPT, RANK, -1)
    cuts = [sum(widths[:k]) for k in range(5)]
    g_ia, g_ib, g_oa, g_ob = (mine[:, :, cuts[k] : cuts[k + 1]] for k in range(4))
    return (
        middles[-1][0],
        input_grad,
        jnp.swapaxes(g_ia, 1, 2),
        g_ib,
        jnp.swapaxes(g_oa, 1, 2),
        g_ob,
    )


def solution(mesh):
    split = P("dp", "ctx", None)
    return jax.shard_map(
        shards,
        mesh=mesh,
        in_specs=(
            split, split, P("dp"), P("dp"), P(), P("dp", None), P(), P(), P(), P(), P(), P(),
            P("dp", None), P(), P(), P(), P(),
        ),
        out_specs=(
            split, split, P(None, "dp", None), P(None, None, "dp"), P(None, "dp", None), P(None, None, "dp"),
        ),
        check_vma=False,
    )
```

```python
import functools

import jax
import jax.numpy as jnp
from jax import lax
from jax.experimental import pallas as pl
from jax.experimental.pallas import tpu as pltpu
from jax.sharding import PartitionSpec as P

HEADS = 24
HDIM = 64
NSTATE = 128
INNER = 1536
CONV_CH = 1792
ZX = 3072
DM = 768
RANK = 16
ADAPT = 8
CHUNK = 128
TILE = 256
RIM = 16
GROUP = 32
LANES = 128
VMEM_LIMIT = 60 * 1024 * 1024

epsilon = 1e-05
bf16 = jnp.bfloat16
f32 = jnp.float32


def dot(left, right):
    return jnp.dot(left, right, preferred_element_type=f32)


def dot_t(left, right):
    return lax.dot_general(
        left, right, (((1,), (1,)), ((), ())), preferred_element_type=f32
    )


def dot_precise(left, right):
    return jnp.dot(
        left, right, preferred_element_type=f32, precision=lax.Precision.HIGHEST
    )


def parts_of(v):
    lane = lax.broadcasted_iota(jnp.int32, v.shape, 1)
    high = v.astype(bf16).astype(f32)
    rest = v - high
    middle = rest.astype(bf16).astype(f32)
    kept = jnp.where(lane < GROUP, high, jnp.where(lane < 2 * GROUP, middle, rest - middle))
    return jnp.where(lane < 3 * GROUP, kept, 0.0).astype(bf16)


def causal(rows):
    t = lax.broadcasted_iota(jnp.int32, (rows, rows), 0)
    s = lax.broadcasted_iota(jnp.int32, (rows, rows), 1)
    return t >= s


def sigmoid(v):
    return 0.5 * jnp.tanh(0.5 * v) + 0.5


def turned(v):
    return jnp.transpose(v.astype(f32)).astype(bf16)


class Operand:
    def __init__(self, arrays, shape, copies, parts=1, late=False):
        self.arrays, self.shape, self.copies, self.parts = list(arrays), tuple(shape), copies, parts
        self.late = late


def view(array, pick=None, shape=None):
    pick = pick or (lambda scalars, ref: ref)
    return Operand([array], shape or array.shape, lambda scalars, refs, to: [(pick(scalars, refs[0]), to)])


def later(operand):
    return Operand(operand.arrays, operand.shape, operand.copies, operand.parts, True)


def made(array):
    return Operand([array], array.shape, lambda scalars, refs, to: [])


def head_spread(shape):
    group = lax.broadcasted_iota(jnp.int32, shape, 0)
    column = lax.broadcasted_iota(jnp.int32, shape, 1)
    hit = jnp.logical_and((group & (GROUP - 1)) == (column >> 6), group < 3 * GROUP)
    return jnp.where(hit, 1.0, 0.0).astype(bf16)


def in_parts(array, parts):
    def copies(scalars, refs, to):
        size = array.shape[0] // parts
        return [(refs[0].at[pl.ds(p * size, size)], to.at[pl.ds(p * size, size)]) for p in range(parts)]

    return Operand([array], array.shape, copies, parts)


def streamed(kernel, name, scalars, operands, outs, scratch, micros, shared=None):
    arrays = [array for operand in operands for array in operand.arrays]
    n_scalar, n_array, n_in, n_out = len(scalars), len(arrays), len(operands), len(outs)
    kinds = [operand.arrays[0].dtype for operand in operands]
    slots, slot, begun = shared or (None, None, None)
    parted_in = any(operand.parts > 1 for operand in operands)
    n_begun = 0 if begun is None else 1

    def body(*refs):
        refs = list(refs)
        take = lambda n: [refs.pop(0) for _ in range(n)]
        smem, sources, _, targets, ins, results = (
            take(n) for n in (n_scalar, n_array, n_begun, n_out, n_in, n_out)
        )
        if shared:
            targets[0] = targets[0].at[slot]
        in_sems, out_sems = refs.pop(-2), refs.pop(-1)
        waiting, parted, late, fill, first_sem = {}, [], [], [], 0
        for k, operand in enumerate(operands):
            mine = [sources.pop(0) for _ in operand.arrays]
            copies = operand.copies(smem, mine, ins[k])
            if operand.parts == 1:
                sem = in_sems.at[first_sem]
                for source, target in copies:
                    copy = pltpu.make_async_copy(source, target, sem)
                    if operand.late:
                        late.append(copy)
                    else:
                        copy.start()
                waiting[id(ins[k])] = [pltpu.make_async_copy(ins[k], ins[k], sem)] if copies else []
                if not copies:
                    fill.append(ins[k])
            else:
                made = [
                    pltpu.make_async_copy(source, target, in_sems.at[first_sem + p])
                    for p, (source, target) in enumerate(copies)
                ]
                waiting[id(ins[k])] = made
                parted.append(list(made))
            first_sem += operand.parts
        while any(parted):
            for made in parted:
                if made:
                    made.pop().start()
        for copy in late:
            copy.start()
        for ref in fill:
            ref[...] = head_spread(ref.shape)

        def ready(*wanted):
            for ref in wanted:
                for copy in waiting.pop(id(ref), ()):
                    copy.wait()

        def ready_last(*wanted):
            for ref in wanted:
                waiting[id(ref)].pop().wait()

        sent = []

        def send(ref, *at):
            k = [id(result) for result in results].index(id(ref))
            if k not in sent:
                sent.append(k)
            source, target = (results[k].at[at], targets[k].at[at]) if at else (results[k], targets[k])
            pltpu.make_async_copy(source, target, out_sems.at[k]).start()

        more = {"ready_last": ready_last} if parted_in else {}
        kernel(*smem, *ins, *results, *refs, ready=ready, send=send, **more)
        ready(*ins)
        for k in sent:
            pltpu.make_async_copy(results[k], targets[k], out_sems.at[k]).wait()

    anywhere = pl.BlockSpec(memory_space=pl.ANY)
    full = [((slots,) + shape if shared and k == 0 else shape, kind) for k, (shape, kind) in enumerate(outs)]
    return pl.pallas_call(
        body,
        in_specs=[pl.BlockSpec(memory_space=pltpu.SMEM)] * n_scalar + [anywhere] * (n_array + n_begun),
        out_specs=[anywhere] * n_out,
        out_shape=[jax.ShapeDtypeStruct(shape, kind) for shape, kind in full],
        scratch_shapes=[pltpu.VMEM(operand.shape, kind) for operand, kind in zip(operands, kinds)]
        + [pltpu.VMEM(shape, kind) for shape, kind in outs]
        + scratch
        + [pltpu.SemaphoreType.DMA((sum(operand.parts for operand in operands),)), pltpu.SemaphoreType.DMA((n_out,))],
        input_output_aliases={n_scalar + n_array: 0} if n_begun else {},
        compiler_params=pltpu.CompilerParams(vmem_limit_bytes=VMEM_LIMIT),
        cost_estimate=pl.CostEstimate(flops=micros * 400000000, bytes_accessed=1000000, transcendentals=0),
        name=name,
    )(*scalars, *arrays, *([begun] if n_begun else []))


def of_sequence(array, seq):
    return view(array, lambda scalars, ref: ref.at[seq], array.shape[1:])


def of_adapter(array, seq, start=0, width=None):
    width = width or array.shape[2]
    pick = lambda scalars, ref: ref.at[scalars[0][seq], :, pl.ds(start, width)]
    return view(array, pick, (array.shape[1], width))


def split_decay(decay):
    high = decay.astype(bf16).astype(f32)
    row = lax.broadcasted_iota(jnp.int32, (RIM, decay.shape[1]), 0)
    return jnp.where(row == 0, high, jnp.where(row == 1, decay - high, 0.0)).astype(bf16)


def decay_of(payload_ref, cols):
    rows = payload_ref[NSTATE:, cols].astype(f32)
    return rows[0:1] + rows[1:2]


def norm_kernel(
    ids, x0_ref, x1_ref, rim_ref, gain_ref, a0_ref, a1_ref, nrm_ref, nrim_ref, lat_ref, lrim_ref, *, ready, send
):
    def normed(x):
        x = x.astype(f32)
        mean = jnp.mean(x * x, -1, keepdims=True)
        return (x * lax.rsqrt(mean + epsilon) * gain_ref[...]).astype(bf16)

    strip = 64
    ready(gain_ref, rim_ref)
    for s, (x_ref, a_ref) in enumerate(((x0_ref, a0_ref), (x1_ref, a1_ref))):
        ready(x_ref, a_ref)
        for i in range(x_ref.shape[0] // strip):
            r = slice(i * strip, (i + 1) * strip)
            nrm_ref[s, r, :] = normed(x_ref[r, :])
        nrim_ref[s] = normed(rim_ref[s])
        lat_ref[s] = dot_t(nrm_ref[s], a_ref[...]).astype(bf16)
        lrim_ref[s] = dot_t(nrim_ref[s], a_ref[...]).astype(bf16)
    for ref in (nrm_ref, nrim_ref, lat_ref, lrim_ref):
        send(ref)


def norm_call(ids, tokens, rim, gain, in_a):
    seqs, rows, _ = tokens.shape
    outs = [
        ((seqs, rows, DM), bf16),
        ((seqs, RIM, DM), bf16),
        ((seqs, rows, RANK), bf16),
        ((seqs, RIM, RANK), bf16),
    ]
    operands = [
        of_sequence(tokens, 0), of_sequence(tokens, 1), view(rim), view(gain), of_adapter(in_a, 0), of_adapter(in_a, 1),
    ]
    return streamed(norm_kernel, "norm", [ids], operands, outs, [], 3)


def front_kernel(
    ids, place, nrm_s, lat_s, wdt_ref, dtb_ref, rate_ref, cw_ref, cb_ref, wx_ref, bx_ref,
    expand_ref, act_ref, dact_ref, dt_ref, cum_ref, sig_ref, pay_ref, marks_ref,
    xs, bt_s, w_s, *, ready, send,
):
    rows = nrm_s.shape[0] - RIM
    ready(nrm_s, lat_s)
    ready(wdt_ref, dtb_ref, rate_ref)
    owners = marks_ref.shape[0]
    for d in range(owners):
        at = d * (wdt_ref.shape[0] // owners)
        marks_ref[d : d + 1, :] = wdt_ref[at : at + 8, :].astype(f32)[0:1]
    send(marks_ref)
    raw = dot(nrm_s[RIM:, :], wdt_ref[...]) + dtb_ref[...]
    step = jnp.maximum(raw, 0.0) + jnp.log1p(jnp.exp(-jnp.abs(raw)))
    dt_ref[...] = step
    sig_ref[...] = jnp.exp(raw - step)
    logs = step * rate_ref[...]
    lower = causal(CHUNK).astype(f32)
    before = jnp.zeros((1, LANES), f32)
    whole = []
    for c in range(rows // CHUNK):
        r = slice(c * CHUNK, (c + 1) * CHUNK)
        cum = dot_precise(lower, logs[r])
        cum_ref[r, :] = cum
        whole.append(cum + before)
        before = before + cum[CHUNK - 1 : CHUNK]
    for c in range(rows // CHUNK):
        r = slice(c * CHUNK, (c + 1) * CHUNK)
        w_s[r, :] = parts_of(jnp.exp(before - whole[c]) * step[r])
    total = parts_of(jnp.broadcast_to(jnp.exp(before), (8, LANES)))
    for ref in (dt_ref, cum_ref, sig_ref):
        send(ref)
    ready(cw_ref, cb_ref, wx_ref, bx_ref, expand_ref)

    def activate(cols, base):
        weights = [cw_ref[j : j + 1, cols] for j in range(4)]
        bias = cb_ref[:, cols]
        low = base.astype(bf16).astype(f32)
        for k in range(2):
            xs[k] = low[:, k * LANES : (k + 1) * LANES]
        strip = 64
        for i in range(rows // strip):
            at = RIM + i * strip
            halves = []
            for k in range(2):
                lanes = slice(k * LANES, (k + 1) * LANES)
                pre = bias[:, lanes] + weights[0][:, lanes] * xs[k, at - 3 : at - 3 + strip, :]
                for j in range(1, 4):
                    pre = pre + weights[j][:, lanes] * xs[k, at - 3 + j : at - 3 + j + strip, :]
                halves.append(pre)
            pre = jnp.concatenate(halves, axis=1)
            gate = sigmoid(pre)
            act = pre * gate
            r = slice(i * strip, (i + 1) * strip)
            act_ref[r, cols] = act.astype(bf16)
            dact_ref[r, cols] = (gate + act * (1.0 - gate)).astype(bf16)
        send(act_ref, slice(None), cols)
        send(dact_ref, slice(None), cols)

    last = pl.ds(INNER, CONV_CH - INNER)
    activate(last, dot(nrm_s[...], wx_ref[:, last]))
    bt_s[...] = turned(act_ref[:, INNER : INNER + NSTATE])
    def tile_body(t, carry):
        cols = pl.ds(pl.multiple_of(t * TILE, TILE), TILE)
        activate(cols, dot(nrm_s[...], wx_ref[:, cols]) + dot(lat_s[...], bx_ref[:, cols]))
        scaled = (act_ref[:, cols].astype(f32) * dot(w_s[...], expand_ref[:, cols])).astype(bf16)
        pay_ref[0:NSTATE, cols] = dot(bt_s[...], scaled).astype(bf16)
        pay_ref[NSTATE:, cols] = split_decay(dot(total, expand_ref[:, cols])[0:1])
        return carry

    lax.fori_loop(0, INNER // TILE, tile_body, 0)
    send(pay_ref)


def front_call(seq, ids, place, nrm, nrim, lat, lrim, wx, wdt, in_b, conv_w, conv_b, dtb, rate, expand):
    rows = nrm.shape[1]
    owners = lax.axis_size("dp")
    outs = [
        ((rows, CONV_CH), bf16),
        ((rows, CONV_CH), bf16),
        ((rows, LANES), f32),
        ((rows, LANES), f32),
        ((rows, LANES), f32),
        ((NSTATE + RIM, INNER), bf16),
        ((owners, LANES), f32),
    ]
    scratch = [
        pltpu.VMEM((2, rows + RIM, LANES), f32),
        pltpu.VMEM((NSTATE, rows), bf16),
        pltpu.VMEM((rows, LANES), bf16),
    ]
    def rim_first(rim, rest):
        def copies(scalars, refs, to):
            return [(refs[0].at[seq], to.at[pl.ds(0, RIM)]), (refs[1].at[seq], to.at[pl.ds(RIM, rows)])]

        return Operand([rim, rest], (RIM + rows, rest.shape[2]), copies)

    operands = [rim_first(nrim, nrm), rim_first(lrim, lat)]
    operands += [wdt] + [view(a) for a in (dtb, rate, conv_w, conv_b)] + [wx]
    operands += [of_adapter(in_b, seq, INNER, INNER), made(expand)]
    return streamed(front_kernel, "front", [ids, place], operands, outs, scratch, 13)


def column(values, head):
    return jnp.broadcast_to(values[:, head : head + 1], values.shape)


def beside(one, two):
    lane = lax.broadcasted_iota(jnp.int32, one.shape, 1)
    return jnp.where(lane < HDIM, one, two)


def decays(cum, cum_t, head):
    gap = column(cum, head) - cum_t[head : head + 1, :]
    return jnp.exp(jnp.minimum(gap, -gap))


def split_heads(pair):
    lane = lax.broadcasted_iota(jnp.int32, pair.shape, 1)
    zero = jnp.zeros_like(pair)
    first = jnp.where(lane < HDIM, pair, zero)
    second = jnp.where(lane < HDIM, zero, pair)
    return jnp.concatenate([first, second], axis=0)


def join_payloads(swap, one_ref, two_ref, out_ref):
    for t in range(INNER // TILE):
        cols = slice(t * TILE, (t + 1) * TILE)
        d_one, d_two = decay_of(one_ref, cols), decay_of(two_ref, cols)
        one = one_ref[0:NSTATE, cols].astype(f32)
        two = two_ref[0:NSTATE, cols].astype(f32)
        state = jnp.where(swap == 1, d_one * two + one, d_two * one + two)
        out_ref[0:NSTATE, cols] = state.astype(bf16)
        out_ref[NSTATE:, cols] = split_decay(d_one * d_two)


def state_in(late, other_ref, before_ref, cols):
    before = before_ref[0:NSTATE, cols].astype(f32)
    joint = decay_of(other_ref, cols) * before + other_ref[0:NSTATE, cols].astype(f32)
    return jnp.where(late == 1, joint, before)


def scan_kernel(
    flags, own_ref, other_ref, act_ref, dt_ref, cum_ref, y_ref, hc_ref, both_ref, state_s, *, ready, send
):
    keep = causal(CHUNK)
    ready(own_ref, other_ref)
    join_payloads(flags[0], own_ref, other_ref, both_ref)
    send(both_ref)
    state_s[...] = jnp.zeros_like(state_s)
    ready(act_ref, dt_ref, cum_ref)

    def one_chunk(c, carry):
        r = pl.ds(pl.multiple_of(c * CHUNK, CHUNK), CHUNK)
        b = act_ref[r, INNER : INNER + NSTATE]
        cc = act_ref[r, INNER + NSTATE :]
        b_t = turned(b)
        masked = jnp.where(keep, dot_t(cc, b), 0.0)
        dt = dt_ref[r, :]
        cum = cum_ref[r, :]
        cum_t = jnp.transpose(cum)
        for t in range(INNER // LANES):
            cols = slice(t * LANES, (t + 1) * LANES)
            heads = (2 * t, 2 * t + 1)
            cums = beside(*(column(cum, head) for head in heads))
            steps = beside(*(column(dt, head) for head in heads))
            ec = jnp.exp(cums)
            xd = act_ref[r, cols].astype(f32) * steps
            xw = (xd * jnp.exp(cums[CHUNK - 1 : CHUNK] - cums)).astype(bf16)
            state = state_s[:, cols]
            low = state.astype(bf16)
            hc_ref[c, :, cols] = low
            far = dot(cc, low) * ec
            state_s[:, cols] = state * ec[CHUNK - 1 : CHUNK] + dot(b_t, xw)
            weights = [(decays(cum, cum_t, head) * masked).astype(bf16) for head in heads]
            near = dot(jnp.concatenate(weights, axis=1), split_heads(xd.astype(bf16)))
            y_ref[r, cols] = (near + far).astype(bf16)
        send(y_ref, r)
        send(hc_ref, pl.ds(c, 1))
        return carry

    chunks = act_ref.shape[0] // CHUNK
    lax.fori_loop(0, chunks, one_chunk, 0)
    hc_ref[chunks] = state_s[...].astype(bf16)
    send(hc_ref, pl.ds(chunks, 1))


def scan_call(flags, own, other, act, dt, cum):
    rows = act.shape[0]
    chunks = rows // CHUNK
    outs = [((rows, INNER), bf16), ((chunks + 1, NSTATE, INNER), bf16), (own.shape, bf16)]
    scratch = [pltpu.VMEM((NSTATE, INNER), f32)]
    operands = [view(a) for a in (own, other, act, dt, cum)]
    return streamed(scan_kernel, "scan", [flags], operands, outs, scratch, 9)


def woven(one, two):
    order = [((n + 0.5) / len(steps), k, step) for k, steps in enumerate((one, two)) for n, step in enumerate(steps)]
    for _, _, step in sorted(order, key=lambda item: item[:2]):
        step()


def middle_kernel(
    ids, lens, flags, place, nrm_ref, lat_ref, bg_ref, wg_ref, cot_ref, b_ref, a_ref, wo_ref, other_ref, before_ref,
    cum_ref, expand_ref, act_ref, y_ref, skip_ref, gain_ref, x_ref,
    out_ref, dy_ref, dg_ref, rowt_ref, pay_ref, tb_ref, ta_ref, enter_ref, runs_ref, d_lat_ref, tg_ref,
    gate_s, z_s, dh_s, hid_s, prod_s, ec_s, y_s, grad_s, tb_s, ta_s, tg_s, *, seq, ready, send,
):
    rows = act_ref.shape[0]
    block = 2 * CHUNK
    strip = 16
    tiles = [slice(t * TILE, (t + 1) * TILE) for t in range(INNER // TILE)]
    blocks = [slice(k * block, (k + 1) * block) for k in range(rows // block)]
    kept = [{} for _ in blocks]

    position = lax.broadcasted_iota(jnp.int32, (rows, 1), 0)
    valid = position < lens[seq]
    ready(nrm_ref, lat_ref, bg_ref, wg_ref)
    for cols in tiles:
        gate_s[:, cols] = dot(nrm_ref[...], wg_ref[:, cols]) + dot(lat_ref[...], bg_ref[:, cols])
    ready(cot_ref, b_ref, a_ref, gain_ref, wo_ref)
    cot_ref[...] = jnp.where(valid, cot_ref[...], jnp.zeros((), bf16))
    d_lat_t = dot_t(b_ref[...], cot_ref[...]).astype(bf16)
    d_lat = turned(d_lat_t)
    for cols in tiles:
        d_hidden = dot_t(cot_ref[...], wo_ref[cols, :]) + dot(d_lat, a_ref[:, cols])
        dh_s[:, cols] = d_hidden * gain_ref[:, cols]
    ready(other_ref, before_ref, cum_ref, expand_ref)
    before = jnp.zeros((1, LANES), f32)
    logs = []
    for c in range(rows // CHUNK):
        logs.append(cum_ref[c * CHUNK : (c + 1) * CHUNK, :] + before)
        before = logs[-1][CHUNK - 1 : CHUNK]
    runs_ref[0] = jnp.ones((1, INNER), f32)
    spread = parts_of(jnp.exp(jnp.concatenate(logs, axis=0)))
    for cols in tiles:
        enter_ref[:, cols] = state_in(flags[0], other_ref, before_ref, cols).astype(bf16)
        ec = dot(spread, expand_ref[:, cols])
        ec_s[:, cols] = ec
        for c in range(rows // CHUNK):
            runs_ref[c + 1, :, cols] = ec[(c + 1) * CHUNK - 1 : (c + 1) * CHUNK]
    send(enter_ref)
    ready(act_ref, y_ref, skip_ref)

    def project(k):
        r = blocks[k]

        def far_tile(cols):
            far = dot(act_ref[r, INNER + NSTATE :], enter_ref[:, cols]) * ec_s[r, cols]
            y_s[r, cols] = y_ref[r, cols].astype(f32) + far

        return [functools.partial(far_tile, cols) for cols in tiles]

    def forward(k):
        def one(i):
            r = slice(k * block + i * strip, k * block + (i + 1) * strip)
            total = jnp.zeros((strip, LANES), f32)
            for cols in tiles:
                gate = gate_s[r, cols]
                u = y_s[r, cols] + skip_ref[:, cols] * act_ref[r, cols].astype(f32)
                sig = sigmoid(gate)
                silu = gate * sig
                z = u * silu
                square = z * z
                total = total + square[:, :LANES] + square[:, LANES:]
                z_s[r, cols] = z
                gate_s[r, cols] = silu
                prod_s[r, cols] = u * (sig + silu * (1.0 - sig))
            root = lax.rsqrt(jnp.sum(total, -1, keepdims=True) / INNER + epsilon)
            kept[k][i] = root
            for cols in tiles:
                hid_s[r, cols] = (z_s[r, cols] * root * gain_ref[:, cols]).astype(bf16)

        return [functools.partial(one, i) for i in range(block // strip)]

    def mix(k):
        r = blocks[k]

        def latent():
            if k == 0:
                ready(x_ref)
            lat_out_t = dot_t(a_ref[...], hid_s[r, :]).astype(bf16)
            kept[k]["lat_out"] = turned(lat_out_t)
            more = dot(lat_out_t, cot_ref[r, :])
            tb_s[...] = more if k == 0 else tb_s[...] + more

        def out_tile(n):
            cols = slice(n * TILE, (n + 1) * TILE)
            mixed = dot(hid_s[r, :], wo_ref[:, cols]) + dot(kept[k]["lat_out"], b_ref[:, cols])
            x = x_ref[r, cols].astype(f32)
            out_ref[r, cols] = jnp.where(valid[r], x + mixed, 0.0).astype(bf16)

        def term_tile(cols):
            more = dot(d_lat_t[:, r], hid_s[r, cols])
            ta_s[:, cols] = more if k == 0 else ta_s[:, cols] + more

        steps = [latent] + [functools.partial(out_tile, n) for n in range(DM // TILE)]
        steps.append(lambda: send(out_ref, pl.ds(k * block, block)))
        return steps + [functools.partial(term_tile, cols) for cols in tiles]

    def backward(k):
        def one(i):
            r = slice(k * block + i * strip, k * block + (i + 1) * strip)
            total = jnp.zeros((strip, LANES), f32)
            for cols in tiles:
                both = dh_s[r, cols] * z_s[r, cols]
                total = total + both[:, :LANES] + both[:, LANES:]
            root = kept[k][i]
            back = jnp.sum(total, -1, keepdims=True) * (root * root * root) / INNER
            for cols in tiles:
                dz = dh_s[r, cols] * root - z_s[r, cols] * back
                dy = (dz * gate_s[r, cols]).astype(bf16)
                dy_ref[r, cols] = dy
                dg_ref[r, cols] = (dz * prod_s[r, cols]).astype(bf16)
                hid_s[r, cols] = (dy.astype(f32) * y_s[r, cols]).astype(bf16)

        return [functools.partial(one, i) for i in range(block // strip)]

    def finish(k):
        r = blocks[k]
        at = pl.ds(k * block, block)

        def out():
            send(dy_ref, at)
            send(dg_ref, at)
            rowt_ref[r, :] = dot_t(hid_s[r, :], expand_ref[...])
            send(rowt_ref, at)

        def state_tile(cols):
            if cols.start == 0:
                kept[k]["c_t"] = turned(act_ref[r, INNER + NSTATE :])
            scaled = (dy_ref[r, cols].astype(f32) * ec_s[r, cols]).astype(bf16)
            more = dot(kept[k]["c_t"], scaled)
            grad_s[:, cols] = more if k == 0 else grad_s[:, cols] + more

        def latent():
            d_lat_ref[:, r] = dot_t(bg_ref[...], dg_ref[r, :])
            kept[k]["lat_t"] = turned(lat_ref[r, :])

        def term_tile(cols):
            more = dot(kept[k]["lat_t"], dg_ref[r, cols])
            tg_s[:, cols] = more if k == 0 else tg_s[:, cols] + more

        steps = [out] + [functools.partial(state_tile, cols) for cols in tiles] + [latent]
        return steps + [functools.partial(term_tile, cols) for cols in tiles]

    last = len(blocks) - 1
    stages = [project, forward, mix, backward, finish]
    for turn in range(len(stages) + last):
        now = [stages[turn - k](k) for k in range(last + 1) if 0 <= turn - k < len(stages)]
        steps = now.pop(0)
        for other in now:
            order = []
            woven([functools.partial(order.append, step) for step in steps], [functools.partial(order.append, step) for step in other])
            steps = order
        for step in steps:
            step()
    pay_ref[0:NSTATE, :] = grad_s[...].astype(bf16)
    pay_ref[NSTATE:, :] = split_decay(runs_ref[rows // CHUNK])
    tb_ref[...] = tb_s[...].astype(bf16)
    ta_ref[...] = ta_s[...].astype(bf16)
    tg_ref[...] = tg_s[...].astype(bf16)
    for ref in (pay_ref, tb_ref, ta_ref, tg_ref, d_lat_ref, runs_ref):
        send(ref)


def middle_call(
    seq, ids, lens, place, flags, begun, tokens, cotangent, nrm, lat, act, cum, other, before, y, wg, in_b, wo, out_a,
    out_b, skip, gain, expand,
):
    rows = act.shape[0]
    outs = [
        ((rows, DM), bf16),
        ((rows, INNER), bf16),
        ((rows, INNER), bf16),
        ((rows, LANES), f32),
        ((NSTATE + RIM, INNER), bf16),
        ((RANK, DM), bf16),
        ((RANK, INNER), bf16),
        ((NSTATE, INNER), bf16),
        ((rows // CHUNK + 1, 1, INNER), f32),
        ((RANK, rows), f32),
        ((RANK, INNER), bf16),
    ]
    wide = pltpu.VMEM((rows, INNER), f32)
    scratch = [
        wide, wide, wide, pltpu.VMEM((rows, INNER), bf16), wide, wide, wide, pltpu.VMEM((NSTATE, INNER), f32),
        pltpu.VMEM((RANK, DM), f32), pltpu.VMEM((RANK, INNER), f32), pltpu.VMEM((RANK, INNER), f32),
    ]
    operands = [
        of_sequence(nrm, seq), of_sequence(lat, seq), of_adapter(in_b, seq, 0, INNER), wg,
        of_sequence(cotangent, seq), of_adapter(out_b, seq), of_adapter(out_a, seq), wo, view(other), view(before),
        view(cum), made(expand), view(act), view(y), view(skip), view(gain), of_sequence(tokens, seq),
    ]
    kernel = functools.partial(middle_kernel, seq=seq)
    shared = (tokens.shape[0], seq, begun)
    return streamed(kernel, "middle", [ids, lens, flags, place], operands, outs, scratch, 15, shared)


def scan_back_kernel(
    flags, other_ref, before_ref, before_other_ref, enter_ref, runs_ref, dt_ref, cum_ref, skip_ref, expand_ref, hc_ref, act_ref, dy_ref,
    dact_ref, rowt_ref, sig_ref, rate_ref, cw_ref, lat_ref, nrm_ref, bx_ref, d_lat_gate_ref,
    dx_ref, draw_ref, tail_ref, head_ref, d_lat_ref, tb_ref, ta_ref,
    grad_s, pre_s, next_s, *, ready, ready_last, send,
):
    rows = act_ref.shape[0]
    chunks = rows // CHUNK
    keep = causal(CHUNK)
    upper = causal(CHUNK).astype(f32).T
    row = lax.broadcasted_iota(jnp.int32, (CHUNK, LANES), 0)
    lane = lax.broadcasted_iota(jnp.int32, (CHUNK, LANES), 1)
    at_b = slice(INNER, INNER + NSTATE)
    at_c = slice(INNER + NSTATE, CONV_CH)
    ready(other_ref, before_ref, before_other_ref)
    for t in range(INNER // TILE):
        cols = slice(t * TILE, (t + 1) * TILE)
        grad_s[:, cols] = state_in_two(flags, other_ref, before_ref, before_other_ref, cols)
    ready(enter_ref, runs_ref)
    ready_last(hc_ref)
    next_s[...] = hc_ref[chunks].astype(f32) + runs_ref[chunks] * enter_ref[...].astype(f32)
    pre_s[:, rows : rows + 8, :] = jnp.zeros((CONV_CH // LANES, 8, LANES), f32)
    ready(dt_ref, cum_ref, skip_ref, expand_ref)
    for c in reversed(range(chunks)):
        r = slice(c * CHUNK, (c + 1) * CHUNK)
        ready_last(hc_ref, act_ref, dy_ref, dact_ref)
        b = act_ref[r, at_b]
        cc = act_ref[r, at_c]
        c_t = turned(cc)
        masked = jnp.where(keep, dot_t(cc, b), 0.0)
        dt = dt_ref[r, :]
        cum = cum_ref[r, :]
        cum_t = jnp.transpose(cum)
        masked_t = jnp.transpose(masked)
        d_scores = jnp.zeros((CHUNK, CHUNK), f32)
        d_b = jnp.zeros((CHUNK, NSTATE), f32)
        d_c = jnp.zeros((CHUNK, NSTATE), f32)
        col = jnp.zeros((CHUNK + RIM, LANES), f32)
        for t in range(INNER // LANES):
            cols = slice(t * LANES, (t + 1) * LANES)
            heads = (2 * t, 2 * t + 1)
            cums = beside(*(column(cum, head) for head in heads))
            dts = beside(*(column(dt, head) for head in heads))
            ec = jnp.exp(cums)
            w = jnp.exp(cums[CHUNK - 1 : CHUNK] - cums)
            x = act_ref[r, cols].astype(f32)
            xd = (x * dts).astype(bf16)
            dy = dy_ref[r, cols]
            dye = (dy.astype(f32) * ec).astype(bf16)
            grad = grad_s[:, cols]
            grad_low = grad.astype(bf16)
            state = hc_ref[c, :, cols].astype(f32) + runs_ref[c, :, cols] * enter_ref[:, cols].astype(f32)
            far = dot(b, grad_low) * w
            xw = (xd.astype(f32) * w).astype(bf16)
            d_b = d_b + dot_t(xw, grad_low)
            d_c = d_c + dot_t(dye, state.astype(bf16))
            end = split_decay(jnp.sum(grad * next_s[:, cols], axis=0, keepdims=True))
            next_s[:, cols] = state
            grad_s[:, cols] = grad * ec[CHUNK - 1 : CHUNK] + dot(c_t, dye)
            w1, w2 = (decays(cum, cum_t, head) for head in heads)
            back = jnp.concatenate([w1 * masked_t, w2 * masked_t], axis=1).astype(bf16)
            d_both = dot_t(dy, split_heads(xd))
            d_scores = d_scores + w1 * d_both[:, :CHUNK] + w2 * d_both[:, CHUNK:]
            d_xd = dot(back, split_heads(dy)) + far
            sums = jnp.concatenate([(d_xd * x).astype(bf16), end], axis=0)
            col = col + dot_t(sums, expand_ref[:, cols])
            d_x = d_xd * dts + skip_ref[:, cols] * dy.astype(f32)
            pre_s[t, r, :] = d_x * dact_ref[r, cols].astype(f32)
        ends = col[CHUNK : CHUNK + 1] + col[CHUNK + 1 : CHUNK + 2]
        col = col[:CHUNK]
        d_low = jnp.where(keep, d_scores, 0.0)
        d_c = d_c + dot(d_low.astype(bf16), b)
        d_b = d_b + dot(turned(d_low), cc)
        pre_s[INNER // LANES, r, :] = d_b * dact_ref[r, at_b].astype(f32)
        pre_s[INNER // LANES + 1, r, :] = d_c * dact_ref[r, at_c].astype(f32)
        if c == chunks - 1:
            ready(rowt_ref, sig_ref, rate_ref, cw_ref)
        d_cum = rowt_ref[r, :] - dt * col
        d_cum = d_cum + jnp.where(row == CHUNK - 1, ends, 0.0)
        d_log = dot_precise(upper, d_cum)
        d_raw = (d_log * rate_ref[...] + col) * sig_ref[r, :]
        draw_ref[r, :] = jnp.where(lane < HEADS, d_raw, 0.0).astype(bf16)

        strip = 64
        for t in range(CONV_CH // LANES):
            cols = slice(t * LANES, (t + 1) * LANES)
            weights = [cw_ref[j : j + 1, cols] for j in range(4)]
            for at in range(c * CHUNK, (c + 1) * CHUNK, strip):
                total = weights[3] * pre_s[t, at : at + strip, :]
                for j in range(3):
                    total = total + weights[j] * pre_s[t, at + 3 - j : at + 3 - j + strip, :]
                dx_ref[at : at + strip, cols] = total.astype(bf16)
                if at + strip == rows:
                    tail_ref[:, cols] = total[strip - RIM :, :]
        send(dx_ref, pl.ds(c * CHUNK, CHUNK))
        if c == chunks - 1:
            send(tail_ref)
    for t in range(CONV_CH // LANES):
        head_ref[:, t * LANES : (t + 1) * LANES] = pre_s[t, 0:RIM, :].astype(bf16)
    send(head_ref)
    send(draw_ref)

    ready(lat_ref, nrm_ref, bx_ref, d_lat_gate_ref)
    d_x = dx_ref[:, :INNER]
    d_lat_t = (d_lat_gate_ref[...] + dot_t(bx_ref[...], d_x)).astype(bf16)
    d_lat_ref[...] = turned(d_lat_t)
    send(d_lat_ref)
    sure = lax.broadcasted_iota(jnp.int32, (RANK, rows), 1) < rows - RIM
    lat_t = jnp.transpose(lat_ref[...].astype(f32))
    tb_ref[...] = dot(jnp.where(sure, lat_t, 0.0).astype(bf16), d_x)
    ta_ref[...] = dot(jnp.where(sure, d_lat_t.astype(f32), 0.0).astype(bf16), nrm_ref[...])
    send(tb_ref)
    send(ta_ref)


def scan_back_call(
    seq, ids, flags, other, before, before_other, act, dact, dt, cum, sig, rowt, dy, hc, enter, runs, lat, nrm, in_b, d_lat_gate, skip,
    rate, conv_w, expand,
):
    rows = act.shape[0]
    chunks = rows // CHUNK
    outs = [
        ((rows, CONV_CH), bf16),
        ((rows, LANES), bf16),
        ((RIM, CONV_CH), f32),
        ((RIM, CONV_CH), bf16),
        ((rows, RANK), bf16),
        ((RANK, INNER), f32),
        ((RANK, DM), f32),
    ]
    scratch = [
        pltpu.VMEM((NSTATE, INNER), f32),
        pltpu.VMEM((CONV_CH // LANES, rows + 8, LANES), f32),
        pltpu.VMEM((NSTATE, INNER), f32),
    ]
    operands = [view(a) for a in (other, before, before_other, enter, runs, dt, cum, skip)] + [made(expand)]
    operands += [in_parts(hc, chunks + 1), in_parts(act, chunks), in_parts(dy, chunks), in_parts(dact, chunks)]
    operands += [later(view(a)) for a in (rowt, sig, rate, conv_w)]
    operands += [later(of_sequence(lat, seq)), later(of_sequence(nrm, seq))]
    operands += [later(of_adapter(in_b, seq, INNER, INNER)), later(view(d_lat_gate))]

    def kernel(ids, flags, *refs, **calls):
        scan_back_kernel(flags, *refs, **calls)

    return streamed(kernel, "scan_back", [ids, flags], operands, outs, scratch, 19)


def terms_kernel(*refs, seqs, owners, ready, send):
    refs = list(refs)[1:]
    per = 11
    ins, outs = refs[: 1 + per * seqs], refs[1 + per * seqs :]
    cw_ref, sent_ref = ins[0], outs[-1]
    ready(cw_ref)
    row = lax.broadcasted_iota(jnp.int32, (RIM, CONV_CH), 0)
    for s in range(seqs):
        tail_ref, next_ref, bx_ref, gate_ref, lat_ref, nrm_ref, tb_ref, ta_ref, tg_ref, ob_ref, oa_ref = ins[
            1 + per * s : 1 + per * (s + 1)
        ]
        last_ref, d_lat_ref = outs[2 * s : 2 * s + 2]
        ready(*ins[1 + per * s : 1 + per * (s + 1)])
        later_rows = next_ref[...].astype(f32)
        total = tail_ref[...]
        for back in range(1, 4):
            term = jnp.zeros((1, CONV_CH), f32)
            for j in range(0, 4 - back):
                term = term + cw_ref[j : j + 1, :] * later_rows[3 - back - j : 4 - back - j, :]
            total = total + jnp.where(row == RIM - back, term, 0.0)
        last = total.astype(bf16)
        last_ref[...] = last
        d_x = last[:, :INNER]
        gate_rows = jnp.transpose(gate_ref[...])[LANES - RIM :, :]
        d_lat = (gate_rows + dot_t(d_x, bx_ref[...])).astype(bf16)
        d_lat_ref[...] = d_lat
        send(last_ref)
        send(d_lat_ref)
        in_b = (tb_ref[...] + dot(turned(lat_ref[...]), d_x)).astype(bf16)
        in_a = (ta_ref[...] + dot(turned(d_lat), nrm_ref[...])).astype(bf16)
        both = jnp.concatenate([tg_ref[...], in_b], axis=1)
        kinds = [in_a, both, oa_ref[...], ob_ref[...]]
        for d in range(owners):
            pieces = []
            for kind in kinds:
                width = kind.shape[1] // owners
                pieces.append(kind[:, d * width : (d + 1) * width])
            sent_ref[d, s] = jnp.concatenate(pieces, axis=1)
    send(sent_ref)


def terms_call(ids, conv_w, items, lat, nrm, in_b, owners):
    seqs, rows, _ = nrm.shape
    last_columns = lambda scalars, ref: ref.at[:, pl.ds(rows - LANES, LANES)]
    operands = [view(conv_w)]
    outs = []
    for s, (tail, following, d_lat_gate, tb, ta, tg, ob, oa) in enumerate(items):
        of_last = lambda scalars, ref, s=s: ref.at[s, pl.ds(rows - RIM, RIM)]
        operands += [
            view(tail), view(following), of_adapter(in_b, s, INNER, INNER), view(d_lat_gate, last_columns, (RANK, LANES)),
            view(lat, of_last, (RIM, RANK)), view(nrm, of_last, (RIM, DM)), view(tb), view(ta), view(tg), view(ob),
            view(oa),
        ]
        outs += [((RIM, CONV_CH), bf16), ((RIM, RANK), bf16)]
    width = (2 * DM + ZX + INNER) // owners
    outs.append(((owners, seqs, RANK, width), bf16))
    kernel = functools.partial(terms_kernel, seqs=seqs, owners=owners)
    return streamed(kernel, "terms", [ids], operands, outs, [], 4)


def input_back_kernel(
    ids, lens, place, dg_ref, wg_ref, last_ref, dx_ref, early_ref, draw_ref, d_lat_ref, d_lat_last_ref, a_ref,
    gain_ref, x_ref, cot_ref, out_ref, dn_s, *, seq, ready, send,
):
    rows = dx_ref.shape[0]
    block = rows // 2
    ready(dg_ref, wg_ref)
    dn_s[...] = dot_t(dg_ref[...], wg_ref[...])
    ready(last_ref, dx_ref, early_ref, draw_ref, d_lat_ref, d_lat_last_ref, a_ref)
    dx_ref[rows - RIM :, :] = last_ref[...]
    d_lat_ref[rows - RIM :, :] = d_lat_last_ref[...]
    ready(gain_ref, x_ref, cot_ref)
    strip = 32
    for k in range(0, rows, block):
        b = slice(k, k + block)
        more = dot_t(dx_ref[b, :], early_ref[:, :CONV_CH]) + dot_t(draw_ref[b, :], early_ref[:, CONV_CH:])
        dn_s[b, :] += more + dot(d_lat_ref[b, :], a_ref[...])
        for i in range(k, k + block, strip):
            r = slice(i, i + strip)
            x = x_ref[r, :].astype(f32)
            root = lax.rsqrt(jnp.mean(x * x, -1, keepdims=True) + epsilon)
            dn = dn_s[r, :] * gain_ref[...]
            back = jnp.mean(dn * x, -1, keepdims=True) * (root * root * root)
            position = i + lax.broadcasted_iota(jnp.int32, (strip, 1), 0)
            kept = jnp.where(position < lens[seq], cot_ref[r, :].astype(f32), 0.0)
            out_ref[r, :] = dn * root - x * back + kept
        send(out_ref, pl.ds(k, block))


def input_back_call(seq, ids, lens, place, begun, tokens, cotangent, dg, last, dx, draw, d_lat, d_lat_last, wg, early, in_a, gain):
    rows = dx.shape[0]
    outs = [((rows, DM), f32)]
    operands = [view(dg), wg, view(last), view(dx), early, view(draw), view(d_lat), view(d_lat_last)]
    operands += [of_adapter(in_a, seq), view(gain), of_sequence(tokens, seq), of_sequence(cotangent, seq)]
    kernel = functools.partial(input_back_kernel, seq=seq)
    scratch = [pltpu.VMEM((rows, DM), f32)]
    shared = (tokens.shape[0], seq, begun)
    return streamed(kernel, "input_back", [ids, lens, place], operands, outs, scratch, 9, shared)[0]


def shifted(value, axis, steps):
    count = lax.axis_size(axis)
    pairs = [(i, i + steps) for i in range(count) if 0 <= i + steps < count]
    return lax.ppermute(value, axis, pairs)


def swapped(value, axis, bit):
    return lax.ppermute(value, axis, [(i, i ^ bit) for i in range(lax.axis_size(axis))])


def after(value, other):
    return lax.optimization_barrier((value, other))[0]


def my_half(shard, core, half):
    return lax.dynamic_slice_in_dim(shard, core * half, half, 0)


def gathered_early(meanwhile, shard):
    owners = lax.axis_size("dp")
    rows, width = shard.shape
    half = rows // 2
    shapes = [(rows * owners, CONV_CH), (rows * owners, LANES)]
    if half % 16 or owners % 2:
        full = lax.all_gather(shard, "dp", axis=0, tiled=True)
        return view(full[:, :CONV_CH]), view(full[:, CONV_CH:]), view(full), None
    core = lax.axis_index("ctx") % 2
    own = {0: my_half(shard, core, half)}
    for k in range(2, owners, 2):
        own[k] = swapped(own[0], "dp", k)
    own[1] = swapped(own[0], "dp", 1)
    for k in range(2, owners, 2):
        waits = (own[min(3, k - 1)], meanwhile) if k == owners - 2 else own[1]
        own[k + 1] = swapped(after(own[k], waits), "dp", 1)
    pieces = [own[k] for k in range(owners)] + [swapped(own[k], "ctx", 1) for k in range(owners)]

    def copies(scalars, refs, to, columns):
        place = scalars[-1]
        pairs = []
        for n, piece in enumerate(refs):
            side = place[1] if n < owners else 1 - place[1]
            at = pl.multiple_of((place[0] ^ (n % owners)) * rows + side * half, 16)
            pairs.append((piece.at[:, columns], to.at[pl.ds(at, half)]))
        return pairs

    main = functools.partial(copies, columns=pl.ds(0, CONV_CH))
    rest = functools.partial(copies, columns=pl.ds(CONV_CH, LANES))
    all_columns = functools.partial(copies, columns=pl.ds(0, width))
    arrived = (tuple(own[k] for k in range(2, owners, 2)), own[owners - 1])
    both = Operand(pieces, (rows * owners, width), all_columns)
    return Operand(pieces, shapes[0], main), Operand(pieces, shapes[1], rest), both, arrived


def gathered_late(gate, out, arrived, fronts, scans, befores):
    owners = lax.axis_size("dp")
    rows = gate.shape[0]
    half = rows // 2
    if arrived is None:
        return (
            view(lax.all_gather(gate, "dp", axis=0, tiled=True)),
            view(lax.all_gather(out, "dp", axis=0, tiled=True)),
        )
    core = lax.axis_index("ctx") % 2
    mine = my_half(jnp.concatenate([gate, out[:rows], out[rows:]], axis=1), core, half)
    own = {0: mine}
    for k in range(2, owners, 2):
        own[k] = swapped(after(mine, arrived[0][0] if k == 2 else arrived[0]), "dp", k)
    for k in range(0, owners, 2):
        waits = arrived[1] if k <= 2 else fronts[-1][5]
        own[k + 1] = swapped(after(own[k], waits), "dp", 1)
    pieces = [own[k] for k in range(owners)]
    hold = (scans[-1][0], befores[0])
    pieces += [swapped(after(own[k], scans[0][0] if k < 4 else hold), "ctx", 1) for k in range(owners)]

    def placed(scalars, refs):
        place = scalars[-1]
        for n, piece in enumerate(refs):
            side = place[1] if n < owners else 1 - place[1]
            yield piece, place[0] ^ (n % owners), side * half

    def gate_copies(scalars, refs, to):
        pairs = []
        for piece, owner, start in placed(scalars, refs):
            at = pl.multiple_of(owner * rows + start, 16)
            pairs.append((piece.at[:, pl.ds(0, INNER)], to.at[pl.ds(at, half)]))
        return pairs

    def out_copies(scalars, refs, to):
        pairs = []
        for piece, owner, start in placed(scalars, refs):
            for k in range(2):
                at = pl.multiple_of((2 * owner + k) * rows + start, 16)
                pairs.append((piece.at[:, pl.ds(INNER + k * DM, DM)], to.at[pl.ds(at, half)]))
        return pairs

    return (
        Operand(pieces, (rows * owners, INNER), gate_copies),
        Operand(pieces, (2 * rows * owners, DM), out_copies),
    )


def join_kernel(swap, one_ref, two_ref, out_ref, *, ready, send):
    ready(one_ref, two_ref)
    join_payloads(swap[0], one_ref, two_ref, out_ref)
    send(out_ref)


def joined(one, two, swap):
    return streamed(join_kernel, "join", [swap], [view(one), view(two)], [(one.shape, bf16)], [], 1)[0]


def state_in_two(flags, other_ref, far_ref, far_other_ref, cols):
    far, far_other, other = (ref[0:NSTATE, cols].astype(f32) for ref in (far_ref, far_other_ref, other_ref))
    behind = decay_of(far_ref, cols) * far_other + far
    ahead = decay_of(far_other_ref, cols) * far + far_other
    before = jnp.where(flags[1] == 1, behind, ahead)
    return jnp.where(flags[0] == 1, decay_of(other_ref, cols) * before + other, before)


def from_before(both, reverse):
    chips = lax.axis_size("ctx") // 2
    sign = -1 if reverse else 1
    in_order = jnp.zeros((1,), jnp.int32)
    before = shifted(both, "ctx", 2 * sign)
    step, run = 1, both
    while 2 * step < chips:
        run = joined(before, both, in_order) if step == 1 else joined(far, run, in_order)
        far = shifted(run, "ctx", 4 * step * sign)
        before = joined(far, before, in_order)
        step *= 2
    return before


def shards(
    tokens, cotangent, lengths, adapter_ids, norm_gain, w_in, conv_weight, conv_bias, dt_bias, a_log,
    skip_scale, inner_gain, w_out, in_a, in_b, out_a, out_b,
):
    seqs, slots, _ = tokens.shape
    owners = lax.axis_size("dp")
    ids = adapter_ids
    lens = jnp.clip(lengths - lax.axis_index("ctx") * slots, 0, slots).astype(jnp.int32)

    def grouped(row):
        padded = jnp.pad(row.reshape(-1, HEADS), ((0, 0), (0, GROUP - HEADS)))
        return jnp.tile(padded, (1, LANES // GROUP))

    rate = grouped(-jnp.exp(a_log))
    dtb = grouped(dt_bias)
    lane = jnp.arange(LANES)[:, None]
    head = jnp.arange(INNER)[None, :] // HDIM
    expand = ((lane % GROUP == head) & (lane < 3 * GROUP)).astype(bf16)
    skip = jnp.repeat(skip_scale, HDIM)[None, :]
    gain = inner_gain[None, :]
    n_gain = norm_gain[None, :]
    conv_b = conv_bias[None, :]

    marks = jnp.broadcast_to(ids.astype(bf16)[None, :], (w_in.shape[0], seqs))
    marks = jnp.pad(marks, ((0, 0), (0, GROUP - HEADS - seqs)))
    steps = jnp.concatenate([w_in[:, INNER + CONV_CH :], marks], axis=1)
    in_a, out_a = jnp.swapaxes(in_a, 1, 2), jnp.swapaxes(out_a, 1, 2)
    rim = shifted(tokens[:, slots - RIM :], "ctx", 1)
    nrm, nrim, lat, lrim = norm_call(ids, tokens, rim, n_gain, in_a)
    wx, wdt, early_all, arrived = gathered_early(
        nrm,
        jnp.concatenate([w_in[:, INNER : INNER + CONV_CH]] + [steps] * (LANES // GROUP), axis=1)
    )

    core = lax.axis_index("ctx") % 2
    place = jnp.stack([lax.axis_index("dp"), core]).astype(jnp.int32)
    late = core.reshape(1).astype(jnp.int32)
    early = 1 - late
    front = functools.partial(
        front_call, in_b=in_b, wx=wx, wdt=wdt, conv_w=conv_weight, conv_b=conv_b, dtb=dtb, rate=rate, expand=expand
    )
    nrm, (skip, gain, lens, late, early) = lax.optimization_barrier((nrm, (skip, gain, lens, late, early)))
    chips = lax.axis_size("ctx") // 2
    flags_back = jnp.concatenate([early, early if chips == 2 else jnp.ones_like(early)])
    fronts, others = [], []
    for s in range(seqs):
        ready = nrm if s == 0 else after(nrm, fronts[-1][5])
        fronts.append(front(s, ids, place, ready, nrim, lat, lrim))
        others.append(swapped(fronts[s][5], "ctx", 1))
    scans, befores = [], []
    for s in range(seqs):
        act, _, dt, cum, _, own, _ = fronts[s]
        ready = after(act, fronts[-1][5]) if s == 0 else after(act, scans[-1][0])
        scans.append(scan_call(late, own, others[s], ready, dt, cum))
        befores.append(from_before(scans[s][2], False))
    full_gate, full_out = gathered_late(w_in[:, :INNER], w_out, arrived, fronts, scans, befores)
    middles, other_grads, later_grads = [], [], []
    for s in range(seqs):
        act, _, _, cum, _, _, _ = fronts[s]
        ready = after(nrm, scans[-1][0] if s == 0 else middles[-1][4])
        middles.append(
            middle_call(
                s, ids, lens, place, late, middles[-1][0] if s else None, tokens, cotangent, ready, lat, act, cum,
                others[s], befores[s], scans[s][0], full_gate, in_b, full_out, out_a, out_b, skip, gain, expand,
            )
        )
        payload = after(middles[s][4], later_grads[-1] if s and chips > 2 else befores[-1])
        other_grads.append(swapped(payload, "ctx", 1))
        if chips == 2:
            later_grads.append(shifted(payload, "ctx", -2))
        else:
            later_grads.append(from_before(joined(payload, other_grads[s], early), True))
    backs, nexts = [], []
    for s in range(seqs):
        act, dact, dt, cum, sig, _, _ = fronts[s]
        _, dy, _, rowt, _, _, _, enter, runs, d_lat_gate, _ = middles[s]
        hold = middles[-1][4] if s == 0 else backs[-1][3]
        ready = after(act, hold)
        later_other = swapped(after(later_grads[s], hold), "ctx", 1) if chips == 2 else jnp.zeros_like(later_grads[s])
        backs.append(
            scan_back_call(
                s, ids, flags_back, other_grads[s], later_grads[s], later_other, ready, dact, dt, cum, sig, rowt, dy, scans[s][1], enter,
                runs, lat, nrm, in_b, d_lat_gate, skip, rate, conv_weight, expand,
            )
        )
        nexts.append(shifted(backs[s][3], "ctx", -1))
    items = [
        (back[2], following, mid[9], back[5], back[6], mid[10], mid[5], mid[6])
        for back, following, mid in zip(backs, nexts, middles)
    ]
    *lasts, sent = terms_call(ids, conv_weight, items, lat, nrm, in_b, owners)

    widths = [width // owners for width in (DM, ZX, INNER, DM)]
    got = lax.all_to_all(sent, "dp", 0, 0)
    held = after(tokens, sent)
    input_grad = None
    for s in range(seqs):
        if s == 1:
            got = after(got, input_grad)
        input_grad = input_back_call(
            s, ids, lens, place, input_grad, held, cotangent, middles[s][2], lasts[2 * s], backs[s][0], backs[s][1],
            backs[s][4], lasts[2 * s + 1], full_gate, early_all, in_a, n_gain,
        )
    every = fronts[0][6][:, HEADS : HEADS + seqs].reshape(1, -1)
    chosen = (every == jnp.arange(ADAPT, dtype=f32)[:, None]).astype(f32)
    flat = got.reshape(owners * seqs, -1).astype(f32)
    mine = jnp.sum(chosen[:, :, None] * flat[None], axis=1)
    if lax.axis_size("ctx") == 4:
        low = mine.astype(bf16)
        mine = mine + sum(swapped(low, "ctx", bits).astype(f32) for bits in (1, 2, 3))
    else:
        bit = 1
        while bit < lax.axis_size("ctx"):
            mine = mine + swapped(mine.astype(bf16), "ctx", bit).astype(f32)
            bit *= 2
    mine = mine.reshape(ADAPT, RANK, -1)
    cuts = [sum(widths[:k]) for k in range(5)]
    g_ia, g_ib, g_oa, g_ob = (mine[:, :, cuts[k] : cuts[k + 1]] for k in range(4))
    return (
        middles[-1][0],
        input_grad,
        jnp.swapaxes(g_ia, 1, 2),
        g_ib,
        jnp.swapaxes(g_oa, 1, 2),
        g_ob,
    )


def solution(mesh):
    split = P("dp", "ctx", None)
    return jax.shard_map(
        shards,
        mesh=mesh,
        in_specs=(
            split, split, P("dp"), P("dp"), P(), P("dp", None), P(), P(), P(), P(), P(), P(),
            P("dp", None), P(), P(), P(), P(),
        ),
        out_specs=(
            split, split, P(None, "dp", None), P(None, None, "dp"), P(None, "dp", None), P(None, None, "dp"),
        ),
        check_vma=False,
    )
```
